32 devices in a mesh: dp: 8 (over z, y), tensor: 4 (over x, core).
Axes of the slice: x: 2, y: 2, z: 4, core: 2. Of those that a mesh axis runs over, the one named last changes fastest.
Arguments:
- tokens: bfloat16 [32768, 768], P(('dp', 'tensor')), may hold values from -6 to 6
- cotangent: bfloat16 [32768, 768], P(('dp', 'tensor')), may hold values from -6 to 6
- segments: int32 [64, 512], P('dp'), may hold values from 0 to 3, never falling along the last dimension, each value on 1 to 256 neighbouring positions
- qkv_weight: float32 [3, 768, 768], P(None, 'dp', 'tensor'), may hold values from -0.21875 to 0.21875
- out_weight: float32 [768, 768], P('tensor', 'dp'), may hold values from -1.75 to 1.75
- inner_weight: float32 [768, 3072], P('dp', 'tensor'), may hold values from -0.21875 to 0.21875
- outer_weight: float32 [3072, 768], P('tensor', 'dp'), may hold values from -0.109375 to 0.109375
- vectors: float32 [12, 768], P(None, ('dp', 'tensor')), may hold values from -1 to 3
- qkv_mean: float32 [3, 768, 768], P(None, 'dp', 'tensor'), may hold values from -512 to 512
- out_mean: float32 [768, 768], P('tensor', 'dp'), may hold values from -224 to 224
- inner_mean: float32 [768, 3072], P('dp', 'tensor'), may hold values from -512 to 512
- outer_mean: float32 [3072, 768], P('tensor', 'dp'), may hold values from -512 to 512
- vector_mean: float32 [12, 768], P(None, ('dp', 'tensor')), may hold values from -1024 to 1024
- qkv_square: float32 [3, 768, 768], P(None, 'dp', 'tensor'), may hold values from 8192 to 32768
- out_square: float32 [768, 768], P('tensor', 'dp'), may hold values from 1310.72 to 5242.88
- inner_square: float32 [768, 3072], P('dp', 'tensor'), may hold values from 8192 to 32768
- outer_square: float32 [3072, 768], P('tensor', 'dp'), may hold values from 8192 to 32768
- vector_square: float32 [12, 768], P(None, ('dp', 'tensor')), may hold values from 32768 to 131072
Outputs:
- layer_output: bfloat16 [32768, 768], P(('dp', 'tensor'))
- input_grad: float32 [32768, 768], P(('dp', 'tensor'))
- new_qkv_mean: float32 [3, 768, 768], P(None, 'dp', 'tensor')
- new_qkv_square: float32 [3, 768, 768], P(None, 'dp', 'tensor')
- new_qkv_weight: float32 [3, 768, 768], P(None, 'dp', 'tensor')
- new_out_mean: float32 [768, 768], P('tensor', 'dp')
- new_out_square: float32 [768, 768], P('tensor', 'dp')
- new_out_weight: float32 [768, 768], P('tensor', 'dp')
- new_inner_mean: float32 [768, 3072], P('dp', 'tensor')
- new_inner_square: float32 [768, 3072], P('dp', 'tensor')
- new_inner_weight: float32 [768, 3072], P('dp', 'tensor')
- new_outer_mean: float32 [3072, 768], P('tensor', 'dp')
- new_outer_square: float32 [3072, 768], P('tensor', 'dp')
- new_outer_weight: float32 [3072, 768], P('tensor', 'dp')
- new_vector_mean: float32 [12, 768], P(None, ('dp', 'tensor'))
- new_vector_square: float32 [12, 768], P(None, ('dp', 'tensor'))
- new_vectors: float32 [12, 768], P(None, ('dp', 'tensor'))
- lamb_norms: float32 [2, 15], replicated
The draws below stay inside these ranges and needn't reach their ends.
Inputs may be any that keep to these rules, and one draw needn't show every extreme that they name: `segments`: along a sequence the segment numbers never fall; a segment holds 1 to 256 tokens, and in every draw some segment holds exactly that many.
All inputs are finite; a program needn't handle non-finite values.
Results may differ from the reference program's by a relative error of at most 0.02.
Values may be sent and summed in bfloat16 or wider, within the bound.
A program may use at most 192 MiB of HBM per device.

```python
import math
import jax
import jax.numpy as jnp
import numpy as np
from jax import lax

D = 768
HEADS = 12
HD = 64
FF = 3072
SEQ_LEN = 512
SEQ_DEV = 8
DOCS = 4
STEP = 5
TOK_DEV = 4096
SEQS = 64
TOKENS = 32768


def draw_vectors(key, part):
    key = jax.random.fold_in(key, 11)
    row_number = 8 + FF // D
    noise_key, bias_key = jax.random.split(key, 2)
    position = jnp.arange(D, dtype=jnp.float32) / (D - 1)
    gain_ramp = 0.6 + 1.2 * position
    biases = jnp.clip(0.2 * jax.random.normal(bias_key, (row_number, D), jnp.float32), -1.0, 1.0)
    rough_factor = jax.random.uniform(noise_key, (2, D), jnp.float32, 0.8, 1.2)
    gain_rows = gain_ramp[None, :] * rough_factor
    return biases.at[0].set(gain_rows[0]).at[2].set(gain_rows[1])


def levels(rng, shape, shards, low, top_value):
    gain, own = 1.0, jax.random.fold_in(rng, 6)
    for dim, shards_of in shards:
        steps = jnp.exp(jax.random.uniform(jax.random.fold_in(own, dim), (shards_of,), jnp.float32, low / len(shards), top_value / len(shards)))
        gain = gain * jnp.repeat(steps, shape[dim] // shards_of).reshape([-1 if axis == dim else 1 for axis in range(len(shape))])
    return gain


def profile(count, total, limit, lean):
    weights = [(1 << 20) // math.isqrt(rank ** lean) + 1 for rank in range(2, count + 1)]
    spare, holding = total - limit - (count - 1), [1] * (count - 1)
    while spare > 0:
        movable = [i for i in range(count - 1) if holding[i] < limit]
        whole, left = sum([weights[i] for i in movable]), spare
        for i in movable:
            extra = min(limit - holding[i], max(1, left * weights[i] // whole), spare)
            holding[i] = holding[i] + extra
            spare = spare - extra
    return np.array([limit] + holding)


def uneven(own_key, number_of, total, bound, slope):
    if number_of == 2:
        one = jax.random.randint(own_key, (), max(1, total - bound), min(bound, total - 1) + 1)
        return jnp.stack([one, total - one])
    tallies = jnp.asarray(profile(number_of, total, bound, slope), jnp.int32)
    twos = (number_of - 1) // 2
    giver, taker = tallies[1:1 + 2 * twos:2], tallies[2:2 + 2 * twos:2]
    margin = jnp.minimum(giver - 1, bound - taker)
    passed = jax.random.randint(jax.random.fold_in(own_key, 1), (twos,), 0, 1 << 20) % (margin + 1)
    tallies = tallies.at[1:1 + 2 * twos:2].set(giver - passed).at[2:2 + 2 * twos:2].set(taker + passed)
    return tallies[jax.random.permutation(jax.random.fold_in(own_key, 2), number_of)]


def normal_values(stream_key, shape, spread, limit, cuts=(), kind=jnp.bfloat16):
    entries = jax.random.normal(stream_key, shape, jnp.float32) * spread
    if len(cuts) > 0:
        entries = levels(stream_key, shape, cuts, -0.22, 0.18) * entries
    return jnp.clip(entries, min=-limit, max=limit).astype(kind)


def setup_inputs(seed: int = 0) -> dict:
    arg_keys = jax.random.split(jax.random.key(seed), 19)
    return {
        "tokens": normal_values(arg_keys[0], (TOKENS, D), 1.0, 6.0, ((0, 32),)),
        "cotangent": normal_values(arg_keys[1], (TOKENS, D), 1.0, 6.0, ((0, 32),)),
        "segments": jax.vmap(lambda own: jnp.searchsorted(jnp.cumsum(uneven(own, DOCS, SEQ_LEN, SEQ_LEN // 2, 0)), jnp.arange(SEQ_LEN), side="right"))(jax.random.split(arg_keys[2], SEQS)).reshape((SEQS, SEQ_LEN)).astype(jnp.int32),
        "qkv_weight": normal_values(arg_keys[3], (3, D, D), D ** -0.5, 0.21875, ((1, 8), (2, 4)), jnp.float32),
        "out_weight": normal_values(arg_keys[4], (D, D), (D // 64) ** -0.5, 1.75, ((0, 4), (1, 8)), jnp.float32),
        "inner_weight": normal_values(arg_keys[5], (D, FF), D ** -0.5, 0.21875, ((0, 8), (1, 4)), jnp.float32),
        "outer_weight": normal_values(arg_keys[6], (FF, D), FF ** -0.5, 0.109375, ((0, 4), (1, 8)), jnp.float32),
        "vectors": draw_vectors(jax.random.fold_in(arg_keys[18], 71), 0),
        "qkv_mean": normal_values(arg_keys[8], (3, D, D), (0.5 * TOKENS ** 0.5), 512.0, ((1, 8), (2, 4)), jnp.float32),
        "out_mean": normal_values(arg_keys[9], (D, D), (0.2 * TOKENS ** 0.5), 224.0, ((0, 4), (1, 8)), jnp.float32),
        "inner_mean": normal_values(arg_keys[10], (D, FF), (0.5 * TOKENS ** 0.5), 512.0, ((0, 8), (1, 4)), jnp.float32),
        "outer_mean": normal_values(arg_keys[11], (FF, D), (0.5 * TOKENS ** 0.5), 512.0, ((0, 4), (1, 8)), jnp.float32),
        "vector_mean": normal_values(arg_keys[12], (8 + FF // D, D), (1.0 * TOKENS ** 0.5), 1024.0, ((1, 32),), jnp.float32),
        "qkv_square": jnp.clip(jnp.exp(math.log(32768.0) - 1.3862944 * jax.random.uniform(arg_keys[13], (3, D, D), jnp.float32) ** levels(arg_keys[13], (3, D, D), ((1, 8), (2, 4)), -0.2, 0.2)), 8192.0, 32768.0),
        "out_square": jnp.clip(jnp.exp(math.log(5242.88) - 1.3862944 * jax.random.uniform(arg_keys[14], (D, D), jnp.float32) ** levels(arg_keys[14], (D, D), ((0, 4), (1, 8)), -0.2, 0.2)), 1310.72, 5242.88),
        "inner_square": jnp.clip(jnp.exp(math.log(32768.0) - 1.3862944 * jax.random.uniform(arg_keys[15], (D, FF), jnp.float32) ** levels(arg_keys[15], (D, FF), ((0, 8), (1, 4)), -0.2, 0.2)), 8192.0, 32768.0),
        "outer_square": jnp.clip(jnp.exp(math.log(32768.0) - 1.3862944 * jax.random.uniform(arg_keys[16], (FF, D), jnp.float32) ** levels(arg_keys[16], (FF, D), ((0, 4), (1, 8)), -0.2, 0.2)), 8192.0, 32768.0),
        "vector_square": jnp.clip(jnp.exp(math.log(131072.0) - 1.3862944 * jax.random.uniform(arg_keys[17], (8 + FF // D, D), jnp.float32) ** levels(arg_keys[17], (8 + FF // D, D), ((1, 32),), -0.2, 0.2)), 32768.0, 131072.0),
    }


HIGHEST = lax.Precision.HIGHEST
NORM_EPS = 1e-05
ADAM_EPS = 1e-06
MOMENT_DECAY = 0.5
LEARN_RATE = 0.5
WEIGHT_DECAY = 0.01
MASKED = -1e+30

@jax.custom_vjp
def low(v):
    return lax.optimization_barrier(v.astype(jnp.bfloat16)).astype(jnp.float32)

@jax.custom_vjp
def low_back(v):
    return v

def low_keep(v):
    return (low(v), None)

def low_pass(kept, grad):
    return (grad,)

def back_keep(v):
    return (v, None)

def back_low(kept, grad):
    return (low(grad),)
low.defvjp(low_keep, low_pass)
low_back.defvjp(back_keep, back_low)

def layer_norm(values, gain_row, shift_row):
    row_mean = lax.optimization_barrier(jnp.mean(values, axis=-1, keepdims=True))
    centred = values - row_mean
    row_var = lax.optimization_barrier(jnp.mean(centred * centred, axis=-1, keepdims=True))
    return centred * lax.rsqrt(row_var + NORM_EPS) * gain_row + shift_row

def attend(query_rows, key_rows, value_rows, seg_rows):
    scores = jnp.einsum('sqhe,skhe->shqk', query_rows, key_rows, precision=HIGHEST) * HD ** (-0.5)
    same_doc = (seg_rows[:, :, None] == seg_rows[:, None, :])[:, None, :, :]
    scores = low_back(jnp.where(same_doc, scores, MASKED))
    row_max = lax.optimization_barrier(jnp.max(scores, axis=-1, keepdims=True))
    expo_terms = jnp.exp(scores - row_max)
    attn_probs = expo_terms / lax.optimization_barrier(jnp.sum(expo_terms, axis=-1, keepdims=True))
    return jnp.einsum('shqk,skhe->sqhe', low(attn_probs), value_rows, precision=HIGHEST)

def layer(rows_in, seg_rows, qkv_weight, out_weight, inner_weight, outer_weight, vectors):
    token_count = rows_in.shape[0]
    seq_count = token_count // SEQ_LEN
    zero_row = jnp.zeros_like(vectors[6])
    proj_bias = jnp.stack([vectors[6], zero_row, vectors[7]])
    projected = jnp.einsum('td,kdc->ktc', rows_in, low(qkv_weight), precision=HIGHEST)
    projected = low(low_back(projected + proj_bias[:, None, :]))
    split_heads = projected.reshape(3, seq_count, SEQ_LEN, HEADS, HD)
    attn_mixed = jax.checkpoint(attend)(split_heads[0], split_heads[1], split_heads[2], seg_rows)
    attn_mixed = low(low_back(attn_mixed.reshape(token_count, D)))
    branch = low_back(jnp.dot(attn_mixed, low(out_weight), precision=HIGHEST))
    normed = layer_norm(rows_in + branch + vectors[4], vectors[0], vectors[1])
    inner_pre = jnp.dot(low(normed), low(inner_weight), precision=HIGHEST) + vectors[8:].reshape(FF)
    inner_pre = low_back(inner_pre)
    hidden = low(jax.nn.gelu(inner_pre, approximate=False))
    second_branch = low_back(jnp.dot(hidden, low(outer_weight), precision=HIGHEST))
    return layer_norm(normed + second_branch + vectors[5], vectors[2], vectors[3])

def adam_direction(grad_sum, old_mean, old_square):
    new_mean = MOMENT_DECAY * old_mean + (1.0 - MOMENT_DECAY) * grad_sum
    new_square = MOMENT_DECAY * old_square + (1.0 - MOMENT_DECAY) * grad_sum * grad_sum
    correction = 1.0 - MOMENT_DECAY ** STEP
    direction = new_mean / correction / (jnp.sqrt(new_square / correction) + ADAM_EPS)
    return (new_mean, new_square, direction)

def group_squares(qkv_part, out_part, inner_part, outer_part, vector_part):
    return jnp.concatenate([lax.optimization_barrier(jnp.sum(qkv_part * qkv_part, axis=(1, 2))), jnp.sum(out_part * out_part)[None], jnp.sum(inner_part * inner_part)[None], jnp.sum(outer_part * outer_part)[None], lax.optimization_barrier(jnp.sum(vector_part[:8] * vector_part[:8], axis=1)), jnp.sum(vector_part[8:] * vector_part[8:])[None]])

def lamb_apply(weight_list, update_list, trust_ratio, row_number):
    qkv_new = weight_list[0] - LEARN_RATE * trust_ratio[0:3, None, None] * update_list[0]
    out_new = weight_list[1] - LEARN_RATE * trust_ratio[3] * update_list[1]
    inner_new = weight_list[2] - LEARN_RATE * trust_ratio[4] * update_list[2]
    outer_new = weight_list[3] - LEARN_RATE * trust_ratio[5] * update_list[3]
    row_ratio = jnp.concatenate([trust_ratio[6:14], jnp.broadcast_to(trust_ratio[14], (row_number - 8,))])
    vector_new = weight_list[4] - LEARN_RATE * row_ratio[:, None] * update_list[4]
    return (qkv_new, out_new, inner_new, outer_new, vector_new)

def reference(tokens, cotangent, segments, qkv_weight, out_weight, inner_weight, outer_weight, vectors, qkv_mean, out_mean, inner_mean, outer_mean, vector_mean, qkv_square, out_square, inner_square, outer_square, vector_square):
    params = (qkv_weight, out_weight, inner_weight, outer_weight, vectors)
    group_count = TOKENS // TOK_DEV
    token_blocks = tokens.astype(jnp.float32).reshape(group_count, TOK_DEV, D)
    back_blocks = cotangent.astype(jnp.float32).reshape(group_count, TOK_DEV, D)
    seg_blocks = segments.reshape(group_count, SEQ_DEV, SEQ_LEN)

    def one_group(totals, group_data):
        rows_in, back_rows, seg_rows = group_data

        def forward(row_values, *weight_list):
            return layer(row_values, seg_rows, *weight_list)
        result, pull_back = jax.vjp(forward, rows_in, *params)
        grad_list = pull_back(back_rows)
        totals = tuple((total + grad_part for total, grad_part in zip(totals, grad_list[1:])))
        return (totals, (result.astype(jnp.bfloat16), grad_list[0]))
    zero_grads = tuple((jnp.zeros_like(param_array) for param_array in params))
    grad_sums, (outputs, input_grads) = lax.scan(one_group, zero_grads, (token_blocks, back_blocks, seg_blocks))
    old_means = (qkv_mean, out_mean, inner_mean, outer_mean, vector_mean)
    old_squares = (qkv_square, out_square, inner_square, outer_square, vector_square)
    decays = (WEIGHT_DECAY, WEIGHT_DECAY, WEIGHT_DECAY, WEIGHT_DECAY, 0.0)
    adam_stats = [adam_direction(grad_sums[index], old_means[index], old_squares[index]) for index in range(5)]
    updates = [adam_stats[index][2] + decays[index] * params[index] for index in range(5)]
    weight_norms = jnp.sqrt(group_squares(*params))
    update_norms = jnp.sqrt(group_squares(*updates))
    trust_ratio = weight_norms / (update_norms + ADAM_EPS)
    new_weights = lamb_apply(params, updates, trust_ratio, vectors.shape[0])
    return (outputs.reshape(TOKENS, D), input_grads.reshape(TOKENS, D), adam_stats[0][0], adam_stats[0][1], new_weights[0], adam_stats[1][0], adam_stats[1][1], new_weights[1], adam_stats[2][0], adam_stats[2][1], new_weights[2], adam_stats[3][0], adam_stats[3][1], new_weights[3], adam_stats[4][0], adam_stats[4][1], new_weights[4], jnp.stack([weight_norms, update_norms]))
```

```python
import functools

import jax
import jax.numpy as jnp
from jax import lax
from jax.experimental import pallas as pl
from jax.experimental.pallas import tpu as pltpu
from jax.sharding import PartitionSpec as P

HD = 64
STEP = 5
NORM_EPS = 1e-05
ADAM_EPS = 1e-06
MOMENT_DECAY = 0.5
LEARN_RATE = 0.5
WEIGHT_DECAY = 0.01
MASKED = -1e30
SCALE = HD ** (-0.5)
F32 = jnp.float32
BF16 = jnp.bfloat16
NT = (((1,), (1,)), ((), ()))
NN = (((1,), (0,)), ((), ()))
TN = (((0,), (0,)), ((), ()))
VMEM_LIMIT = 60 * 1024 * 1024


def dot(a, b, dims=NN):
    return lax.dot_general(a, b, dims, preferred_element_type=F32)


def params(**kw):
    return pltpu.CompilerParams(vmem_limit_bytes=VMEM_LIMIT, **kw)


HEADS = 3
DOCS = 4
LANES = 768
Q_AT, K_AT, V_AT, O_AT = (0, 64, 384), (128, 192, 640), (256, 320, 448), (512, 576, 704)
Q_TILE, K_TILE, V_TILE = (0, 0, 3), (1, 1, 5), (2, 2, 3)
UPPER = (False, True, False)
V_UPPER = (False, True, True)


def spread(q, k, v, o):
    parts = {}
    for places, values in ((Q_AT, q), (K_AT, k), (V_AT, v), (O_AT, o)):
        for h, at in enumerate(places):
            parts[at] = values[:, h * HD : (h + 1) * HD]
    return jnp.concatenate([parts[at] for at in sorted(parts)], axis=1)


def collect(values, places):
    return jnp.concatenate([values[:, at : at + HD] for at in places], axis=1)


def tile_of(ref, n, rows=slice(None)):
    return ref[rows, n * 128 : (n + 1) * 128]


def is_low(shape):
    return lax.broadcasted_iota(jnp.int32, shape, 1) < HD


def halves(low, high):
    return jnp.where(is_low(low.shape), low, high)


def document_lanes(row):
    length = row.shape[1]
    number = jnp.broadcast_to(row.astype(F32), (128, length)).T
    lane = lax.broadcasted_iota(jnp.int32, (length, 128), 1) % HD
    same = number == lane.astype(F32)
    for_query = jnp.where(same, 1.0, 0.0).astype(BF16)
    for_key = jnp.where(same, 0.0, jnp.where(lane < DOCS, MASKED, 0.0)).astype(BF16)
    return for_query, for_key


def attend_heads(pm_ref, row, lse_ref, chunk):
    length = pm_ref.shape[0]
    chunks = length // chunk
    doc_q, doc_k = document_lanes(row)
    ones = jnp.ones((16, length), BF16)
    units = [(h, c) for h in range(HEADS) for c in range(chunks)]
    keys, queries, values = {}, {}, {}
    for h in range(HEADS):
        q, k = tile_of(pm_ref, Q_TILE[h]) * SCALE, tile_of(pm_ref, K_TILE[h])
        queries[h] = halves(doc_q, q) if UPPER[h] else halves(q, doc_q)
        keys[h] = halves(doc_k, k) if UPPER[h] else halves(k, doc_k)
        vt = tile_of(pm_ref, V_TILE[h]).T
        vt = vt[HD:] if V_UPPER[h] else vt[:HD]
        values[h] = jnp.concatenate([vt, ones], axis=0)

    def scores(unit):
        h, c = unit
        return dot(keys[h], queries[h][c * chunk : (c + 1) * chunk], NT)

    outs = {h: [] for h in range(HEADS)}
    ahead = scores(units[0])
    for n, (h, c) in enumerate(units):
        s = ahead
        if n + 1 < len(units):
            ahead = scores(units[n + 1])
        m = jnp.max(s, axis=0, keepdims=True)
        p = jnp.exp(s - m).astype(BF16)
        ot = dot(values[h], p)
        total = ot[HD : HD + 1]
        outs[h].append((ot[:HD] * (1.0 / total)).astype(BF16))
        lse_ref[0, 0, h : h + 1, c * chunk : (c + 1) * chunk] = m + jnp.log(total)
    out = [jnp.concatenate(outs[h], axis=1) for h in range(HEADS)]
    pm_ref[:, 512:640] = jnp.concatenate([out[0], out[1]], axis=0).T
    last = jnp.concatenate([jnp.zeros_like(out[2]), out[2]], axis=0).T
    pm_ref[:, 640:768] = halves(tile_of(pm_ref, 5), last)


def attend_fwd_kernel(x_ref, w_ref, bias_ref, seg_ref, pm_ref, lse_ref, *, chunk):
    proj = dot(x_ref[...], w_ref[0]) + bias_ref[0, 0:1, :]
    pm_ref[0] = proj.astype(BF16)
    attend_heads(pm_ref.at[0], seg_ref[0, 0:1], lse_ref, chunk)


def attend_fwd(x, wa, bias, seg, length):
    tokens, width = x.shape
    groups, _, lanes = wa.shape
    seqs = tokens // length
    return pl.pallas_call(
        functools.partial(attend_fwd_kernel, chunk=min(256, length)),
        grid=(groups, seqs),
        in_specs=[
            pl.BlockSpec((length, width), lambda t, s: (s, 0)),
            pl.BlockSpec((1, width, lanes), lambda t, s: (t, 0, 0)),
            pl.BlockSpec((1, 8, lanes), lambda t, s: (t, 0, 0)),
            pl.BlockSpec((1, 8, length), lambda t, s: (s, 0, 0)),
        ],
        out_specs=[
            pl.BlockSpec((1, length, lanes), lambda t, s: (t, s, 0)),
            pl.BlockSpec((1, 1, 8, length), lambda t, s: (t, s, 0, 0)),
        ],
        out_shape=[
            jax.ShapeDtypeStruct((groups, tokens, lanes), BF16),
            jax.ShapeDtypeStruct((groups, seqs, 8, length), F32),
        ],
        compiler_params=params(),
        name="attend_fwd",
    )(x, wa, bias, seg)


def attend_back(pm_ref, gm_ref, lse_ref, row, gp_ref, chunk):
    length = pm_ref.shape[0]
    chunks = length // chunk
    prod = gm_ref[...].astype(F32) * pm_ref[:, 512:768].astype(F32)
    hi = prod.astype(BF16)
    lo = (prod - hi.astype(F32)).astype(BF16)
    lane = lax.broadcasted_iota(jnp.int32, (8, 256), 1)
    line = lax.broadcasted_iota(jnp.int32, (8, 256), 0)
    start = jnp.where(line == 2, O_AT[2] - 512, line * HD)
    pick = jnp.where((lane >= start) & (lane < start + HD) & (line < HEADS), 1.0, 0.0).astype(BF16)
    dsum = dot(pick, hi, NT) + dot(pick, lo, NT)
    doc_q, doc_k = document_lanes(row)
    none = jnp.zeros((length, 128), BF16)
    units = [(h, c) for h in range(HEADS) for c in range(chunks)]
    keys, queries, plain, values, kts, grads = {}, {}, {}, {}, {}, {}
    for h in range(HEADS):
        q, k = tile_of(pm_ref, Q_TILE[h]) * SCALE, tile_of(pm_ref, K_TILE[h])
        plain[h] = q
        queries[h] = halves(doc_q, q) if UPPER[h] else halves(q, doc_q)
        keys[h] = halves(doc_k, k) if UPPER[h] else halves(k, doc_k)
        kt = k.T
        kts[h] = kt[HD:] if UPPER[h] else kt[:HD]
        v = tile_of(pm_ref, V_TILE[h])
        values[h] = halves(none, v) if V_UPPER[h] else halves(v, none)
        grads[h] = tile_of(gm_ref, 0 if h < 2 else 1)

    def rows_of(c):
        return slice(c * chunk, (c + 1) * chunk)

    def products(unit):
        h, c = unit
        return dot(keys[h], queries[h][rows_of(c)], NT), dot(values[h], grads[h][rows_of(c)], NT)

    dqs = {h: [] for h in range(HEADS)}
    dks, dvs = {}, {}
    ahead = products(units[0])
    for n, (h, c) in enumerate(units):
        s, dp = ahead
        if n + 1 < len(units):
            ahead = products(units[n + 1])
        rows = rows_of(c)
        p = jnp.exp(s - lse_ref[0, 0, h : h + 1, rows])
        ds = (p * (dp - dsum[h : h + 1, rows])).astype(BF16)
        dv = dot(p.astype(BF16), grads[h][rows])
        dk = dot(ds, plain[h][rows])
        dvs[h] = dv if c == 0 else dvs[h] + dv
        dks[h] = dk if c == 0 else dks[h] + dk
        dqs[h].append((dot(kts[h], ds) * SCALE).astype(BF16))
    dq = [jnp.concatenate(dqs[h], axis=1) for h in range(HEADS)]
    gp_ref[:, 0:128] = jnp.concatenate([dq[0], dq[1]], axis=0).T
    gp_ref[:, 128:256] = halves(dks[0], dks[1]).astype(BF16)
    gp_ref[:, 256:384] = halves(dvs[0], dvs[1]).astype(BF16)
    last = jnp.concatenate([dq[2], jnp.zeros_like(dq[2])], axis=0).T
    gp_ref[:, 384:512] = halves(last, dvs[2].astype(BF16))
    gp_ref[:, 512:640] = tile_of(pm_ref, 4)
    gp_ref[:, 640:768] = halves(dks[2].astype(BF16), tile_of(pm_ref, 5))


def attend_bwd_kernel(pm_ref, gm_ref, lse_ref, seg_ref, gp_ref, gsum_ref, *, chunk):
    attend_back(pm_ref.at[0], gm_ref.at[0], lse_ref, seg_ref[0, 0:1], gp_ref.at[0], chunk)

    @pl.when(pl.program_id(1) == 0)
    def _():
        gsum_ref[...] = jnp.zeros_like(gsum_ref)

    gsum_ref[0, 0:1, :] += jnp.sum(gp_ref[0].astype(F32), axis=0, keepdims=True)


def attend_bwd(pm, gm, lse, seg):
    groups, tokens, lanes = pm.shape
    seqs, length = lse.shape[1], lse.shape[3]
    return pl.pallas_call(
        functools.partial(attend_bwd_kernel, chunk=min(256, length)),
        grid=(groups, seqs),
        in_specs=[
            pl.BlockSpec((1, length, lanes), lambda t, s: (t, s, 0)),
            pl.BlockSpec((1, length, gm.shape[2]), lambda t, s: (t, s, 0)),
            pl.BlockSpec((1, 1, 8, length), lambda t, s: (t, s, 0, 0)),
            pl.BlockSpec((1, 8, length), lambda t, s: (s, 0, 0)),
        ],
        out_specs=[
            pl.BlockSpec((1, length, lanes), lambda t, s: (t, s, 0)),
            pl.BlockSpec((1, 8, lanes), lambda t, s: (t, 0, 0)),
        ],
        out_shape=[
            jax.ShapeDtypeStruct((groups, tokens, lanes), BF16),
            jax.ShapeDtypeStruct((groups, 8, lanes), F32),
        ],
        compiler_params=params(),
        name="attend_bwd",
    )(pm, gm, lse, seg)


def mixed_only(tail):
    lane = lax.broadcasted_iota(jnp.int32, tail.shape, 1)
    return jnp.where((lane < 128) | (lane >= 192), tail, jnp.zeros((), BF16))


def gelu_parts(pre):
    cdf = 0.5 * (1.0 + lax.erf(pre * (2.0**-0.5)))
    pdf = jnp.exp(-0.5 * pre * pre) * 0.3989422804014327
    return pre * cdf, cdf + pre * pdf


def mean_of(values):
    return jnp.mean(values, axis=-1, keepdims=True)


def norm_parts(values):
    centred = values - mean_of(values)
    inverse = lax.rsqrt(mean_of(centred * centred) + NORM_EPS)
    return centred * inverse, inverse


def norm_back(incoming, normal, inverse, gain):
    scaled = incoming * gain
    return inverse * (scaled - mean_of(scaled) - normal * mean_of(scaled * normal))


def ffn_kernel(
    x_ref, cot_ref, pm_ref, wo_ref, wb_ref, wc_ref, vec_ref, bias_ref,
    out_ref, hid_ref, gi_ref, nl_ref, gsl_ref, gbl_ref, gb_ref, gm_ref, vg_ref, bg_ref,
    slope_ref,
):
    groups = wb_ref.shape[0]

    @pl.when(pl.program_id(0) == 0)
    def _():
        vg_ref[...] = jnp.zeros_like(vg_ref)
        bg_ref[...] = jnp.zeros_like(bg_ref)

    total = x_ref[...].astype(F32) + vec_ref[4:5, :]
    for t in range(groups):
        total = total + dot(mixed_only(pm_ref[t]), wo_ref[t], NT)
    normal_one, inverse_one = norm_parts(total)
    normed = normal_one * vec_ref[0:1, :] + vec_ref[1:2, :]
    low = normed.astype(BF16)
    nl_ref[...] = low
    second = normed + vec_ref[5:6, :]
    for t in range(groups):
        pre = dot(low, wb_ref[t]) + bias_ref[t : t + 1, :]
        act, slope = gelu_parts(pre)
        act = act.astype(BF16)
        hid_ref[t] = act
        slope_ref[t] = slope
        second = second + dot(act, wc_ref[t], NT)
    normal_two, inverse_two = norm_parts(second)
    out_ref[...] = (normal_two * vec_ref[2:3, :] + vec_ref[3:4, :]).astype(BF16)
    cot = cot_ref[...].astype(F32)
    grad_second = norm_back(cot, normal_two, inverse_two, vec_ref[2:3, :])
    vg_ref[2:3, :] += jnp.sum(cot * normal_two, axis=0, keepdims=True)
    vg_ref[3:4, :] += jnp.sum(cot, axis=0, keepdims=True)
    vg_ref[5:6, :] += jnp.sum(grad_second, axis=0, keepdims=True)
    gs_low = grad_second.astype(BF16)
    gsl_ref[...] = gs_low
    grad_normed = grad_second
    for t in range(groups):
        grad_inner = (dot(gs_low, wc_ref[t]) * slope_ref[t]).astype(BF16)
        gi_ref[t] = grad_inner
        bg_ref[t : t + 1, :] += jnp.sum(grad_inner.astype(F32), axis=0, keepdims=True)
        grad_normed = grad_normed + dot(grad_inner, wb_ref[t], NT)
    grad_branch = norm_back(grad_normed, normal_one, inverse_one, vec_ref[0:1, :])
    vg_ref[0:1, :] += jnp.sum(grad_normed * normal_one, axis=0, keepdims=True)
    vg_ref[1:2, :] += jnp.sum(grad_normed, axis=0, keepdims=True)
    vg_ref[4:5, :] += jnp.sum(grad_branch, axis=0, keepdims=True)
    gb_ref[...] = grad_branch
    gb_low = grad_branch.astype(BF16)
    gbl_ref[...] = gb_low
    for t in range(groups):
        gm_ref[t] = dot(gb_low, wo_ref[t]).astype(BF16)


def ffn(x, cot, pm, wa, wb, wc, vec, bias):
    tokens, width = x.shape
    groups, _, lanes = wa.shape
    hidden = wb.shape[2]
    tail = 256
    tile = 256
    last = lanes // tail - 1
    once = pl.Buffered(1)
    row = pl.BlockSpec((tile, width), lambda i: (i, 0))
    wide = pl.BlockSpec((groups, tile, hidden), lambda i: (0, i, 0))
    return pl.pallas_call(
        ffn_kernel,
        grid=(tokens // tile,),
        in_specs=[
            row,
            row,
            pl.BlockSpec((groups, tile, tail), lambda i: (0, i, last)),
            pl.BlockSpec((groups, width, tail), lambda i: (0, 0, last), pipeline_mode=once),
            pl.BlockSpec((groups, width, hidden), lambda i: (0, 0, 0), pipeline_mode=once),
            pl.BlockSpec((groups, width, hidden), lambda i: (0, 0, 0), pipeline_mode=once),
            pl.BlockSpec(vec.shape, lambda i: (0, 0)),
            pl.BlockSpec(bias.shape, lambda i: (0, 0)),
        ],
        out_specs=[
            row,
            wide,
            wide,
            row,
            row,
            row,
            row,
            pl.BlockSpec((groups, tile, tail), lambda i: (0, i, 0)),
            pl.BlockSpec((8, width), lambda i: (0, 0)),
            pl.BlockSpec((8, hidden), lambda i: (0, 0)),
        ],
        out_shape=[
            jax.ShapeDtypeStruct((tokens, width), BF16),
            jax.ShapeDtypeStruct((groups, tokens, hidden), BF16),
            jax.ShapeDtypeStruct((groups, tokens, hidden), BF16),
            jax.ShapeDtypeStruct((tokens, width), BF16),
            jax.ShapeDtypeStruct((tokens, width), BF16),
            jax.ShapeDtypeStruct((tokens, width), BF16),
            jax.ShapeDtypeStruct((tokens, width), F32),
            jax.ShapeDtypeStruct((groups, tokens, tail), BF16),
            jax.ShapeDtypeStruct((8, width), F32),
            jax.ShapeDtypeStruct((8, hidden), F32),
        ],
        scratch_shapes=[pltpu.VMEM((groups, tile, hidden), F32)],
        compiler_params=params(),
        name="ffn",
    )(x, cot, pm, wa, wb, wc, vec, bias)


MESH = pl.DeviceIdType.MESH


class Place:
    def __init__(self, sizes):
        dp, tensor = lax.axis_index("dp"), lax.axis_index("tensor")
        self.deep = sizes[0] // 2
        self.z, self.y = dp // 2, dp % 2
        self.x, self.c = tensor // 2, tensor % 2

    def to_z(self, step):
        return {"dp": lax.rem(self.z + step, self.deep) * 2 + self.y}

    def to_y(self):
        return {"dp": self.z * 2 + 1 - self.y}

    def to_x(self):
        return {"tensor": (1 - self.x) * 2 + self.c}

    def to_c(self):
        return {"tensor": self.x * 2 + 1 - self.c}

    def from_z(self, step):
        return lax.rem(self.z + self.deep - step, self.deep)

    def partners(self):
        return [self.to_z(j) for j in range(1, self.deep)] + [self.to_y(), self.to_x(), self.to_c()]

    def peers(self):
        found = []
        for r in range(1, 8):
            x = 1 - self.x if r & 4 else self.x
            y = 1 - self.y if r & 2 else self.y
            c = 1 - self.c if r & 1 else self.c
            found.append((x * 4 + y * 2 + c, {"dp": self.z * 2 + y, "tensor": x * 2 + c}))
        return found

    def greet(self, everyone=False):
        barrier = pltpu.get_barrier_semaphore()
        partners = self.partners()
        if everyone:
            partners = partners[: self.deep - 1] + [device for _, device in self.peers()]
        for partner in partners:
            pl.semaphore_signal(barrier, inc=1, device_id=partner, device_id_type=MESH)
        pl.semaphore_wait(barrier, len(partners))


class Links:
    def __init__(self, send, recv):
        self.send, self.recv = send, recv

    def copy(self, k, ref, to, dst=None):
        return pltpu.make_async_remote_copy(
            src_ref=ref,
            dst_ref=ref if dst is None else dst,
            send_sem=self.send.at[k],
            recv_sem=self.recv.at[k],
            device_id=to,
            device_id_type=MESH,
        )

    def landed(self, k, ref, to):
        self.copy(k, ref, to).wait_recv()


def add_everywhere(place, links, base, own, slots):
    deep = place.deep
    hops = [place.to_c(), place.to_y(), place.to_x()]

    def start(i):
        def run():
            if i:
                links.copy(base + i - 1, own, hops[i - 1], slots.at[i - 1]).wait_send()
                links.landed(base + i - 1, slots.at[i - 1], hops[i - 1])
                own[...] = own[...] + slots[i - 1]
            if i < 3:
                links.copy(base + i, own, hops[i], slots.at[i]).start()
            else:
                for j in range(1, deep):
                    links.copy(base + 2 + j, own, place.to_z(j), slots.at[2 + j]).start()

        return run

    def last():
        for j in range(1, deep):
            links.copy(base + 2 + j, own, place.to_z(j), slots.at[2 + j]).wait_send()
            links.landed(base + 2 + j, slots.at[2 + j], place.to_z(j))
        slots[2] = own[...]
        total = slots[2 + lax.rem(place.z + deep, deep)]
        for z in range(1, deep):
            total = total + slots[2 + lax.rem(place.z + deep - z, deep)]
        own[...] = total

    return [start(0), start(1), start(2), start(3), last]


def add_in_two(place, links, base, own, slots):
    p, deep = place, place.deep
    me = p.x * 4 + p.y * 2 + p.c
    peers = p.peers()

    def near(r):
        return links.copy(base + r, own, peers[r - 1][1], slots.at[me])

    def far(j):
        return links.copy(base + 7 + j, own, p.to_z(j), slots.at[8 + p.z])

    def start():
        for r in range(1, 8):
            near(r).start()
        slots[me] = own[...]

    def middle():
        for r in range(1, 8):
            near(r).wait_send()
            links.landed(base + r, slots.at[peers[r - 1][0]], peers[r - 1][1])
        total = slots[0]
        for k in range(1, 8):
            total = total + slots[k]
        own[...] = total
        for j in range(1, deep):
            far(j).start()
        slots[8 + p.z] = total

    def last():
        for j in range(1, deep):
            far(j).wait_send()
            links.landed(base + 7 + j, slots.at[8 + p.from_z(j)], p.to_z(j))
        total = slots[8]
        for k in range(1, deep):
            total = total + slots[8 + k]
        own[...] = total

    return [start, middle, last]


def gather_small(place, links, base, whole):
    p, deep = place, place.deep
    mine, line, plane = whole.at[p.x, p.c, p.z, p.y], whole.at[p.x, p.c, :, p.y], whole.at[p.x, p.c]
    half = whole.at[:, p.c]

    def over_z(j):
        return links.copy(base + j, mine, p.to_z(j))

    def stage0():
        for j in range(1, deep):
            over_z(j).start()

    def stage1():
        for j in range(1, deep):
            links.landed(base + j, whole.at[p.x, p.c, p.from_z(j), p.y], p.to_z(j))
        links.copy(base + deep, line, p.to_y()).start()

    def stage2():
        links.landed(base + deep, whole.at[p.x, p.c, :, 1 - p.y], p.to_y())
        links.copy(base + deep + 1, plane, p.to_x()).start()

    def stage3():
        links.landed(base + deep + 1, whole.at[1 - p.x, p.c], p.to_x())
        links.copy(base + deep + 2, half, p.to_c()).start()

    def stage4():
        links.landed(base + deep + 2, whole.at[:, 1 - p.c], p.to_c())
        for j in range(1, deep):
            over_z(j).wait_send()
        links.copy(base + deep, line, p.to_y()).wait_send()
        links.copy(base + deep + 1, plane, p.to_x()).wait_send()
        links.copy(base + deep + 2, half, p.to_c()).wait_send()

    return [stage0, stage1, stage2, stage3, stage4]


def gather_stages(place, links, base, own, whole, start=0, count=None):
    p, deep = place, place.deep
    count = own.shape[0] if count is None else count
    half = count // 2
    rows, first, later = pl.ds(start, count), pl.ds(start, half), pl.ds(start + half, half)
    own = own.at[rows]
    mine = whole.at[p.x, p.c, p.z, p.y, rows]
    line = whole.at[p.x, p.c, :, p.y, rows]
    ax = whole.at[p.x, p.c, :, p.y, first]
    ax_in = whole.at[1 - p.x, p.c, :, p.y, first]
    by = whole.at[p.x, p.c, :, p.y, later]
    by_in = whole.at[p.x, p.c, :, 1 - p.y, later]
    ay = whole.at[:, p.c, :, p.y, first]
    ay_in = whole.at[:, p.c, :, 1 - p.y, first]
    bx = whole.at[p.x, p.c, :, :, later]
    bx_in = whole.at[1 - p.x, p.c, :, :, later]
    kz, ka, kb, ks = base, base + deep, base + deep + 2, base + deep + 4

    def keep():
        return pltpu.make_async_copy(own, mine, links.send.at[kz])

    def stage0():
        keep().start()
        for j in range(1, deep):
            links.copy(kz + j, own, p.to_z(j), mine).start()

    def sent():
        for j in range(1, deep):
            links.copy(kz + j, own, p.to_z(j), mine).wait_send()

    def stage1():
        keep().wait()
        for j in range(1, deep):
            links.landed(kz + j, whole.at[p.x, p.c, p.from_z(j), p.y, rows], p.to_z(j))
        links.copy(ka, ax, p.to_x()).start()
        links.copy(kb, by, p.to_y()).start()
        links.copy(ks, line, p.to_c()).start()

    def stage2():
        links.landed(ka, ax_in, p.to_x())
        links.copy(ka + 1, ay, p.to_y()).start()
        links.copy(ks + 1, ax_in, p.to_c()).start()
        links.landed(kb, by_in, p.to_y())
        links.copy(kb + 1, bx, p.to_x()).start()
        links.copy(ks + 2, by_in, p.to_c()).start()

    def stage3():
        links.landed(ka + 1, ay_in, p.to_y())
        links.copy(ks + 3, ay_in, p.to_c()).start()
        links.landed(kb + 1, bx_in, p.to_x())
        links.copy(ks + 4, bx_in, p.to_c()).start()

    def stage4():
        o = 1 - p.c
        links.landed(ks, whole.at[p.x, o, :, p.y, rows], p.to_c())
        links.landed(ks + 1, whole.at[1 - p.x, o, :, p.y, first], p.to_c())
        links.landed(ks + 2, whole.at[p.x, o, :, 1 - p.y, later], p.to_c())
        links.landed(ks + 3, whole.at[:, o, :, 1 - p.y, first], p.to_c())
        links.landed(ks + 4, whole.at[1 - p.x, o, :, :, later], p.to_c())
        links.copy(ka, ax, p.to_x()).wait_send()
        links.copy(kb, by, p.to_y()).wait_send()
        links.copy(ka + 1, ay, p.to_y()).wait_send()
        links.copy(kb + 1, bx, p.to_x()).wait_send()
        links.copy(ks, line, p.to_c()).wait_send()
        links.copy(ks + 1, ax_in, p.to_c()).wait_send()
        links.copy(ks + 2, by_in, p.to_c()).wait_send()
        links.copy(ks + 3, ay_in, p.to_c()).wait_send()
        links.copy(ks + 4, bx_in, p.to_c()).wait_send()

    return [stage0, stage1, stage2, stage3, stage4, sent]


def gather_stages_late(place, links, base, own, whole, start=0, count=None):
    p, deep = place, place.deep
    count = own.shape[0] if count is None else count
    half = count // 2
    rows, first, later = pl.ds(start, count), pl.ds(start, half), pl.ds(start + half, half)
    mine = whole.at[p.x, p.c, p.z, p.y]
    pair_f, pair_l = whole.at[:, p.c, p.z, p.y, first], whole.at[p.x, p.c, p.z, :, later]
    line_f, line_l = whole.at[:, p.c, :, p.y, first], whole.at[p.x, p.c, :, :, later]
    line_f_in = whole.at[:, p.c, :, 1 - p.y, first]
    line_l_in = whole.at[1 - p.x, p.c, :, :, later]
    kf, kl = base + 8, base + 8 + deep

    def keep():
        return pltpu.make_async_copy(own.at[rows], mine.at[rows], links.send.at[base])

    def to_x():
        return links.copy(base + 1, own.at[first], p.to_x(), mine.at[first])

    def to_y():
        return links.copy(base + 2, own.at[later], p.to_y(), mine.at[later])

    def stage0():
        keep().start()
        to_x().start()
        to_y().start()

    def stage1():
        keep().wait()
        links.landed(base + 1, whole.at[1 - p.x, p.c, p.z, p.y, first], p.to_x())
        links.landed(base + 2, whole.at[p.x, p.c, p.z, 1 - p.y, later], p.to_y())
        for j in range(1, deep):
            links.copy(kf + j, pair_f, p.to_z(j)).start()
            links.copy(kl + j, pair_l, p.to_z(j)).start()

    def sent():
        for j in range(1, deep):
            links.copy(kf + j, pair_f, p.to_z(j)).wait_send()
            links.copy(kl + j, pair_l, p.to_z(j)).wait_send()

    def stage2():
        for j in range(1, deep):
            z = p.from_z(j)
            links.landed(kf + j, whole.at[:, p.c, z, p.y, first], p.to_z(j))
            links.landed(kl + j, whole.at[p.x, p.c, z, :, later], p.to_z(j))
        links.copy(base + 3, line_f, p.to_y()).start()
        links.copy(base + 4, line_l, p.to_x()).start()
        links.copy(base + 5, line_f, p.to_c()).start()
        links.copy(base + 6, line_l, p.to_c()).start()

    def stage3():
        links.landed(base + 3, line_f_in, p.to_y())
        links.copy(base + 7, line_f_in, p.to_c()).start()
        links.landed(base + 4, line_l_in, p.to_x())
        links.copy(base + 8, line_l_in, p.to_c()).start()

    def stage4():
        o = 1 - p.c
        links.landed(base + 5, whole.at[:, o, :, p.y, first], p.to_c())
        links.landed(base + 6, whole.at[p.x, o, :, :, later], p.to_c())
        links.landed(base + 7, whole.at[:, o, :, 1 - p.y, first], p.to_c())
        links.landed(base + 8, whole.at[1 - p.x, o, :, :, later], p.to_c())
        to_x().wait_send()
        to_y().wait_send()
        links.copy(base + 3, line_f, p.to_y()).wait_send()
        links.copy(base + 4, line_l, p.to_x()).wait_send()
        links.copy(base + 5, line_f, p.to_c()).wait_send()
        links.copy(base + 6, line_l, p.to_c()).wait_send()
        links.copy(base + 7, line_f_in, p.to_c()).wait_send()
        links.copy(base + 8, line_l_in, p.to_c()).wait_send()

    return [stage0, stage1, stage2, stage3, stage4, sent]


GATHER_COPIES = 9


def add_into(out, one, two):
    out[...] = one[...] + two[...]


def scatter_core(place, links, base, acc, in_c):
    def move(part):
        return links.copy(base + part, acc.at[2 + part], place.to_c(), in_c.at[part])

    def send(part):
        return lambda: move(part).start()

    def add(part, x):
        def run():
            move(part).wait_send()
            links.landed(base + part, in_c.at[part], place.to_c())

            def one(z, _):
                for y in range(2):
                    there = acc.at[x, z, y]
                    add_into(there, there, in_c.at[part, z, y])
                return 0

            lax.fori_loop(0, place.deep, one, 0)

        return run

    return send, add


def add_line(place, acc, x, y, rows, arrived):
    def add(z, _):
        there = acc.at[x, z, y, rows]
        add_into(there, there, arrived.at[z])
        return 0

    lax.fori_loop(0, place.deep, add, 0)


def scatter_plane(place, links, base, acc, ay_in, ax_in, bx_in, by_in):
    p = place
    half = acc.shape[3] // 2
    first, later, both = pl.ds(0, half), pl.ds(half, half), pl.ds(0, 2)

    def ay():
        return links.copy(base, acc.at[both, :, 1 - p.y, first], p.to_y(), ay_in)

    def bx():
        return links.copy(base + 1, acc.at[1 - p.x, :, :, later], p.to_x(), bx_in)

    def ax():
        return links.copy(base + 2, acc.at[1 - p.x, :, p.y, first], p.to_x(), ax_in)

    def by():
        return links.copy(base + 3, acc.at[p.x, :, 1 - p.y, later], p.to_y(), by_in)

    def start():
        ay().start()
        bx().start()

    def middle():
        links.landed(base, ay_in, p.to_y())
        for x in range(2):
            add_line(p, acc, x, p.y, first, ay_in.at[x])
        ax().start()
        links.landed(base + 1, bx_in, p.to_x())
        for y in range(2):
            add_line(p, acc, p.x, y, later, bx_in.at[:, y])
        by().start()

    def finish():
        links.landed(base + 2, ax_in, p.to_x())
        add_line(p, acc, p.x, p.y, first, ax_in)
        links.landed(base + 3, by_in, p.to_y())
        add_line(p, acc, p.x, p.y, later, by_in)

    def settle():
        for move in (ay, bx, ax, by):
            move().wait_send()

    return start, middle, finish, settle


def scatter_in_pairs(place, links, base, acc, in_c, ay_in, ax_in, bx_in, by_in, in_z, out):
    p, deep = place, place.deep
    half = acc.shape[3] // 2
    first, later = pl.ds(0, half), pl.ds(half, half)
    far, near = 1 - p.x, p.x
    kf, kl = base + 6, base + 6 + deep
    send, add = scatter_core(place, links, base, acc, in_c)

    def over_y(part, x):
        return links.copy(base + 2 + part, acc.at[x, :, 1 - p.y, first], p.to_y(), ay_in.at[part])

    def far_later():
        return links.copy(base + 4, acc.at[far, :, :, later], p.to_x(), bx_in)

    def far_first():
        return links.copy(base + 5, acc.at[far, :, p.y, first], p.to_x(), ax_in)

    def near_later():
        return links.copy(base + 6, acc.at[near, :, 1 - p.y, later], p.to_y(), by_in)

    def over_z(k, j, rows):
        to = lax.rem(p.z + j, deep)
        return links.copy(k + j, acc.at[near, to, p.y, rows], p.to_z(j), in_z.at[j, rows])

    def far1():
        add(0, far)()
        over_y(0, far).start()
        far_later().start()

    def far2():
        links.landed(base + 2, ay_in.at[0], p.to_y())
        add_line(p, acc, far, p.y, first, ay_in.at[0])
        far_first().start()

    def near1():
        over_y(1, near).start()

    def near_x():
        links.landed(base + 4, bx_in, p.to_x())
        for y in range(2):
            add_line(p, acc, near, y, later, bx_in.at[:, y])
        near_later().start()

    def near2():
        links.landed(base + 3, ay_in.at[1], p.to_y())
        add_line(p, acc, near, p.y, first, ay_in.at[1])
        links.landed(base + 5, ax_in, p.to_x())
        add_line(p, acc, near, p.y, first, ax_in)
        for j in range(1, deep):
            over_z(kf, j, first).start()

    def near3():
        links.landed(base + 6, by_in, p.to_y())
        add_line(p, acc, near, p.y, later, by_in)
        for j in range(1, deep):
            over_z(kl, j, later).start()

    def near4():
        for k, rows in ((kf, first), (kl, later)):
            total = acc[near, p.z, p.y, rows].astype(F32)
            for j in range(1, deep):
                links.landed(k + j, in_z.at[j, rows], p.to_z(j))
                total = total + in_z[j, rows].astype(F32)
            out[rows] = total
            for j in range(1, deep):
                over_z(k, j, rows).wait_send()
        over_y(0, far).wait_send()
        over_y(1, near).wait_send()
        far_later().wait_send()
        far_first().wait_send()
        near_later().wait_send()

    return [send(0), far1, far2, send(1), add(1, near), near1, near_x, near2, near3, near4]


def scatter_tail(place, links, base, part, in_z, out):
    deep = place.deep

    def send(j):
        return links.copy(
            base + j, part.at[lax.rem(place.z + j, deep)], place.to_z(j), in_z.at[j]
        )

    def stage0():
        for j in range(1, deep):
            send(j).start()

    def stage1():
        for j in range(1, deep):
            links.landed(base + j, in_z.at[j], place.to_z(j))
        total = part[place.z].astype(F32)
        for j in range(1, deep):
            total = total + in_z[j].astype(F32)
        out[...] = total
        for j in range(1, deep):
            send(j).wait_send()

    return [stage0, stage1]


def core_buffers(deep, rows, lanes):
    return [
        pltpu.VMEM((4, deep, 2, rows, lanes), BF16),
        pltpu.VMEM((2, deep, 2, rows, lanes), BF16),
    ]


def plane_buffers(deep, rows, lanes):
    half = rows // 2
    return [
        pltpu.VMEM((2, deep, half, lanes), BF16),
        pltpu.VMEM((deep, half, lanes), BF16),
        pltpu.VMEM((deep, 2, half, lanes), BF16),
        pltpu.VMEM((deep, half, lanes), BF16),
    ]


def gather_blocks(block, sizes):
    whole = lax.all_gather(block, ("dp", "tensor"), axis=0, tiled=False)
    whole = whole.reshape(sizes + block.shape)
    return jnp.swapaxes(whole, 0, 1).reshape((sizes[1], -1) + block.shape[1:])


def scatter_blocks(grads, sizes):
    parts = grads.reshape((sizes[1], sizes[0], -1) + grads.shape[2:])
    parts = jnp.swapaxes(parts, 0, 1).reshape((sizes[0] * sizes[1],) + parts.shape[2:])
    return lax.psum_scatter(parts, ("dp", "tensor"), scatter_dimension=0, tiled=False)


def adam_parts(grad, mean, square):
    new_mean = MOMENT_DECAY * mean + (1.0 - MOMENT_DECAY) * grad
    new_square = MOMENT_DECAY * square + (1.0 - MOMENT_DECAY) * grad * grad
    correction = 1.0 - MOMENT_DECAY**STEP
    direction = new_mean / correction / (jnp.sqrt(new_square / correction) + ADAM_EPS)
    return new_mean, new_square, direction


def sum_all(values):
    return jnp.sum(jnp.sum(values, axis=1, keepdims=True), axis=0, keepdims=True)


def group_squares(qkv_part, out_part, inner_part, outer_part, vector_part):
    return jnp.concatenate(
        [
            jnp.sum(qkv_part * qkv_part, axis=(1, 2)),
            jnp.sum(out_part * out_part)[None],
            jnp.sum(inner_part * inner_part)[None],
            jnp.sum(outer_part * outer_part)[None],
            jnp.sum(vector_part[:8] * vector_part[:8], axis=1),
            jnp.sum(vector_part[8:] * vector_part[8:])[None],
        ]
    )


def lamb_apply(weight_list, update_list, trust_ratio, row_number):
    qkv_new = weight_list[0] - LEARN_RATE * trust_ratio[0:3, None, None] * update_list[0]
    out_new = weight_list[1] - LEARN_RATE * trust_ratio[3] * update_list[1]
    inner_new = weight_list[2] - LEARN_RATE * trust_ratio[4] * update_list[2]
    outer_new = weight_list[3] - LEARN_RATE * trust_ratio[5] * update_list[3]
    row_ratio = jnp.concatenate(
        [trust_ratio[6:14], jnp.broadcast_to(trust_ratio[14], (row_number - 8,))]
    )
    vector_new = weight_list[4] - LEARN_RATE * row_ratio[:, None] * update_list[4]
    return (qkv_new, out_new, inner_new, outer_new, vector_new)


def lamb_plain(sum_a, sum_b, sum_c, vector_sum, weights, old_means, old_squares):
    qkv_sum = jnp.stack([collect(sum_a, at) for at in (Q_AT, K_AT, V_AT)])
    grad_sums = (qkv_sum, collect(sum_a, O_AT).T, sum_b, sum_c.T, vector_sum)
    decays = (WEIGHT_DECAY, WEIGHT_DECAY, WEIGHT_DECAY, WEIGHT_DECAY, 0.0)
    stats = [adam_parts(*entry) for entry in zip(grad_sums, old_means, old_squares)]
    updates = [stats[i][2] + decays[i] * weights[i] for i in range(5)]
    weight_squares, update_squares = lax.psum(
        (group_squares(*weights), group_squares(*updates)), ("dp", "tensor")
    )
    weight_norms = jnp.sqrt(weight_squares)
    update_norms = jnp.sqrt(update_squares)
    trust_ratio = weight_norms / (update_norms + ADAM_EPS)
    new = lamb_apply(weights, updates, trust_ratio, weights[4].shape[0])
    outs = []
    for i in range(5):
        outs += [stats[i][0], stats[i][1], new[i]]
    return outs + [jnp.stack([weight_norms, update_norms])]


A_ROWS = ((0, 32), (32, 32), (64, 32))
B_ROWS = ((0, 64), (64, 32))


def gather_attend_kernel(
    qkv_ref, out_ref, inner_ref, outer_ref, vec_ref, x_ref, seg_ref,
    wa_hbm, wb_hbm, wc_hbm, full, pm_ref, lse_ref, hid_ref, slope_ref, nlt_ref, xt_ref, n1_ref,
    inv_ref,
    send, recv, slots, pack_a, pack_b, pack_c, wa, wb, wc, bias, low, out_sem,
    *, sizes, chunk,
):
    step = pl.program_id(0)
    groups, deep = sizes[1], sizes[0] // 2
    place = Place(sizes)
    links = Links(send, recv)
    each = GATHER_COPIES + deep
    cols = qkv_ref.shape[2]
    tokens, width = x_ref.shape
    lanes = pack_a.shape[1]
    length = tokens // 2
    tail = 256
    ga = [
        gather_stages(place, links, k * each, pack_a, wa, *rows) for k, rows in enumerate(A_ROWS)
    ]
    more = len(A_ROWS) * each
    gb = [
        gather_stages(place, links, more + k * each, pack_b, wb, *rows)
        for k, rows in enumerate(B_ROWS)
    ]
    more += len(B_ROWS) * each
    small = gather_small(place, links, more, slots)
    more += deep + 3
    gc = [
        gather_stages_late(place, links, more + k * (each + deep), pack_c, wc, *rows)
        for k, rows in enumerate(B_ROWS)
    ]
    sent = 5
    t, s = step // 2, step % 2
    last = 2 * groups + groups - 1

    def keep(k):
        pairs = ((wa, wa_hbm), (wb, wb_hbm), (wc, wc_hbm))
        return pltpu.make_async_copy(*pairs[k], out_sem.at[k])

    @pl.when(step == 0)
    def _():
        out_rows = out_ref[...].T
        pack_a[...] = spread(qkv_ref[0], qkv_ref[1], qkv_ref[2], out_rows).astype(BF16)
        count, mine = vec_ref.shape
        slots[place.x, place.c, place.z, place.y, 0:count, 0:mine] = vec_ref[...]
        place.greet()
        small[0]()
        ga[0][0]()
        pack_c[...] = outer_ref[...].astype(BF16)
        gc[0][0]()
        gc[1][0]()
        ga[0][sent]()
        ga[1][0]()
        small[1]()
        ga[0][1]()
        ga[1][sent]()
        ga[2][0]()
        pack_b[...] = inner_ref[...].astype(BF16)
        small[2]()
        ga[1][1]()
        ga[0][2]()
        ga[2][sent]()
        gb[0][0]()
        small[3]()
        ga[2][1]()
        ga[1][2]()
        ga[0][3]()
        xt_ref[...] = x_ref[...].T
        ga[2][2]()
        gb[0][sent]()
        gb[1][0]()
        ga[1][3]()
        small[4]()
        full[...] = jnp.zeros_like(full)
        for k in range(sizes[0] * groups):
            dp, tensor = k // groups, k % groups
            block = slots[tensor // 2, tensor % 2, dp // 2, dp % 2, 0:count, 0:mine]
            full[0:count, k * mine : (k + 1) * mine] = block
        gb[1][sent]()
        gc[0][1]()
        gb[0][1]()
        ga[2][3]()
        for g in range(groups):
            bias[g] = jnp.zeros(bias.shape[1:], F32)
            for h in range(HEADS):
                here = slice(g * cols + h * HD, g * cols + (h + 1) * HD)
                bias[g, 0:1, Q_AT[h] : Q_AT[h] + HD] = full[6:7, here]
                bias[g, 0:1, V_AT[h] : V_AT[h] + HD] = full[7:8, here]
        n1_ref[...] = x_ref[...].astype(F32) + full[4:5, :]
        gb[1][1]()
        for piece in ga:
            piece[4]()
        keep(0).start()

    @pl.when(step == 1)
    def _():
        gb[0][2]()
        gb[1][2]()

    @pl.when(step == 3)
    def _():
        gc[0][sent]()
        gc[1][1]()

    @pl.when(step == 4)
    def _():
        gc[0][2]()

    @pl.when(step == 5)
    def _():
        gb[0][3]()

    @pl.when(step == 7)
    def _():
        gb[1][3]()
        gc[1][sent]()
        gc[1][2]()

    @pl.when(step == 2 * groups + 2)
    def _():
        gc[0][3]()
        keep(1).start()

    @pl.when((step < 2 * groups) & (s == 0))
    def _():
        weight = wa[t // 2, t % 2].reshape(width, lanes)
        for n in range(lanes // 256):
            here = slice(n * 256, (n + 1) * 256)
            proj = dot(x_ref[...], weight[:, here]) + bias[t, 0:1, here]
            pm_ref[0, :, here] = proj.astype(BF16)

    @pl.when(step < 2 * groups)
    def _():
        rows = pl.ds(pl.multiple_of(s * length, length), length)
        row = seg_ref[pl.ds(lax.axis_index("tensor") * 2 + s, 1)]
        attend_heads(pm_ref.at[0, rows], row, lse_ref, chunk)

    @pl.when((step < 2 * groups) & (s == 1))
    def _():
        mixed = mixed_only(pm_ref[0, :, lanes - tail :])
        weight = wa[t // 2, t % 2, :, :, :, lanes - tail :].reshape(width, tail)
        for n in range(width // 256):
            here = slice(n * 256, (n + 1) * 256)
            n1_ref[:, here] += dot(mixed, weight[here], NT)

    @pl.when(step == 2 * groups)
    def _():
        for r in range(tokens // 256):
            rows = slice(r * 256, (r + 1) * 256)
            normal_one, inverse_one = norm_parts(n1_ref[rows])
            n1_ref[rows] = normal_one
            inv_ref[rows] = inverse_one
            part = (normal_one * full[0:1, :] + full[1:2, :]).astype(BF16)
            low[rows] = part
            nlt_ref[:, rows] = part.T
        gb[0][4]()
        gb[1][4]()

    @pl.when(step >= 2 * groups)
    def _():
        g = step - 2 * groups
        weight = wb[g // 2, g % 2].reshape(width, lanes)
        for n in range(lanes // 256):
            here = slice(n * 256, (n + 1) * 256)
            pre = dot(low[...], weight[:, here]) + full[pl.ds(8 + g, 1), here]
            act, turn = gelu_parts(pre)
            hid_ref[0, :, here] = act.astype(BF16)
            slope_ref[0, :, here] = turn.astype(BF16)

    @pl.when(step == last)
    def _():
        gc[1][3]()
        gc[0][4]()
        gc[1][4]()
        keep(2).start()
        for k in range(3):
            keep(k).wait()


def once(shape):
    return pl.BlockSpec(shape, lambda *_: (0,) * len(shape), pipeline_mode=pl.Buffered(1))


def gather_attend(weights, x, seg, sizes):
    qkv, out, inner, outer, vec = weights
    deep, groups = sizes[0] // 2, sizes[1]
    each = GATHER_COPIES + deep
    copies = len(A_ROWS) * each + len(B_ROWS) * (2 * each + deep) + deep + 3
    tokens, width = x.shape
    length = seg.shape[1]
    seqs = tokens // length
    rows, lanes = inner.shape
    steps = groups * seqs
    anywhere = pl.BlockSpec(memory_space=pl.ANY)
    parts = (2, 2, deep, 2, rows, lanes)
    whole = jax.ShapeDtypeStruct(parts, BF16)

    def now(i):
        return jnp.minimum(i, steps - 1)

    def part(i):
        return jnp.clip(i - steps, 0, groups - 1)

    wa, wb, wc, *rest = pl.pallas_call(
        functools.partial(gather_attend_kernel, sizes=sizes, chunk=min(256, length)),
        grid=(steps + groups,),
        in_specs=[once(w.shape) for w in weights]
        + [
            once(x.shape),
            once(seg.shape),
        ],
        out_specs=[anywhere] * 3
        + [
            once((16, width)),
            pl.BlockSpec((1, tokens, lanes), lambda i: (now(i) // 2, 0, 0)),
            pl.BlockSpec((1, 1, 8, length), lambda i: (now(i) // 2, now(i) % 2, 0, 0)),
            pl.BlockSpec((1, tokens, lanes), lambda i: (part(i), 0, 0)),
            pl.BlockSpec((1, tokens, lanes), lambda i: (part(i), 0, 0)),
            once((width, tokens)),
            once((width, tokens)),
            once((tokens, width)),
            once((tokens, 1)),
        ],
        out_shape=[whole] * 3
        + [
            jax.ShapeDtypeStruct((16, width), F32),
            jax.ShapeDtypeStruct((groups, tokens, lanes), BF16),
            jax.ShapeDtypeStruct((groups, seqs, 8, length), F32),
            jax.ShapeDtypeStruct((groups, tokens, lanes), BF16),
            jax.ShapeDtypeStruct((groups, tokens, lanes), BF16),
            jax.ShapeDtypeStruct((width, tokens), BF16),
            jax.ShapeDtypeStruct((width, tokens), BF16),
            jax.ShapeDtypeStruct((tokens, width), F32),
            jax.ShapeDtypeStruct((tokens, 1), F32),
        ],
        scratch_shapes=[
            pltpu.SemaphoreType.DMA((copies,)),
            pltpu.SemaphoreType.DMA((copies,)),
            pltpu.VMEM((2, 2, deep, 2, 16, 128), F32),
            pltpu.VMEM((rows, lanes), BF16),
            pltpu.VMEM((rows, lanes), BF16),
            pltpu.VMEM((rows, lanes), BF16),
            pltpu.VMEM(parts, BF16),
            pltpu.VMEM(parts, BF16),
            pltpu.VMEM(parts, BF16),
            pltpu.VMEM((groups, 8, lanes), F32),
            pltpu.VMEM((tokens, width), BF16),
            pltpu.SemaphoreType.DMA((3,)),
        ],
        compiler_params=params(collective_id=0, has_side_effects=True),
        name="gather_attend",
    )(*weights, x, seg)
    shape = (groups, sizes[0] * rows, lanes)
    return [wa.reshape(shape), wb.reshape(shape), wc.reshape(shape)] + rest


def other_first(order):
    c = lax.axis_index("tensor") % 2
    return order % 2 * 2 + jnp.where(order < 2, 1 - c, c)


def layer_kernel(
    cot_ref, hid_ref, slope_ref, inv_ref, vec_ref, n1_hbm, nlt_hbm, wa_hbm, wb_hbm, wc_hbm,
    out_hbm, gb_hbm, gm_hbm, gbt_hbm, accb_hbm, part_ref, vg_ref, bg_ref,
    n1_ref, nlt_ref, wo_ref, wb_ref, wc_ref, acc, low, gst, gi, out_ref, gm_ref, gbt_ref,
    in_sem, out_sem, send, recv, accc, in_cc, accb, in_cb, ay_in, ax_in, bx_in, by_in, *, sizes,
):
    step = pl.program_id(0)
    tokens, width = acc.shape
    groups, deep = sizes[1], sizes[0] // 2
    lanes = wa_hbm.shape[2]
    tail = wo_ref.shape[2]
    last = 3 * groups - 1
    place = Place(sizes)
    links = Links(send, recv)
    send_c, add_c = scatter_core(place, links, 0, accc, in_cc)
    send_b, add_b = scatter_core(place, links, 2, accb, in_cb)
    start, middle, finish, settle = scatter_plane(
        place, links, 4, accc, ay_in, ax_in, bx_in, by_in
    )
    blocks = [slice(r * 256, (r + 1) * 256) for r in range(tokens // 256)]
    columns = [slice(n * 256, (n + 1) * 256) for n in range(width // 256)]

    def outer(t):
        return pltpu.make_async_copy(wc_hbm.at[t], wc_ref.at[t], in_sem.at[t])

    def inner(t):
        return pltpu.make_async_copy(wb_hbm.at[t], wb_ref.at[t], in_sem.at[groups + t])

    def load(k):
        pairs = (
            (n1_hbm, n1_ref), (nlt_hbm, nlt_ref), (wa_hbm.at[:, :, pl.ds(lanes - tail, tail)], wo_ref)
        )
        return pltpu.make_async_copy(*pairs[k], in_sem.at[2 * groups + k])

    def store(k):
        pairs = (
            (out_ref, out_hbm), (gbt_ref, gbt_hbm), (accb.at[pl.ds(0, 2)], accb_hbm), (acc, gb_hbm)
        )
        return pltpu.make_async_copy(*pairs[k], out_sem.at[k])

    def store_mixed(t):
        return pltpu.make_async_copy(gm_ref.at[t], gm_hbm.at[t], out_sem.at[4 + t])

    @pl.when(step == 0)
    def _():
        for t in range(groups):
            outer(t).start()
        load(0).start()
        for t in range(groups):
            inner(t).start()
        load(1).start()
        load(2).start()
        place.greet()
        vg_ref[...] = jnp.zeros_like(vg_ref)
        bg_ref[...] = jnp.zeros_like(bg_ref)
        acc[...] = jnp.zeros_like(acc)

    @pl.when(step < groups)
    def _():
        outer(step).wait()
        for here in columns:
            acc[:, here] += dot(hid_ref[0], wc_ref[step, here], NT)

    @pl.when(step == groups - 1)
    def _():
        load(0).wait()
        for rows in blocks:
            second = n1_ref[rows] * vec_ref[0:1, :] + vec_ref[1:2, :] + vec_ref[5:6, :]
            normal_two, inverse_two = norm_parts(second + acc[rows])
            out_ref[rows] = (normal_two * vec_ref[2:3, :] + vec_ref[3:4, :]).astype(BF16)
            cot = cot_ref[rows].astype(F32)
            grad_second = norm_back(cot, normal_two, inverse_two, vec_ref[2:3, :])
            vg_ref[2:3, :] += jnp.sum(cot * normal_two, axis=0, keepdims=True)
            vg_ref[3:4, :] += jnp.sum(cot, axis=0, keepdims=True)
            vg_ref[5:6, :] += jnp.sum(grad_second, axis=0, keepdims=True)
            acc[rows] = grad_second
            part = grad_second.astype(BF16)
            low[rows] = part
            gst[:, rows] = part.T
        store(0).start()

    @pl.when((step >= groups) & (step < 2 * groups))
    def _():
        slot = lax.rem(step - groups + 2, 4)
        for here in columns:
            part = dot(gst[...], hid_ref[0, :, here]).astype(BF16)
            accc[slot, :, :, :, here] = part.reshape(deep, 2, -1, 256)

    @pl.when(step == groups + 1)
    def _():
        send_c(0)()

    @pl.when(step == groups + 2)
    def _():
        send_c(1)()

    @pl.when(step == 2 * groups)
    def _():
        add_c(0, 0)()
        add_c(1, 1)()
        start()
        for t in range(groups):
            inner(t).wait()
        load(1).wait()
        load(2).wait()

    @pl.when(step == last)
    def _():
        middle()

    @pl.when(step >= 2 * groups)
    def _():
        order = step - 2 * groups
        slot = lax.rem(order + 2, 4)
        t = other_first(order)
        for here in columns:
            grad_hidden = dot(low[...], wc_ref[t, :, here])
            part = (grad_hidden * slope_ref[0, :, here].astype(F32)).astype(BF16)
            gi[:, here] = part
            bg_ref[pl.ds(t, 1), here] = jnp.sum(part.astype(F32), axis=0, keepdims=True)
        for here in columns:
            acc[:, here] += dot(gi[...], wb_ref[t, here], NT)
        for here in columns:
            part = dot(nlt_ref[...], gi[:, here]).astype(BF16)
            accb[slot, :, :, :, here] = part.reshape(deep, 2, -1, 256)

    @pl.when(step == 2 * groups + 1)
    def _():
        send_b(0)()

    @pl.when(step == 2 * groups + 2)
    def _():
        send_b(1)()

    @pl.when(step == last)
    def _():
        for rows in blocks:
            grad_normed = acc[rows]
            normal_one = n1_ref[rows]
            grad_branch = norm_back(grad_normed, normal_one, inv_ref[rows], vec_ref[0:1, :])
            vg_ref[0:1, :] += jnp.sum(grad_normed * normal_one, axis=0, keepdims=True)
            vg_ref[1:2, :] += jnp.sum(grad_normed, axis=0, keepdims=True)
            vg_ref[4:5, :] += jnp.sum(grad_branch, axis=0, keepdims=True)
            acc[rows] = grad_branch
            part = grad_branch.astype(BF16)
            low[rows] = part
            gbt_ref[:, rows] = part.T
        store(3).start()
        store(1).start()
        for t in range(groups):
            gm_ref[t] = dot(low[...], wo_ref[t]).astype(BF16)
            store_mixed(t).start()
        add_b(0, 0)()
        add_b(1, 1)()
        store(2).start()
        finish()
        part_ref[...] = accc[place.x, :, place.y]
        settle()
        for k in range(4):
            store(k).wait()
        for t in range(groups):
            store_mixed(t).wait()


def layer(cot, hid, slope, n1, inv1, nlt, wa, wb, wc, vec, sizes):
    tokens, width = cot.shape
    groups, _, lanes = wa.shape
    hidden = wb.shape[2]
    deep = sizes[0] // 2
    rows = width // sizes[0]
    tail = 256
    anywhere = pl.BlockSpec(memory_space=pl.ANY)

    def used(i):
        return jnp.where(i < groups, i, other_first(jnp.clip(i - groups, 0, groups - 1)))

    def back_group(i):
        return other_first(jnp.clip(i - 2 * groups, 0, groups - 1))

    copies = 8
    parts = (2, deep, 2, rows, hidden)
    matrix = pltpu.VMEM((groups, width, hidden), BF16)
    return pl.pallas_call(
        functools.partial(layer_kernel, sizes=sizes),
        grid=(3 * groups,),
        in_specs=[
            once(cot.shape),
            pl.BlockSpec((1, tokens, hidden), lambda i: (used(i), 0, 0)),
            pl.BlockSpec((1, tokens, hidden), lambda i: (back_group(i), 0, 0)),
            once(inv1.shape),
            once(vec.shape),
        ]
        + [anywhere] * 5,
        out_specs=[anywhere] * 5
        + [once((deep, rows, hidden)), once((8, width)), once((8, hidden))],
        out_shape=[
            jax.ShapeDtypeStruct((tokens, width), BF16),
            jax.ShapeDtypeStruct((tokens, width), F32),
            jax.ShapeDtypeStruct((groups, tokens, tail), BF16),
            jax.ShapeDtypeStruct((width, tokens), BF16),
            jax.ShapeDtypeStruct(parts, BF16),
            jax.ShapeDtypeStruct((deep, rows, hidden), BF16),
            jax.ShapeDtypeStruct((8, width), F32),
            jax.ShapeDtypeStruct((8, hidden), F32),
        ],
        scratch_shapes=[
            pltpu.VMEM(n1.shape, F32),
            pltpu.VMEM(nlt.shape, BF16),
            pltpu.VMEM((groups, width, tail), BF16),
            matrix,
            matrix,
            pltpu.VMEM((tokens, width), F32),
            pltpu.VMEM((tokens, width), BF16),
            pltpu.VMEM((width, tokens), BF16),
            pltpu.VMEM((tokens, hidden), BF16),
            pltpu.VMEM((tokens, width), BF16),
            pltpu.VMEM((groups, tokens, tail), BF16),
            pltpu.VMEM((width, tokens), BF16),
            pltpu.SemaphoreType.DMA((2 * groups + 3,)),
            pltpu.SemaphoreType.DMA((4 + groups,)),
            pltpu.SemaphoreType.DMA((copies,)),
            pltpu.SemaphoreType.DMA((copies,)),
        ]
        + core_buffers(deep, rows, hidden) * 2
        + plane_buffers(deep, rows, hidden),
        compiler_params=params(collective_id=1, has_side_effects=True),
        name="layer",
    )(cot, hid, slope, inv1, vec, n1, nlt, wa, wb, wc)


def far_first(step, groups):
    tensor = lax.axis_index("tensor")
    x, c = tensor // 2, tensor % 2
    return jnp.where(step < groups, 1 - x, x) * 2 + jnp.where(step % groups < 2, 1 - c, c)


def back_kernel(
    pm_ref, gm_ref, lse_ref, seg_ref, wa_hbm, xt_hbm, gbt_hbm, gb_hbm,
    accb_hbm, part_ref, vg_ref, bg_ref, *refs, sizes, chunk,
):
    weights, means, squares = refs[0:5], refs[5:10], refs[10:15]
    grads, updates, norms, ig_ref = refs[15:20], refs[20:25], refs[25], refs[26]
    gp, gsum, send, recv, slots, hslots, nslots, vec, hvec, load_sem, sa = refs[27:38]
    wa_ref, xt_ref, gbt_ref, gb_ref, accb, inz_b, inz_c = refs[38:45]
    bufs_b, bufs_a, acc = refs[45:49], refs[49:56], refs[49]
    sb, sc = grads[2], grads[3]
    step = pl.program_id(0)
    groups, deep = sizes[1], sizes[0] // 2
    cols = HEADS * HD
    tokens, width = gb_ref.shape
    lanes = pm_ref.shape[2]
    last = 2 * groups - 1
    length = pm_ref.shape[1]
    place = Place(sizes)
    links = Links(send, recv)
    a = scatter_in_pairs(place, links, 0, *bufs_a, sa)
    more = 7 + 2 * deep
    start, middle, finish, settle = scatter_plane(place, links, more, accb, *bufs_b)
    b = scatter_tail(place, links, more + 4, accb.at[place.x, :, place.y], inz_b, sb)
    c = scatter_tail(place, links, more + 4 + deep, part_ref, inz_c, sc)
    early = add_everywhere(place, links, more + 4 + 2 * deep, vec, slots)
    small = add_everywhere(place, links, more + 6 + 3 * deep, hvec, hslots)
    final = add_in_two(place, links, more + 8 + 4 * deep, norms, nslots)
    t, s = far_first(step, groups), step % 2

    def load(k):
        pairs = ((accb_hbm, accb), (xt_hbm, xt_ref), (gbt_hbm, gbt_ref), (wa_hbm, wa_ref), (gb_hbm, gb_ref))
        return pltpu.make_async_copy(*pairs[k], load_sem.at[k])

    @pl.when(step == 0)
    def _():
        load(0).start()
        place.greet(everyone=True)
        c[0]()
        load(0).wait()
        start()
        for k in range(1, 5):
            load(k).start()
        gsum[...] = jnp.zeros_like(gsum)
        vec[...] = jnp.zeros_like(vec)
        hvec[...] = jnp.zeros_like(hvec)
        vec[0:6] = vg_ref[0:6]
        vec[8 : 8 + groups] = bg_ref[0:groups]
        early[0]()

    @pl.when(step == 1)
    def _():
        load(1).wait()
        load(2).wait()

    @pl.when(step == 2)
    def _():
        a[0]()
        early[1]()

    @pl.when(step == 4)
    def _():
        early[2]()
        middle()
        a[1]()

    @pl.when(step == 5)
    def _():
        c[1]()

    @pl.when(step == 6)
    def _():
        a[3]()
        early[3]()

    @pl.when(step == 7)
    def _():
        finish()
        b[0]()

    rows = pl.ds(pl.multiple_of(s * length, length), length)
    row = seg_ref[pl.ds(lax.axis_index("tensor") * 2 + s, 1)]
    attend_back(pm_ref.at[0], gm_ref.at[0], lse_ref, row, gp.at[t, rows], chunk)
    gsum[t, 0:1, :] += jnp.sum(gp[t, rows].astype(F32), axis=0, keepdims=True)

    @pl.when(s == 1)
    def _():
        order = step // 2
        slot = jnp.where(order % 2 == 0, 2 + order // 2, t // 2)
        for n in range(lanes // 256):
            here = slice(n * 256, (n + 1) * 256)
            if n < lanes // 256 - 1:
                part = dot(xt_ref[...], gp[t, :, here])
            else:
                from_x = dot(xt_ref[...], gp[t, :, here])
                part = dot(gbt_ref[...], gp[t, :, here])
                lane = lax.broadcasted_iota(jnp.int32, part.shape, 1)
                part = jnp.where((lane >= 128) & (lane < 192), from_x, part)
            acc[slot, :, :, :, here] = part.astype(BF16).reshape(deep, 2, -1, 256)

    def input_columns(n):
        here = slice(n * 256, (n + 1) * 256)
        total = gb_ref[:, here]
        for g in range(groups):
            part = gp[g, :, 640:768]
            part = halves(part, jnp.zeros_like(part))
            total = total + dot(gp[g, :, 0:512], wa_ref[g, here, 0:512], NT)
            total = total + dot(part, wa_ref[g, here, 640:768], NT)
        ig_ref[:, here] = total

    @pl.when(step == last)
    def _():
        for g in range(groups):
            for h in range(HEADS):
                at = g * cols + h * HD
                line, lane = at // 256, slice(at % 256, at % 256 + HD)
                hvec[line : line + 1, lane] = gsum[g, 0:1, Q_AT[h] : Q_AT[h] + HD]
                hvec[3 + line : 4 + line, lane] = gsum[g, 0:1, V_AT[h] : V_AT[h] + HD]
        small[0]()
        a[4]()
        a[5]()
        a[2]()
        load(3).wait()
        load(4).wait()
        input_columns(0)
        small[1]()
        a[6]()
        early[4]()
        input_columns(1)
        small[2]()
        a[7]()
        input_columns(2)
        a[8]()
        small[3]()
        b[1]()
        settle()
        found = group_sums([None] * 4 + [sb[...], sc[...], None], weights, means, squares, updates)
        small[4]()
        for k in range(3):
            lanes_of = slice(k * 256, (k + 1) * 256)
            vec[6:7, lanes_of] = hvec[k : k + 1]
            vec[7:8, lanes_of] = hvec[3 + k : 4 + k]
        count, mine = weights[4].shape
        index = lax.axis_index("dp") * groups + lax.axis_index("tensor")
        turned = pltpu.roll(vec[...], width - index * mine, 1)
        grads[4][...] = turned[0:count, 0:mine]
        found = found + group_sums(
            [None] * 6 + [grads[4][...]], weights, means, squares, updates
        )
        a[9]()
        total = sa[...]
        for k, at in enumerate((Q_AT, K_AT, V_AT)):
            grads[0][k] = collect(total, at)
        grads[1][...] = collect(total, O_AT).T
        parts = [grads[0][k] for k in range(3)] + [grads[1][...]]
        norms[...] = found + group_sums(parts + [None] * 3, weights, means, squares, updates)
        for run in final:
            run()


def group_sums(grads, weights, means, squares, updates):
    lane = lax.broadcasted_iota(jnp.int32, (8, 128), 1)
    line = lax.broadcasted_iota(jnp.int32, (8, 128), 0)
    found = jnp.zeros((8, 128), F32)
    for group, grad in enumerate(grads):
        if grad is None:
            continue
        i, k = (0, group) if group < 3 else (group - 2, ...)
        weight, mean, square = (ref[i][k] for ref in (weights, means, squares))
        update = adam_parts(grad, mean, square)[2]
        if i < 4:
            update = update + WEIGHT_DECAY * weight
        updates[i][k] = update
        if i < 4:
            pair = (sum_all(weight * weight), sum_all(update * update))
            for which in range(2):
                hit = (lane == group) & (line == which)
                found = found + jnp.where(hit, pair[which], 0.0)
            continue
        for which, values in enumerate((weight, update)):
            per_row = jnp.sum(values * values, axis=1, keepdims=True)
            for row in range(weight.shape[0]):
                hit = (lane == 6 + min(row, 8)) & (line == which)
                found = found + jnp.where(hit, per_row[row : row + 1], 0.0)
    return found


def back(pm, gm, lse, seg, wa, xt, gbt, gb, accb, part, vg, bg,
         weights, means, squares, sizes):
    deep, groups = sizes[0] // 2, sizes[1]
    tokens, width = gb.shape
    lanes = pm.shape[2]
    length = seg.shape[1]
    seqs = tokens // length
    rows = width // sizes[0]
    copies = 7 + 2 * deep + 4 + 2 * deep + 2 * (deep + 2) + 7 + deep
    small = [weights, means, squares]
    anywhere = pl.BlockSpec(memory_space=pl.ANY)
    outs = [jax.ShapeDtypeStruct(weight.shape, F32) for weight in weights] * 2 + [
        jax.ShapeDtypeStruct((8, 128), F32),
        jax.ShapeDtypeStruct((tokens, width), F32),
    ]
    return pl.pallas_call(
        functools.partial(back_kernel, sizes=sizes, chunk=min(256, length)),
        grid=(groups * seqs,),
        in_specs=[
            pl.BlockSpec((1, length, lanes), lambda i: (far_first(i, groups), i % 2, 0)),
            pl.BlockSpec((1, length, gm.shape[2]), lambda i: (far_first(i, groups), i % 2, 0)),
            pl.BlockSpec((1, 1, 8, length), lambda i: (far_first(i, groups), i % 2, 0, 0)),
            once(seg.shape),
            anywhere,
            anywhere,
            anywhere,
            anywhere,
            anywhere,
            once(part.shape),
            once(vg.shape),
            once(bg.shape),
        ]
        + [once(ref.shape) for group in small for ref in group],
        out_specs=[once(ref.shape) for ref in outs],
        out_shape=outs,
        scratch_shapes=[
            pltpu.VMEM((groups, tokens, lanes), BF16),
            pltpu.VMEM((groups, 8, lanes), F32),
            pltpu.SemaphoreType.DMA((copies,)),
            pltpu.SemaphoreType.DMA((copies,)),
            pltpu.VMEM((deep + 2, 16, width), F32),
            pltpu.VMEM((deep + 2, 8, 256), F32),
            pltpu.VMEM((8 + deep, 8, 128), F32),
            pltpu.VMEM((16, width), F32),
            pltpu.VMEM((8, 256), F32),
            pltpu.SemaphoreType.DMA((5,)),
            pltpu.VMEM((rows, lanes), F32),
            pltpu.VMEM(wa.shape, BF16),
            pltpu.VMEM(xt.shape, BF16),
            pltpu.VMEM(gbt.shape, BF16),
            pltpu.VMEM(gb.shape, F32),
            pltpu.VMEM(accb.shape, BF16),
            pltpu.VMEM((deep, rows, lanes), BF16),
            pltpu.VMEM((deep, rows, lanes), BF16),
        ]
        + plane_buffers(deep, rows, lanes)
        + core_buffers(deep, rows, lanes)
        + plane_buffers(deep, rows, lanes)
        + [pltpu.VMEM((deep, rows, lanes), BF16)],
        compiler_params=params(collective_id=2, has_side_effects=True),
        name="back",
    )(
        pm, gm, lse, seg, wa, xt, gbt, gb,
        accb, part, vg, bg,
        *weights, *means, *squares,
    )


def apply_kernel(*refs):
    grads, updates, sums = refs[0:5], refs[5:10], refs[10]
    weights, means, squares = refs[11:16], refs[16:21], refs[21:26]
    passed, outs, norms = refs[26:28], refs[28:43], refs[43]
    stores = [pltpu.make_async_copy(passed[k], refs[44 + k], refs[46].at[k]) for k in range(2)]
    for move in stores:
        move.start()
    roots = jnp.sqrt(sums[...])
    norms[...] = roots[0:2, 0:15]
    ratio = LEARN_RATE * roots[0:1] / (roots[1:2] + ADAM_EPS)
    for i in range(5):
        grad = grads[i][...]
        outs[3 * i][...] = MOMENT_DECAY * means[i][...] + (1.0 - MOMENT_DECAY) * grad
        outs[3 * i + 1][...] = (
            MOMENT_DECAY * squares[i][...] + (1.0 - MOMENT_DECAY) * grad * grad
        )
        target = outs[3 * i + 2]
        if i == 0:
            for k in range(3):
                target[k] = weights[i][k] - ratio[:, k : k + 1] * updates[i][k]
        elif i < 4:
            target[...] = weights[i][...] - ratio[:, 2 + i : 3 + i] * updates[i][...]
        else:
            for row in range(target.shape[0]):
                here = slice(row, row + 1)
                step = ratio[:, 6 + min(row, 8) : 7 + min(row, 8)]
                target[here] = weights[i][here] - step * updates[i][here]
    for move in stores:
        move.wait()


def apply(grads, updates, sums, weights, means, squares, passed):
    inside = pl.BlockSpec(memory_space=pltpu.VMEM)
    shapes = []
    for weight in weights:
        shapes += [jax.ShapeDtypeStruct(weight.shape, F32)] * 3
    shapes.append(jax.ShapeDtypeStruct((2, 15), F32))
    shapes += [jax.ShapeDtypeStruct(entry.shape, entry.dtype) for entry in passed]
    anywhere = [pl.BlockSpec(memory_space=pl.ANY)] * 2
    return pl.pallas_call(
        apply_kernel,
        in_specs=[inside] * 28,
        out_specs=[inside] * 16 + anywhere,
        out_shape=shapes,
        scratch_shapes=[pltpu.SemaphoreType.DMA((2,))],
        compiler_params=params(),
        name="apply",
    )(*grads, *updates, sums, *weights, *means, *squares, *passed)


def make_body(sizes):
    def body(
        tokens, cotangent, segments,
        qkv_weight, out_weight, inner_weight, outer_weight, vectors,
        qkv_mean, out_mean, inner_mean, outer_mean, vector_mean,
        qkv_square, out_square, inner_square, outer_square, vector_square,
    ):
        groups = sizes[1]
        token_count, width = tokens.shape
        length = segments.shape[1]
        seqs = token_count // length
        cols = qkv_weight.shape[2]
        tensor_index = lax.axis_index("tensor")
        weights = (qkv_weight, out_weight, inner_weight, outer_weight, vectors)
        old_means = (qkv_mean, out_mean, inner_mean, outer_mean, vector_mean)
        old_squares = (qkv_square, out_square, inner_square, outer_square, vector_square)
        if sizes[0] % 2 == 0 and groups == 4 and qkv_weight.shape[1] % 96 == 0:
            weights, old_means, old_squares = (
                entry[:3] + (entry[3].T, entry[4]) for entry in (weights, old_means, old_squares)
            )
            wa, wb, wc, full, pm, lse, hid, slope, nlt, xt, n1, inv1 = gather_attend(
                weights, tokens, segments, sizes
            )
            result, gb, gm, gbt, accb, part, vg, bg = layer(
                cotangent, hid, slope, n1, inv1, nlt, wa, wb, wc, full, sizes
            )
            *changes, sums, input_grad = back(
                pm, gm, lse, segments, wa, xt, gbt, gb, accb, part, vg, bg,
                weights, old_means, old_squares, sizes,
            )
            passed = (result, input_grad)
            new = list(
                apply(changes[:5], changes[5:], sums, weights, old_means, old_squares, passed)
            )
            new[9:12] = [entry.T for entry in new[9:12]]
            return tuple(new[16:]) + tuple(new[:16])
        seg = lax.dynamic_slice_in_dim(segments, tensor_index * seqs, seqs, 0)
        seg = jnp.broadcast_to(seg[:, None, :], (seqs, 8, length))
        pack_a = spread(qkv_weight[0], qkv_weight[1], qkv_weight[2], out_weight.T).astype(BF16)
        pack_b = inner_weight.astype(BF16)
        pack_c = outer_weight.T.astype(BF16)
        wa, wb, wc = (gather_blocks(pack, sizes) for pack in (pack_a, pack_b, pack_c))
        full = lax.all_gather(vectors, ("dp", "tensor"), axis=1, tiled=True)
        q_bias = full[6].reshape(groups, cols)
        v_bias = full[7].reshape(groups, cols)
        none = jnp.zeros_like(q_bias)
        proj_bias = spread(q_bias, none, v_bias, none)
        proj_bias = jnp.broadcast_to(proj_bias[:, None, :], (groups, 8, 4 * cols))
        inner_bias = full[8:].reshape(groups, -1)
        pm, lse = attend_fwd(tokens, wa, proj_bias, seg, length)
        result, hid, gi, nl, gsl, gbl, gb, gm, vg, bg = ffn(
            tokens, cotangent, pm, wa, wb, wc, full, inner_bias
        )
        gp, gsum = attend_bwd(pm, gm, lse, seg)

        grad_c = jnp.einsum("td,gtf->gdf", gsl, hid, preferred_element_type=F32).astype(BF16)
        grad_b = jnp.einsum("td,gtf->gdf", nl, gi, preferred_element_type=F32).astype(BF16)
        from_tokens = jnp.einsum("td,gtc->gdc", tokens, gp, preferred_element_type=F32)
        from_branch = jnp.einsum("td,gtc->gdc", gbl, pm, preferred_element_type=F32)
        lane = lax.broadcasted_iota(jnp.int32, (1, 1, LANES), 2)
        is_mixed = (lane >= 512) & ((lane < 640) | (lane >= 704))
        grad_a = jnp.where(is_mixed, from_branch, from_tokens).astype(BF16)
        input_grad = gb + jnp.einsum(
            "gtc,gdc->td",
            jnp.where(is_mixed, jnp.zeros((), BF16), gp),
            wa,
            preferred_element_type=F32,
        )
        head_rows = jnp.stack([collect(gsum[:, 0], at).reshape(-1) for at in (Q_AT, V_AT)])
        vector_grad = jnp.concatenate([vg[:6], head_rows, bg[:groups].reshape(-1, width)], axis=0)
        sum_a, sum_b, sum_c = (
            scatter_blocks(grad, sizes).astype(F32) for grad in (grad_a, grad_b, grad_c)
        )
        vector_sum = lax.psum_scatter(
            vector_grad, ("dp", "tensor"), scatter_dimension=1, tiled=True
        )
        new = lamb_plain(sum_a, sum_b, sum_c, vector_sum, weights, old_means, old_squares)
        return (result, input_grad) + tuple(new)

    return body

def solution(mesh):
    sizes = (mesh.shape["dp"], mesh.shape["tensor"])
    rows = P(("dp", "tensor"), None)
    qkv = P(None, "dp", "tensor")
    out = P("tensor", "dp")
    inner = P("dp", "tensor")
    vec = P(None, ("dp", "tensor"))
    weights = (qkv, out, inner, out, vec)
    return jax.shard_map(
        make_body(sizes),
        mesh=mesh,
        in_specs=(rows, rows, P("dp", None)) + weights * 3,
        out_specs=(rows, rows) + (qkv,) * 3 + (out,) * 3 + (inner,) * 3 + (out,) * 3 + (vec,) * 3 + (P(),),
        check_vma=False,
    )
```

```python
import functools

import jax
import jax.numpy as jnp
from jax import lax
from jax.experimental import pallas as pl
from jax.experimental.pallas import tpu as pltpu
from jax.sharding import PartitionSpec as P

HD = 64
STEP = 5
NORM_EPS = 1e-05
ADAM_EPS = 1e-06
MOMENT_DECAY = 0.5
LEARN_RATE = 0.5
WEIGHT_DECAY = 0.01
MASKED = -1e30
SCALE = HD ** (-0.5)
F32 = jnp.float32
BF16 = jnp.bfloat16
NT = (((1,), (1,)), ((), ()))
NN = (((1,), (0,)), ((), ()))
TN = (((0,), (0,)), ((), ()))
VMEM_LIMIT = 60 * 1024 * 1024


def dot(a, b, dims=NN):
    return lax.dot_general(a, b, dims, preferred_element_type=F32)


def params(**kw):
    return pltpu.CompilerParams(vmem_limit_bytes=VMEM_LIMIT, **kw)


HEADS = 3
DOCS = 4
LANES = 768
Q_AT, K_AT, V_AT, O_AT = (0, 64, 384), (128, 192, 640), (256, 320, 448), (512, 576, 704)
Q_TILE, K_TILE, V_TILE = (0, 0, 3), (1, 1, 5), (2, 2, 3)
UPPER = (False, True, False)
V_UPPER = (False, True, True)


def spread(q, k, v, o):
    parts = {}
    for places, values in ((Q_AT, q), (K_AT, k), (V_AT, v), (O_AT, o)):
        for h, at in enumerate(places):
            parts[at] = values[:, h * HD : (h + 1) * HD]
    return jnp.concatenate([parts[at] for at in sorted(parts)], axis=1)


def collect(values, places):
    return jnp.concatenate([values[:, at : at + HD] for at in places], axis=1)


def tile_of(ref, n, rows=slice(None)):
    return ref[rows, n * 128 : (n + 1) * 128]


def is_low(shape):
    return lax.broadcasted_iota(jnp.int32, shape, 1) < HD


def halves(low, high):
    return jnp.where(is_low(low.shape), low, high)


def document_lanes(row):
    length = row.shape[1]
    number = jnp.broadcast_to(row.astype(F32), (128, length)).T
    lane = lax.broadcasted_iota(jnp.int32, (length, 128), 1) % HD
    same = number == lane.astype(F32)
    for_query = jnp.where(same, 1.0, 0.0).astype(BF16)
    for_key = jnp.where(same, 0.0, jnp.where(lane < DOCS, MASKED, 0.0)).astype(BF16)
    return for_query, for_key


def attend_heads(pm_ref, row, lse_ref, chunk):
    length = pm_ref.shape[0]
    chunks = length // chunk
    doc_q, doc_k = document_lanes(row)
    ones = jnp.ones((16, length), BF16)
    units = [(h, c) for h in range(HEADS) for c in range(chunks)]
    keys, queries, values = {}, {}, {}
    for h in range(HEADS):
        q, k = tile_of(pm_ref, Q_TILE[h]) * SCALE, tile_of(pm_ref, K_TILE[h])
        queries[h] = halves(doc_q, q) if UPPER[h] else halves(q, doc_q)
        keys[h] = halves(doc_k, k) if UPPER[h] else halves(k, doc_k)
        vt = tile_of(pm_ref, V_TILE[h]).T
        vt = vt[HD:] if V_UPPER[h] else vt[:HD]
        values[h] = jnp.concatenate([vt, ones], axis=0)

    def scores(unit):
        h, c = unit
        return dot(keys[h], queries[h][c * chunk : (c + 1) * chunk], NT)

    outs = {h: [] for h in range(HEADS)}
    ahead = scores(units[0])
    for n, (h, c) in enumerate(units):
        s = ahead
        if n + 1 < len(units):
            ahead = scores(units[n + 1])
        m = jnp.max(s, axis=0, keepdims=True)
        p = jnp.exp(s - m).astype(BF16)
        ot = dot(values[h], p)
        total = ot[HD : HD + 1]
        outs[h].append((ot[:HD] * (1.0 / total)).astype(BF16))
        lse_ref[0, 0, h : h + 1, c * chunk : (c + 1) * chunk] = m + jnp.log(total)
    out = [jnp.concatenate(outs[h], axis=1) for h in range(HEADS)]
    pm_ref[:, 512:640] = jnp.concatenate([out[0], out[1]], axis=0).T
    last = jnp.concatenate([jnp.zeros_like(out[2]), out[2]], axis=0).T
    pm_ref[:, 640:768] = halves(tile_of(pm_ref, 5), last)


def attend_fwd_kernel(x_ref, w_ref, bias_ref, seg_ref, pm_ref, lse_ref, *, chunk):
    proj = dot(x_ref[...], w_ref[0]) + bias_ref[0, 0:1, :]
    pm_ref[0] = proj.astype(BF16)
    attend_heads(pm_ref.at[0], seg_ref[0, 0:1], lse_ref, chunk)


def attend_fwd(x, wa, bias, seg, length):
    tokens, width = x.shape
    groups, _, lanes = wa.shape
    seqs = tokens // length
    return pl.pallas_call(
        functools.partial(attend_fwd_kernel, chunk=min(256, length)),
        grid=(groups, seqs),
        in_specs=[
            pl.BlockSpec((length, width), lambda t, s: (s, 0)),
            pl.BlockSpec((1, width, lanes), lambda t, s: (t, 0, 0)),
            pl.BlockSpec((1, 8, lanes), lambda t, s: (t, 0, 0)),
            pl.BlockSpec((1, 8, length), lambda t, s: (s, 0, 0)),
        ],
        out_specs=[
            pl.BlockSpec((1, length, lanes), lambda t, s: (t, s, 0)),
            pl.BlockSpec((1, 1, 8, length), lambda t, s: (t, s, 0, 0)),
        ],
        out_shape=[
            jax.ShapeDtypeStruct((groups, tokens, lanes), BF16),
            jax.ShapeDtypeStruct((groups, seqs, 8, length), F32),
        ],
        compiler_params=params(),
        name="attend_fwd",
    )(x, wa, bias, seg)


def attend_back(pm_ref, gm_ref, lse_ref, row, gp_ref, chunk):
    length = pm_ref.shape[0]
    chunks = length // chunk
    prod = gm_ref[...].astype(F32) * pm_ref[:, 512:768].astype(F32)
    hi = prod.astype(BF16)
    lo = (prod - hi.astype(F32)).astype(BF16)
    lane = lax.broadcasted_iota(jnp.int32, (8, 256), 1)
    line = lax.broadcasted_iota(jnp.int32, (8, 256), 0)
    start = jnp.where(line == 2, O_AT[2] - 512, line * HD)
    pick = jnp.where((lane >= start) & (lane < start + HD) & (line < HEADS), 1.0, 0.0).astype(BF16)
    dsum = dot(pick, hi, NT) + dot(pick, lo, NT)
    doc_q, doc_k = document_lanes(row)
    none = jnp.zeros((length, 128), BF16)
    units = [(h, c) for h in range(HEADS) for c in range(chunks)]
    keys, queries, plain, values, kts, grads = {}, {}, {}, {}, {}, {}
    for h in range(HEADS):
        q, k = tile_of(pm_ref, Q_TILE[h]) * SCALE, tile_of(pm_ref, K_TILE[h])
        plain[h] = q
        queries[h] = halves(doc_q, q) if UPPER[h] else halves(q, doc_q)
        keys[h] = halves(doc_k, k) if UPPER[h] else halves(k, doc_k)
        kt = k.T
        kts[h] = kt[HD:] if UPPER[h] else kt[:HD]
        v = tile_of(pm_ref, V_TILE[h])
        values[h] = halves(none, v) if V_UPPER[h] else halves(v, none)
        grads[h] = tile_of(gm_ref, 0 if h < 2 else 1)

    def rows_of(c):
        return slice(c * chunk, (c + 1) * chunk)

    def products(unit):
        h, c = unit
        return dot(keys[h], queries[h][rows_of(c)], NT), dot(values[h], grads[h][rows_of(c)], NT)

    dqs = {h: [] for h in range(HEADS)}
    dks, dvs = {}, {}
    ahead = products(units[0])
    for n, (h, c) in enumerate(units):
        s, dp = ahead
        if n + 1 < len(units):
            ahead = products(units[n + 1])
        rows = rows_of(c)
        p = jnp.exp(s - lse_ref[0, 0, h : h + 1, rows])
        ds = (p * (dp - dsum[h : h + 1, rows])).astype(BF16)
        dv = dot(p.astype(BF16), grads[h][rows])
        dk = dot(ds, plain[h][rows])
        dvs[h] = dv if c == 0 else dvs[h] + dv
        dks[h] = dk if c == 0 else dks[h] + dk
        dqs[h].append((dot(kts[h], ds) * SCALE).astype(BF16))
    dq = [jnp.concatenate(dqs[h], axis=1) for h in range(HEADS)]
    gp_ref[:, 0:128] = jnp.concatenate([dq[0], dq[1]], axis=0).T
    gp_ref[:, 128:256] = halves(dks[0], dks[1]).astype(BF16)
    gp_ref[:, 256:384] = halves(dvs[0], dvs[1]).astype(BF16)
    last = jnp.concatenate([dq[2], jnp.zeros_like(dq[2])], axis=0).T
    gp_ref[:, 384:512] = halves(last, dvs[2].astype(BF16))
    gp_ref[:, 512:640] = tile_of(pm_ref, 4)
    gp_ref[:, 640:768] = halves(dks[2].astype(BF16), tile_of(pm_ref, 5))


def attend_bwd_kernel(pm_ref, gm_ref, lse_ref, seg_ref, gp_ref, gsum_ref, *, chunk):
    attend_back(pm_ref.at[0], gm_ref.at[0], lse_ref, seg_ref[0, 0:1], gp_ref.at[0], chunk)

    @pl.when(pl.program_id(1) == 0)
    def _():
        gsum_ref[...] = jnp.zeros_like(gsum_ref)

    gsum_ref[0, 0:1, :] += jnp.sum(gp_ref[0].astype(F32), axis=0, keepdims=True)


def attend_bwd(pm, gm, lse, seg):
    groups, tokens, lanes = pm.shape
    seqs, length = lse.shape[1], lse.shape[3]
    return pl.pallas_call(
        functools.partial(attend_bwd_kernel, chunk=min(256, length)),
        grid=(groups, seqs),
        in_specs=[
            pl.BlockSpec((1, length, lanes), lambda t, s: (t, s, 0)),
            pl.BlockSpec((1, length, gm.shape[2]), lambda t, s: (t, s, 0)),
            pl.BlockSpec((1, 1, 8, length), lambda t, s: (t, s, 0, 0)),
            pl.BlockSpec((1, 8, length), lambda t, s: (s, 0, 0)),
        ],
        out_specs=[
            pl.BlockSpec((1, length, lanes), lambda t, s: (t, s, 0)),
            pl.BlockSpec((1, 8, lanes), lambda t, s: (t, 0, 0)),
        ],
        out_shape=[
            jax.ShapeDtypeStruct((groups, tokens, lanes), BF16),
            jax.ShapeDtypeStruct((groups, 8, lanes), F32),
        ],
        compiler_params=params(),
        name="attend_bwd",
    )(pm, gm, lse, seg)


def mixed_only(tail):
    lane = lax.broadcasted_iota(jnp.int32, tail.shape, 1)
    return jnp.where((lane < 128) | (lane >= 192), tail, jnp.zeros((), BF16))


def gelu_parts(pre):
    cdf = 0.5 * (1.0 + lax.erf(pre * (2.0**-0.5)))
    pdf = jnp.exp(-0.5 * pre * pre) * 0.3989422804014327
    return pre * cdf, cdf + pre * pdf


def mean_of(values):
    return jnp.mean(values, axis=-1, keepdims=True)


def norm_parts(values):
    centred = values - mean_of(values)
    inverse = lax.rsqrt(mean_of(centred * centred) + NORM_EPS)
    return centred * inverse, inverse


def norm_back(incoming, normal, inverse, gain):
    scaled = incoming * gain
    return inverse * (scaled - mean_of(scaled) - normal * mean_of(scaled * normal))


def ffn_kernel(
    x_ref, cot_ref, pm_ref, wo_ref, wb_ref, wc_ref, vec_ref, bias_ref,
    out_ref, hid_ref, gi_ref, nl_ref, gsl_ref, gbl_ref, gb_ref, gm_ref, vg_ref, bg_ref,
    slope_ref,
):
    groups = wb_ref.shape[0]

    @pl.when(pl.program_id(0) == 0)
    def _():
        vg_ref[...] = jnp.zeros_like(vg_ref)
        bg_ref[...] = jnp.zeros_like(bg_ref)

    total = x_ref[...].astype(F32) + vec_ref[4:5, :]
    for t in range(groups):
        total = total + dot(mixed_only(pm_ref[t]), wo_ref[t], NT)
    normal_one, inverse_one = norm_parts(total)
    normed = normal_one * vec_ref[0:1, :] + vec_ref[1:2, :]
    low = normed.astype(BF16)
    nl_ref[...] = low
    second = normed + vec_ref[5:6, :]
    for t in range(groups):
        pre = dot(low, wb_ref[t]) + bias_ref[t : t + 1, :]
        act, slope = gelu_parts(pre)
        act = act.astype(BF16)
        hid_ref[t] = act
        slope_ref[t] = slope
        second = second + dot(act, wc_ref[t], NT)
    normal_two, inverse_two = norm_parts(second)
    out_ref[...] = (normal_two * vec_ref[2:3, :] + vec_ref[3:4, :]).astype(BF16)
    cot = cot_ref[...].astype(F32)
    grad_second = norm_back(cot, normal_two, inverse_two, vec_ref[2:3, :])
    vg_ref[2:3, :] += jnp.sum(cot * normal_two, axis=0, keepdims=True)
    vg_ref[3:4, :] += jnp.sum(cot, axis=0, keepdims=True)
    vg_ref[5:6, :] += jnp.sum(grad_second, axis=0, keepdims=True)
    gs_low = grad_second.astype(BF16)
    gsl_ref[...] = gs_low
    grad_normed = grad_second
    for t in range(groups):
        grad_inner = (dot(gs_low, wc_ref[t]) * slope_ref[t]).astype(BF16)
        gi_ref[t] = grad_inner
        bg_ref[t : t + 1, :] += jnp.sum(grad_inner.astype(F32), axis=0, keepdims=True)
        grad_normed = grad_normed + dot(grad_inner, wb_ref[t], NT)
    grad_branch = norm_back(grad_normed, normal_one, inverse_one, vec_ref[0:1, :])
    vg_ref[0:1, :] += jnp.sum(grad_normed * normal_one, axis=0, keepdims=True)
    vg_ref[1:2, :] += jnp.sum(grad_normed, axis=0, keepdims=True)
    vg_ref[4:5, :] += jnp.sum(grad_branch, axis=0, keepdims=True)
    gb_ref[...] = grad_branch
    gb_low = grad_branch.astype(BF16)
    gbl_ref[...] = gb_low
    for t in range(groups):
        gm_ref[t] = dot(gb_low, wo_ref[t]).astype(BF16)


def ffn(x, cot, pm, wa, wb, wc, vec, bias):
    tokens, width = x.shape
    groups, _, lanes = wa.shape
    hidden = wb.shape[2]
    tail = 256
    tile = 256
    last = lanes // tail - 1
    once = pl.Buffered(1)
    row = pl.BlockSpec((tile, width), lambda i: (i, 0))
    wide = pl.BlockSpec((groups, tile, hidden), lambda i: (0, i, 0))
    return pl.pallas_call(
        ffn_kernel,
        grid=(tokens // tile,),
        in_specs=[
            row,
            row,
            pl.BlockSpec((groups, tile, tail), lambda i: (0, i, last)),
            pl.BlockSpec((groups, width, tail), lambda i: (0, 0, last), pipeline_mode=once),
            pl.BlockSpec((groups, width, hidden), lambda i: (0, 0, 0), pipeline_mode=once),
            pl.BlockSpec((groups, width, hidden), lambda i: (0, 0, 0), pipeline_mode=once),
            pl.BlockSpec(vec.shape, lambda i: (0, 0)),
            pl.BlockSpec(bias.shape, lambda i: (0, 0)),
        ],
        out_specs=[
            row,
            wide,
            wide,
            row,
            row,
            row,
            row,
            pl.BlockSpec((groups, tile, tail), lambda i: (0, i, 0)),
            pl.BlockSpec((8, width), lambda i: (0, 0)),
            pl.BlockSpec((8, hidden), lambda i: (0, 0)),
        ],
        out_shape=[
            jax.ShapeDtypeStruct((tokens, width), BF16),
            jax.ShapeDtypeStruct((groups, tokens, hidden), BF16),
            jax.ShapeDtypeStruct((groups, tokens, hidden), BF16),
            jax.ShapeDtypeStruct((tokens, width), BF16),
            jax.ShapeDtypeStruct((tokens, width), BF16),
            jax.ShapeDtypeStruct((tokens, width), BF16),
            jax.ShapeDtypeStruct((tokens, width), F32),
            jax.ShapeDtypeStruct((groups, tokens, tail), BF16),
            jax.ShapeDtypeStruct((8, width), F32),
            jax.ShapeDtypeStruct((8, hidden), F32),
        ],
        scratch_shapes=[pltpu.VMEM((groups, tile, hidden), F32)],
        compiler_params=params(),
        name="ffn",
    )(x, cot, pm, wa, wb, wc, vec, bias)


MESH = pl.DeviceIdType.MESH


class Place:
    def __init__(self, sizes):
        dp, tensor = lax.axis_index("dp"), lax.axis_index("tensor")
        self.deep = sizes[0] // 2
        self.z, self.y = dp // 2, dp % 2
        self.x, self.c = tensor // 2, tensor % 2

    def to_z(self, step):
        return {"dp": lax.rem(self.z + step, self.deep) * 2 + self.y}

    def to_y(self):
        return {"dp": self.z * 2 + 1 - self.y}

    def to_x(self):
        return {"tensor": (1 - self.x) * 2 + self.c}

    def to_c(self):
        return {"tensor": self.x * 2 + 1 - self.c}

    def from_z(self, step):
        return lax.rem(self.z + self.deep - step, self.deep)

    def partners(self):
        return [self.to_z(j) for j in range(1, self.deep)] + [self.to_y(), self.to_x(), self.to_c()]

    def peers(self):
        found = []
        for r in range(1, 8):
            x = 1 - self.x if r & 4 else self.x
            y = 1 - self.y if r & 2 else self.y
            c = 1 - self.c if r & 1 else self.c
            found.append((x * 4 + y * 2 + c, {"dp": self.z * 2 + y, "tensor": x * 2 + c}))
        return found

    def greet(self, everyone=False):
        barrier = pltpu.get_barrier_semaphore()
        partners = self.partners()
        if everyone:
            partners = partners[: self.deep - 1] + [device for _, device in self.peers()]
        for partner in partners:
            pl.semaphore_signal(barrier, inc=1, device_id=partner, device_id_type=MESH)
        pl.semaphore_wait(barrier, len(partners))


class Links:
    def __init__(self, send, recv):
        self.send, self.recv = send, recv

    def copy(self, k, ref, to, dst=None):
        return pltpu.make_async_remote_copy(
            src_ref=ref,
            dst_ref=ref if dst is None else dst,
            send_sem=self.send.at[k],
            recv_sem=self.recv.at[k],
            device_id=to,
            device_id_type=MESH,
        )

    def landed(self, k, ref, to):
        self.copy(k, ref, to).wait_recv()


def add_everywhere(place, links, base, own, slots):
    deep = place.deep
    hops = [place.to_c(), place.to_y(), place.to_x()]

    def start(i):
        def run():
            if i:
                links.copy(base + i - 1, own, hops[i - 1], slots.at[i - 1]).wait_send()
                links.landed(base + i - 1, slots.at[i - 1], hops[i - 1])
                own[...] = own[...] + slots[i - 1]
            if i < 3:
                links.copy(base + i, own, hops[i], slots.at[i]).start()
            else:
                for j in range(1, deep):
                    links.copy(base + 2 + j, own, place.to_z(j), slots.at[2 + j]).start()

        return run

    def last():
        for j in range(1, deep):
            links.copy(base + 2 + j, own, place.to_z(j), slots.at[2 + j]).wait_send()
            links.landed(base + 2 + j, slots.at[2 + j], place.to_z(j))
        slots[2] = own[...]
        total = slots[2 + lax.rem(place.z + deep, deep)]
        for z in range(1, deep):
            total = total + slots[2 + lax.rem(place.z + deep - z, deep)]
        own[...] = total

    return [start(0), start(1), start(2), start(3), last]


def add_in_two(place, links, base, own, slots):
    p, deep = place, place.deep
    me = p.x * 4 + p.y * 2 + p.c
    peers = p.peers()

    def near(r):
        return links.copy(base + r, own, peers[r - 1][1], slots.at[me])

    def far(j):
        return links.copy(base + 7 + j, own, p.to_z(j), slots.at[8 + p.z])

    def start():
        for r in range(1, 8):
            near(r).start()
        slots[me] = own[...]

    def middle():
        for r in range(1, 8):
            near(r).wait_send()
            links.landed(base + r, slots.at[peers[r - 1][0]], peers[r - 1][1])
        total = slots[0]
        for k in range(1, 8):
            total = total + slots[k]
        own[...] = total
        for j in range(1, deep):
            far(j).start()
        slots[8 + p.z] = total

    def last():
        for j in range(1, deep):
            far(j).wait_send()
            links.landed(base + 7 + j, slots.at[8 + p.from_z(j)], p.to_z(j))
        total = slots[8]
        for k in range(1, deep):
            total = total + slots[8 + k]
        own[...] = total

    return [start, middle, last]


def gather_stages(place, links, base, own, whole, start=0, count=None):
    p, deep = place, place.deep
    count = own.shape[0] if count is None else count
    half = count // 2
    rows, first, later = pl.ds(start, count), pl.ds(start, half), pl.ds(start + half, half)
    own = own.at[rows]
    mine = whole.at[p.x, p.c, p.z, p.y, rows]
    line = whole.at[p.x, p.c, :, p.y, rows]
    ax = whole.at[p.x, p.c, :, p.y, first]
    ax_in = whole.at[1 - p.x, p.c, :, p.y, first]
    by = whole.at[p.x, p.c, :, p.y, later]
    by_in = whole.at[p.x, p.c, :, 1 - p.y, later]
    ay = whole.at[:, p.c, :, p.y, first]
    ay_in = whole.at[:, p.c, :, 1 - p.y, first]
    bx = whole.at[p.x, p.c, :, :, later]
    bx_in = whole.at[1 - p.x, p.c, :, :, later]
    kz, ka, kb, ks = base, base + deep, base + deep + 2, base + deep + 4

    def keep():
        return pltpu.make_async_copy(own, mine, links.send.at[kz])

    def stage0():
        keep().start()
        for j in range(1, deep):
            links.copy(kz + j, own, p.to_z(j), mine).start()

    def stage1():
        keep().wait()
        for j in range(1, deep):
            links.landed(kz + j, whole.at[p.x, p.c, p.from_z(j), p.y, rows], p.to_z(j))
        links.copy(ka, ax, p.to_x()).start()
        links.copy(kb, by, p.to_y()).start()
        links.copy(ks, line, p.to_c()).start()

    def stage2():
        links.landed(ka, ax_in, p.to_x())
        links.copy(ka + 1, ay, p.to_y()).start()
        links.copy(ks + 1, ax_in, p.to_c()).start()
        links.landed(kb, by_in, p.to_y())
        links.copy(kb + 1, bx, p.to_x()).start()
        links.copy(ks + 2, by_in, p.to_c()).start()

    def stage3():
        links.landed(ka + 1, ay_in, p.to_y())
        links.copy(ks + 3, ay_in, p.to_c()).start()
        links.landed(kb + 1, bx_in, p.to_x())
        links.copy(ks + 4, bx_in, p.to_c()).start()

    def stage4():
        o = 1 - p.c
        links.landed(ks, whole.at[p.x, o, :, p.y, rows], p.to_c())
        links.landed(ks + 1, whole.at[1 - p.x, o, :, p.y, first], p.to_c())
        links.landed(ks + 2, whole.at[p.x, o, :, 1 - p.y, later], p.to_c())
        links.landed(ks + 3, whole.at[:, o, :, 1 - p.y, first], p.to_c())
        links.landed(ks + 4, whole.at[1 - p.x, o, :, :, later], p.to_c())
        for j in range(1, deep):
            links.copy(kz + j, own, p.to_z(j), mine).wait_send()
        links.copy(ka, ax, p.to_x()).wait_send()
        links.copy(kb, by, p.to_y()).wait_send()
        links.copy(ka + 1, ay, p.to_y()).wait_send()
        links.copy(kb + 1, bx, p.to_x()).wait_send()
        links.copy(ks, line, p.to_c()).wait_send()
        links.copy(ks + 1, ax_in, p.to_c()).wait_send()
        links.copy(ks + 2, by_in, p.to_c()).wait_send()
        links.copy(ks + 3, ay_in, p.to_c()).wait_send()
        links.copy(ks + 4, bx_in, p.to_c()).wait_send()

    return [stage0, stage1, stage2, stage3, stage4]


def gather_stages_late(place, links, base, own, whole):
    p, deep = place, place.deep
    half = own.shape[0] // 2
    first, later = pl.ds(0, half), pl.ds(half, half)
    mine = whole.at[p.x, p.c, p.z, p.y]
    pair_f, pair_l = whole.at[:, p.c, p.z, p.y, first], whole.at[p.x, p.c, p.z, :, later]
    line_f, line_l = whole.at[:, p.c, :, p.y, first], whole.at[p.x, p.c, :, :, later]
    line_f_in = whole.at[:, p.c, :, 1 - p.y, first]
    line_l_in = whole.at[1 - p.x, p.c, :, :, later]
    kf, kl = base + 8, base + 8 + deep

    def keep():
        return pltpu.make_async_copy(own, mine, links.send.at[base])

    def to_x():
        return links.copy(base + 1, own.at[first], p.to_x(), mine.at[first])

    def to_y():
        return links.copy(base + 2, own.at[later], p.to_y(), mine.at[later])

    def stage0():
        keep().start()
        to_x().start()
        to_y().start()

    def stage1():
        keep().wait()
        links.landed(base + 1, whole.at[1 - p.x, p.c, p.z, p.y, first], p.to_x())
        links.landed(base + 2, whole.at[p.x, p.c, p.z, 1 - p.y, later], p.to_y())
        for j in range(1, deep):
            links.copy(kf + j, pair_f, p.to_z(j)).start()
            links.copy(kl + j, pair_l, p.to_z(j)).start()

    def stage2():
        for j in range(1, deep):
            z = p.from_z(j)
            links.landed(kf + j, whole.at[:, p.c, z, p.y, first], p.to_z(j))
            links.landed(kl + j, whole.at[p.x, p.c, z, :, later], p.to_z(j))
        links.copy(base + 3, line_f, p.to_y()).start()
        links.copy(base + 4, line_l, p.to_x()).start()
        links.copy(base + 5, line_f, p.to_c()).start()
        links.copy(base + 6, line_l, p.to_c()).start()

    def stage3():
        links.landed(base + 3, line_f_in, p.to_y())
        links.copy(base + 7, line_f_in, p.to_c()).start()
        links.landed(base + 4, line_l_in, p.to_x())
        links.copy(base + 8, line_l_in, p.to_c()).start()

    def stage4():
        o = 1 - p.c
        links.landed(base + 5, whole.at[:, o, :, p.y, first], p.to_c())
        links.landed(base + 6, whole.at[p.x, o, :, :, later], p.to_c())
        links.landed(base + 7, whole.at[:, o, :, 1 - p.y, first], p.to_c())
        links.landed(base + 8, whole.at[1 - p.x, o, :, :, later], p.to_c())
        to_x().wait_send()
        to_y().wait_send()
        for j in range(1, deep):
            links.copy(kf + j, pair_f, p.to_z(j)).wait_send()
            links.copy(kl + j, pair_l, p.to_z(j)).wait_send()
        links.copy(base + 3, line_f, p.to_y()).wait_send()
        links.copy(base + 4, line_l, p.to_x()).wait_send()
        links.copy(base + 5, line_f, p.to_c()).wait_send()
        links.copy(base + 6, line_l, p.to_c()).wait_send()
        links.copy(base + 7, line_f_in, p.to_c()).wait_send()
        links.copy(base + 8, line_l_in, p.to_c()).wait_send()

    return [stage0, stage1, stage2, stage3, stage4]


GATHER_COPIES = 9


def add_into(out, one, two):
    out[...] = one[...] + two[...]


def scatter_core(place, links, base, acc, in_c):
    def move(part):
        return links.copy(base + part, acc.at[2 + part], place.to_c(), in_c.at[part])

    def send(part):
        return lambda: move(part).start()

    def add(part, x):
        def run():
            move(part).wait_send()
            links.landed(base + part, in_c.at[part], place.to_c())

            def one(z, _):
                for y in range(2):
                    there = acc.at[x, z, y]
                    add_into(there, there, in_c.at[part, z, y])
                return 0

            lax.fori_loop(0, place.deep, one, 0)

        return run

    return send, add


def add_line(place, acc, x, y, rows, arrived):
    def add(z, _):
        there = acc.at[x, z, y, rows]
        add_into(there, there, arrived.at[z])
        return 0

    lax.fori_loop(0, place.deep, add, 0)


def scatter_plane(place, links, base, acc, ay_in, ax_in, bx_in, by_in):
    p = place
    half = acc.shape[3] // 2
    first, later, both = pl.ds(0, half), pl.ds(half, half), pl.ds(0, 2)

    def ay():
        return links.copy(base, acc.at[both, :, 1 - p.y, first], p.to_y(), ay_in)

    def bx():
        return links.copy(base + 1, acc.at[1 - p.x, :, :, later], p.to_x(), bx_in)

    def ax():
        return links.copy(base + 2, acc.at[1 - p.x, :, p.y, first], p.to_x(), ax_in)

    def by():
        return links.copy(base + 3, acc.at[p.x, :, 1 - p.y, later], p.to_y(), by_in)

    def start():
        ay().start()
        bx().start()

    def middle():
        links.landed(base, ay_in, p.to_y())
        for x in range(2):
            add_line(p, acc, x, p.y, first, ay_in.at[x])
        ax().start()
        links.landed(base + 1, bx_in, p.to_x())
        for y in range(2):
            add_line(p, acc, p.x, y, later, bx_in.at[:, y])
        by().start()

    def finish():
        links.landed(base + 2, ax_in, p.to_x())
        add_line(p, acc, p.x, p.y, first, ax_in)
        links.landed(base + 3, by_in, p.to_y())
        add_line(p, acc, p.x, p.y, later, by_in)

    def settle():
        for move in (ay, bx, ax, by):
            move().wait_send()

    return start, middle, finish, settle


def scatter_in_pairs(place, links, base, acc, in_c, ay_in, ax_in, bx_in, by_in, in_z, out):
    p, deep = place, place.deep
    half = acc.shape[3] // 2
    first, later = pl.ds(0, half), pl.ds(half, half)
    far, near = 1 - p.x, p.x
    kf, kl = base + 6, base + 6 + deep
    send, add = scatter_core(place, links, base, acc, in_c)

    def over_y(part, x):
        return links.copy(base + 2 + part, acc.at[x, :, 1 - p.y, first], p.to_y(), ay_in.at[part])

    def far_later():
        return links.copy(base + 4, acc.at[far, :, :, later], p.to_x(), bx_in)

    def far_first():
        return links.copy(base + 5, acc.at[far, :, p.y, first], p.to_x(), ax_in)

    def near_later():
        return links.copy(base + 6, acc.at[near, :, 1 - p.y, later], p.to_y(), by_in)

    def over_z(k, j, rows):
        to = lax.rem(p.z + j, deep)
        return links.copy(k + j, acc.at[near, to, p.y, rows], p.to_z(j), in_z.at[j, rows])

    def far1():
        add(0, far)()
        over_y(0, far).start()
        far_later().start()

    def far2():
        links.landed(base + 2, ay_in.at[0], p.to_y())
        add_line(p, acc, far, p.y, first, ay_in.at[0])
        far_first().start()

    def near1():
        over_y(1, near).start()

    def near_x():
        links.landed(base + 4, bx_in, p.to_x())
        for y in range(2):
            add_line(p, acc, near, y, later, bx_in.at[:, y])
        near_later().start()

    def near2():
        links.landed(base + 3, ay_in.at[1], p.to_y())
        add_line(p, acc, near, p.y, first, ay_in.at[1])
        links.landed(base + 5, ax_in, p.to_x())
        add_line(p, acc, near, p.y, first, ax_in)
        for j in range(1, deep):
            over_z(kf, j, first).start()

    def near3():
        links.landed(base + 6, by_in, p.to_y())
        add_line(p, acc, near, p.y, later, by_in)
        for j in range(1, deep):
            over_z(kl, j, later).start()

    def near4():
        for k, rows in ((kf, first), (kl, later)):
            total = acc[near, p.z, p.y, rows].astype(F32)
            for j in range(1, deep):
                links.landed(k + j, in_z.at[j, rows], p.to_z(j))
                total = total + in_z[j, rows].astype(F32)
            out[rows] = total
            for j in range(1, deep):
                over_z(k, j, rows).wait_send()
        over_y(0, far).wait_send()
        over_y(1, near).wait_send()
        far_later().wait_send()
        far_first().wait_send()
        near_later().wait_send()

    return [send(0), far1, far2, send(1), add(1, near), near1, near_x, near2, near3, near4]


def scatter_tail(place, links, base, part, in_z, out):
    deep = place.deep

    def send(j):
        return links.copy(
            base + j, part.at[lax.rem(place.z + j, deep)], place.to_z(j), in_z.at[j]
        )

    def stage0():
        for j in range(1, deep):
            send(j).start()

    def stage1():
        for j in range(1, deep):
            links.landed(base + j, in_z.at[j], place.to_z(j))
        total = part[place.z].astype(F32)
        for j in range(1, deep):
            total = total + in_z[j].astype(F32)
        out[...] = total
        for j in range(1, deep):
            send(j).wait_send()

    return [stage0, stage1]


def core_buffers(deep, rows, lanes):
    return [
        pltpu.VMEM((4, deep, 2, rows, lanes), BF16),
        pltpu.VMEM((2, deep, 2, rows, lanes), BF16),
    ]


def plane_buffers(deep, rows, lanes):
    half = rows // 2
    return [
        pltpu.VMEM((2, deep, half, lanes), BF16),
        pltpu.VMEM((deep, half, lanes), BF16),
        pltpu.VMEM((deep, 2, half, lanes), BF16),
        pltpu.VMEM((deep, half, lanes), BF16),
    ]


def gather_blocks(block, sizes):
    whole = lax.all_gather(block, ("dp", "tensor"), axis=0, tiled=False)
    whole = whole.reshape(sizes + block.shape)
    return jnp.swapaxes(whole, 0, 1).reshape((sizes[1], -1) + block.shape[1:])


def scatter_blocks(grads, sizes):
    parts = grads.reshape((sizes[1], sizes[0], -1) + grads.shape[2:])
    parts = jnp.swapaxes(parts, 0, 1).reshape((sizes[0] * sizes[1],) + parts.shape[2:])
    return lax.psum_scatter(parts, ("dp", "tensor"), scatter_dimension=0, tiled=False)


def adam_parts(grad, mean, square):
    new_mean = MOMENT_DECAY * mean + (1.0 - MOMENT_DECAY) * grad
    new_square = MOMENT_DECAY * square + (1.0 - MOMENT_DECAY) * grad * grad
    correction = 1.0 - MOMENT_DECAY**STEP
    direction = new_mean / correction / (jnp.sqrt(new_square / correction) + ADAM_EPS)
    return new_mean, new_square, direction


def sum_all(values):
    return jnp.sum(jnp.sum(values, axis=1, keepdims=True), axis=0, keepdims=True)


def group_squares(qkv_part, out_part, inner_part, outer_part, vector_part):
    return jnp.concatenate(
        [
            jnp.sum(qkv_part * qkv_part, axis=(1, 2)),
            jnp.sum(out_part * out_part)[None],
            jnp.sum(inner_part * inner_part)[None],
            jnp.sum(outer_part * outer_part)[None],
            jnp.sum(vector_part[:8] * vector_part[:8], axis=1),
            jnp.sum(vector_part[8:] * vector_part[8:])[None],
        ]
    )


def lamb_apply(weight_list, update_list, trust_ratio, row_number):
    qkv_new = weight_list[0] - LEARN_RATE * trust_ratio[0:3, None, None] * update_list[0]
    out_new = weight_list[1] - LEARN_RATE * trust_ratio[3] * update_list[1]
    inner_new = weight_list[2] - LEARN_RATE * trust_ratio[4] * update_list[2]
    outer_new = weight_list[3] - LEARN_RATE * trust_ratio[5] * update_list[3]
    row_ratio = jnp.concatenate(
        [trust_ratio[6:14], jnp.broadcast_to(trust_ratio[14], (row_number - 8,))]
    )
    vector_new = weight_list[4] - LEARN_RATE * row_ratio[:, None] * update_list[4]
    return (qkv_new, out_new, inner_new, outer_new, vector_new)


def lamb_plain(sum_a, sum_b, sum_c, vector_sum, weights, old_means, old_squares):
    qkv_sum = jnp.stack([collect(sum_a, at) for at in (Q_AT, K_AT, V_AT)])
    grad_sums = (qkv_sum, collect(sum_a, O_AT).T, sum_b, sum_c.T, vector_sum)
    decays = (WEIGHT_DECAY, WEIGHT_DECAY, WEIGHT_DECAY, WEIGHT_DECAY, 0.0)
    stats = [adam_parts(*entry) for entry in zip(grad_sums, old_means, old_squares)]
    updates = [stats[i][2] + decays[i] * weights[i] for i in range(5)]
    weight_squares, update_squares = lax.psum(
        (group_squares(*weights), group_squares(*updates)), ("dp", "tensor")
    )
    weight_norms = jnp.sqrt(weight_squares)
    update_norms = jnp.sqrt(update_squares)
    trust_ratio = weight_norms / (update_norms + ADAM_EPS)
    new = lamb_apply(weights, updates, trust_ratio, weights[4].shape[0])
    outs = []
    for i in range(5):
        outs += [stats[i][0], stats[i][1], new[i]]
    return outs + [jnp.stack([weight_norms, update_norms])]


A_PIECES = 3


def own_first(order):
    tensor = lax.axis_index("tensor")
    x, c = tensor // 2, tensor % 2
    return jnp.where(order % 2 == 0, x, 1 - x) * 2 + jnp.where(order < 2, c, 1 - c)


def gather_attend_kernel(
    qkv_ref, out_ref, inner_ref, outer_ref, vec_ref, x_ref, seg_ref,
    wa_hbm, wb_hbm, wc_hbm, full, pm_ref, lse_ref, hid_ref, slope_ref, nlt_ref, xt_ref, n1_ref,
    inv_ref,
    send, recv, slots, pack_a, pack_b, pack_c, wa, wb, wc, bias, low, out_sem,
    *, sizes, chunk,
):
    step = pl.program_id(0)
    groups, deep = sizes[1], sizes[0] // 2
    place = Place(sizes)
    links = Links(send, recv)
    each = GATHER_COPIES + deep
    cols = qkv_ref.shape[2]
    tokens, width = x_ref.shape
    lanes = pack_a.shape[1]
    length = tokens // 2
    tail = 256
    count = pack_a.shape[0] // A_PIECES
    ga = [
        gather_stages(place, links, k * each, pack_a, wa, k * count, count) for k in range(A_PIECES)
    ]
    gb = gather_stages(place, links, A_PIECES * each, pack_b, wb)
    more = (A_PIECES + 1) * each
    small = add_everywhere(place, links, more, full, slots)
    gc = gather_stages_late(place, links, more + deep + 2, pack_c, wc)
    t, s = own_first(jnp.minimum(step // 2, groups - 1)), step % 2
    last = 2 * groups + groups - 1

    def keep(k):
        pairs = ((wa, wa_hbm), (wb, wb_hbm), (wc, wc_hbm))
        return pltpu.make_async_copy(*pairs[k], out_sem.at[k])

    @pl.when(step == 0)
    def _():
        out_rows = out_ref[...].T
        pack_a[...] = spread(qkv_ref[0], qkv_ref[1], qkv_ref[2], out_rows).astype(BF16)
        place.greet()
        for k in range(A_PIECES):
            ga[k][0]()
        pack_c[...] = outer_ref[...].astype(BF16)
        gc[0]()
        pack_b[...] = inner_ref[...].astype(BF16)
        full[...] = jnp.zeros_like(full)
        mine = vec_ref.shape[1]
        full[0 : vec_ref.shape[0], 0:mine] = vec_ref[...]
        index = lax.axis_index("dp") * groups + lax.axis_index("tensor")
        full[...] = pltpu.roll(full[...], index * mine, 1)
        small[0]()
        small[1]()
        ga[0][1]()
        small[2]()
        ga[0][2]()
        ga[1][1]()
        small[3]()
        gb[0]()
        ga[2][1]()
        ga[1][2]()
        ga[2][2]()
        ga[0][3]()
        small[4]()
        for g in range(groups):
            bias[g] = jnp.zeros(bias.shape[1:], F32)
            for h in range(HEADS):
                mine = slice(g * cols + h * HD, g * cols + (h + 1) * HD)
                bias[g, 0:1, Q_AT[h] : Q_AT[h] + HD] = full[6:7, mine]
                bias[g, 0:1, V_AT[h] : V_AT[h] + HD] = full[7:8, mine]
        xt_ref[...] = x_ref[...].T
        n1_ref[...] = x_ref[...].astype(F32) + full[4:5, :]
        ga[1][3]()
        gb[1]()
        gc[1]()
        ga[2][3]()

    @pl.when(step == groups)
    def _():
        for k in range(A_PIECES):
            ga[k][4]()
        keep(0).start()

    @pl.when(step == 2)
    def _():
        gb[2]()

    @pl.when(step == 6)
    def _():
        gb[3]()
        gc[2]()

    @pl.when(step == 2 * groups + 2)
    def _():
        gb[4]()
        keep(1).start()
        gc[3]()

    @pl.when(step == last)
    def _():
        gc[4]()
        keep(2).start()

    @pl.when((step < 2 * groups) & (s == 0))
    def _():
        weight = wa[t // 2, t % 2].reshape(width, lanes)
        for n in range(lanes // 256):
            here = slice(n * 256, (n + 1) * 256)
            proj = dot(x_ref[...], weight[:, here]) + bias[t, 0:1, here]
            pm_ref[0, :, here] = proj.astype(BF16)

    @pl.when(step < 2 * groups)
    def _():
        rows = pl.ds(pl.multiple_of(s * length, length), length)
        row = seg_ref[pl.ds(lax.axis_index("tensor") * 2 + s, 1)]
        attend_heads(pm_ref.at[0, rows], row, lse_ref, chunk)

    @pl.when((step < 2 * groups) & (s == 1))
    def _():
        mixed = mixed_only(pm_ref[0, :, lanes - tail :])
        weight = wa[t // 2, t % 2, :, :, :, lanes - tail :].reshape(width, tail)
        for n in range(width // 256):
            here = slice(n * 256, (n + 1) * 256)
            n1_ref[:, here] += dot(mixed, weight[here], NT)

    @pl.when(step == 2 * groups)
    def _():
        for r in range(tokens // 256):
            rows = slice(r * 256, (r + 1) * 256)
            normal_one, inverse_one = norm_parts(n1_ref[rows])
            n1_ref[rows] = normal_one
            inv_ref[rows] = inverse_one
            part = (normal_one * full[0:1, :] + full[1:2, :]).astype(BF16)
            low[rows] = part
            nlt_ref[:, rows] = part.T

    @pl.when(step >= 2 * groups)
    def _():
        g = own_first(step - 2 * groups)
        weight = wb[g // 2, g % 2].reshape(width, lanes)
        for n in range(lanes // 256):
            here = slice(n * 256, (n + 1) * 256)
            pre = dot(low[...], weight[:, here]) + full[pl.ds(8 + g, 1), here]
            act, turn = gelu_parts(pre)
            hid_ref[0, :, here] = act.astype(BF16)
            slope_ref[0, :, here] = turn.astype(BF16)

    @pl.when(step == last)
    def _():
        for k in range(3):
            keep(k).wait()


def once(shape):
    return pl.BlockSpec(shape, lambda *_: (0,) * len(shape), pipeline_mode=pl.Buffered(1))


def gather_attend(weights, x, seg, sizes):
    qkv, out, inner, outer, vec = weights
    deep, groups = sizes[0] // 2, sizes[1]
    copies = (A_PIECES + 1) * (GATHER_COPIES + deep) + deep + 2 + GATHER_COPIES + 2 * deep
    tokens, width = x.shape
    length = seg.shape[1]
    seqs = tokens // length
    rows, lanes = inner.shape
    steps = groups * seqs
    anywhere = pl.BlockSpec(memory_space=pl.ANY)
    parts = (2, 2, deep, 2, rows, lanes)
    whole = jax.ShapeDtypeStruct(parts, BF16)

    def now(i):
        i = jnp.minimum(i, steps - 1)
        return own_first(i // 2), i % 2

    def part(i):
        return own_first(jnp.clip(i - steps, 0, groups - 1))

    wa, wb, wc, *rest = pl.pallas_call(
        functools.partial(gather_attend_kernel, sizes=sizes, chunk=min(256, length)),
        grid=(steps + groups,),
        in_specs=[once(w.shape) for w in weights]
        + [
            once(x.shape),
            once(seg.shape),
        ],
        out_specs=[anywhere] * 3
        + [
            once((16, width)),
            pl.BlockSpec((1, tokens, lanes), lambda i: (now(i)[0], 0, 0)),
            pl.BlockSpec((1, 1, 8, length), lambda i: (*now(i), 0, 0)),
            pl.BlockSpec((1, tokens, lanes), lambda i: (part(i), 0, 0)),
            pl.BlockSpec((1, tokens, lanes), lambda i: (part(i), 0, 0)),
            once((width, tokens)),
            once((width, tokens)),
            once((tokens, width)),
            once((tokens, 1)),
        ],
        out_shape=[whole] * 3
        + [
            jax.ShapeDtypeStruct((16, width), F32),
            jax.ShapeDtypeStruct((groups, tokens, lanes), BF16),
            jax.ShapeDtypeStruct((groups, seqs, 8, length), F32),
            jax.ShapeDtypeStruct((groups, tokens, lanes), BF16),
            jax.ShapeDtypeStruct((groups, tokens, lanes), BF16),
            jax.ShapeDtypeStruct((width, tokens), BF16),
            jax.ShapeDtypeStruct((width, tokens), BF16),
            jax.ShapeDtypeStruct((tokens, width), F32),
            jax.ShapeDtypeStruct((tokens, 1), F32),
        ],
        scratch_shapes=[
            pltpu.SemaphoreType.DMA((copies,)),
            pltpu.SemaphoreType.DMA((copies,)),
            pltpu.VMEM((deep + 2, 16, width), F32),
            pltpu.VMEM((rows, lanes), BF16),
            pltpu.VMEM((rows, lanes), BF16),
            pltpu.VMEM((rows, lanes), BF16),
            pltpu.VMEM(parts, BF16),
            pltpu.VMEM(parts, BF16),
            pltpu.VMEM(parts, BF16),
            pltpu.VMEM((groups, 8, lanes), F32),
            pltpu.VMEM((tokens, width), BF16),
            pltpu.SemaphoreType.DMA((3,)),
        ],
        compiler_params=params(collective_id=0, has_side_effects=True),
        name="gather_attend",
    )(*weights, x, seg)
    shape = (groups, sizes[0] * rows, lanes)
    return [wa.reshape(shape), wb.reshape(shape), wc.reshape(shape)] + rest


def other_first(order):
    c = lax.axis_index("tensor") % 2
    return order % 2 * 2 + jnp.where(order < 2, 1 - c, c)


def layer_kernel(
    cot_ref, hid_ref, slope_ref, inv_ref, vec_ref, n1_hbm, nlt_hbm, wa_hbm, wb_hbm, wc_hbm,
    out_hbm, gb_hbm, gm_hbm, gbt_hbm, accb_hbm, part_ref, vg_ref, bg_ref,
    n1_ref, nlt_ref, wo_ref, wb_ref, wc_ref, acc, low, gst, gi, out_ref, gm_ref, gbt_ref,
    in_sem, out_sem, send, recv, accc, in_cc, accb, in_cb, ay_in, ax_in, bx_in, by_in, *, sizes,
):
    step = pl.program_id(0)
    tokens, width = acc.shape
    groups, deep = sizes[1], sizes[0] // 2
    lanes = wa_hbm.shape[2]
    tail = wo_ref.shape[2]
    last = 3 * groups - 1
    place = Place(sizes)
    links = Links(send, recv)
    send_c, add_c = scatter_core(place, links, 0, accc, in_cc)
    send_b, add_b = scatter_core(place, links, 2, accb, in_cb)
    start, middle, finish, settle = scatter_plane(
        place, links, 4, accc, ay_in, ax_in, bx_in, by_in
    )
    blocks = [slice(r * 256, (r + 1) * 256) for r in range(tokens // 256)]
    columns = [slice(n * 256, (n + 1) * 256) for n in range(width // 256)]

    def outer(t):
        return pltpu.make_async_copy(wc_hbm.at[t], wc_ref.at[t], in_sem.at[t])

    def inner(t):
        return pltpu.make_async_copy(wb_hbm.at[t], wb_ref.at[t], in_sem.at[groups + t])

    def load(k):
        pairs = (
            (n1_hbm, n1_ref), (nlt_hbm, nlt_ref.at[pl.ds(0, width)]), (wa_hbm.at[:, :, pl.ds(lanes - tail, tail)], wo_ref)
        )
        return pltpu.make_async_copy(*pairs[k], in_sem.at[2 * groups + k])

    def store(k):
        pairs = (
            (out_ref, out_hbm), (gbt_ref, gbt_hbm), (accb.at[pl.ds(0, 2)], accb_hbm), (acc, gb_hbm)
        )
        return pltpu.make_async_copy(*pairs[k], out_sem.at[k])

    def store_mixed(t):
        return pltpu.make_async_copy(gm_ref.at[t], gm_hbm.at[t], out_sem.at[4 + t])

    @pl.when(step == 0)
    def _():
        for t in range(groups):
            outer(t).start()
        load(0).start()
        for t in range(groups):
            inner(t).start()
        load(1).start()
        load(2).start()
        place.greet()
        vg_ref[...] = jnp.zeros_like(vg_ref)
        bg_ref[...] = jnp.zeros_like(bg_ref)
        acc[...] = jnp.zeros_like(acc)
        nlt_ref[width:] = jnp.ones((nlt_ref.shape[0] - width, tokens), BF16)

    @pl.when(step < groups)
    def _():
        outer(step).wait()
        for here in columns:
            acc[:, here] += dot(hid_ref[0], wc_ref[step, here], NT)

    @pl.when(step == groups - 1)
    def _():
        load(0).wait()
        for rows in blocks:
            second = n1_ref[rows] * vec_ref[0:1, :] + vec_ref[1:2, :] + vec_ref[5:6, :]
            normal_two, inverse_two = norm_parts(second + acc[rows])
            out_ref[rows] = (normal_two * vec_ref[2:3, :] + vec_ref[3:4, :]).astype(BF16)
            cot = cot_ref[rows].astype(F32)
            grad_second = norm_back(cot, normal_two, inverse_two, vec_ref[2:3, :])
            vg_ref[2:3, :] += jnp.sum(cot * normal_two, axis=0, keepdims=True)
            vg_ref[3:4, :] += jnp.sum(cot, axis=0, keepdims=True)
            vg_ref[5:6, :] += jnp.sum(grad_second, axis=0, keepdims=True)
            acc[rows] = grad_second
            part = grad_second.astype(BF16)
            low[rows] = part
            gst[:, rows] = part.T
        store(0).start()

    @pl.when((step >= groups) & (step < 2 * groups))
    def _():
        slot = lax.rem(step - groups + 2, 4)
        for here in columns:
            part = dot(gst[...], hid_ref[0, :, here]).astype(BF16)
            accc[slot, :, :, :, here] = part.reshape(deep, 2, -1, 256)

    @pl.when(step == groups + 1)
    def _():
        send_c(0)()

    @pl.when(step == groups + 2)
    def _():
        send_c(1)()

    @pl.when(step == 2 * groups)
    def _():
        add_c(0, 0)()
        add_c(1, 1)()
        start()
        for t in range(groups):
            inner(t).wait()
        load(1).wait()
        load(2).wait()

    @pl.when(step == last)
    def _():
        middle()

    @pl.when(step >= 2 * groups)
    def _():
        order = step - 2 * groups
        slot = lax.rem(order + 2, 4)
        t = other_first(order)
        for here in columns:
            grad_hidden = dot(low[...], wc_ref[t, :, here])
            part = (grad_hidden * slope_ref[0, :, here].astype(F32)).astype(BF16)
            gi[:, here] = part
        for here in columns:
            acc[:, here] += dot(gi[...], wb_ref[t, here], NT)
        for here in columns:
            part = dot(nlt_ref[...], gi[:, here])
            bg_ref[pl.ds(t, 1), here] = part[width : width + 1]
            accb[slot, :, :, :, here] = part[:width].astype(BF16).reshape(deep, 2, -1, 256)

    @pl.when(step == 2 * groups + 1)
    def _():
        send_b(0)()

    @pl.when(step == 2 * groups + 2)
    def _():
        send_b(1)()

    @pl.when(step == last)
    def _():
        for rows in blocks:
            grad_normed = acc[rows]
            normal_one = n1_ref[rows]
            grad_branch = norm_back(grad_normed, normal_one, inv_ref[rows], vec_ref[0:1, :])
            vg_ref[0:1, :] += jnp.sum(grad_normed * normal_one, axis=0, keepdims=True)
            vg_ref[1:2, :] += jnp.sum(grad_normed, axis=0, keepdims=True)
            vg_ref[4:5, :] += jnp.sum(grad_branch, axis=0, keepdims=True)
            acc[rows] = grad_branch
            part = grad_branch.astype(BF16)
            low[rows] = part
            gbt_ref[:, rows] = part.T
        store(3).start()
        store(1).start()
        for t in range(groups):
            gm_ref[t] = dot(low[...], wo_ref[t]).astype(BF16)
            store_mixed(t).start()
        add_b(0, 0)()
        add_b(1, 1)()
        store(2).start()
        finish()
        part_ref[...] = accc[place.x, :, place.y]
        settle()
        for k in range(4):
            store(k).wait()
        for t in range(groups):
            store_mixed(t).wait()


def layer(cot, hid, slope, n1, inv1, nlt, wa, wb, wc, vec, sizes):
    tokens, width = cot.shape
    groups, _, lanes = wa.shape
    hidden = wb.shape[2]
    deep = sizes[0] // 2
    rows = width // sizes[0]
    tail = 256
    anywhere = pl.BlockSpec(memory_space=pl.ANY)

    def used(i):
        return jnp.where(i < groups, i, other_first(jnp.clip(i - groups, 0, groups - 1)))

    def back_group(i):
        return other_first(jnp.clip(i - 2 * groups, 0, groups - 1))

    copies = 8
    parts = (2, deep, 2, rows, hidden)
    matrix = pltpu.VMEM((groups, width, hidden), BF16)
    return pl.pallas_call(
        functools.partial(layer_kernel, sizes=sizes),
        grid=(3 * groups,),
        in_specs=[
            once(cot.shape),
            pl.BlockSpec((1, tokens, hidden), lambda i: (used(i), 0, 0)),
            pl.BlockSpec((1, tokens, hidden), lambda i: (back_group(i), 0, 0)),
            once(inv1.shape),
            once(vec.shape),
        ]
        + [anywhere] * 5,
        out_specs=[anywhere] * 5
        + [once((deep, rows, hidden)), once((8, width)), once((8, hidden))],
        out_shape=[
            jax.ShapeDtypeStruct((tokens, width), BF16),
            jax.ShapeDtypeStruct((tokens, width), F32),
            jax.ShapeDtypeStruct((groups, tokens, tail), BF16),
            jax.ShapeDtypeStruct((width, tokens), BF16),
            jax.ShapeDtypeStruct(parts, BF16),
            jax.ShapeDtypeStruct((deep, rows, hidden), BF16),
            jax.ShapeDtypeStruct((8, width), F32),
            jax.ShapeDtypeStruct((8, hidden), F32),
        ],
        scratch_shapes=[
            pltpu.VMEM(n1.shape, F32),
            pltpu.VMEM((width + 16, tokens), BF16),
            pltpu.VMEM((groups, width, tail), BF16),
            matrix,
            matrix,
            pltpu.VMEM((tokens, width), F32),
            pltpu.VMEM((tokens, width), BF16),
            pltpu.VMEM((width, tokens), BF16),
            pltpu.VMEM((tokens, hidden), BF16),
            pltpu.VMEM((tokens, width), BF16),
            pltpu.VMEM((groups, tokens, tail), BF16),
            pltpu.VMEM((width, tokens), BF16),
            pltpu.SemaphoreType.DMA((2 * groups + 3,)),
            pltpu.SemaphoreType.DMA((4 + groups,)),
            pltpu.SemaphoreType.DMA((copies,)),
            pltpu.SemaphoreType.DMA((copies,)),
        ]
        + core_buffers(deep, rows, hidden) * 2
        + plane_buffers(deep, rows, hidden),
        compiler_params=params(collective_id=1, has_side_effects=True),
        name="layer",
    )(cot, hid, slope, inv1, vec, n1, nlt, wa, wb, wc)


def far_first(step, groups):
    tensor = lax.axis_index("tensor")
    x, c = tensor // 2, tensor % 2
    return jnp.where(step < groups, 1 - x, x) * 2 + jnp.where(step % groups < 2, 1 - c, c)


def back_kernel(
    pm_ref, gm_ref, lse_ref, seg_ref, wa_hbm, xt_hbm, gbt_hbm, gb_hbm,
    accb_hbm, part_ref, vg_ref, bg_ref, *refs, sizes, chunk,
):
    weights, means, squares = refs[0:5], refs[5:10], refs[10:15]
    grads, updates, norms, ig_ref = refs[15:20], refs[20:25], refs[25], refs[26]
    gp, gsum, send, recv, slots, hslots, nslots, vec, hvec, load_sem, sa = refs[27:38]
    wa_ref, xt_ref, gbt_ref, gb_ref, accb, inz_b, inz_c = refs[38:45]
    bufs_b, bufs_a, acc = refs[45:49], refs[49:56], refs[49]
    sb, sc = grads[2], grads[3]
    step = pl.program_id(0)
    groups, deep = sizes[1], sizes[0] // 2
    cols = HEADS * HD
    tokens, width = gb_ref.shape
    lanes = pm_ref.shape[2]
    last = 2 * groups - 1
    length = pm_ref.shape[1]
    place = Place(sizes)
    links = Links(send, recv)
    a = scatter_in_pairs(place, links, 0, *bufs_a, sa)
    more = 7 + 2 * deep
    start, middle, finish, settle = scatter_plane(place, links, more, accb, *bufs_b)
    b = scatter_tail(place, links, more + 4, accb.at[place.x, :, place.y], inz_b, sb)
    c = scatter_tail(place, links, more + 4 + deep, part_ref, inz_c, sc)
    early = add_everywhere(place, links, more + 4 + 2 * deep, vec, slots)
    small = add_everywhere(place, links, more + 6 + 3 * deep, hvec, hslots)
    final = add_in_two(place, links, more + 8 + 4 * deep, norms, nslots)
    t, s = far_first(step, groups), step % 2

    def load(k):
        pairs = ((accb_hbm, accb), (xt_hbm, xt_ref.at[pl.ds(0, width)]), (gbt_hbm, gbt_ref), (wa_hbm, wa_ref), (gb_hbm, gb_ref))
        return pltpu.make_async_copy(*pairs[k], load_sem.at[k])

    @pl.when(step == 0)
    def _():
        load(0).start()
        place.greet(everyone=True)
        c[0]()
        load(0).wait()
        start()
        for k in range(1, 5):
            load(k).start()
        xt_ref[width:] = jnp.ones((xt_ref.shape[0] - width, tokens), BF16)
        vec[...] = jnp.zeros_like(vec)
        hvec[...] = jnp.zeros_like(hvec)
        vec[0:6] = vg_ref[0:6]
        vec[8 : 8 + groups] = bg_ref[0:groups]
        early[0]()

    @pl.when(step == 1)
    def _():
        load(1).wait()
        load(2).wait()

    @pl.when(step == 2)
    def _():
        a[0]()
        early[1]()

    @pl.when(step == 4)
    def _():
        early[2]()
        middle()
        a[1]()

    @pl.when(step == 5)
    def _():
        c[1]()

    @pl.when(step == 6)
    def _():
        a[3]()
        early[3]()

    @pl.when(step == 7)
    def _():
        finish()
        b[0]()

    rows = pl.ds(pl.multiple_of(s * length, length), length)
    row = seg_ref[pl.ds(lax.axis_index("tensor") * 2 + s, 1)]
    attend_back(pm_ref.at[0], gm_ref.at[0], lse_ref, row, gp.at[t, rows], chunk)

    @pl.when(s == 1)
    def _():
        order = step // 2
        slot = jnp.where(order % 2 == 0, 2 + order // 2, t // 2)
        for n in range(lanes // 256):
            here = slice(n * 256, (n + 1) * 256)
            if n < lanes // 256 - 1:
                part = dot(xt_ref[...], gp[t, :, here])
                gsum[t, 0:1, here] = part[width : width + 1]
                part = part[:width]
            else:
                from_x = dot(xt_ref[0:width], gp[t, :, here])
                part = dot(gbt_ref[...], gp[t, :, here])
                lane = lax.broadcasted_iota(jnp.int32, part.shape, 1)
                part = jnp.where((lane >= 128) & (lane < 192), from_x, part)
            acc[slot, :, :, :, here] = part.astype(BF16).reshape(deep, 2, -1, 256)

    def input_columns(n):
        here = slice(n * 256, (n + 1) * 256)
        total = gb_ref[:, here]
        for g in range(groups):
            part = gp[g, :, 640:768]
            part = halves(part, jnp.zeros_like(part))
            total = total + dot(gp[g, :, 0:512], wa_ref[g, here, 0:512], NT)
            total = total + dot(part, wa_ref[g, here, 640:768], NT)
        ig_ref[:, here] = total.astype(BF16)

    @pl.when(step == last)
    def _():
        for g in range(groups):
            for h in range(HEADS):
                at = g * cols + h * HD
                line, lane = at // 256, slice(at % 256, at % 256 + HD)
                hvec[line : line + 1, lane] = gsum[g, 0:1, Q_AT[h] : Q_AT[h] + HD]
                hvec[3 + line : 4 + line, lane] = gsum[g, 0:1, V_AT[h] : V_AT[h] + HD]
        small[0]()
        a[4]()
        a[5]()
        a[2]()
        load(3).wait()
        load(4).wait()
        input_columns(0)
        small[1]()
        a[6]()
        early[4]()
        input_columns(1)
        small[2]()
        a[7]()
        input_columns(2)
        a[8]()
        small[3]()
        b[1]()
        settle()
        found = group_sums([None] * 4 + [sb[...], sc[...], None], weights, means, squares, updates)
        small[4]()
        for k in range(3):
            lanes_of = slice(k * 256, (k + 1) * 256)
            vec[6:7, lanes_of] = hvec[k : k + 1]
            vec[7:8, lanes_of] = hvec[3 + k : 4 + k]
        count, mine = weights[4].shape
        index = lax.axis_index("dp") * groups + lax.axis_index("tensor")
        turned = pltpu.roll(vec[...], width - index * mine, 1)
        grads[4][...] = turned[0:count, 0:mine]
        found = found + group_sums(
            [None] * 6 + [grads[4][...]], weights, means, squares, updates
        )
        a[9]()
        total = sa[...]
        for k, at in enumerate((Q_AT, K_AT, V_AT)):
            grads[0][k] = collect(total, at)
        grads[1][...] = collect(total, O_AT).T
        parts = [grads[0][k] for k in range(3)] + [grads[1][...]]
        norms[...] = found + group_sums(parts + [None] * 3, weights, means, squares, updates)
        for run in final:
            run()


def group_sums(grads, weights, means, squares, updates):
    lane = lax.broadcasted_iota(jnp.int32, (8, 128), 1)
    line = lax.broadcasted_iota(jnp.int32, (8, 128), 0)
    found = jnp.zeros((8, 128), F32)
    for group, grad in enumerate(grads):
        if grad is None:
            continue
        i, k = (0, group) if group < 3 else (group - 2, ...)
        weight, mean, square = (ref[i][k] for ref in (weights, means, squares))
        update = adam_parts(grad, mean, square)[2]
        if i < 4:
            update = update + WEIGHT_DECAY * weight
        updates[i][k] = update
        if i < 4:
            pair = (sum_all(weight * weight), sum_all(update * update))
            for which in range(2):
                hit = (lane == group) & (line == which)
                found = found + jnp.where(hit, pair[which], 0.0)
            continue
        for which, values in enumerate((weight, update)):
            per_row = jnp.sum(values * values, axis=1, keepdims=True)
            for row in range(weight.shape[0]):
                hit = (lane == 6 + min(row, 8)) & (line == which)
                found = found + jnp.where(hit, per_row[row : row + 1], 0.0)
    return found


def back(pm, gm, lse, seg, wa, xt, gbt, gb, accb, part, vg, bg,
         weights, means, squares, sizes):
    deep, groups = sizes[0] // 2, sizes[1]
    tokens, width = gb.shape
    lanes = pm.shape[2]
    length = seg.shape[1]
    seqs = tokens // length
    rows = width // sizes[0]
    copies = 7 + 2 * deep + 4 + 2 * deep + 2 * (deep + 2) + 7 + deep
    small = [weights, means, squares]
    anywhere = pl.BlockSpec(memory_space=pl.ANY)
    outs = [jax.ShapeDtypeStruct(weight.shape, F32) for weight in weights] * 2 + [
        jax.ShapeDtypeStruct((8, 128), F32),
        jax.ShapeDtypeStruct((tokens, width), BF16),
    ]
    return pl.pallas_call(
        functools.partial(back_kernel, sizes=sizes, chunk=min(256, length)),
        grid=(groups * seqs,),
        in_specs=[
            pl.BlockSpec((1, length, lanes), lambda i: (far_first(i, groups), i % 2, 0)),
            pl.BlockSpec((1, length, gm.shape[2]), lambda i: (far_first(i, groups), i % 2, 0)),
            pl.BlockSpec((1, 1, 8, length), lambda i: (far_first(i, groups), i % 2, 0, 0)),
            once(seg.shape),
            anywhere,
            anywhere,
            anywhere,
            anywhere,
            anywhere,
            once(part.shape),
            once(vg.shape),
            once(bg.shape),
        ]
        + [once(ref.shape) for group in small for ref in group],
        out_specs=[once(ref.shape) for ref in outs],
        out_shape=outs,
        scratch_shapes=[
            pltpu.VMEM((groups, tokens, lanes), BF16),
            pltpu.VMEM((groups, 8, lanes), F32),
            pltpu.SemaphoreType.DMA((copies,)),
            pltpu.SemaphoreType.DMA((copies,)),
            pltpu.VMEM((deep + 2, 16, width), F32),
            pltpu.VMEM((deep + 2, 8, 256), F32),
            pltpu.VMEM((8 + deep, 8, 128), F32),
            pltpu.VMEM((16, width), F32),
            pltpu.VMEM((8, 256), F32),
            pltpu.SemaphoreType.DMA((5,)),
            pltpu.VMEM((rows, lanes), F32),
            pltpu.VMEM(wa.shape, BF16),
            pltpu.VMEM((width + 16, tokens), BF16),
            pltpu.VMEM(gbt.shape, BF16),
            pltpu.VMEM(gb.shape, F32),
            pltpu.VMEM(accb.shape, BF16),
            pltpu.VMEM((deep, rows, lanes), BF16),
            pltpu.VMEM((deep, rows, lanes), BF16),
        ]
        + plane_buffers(deep, rows, lanes)
        + core_buffers(deep, rows, lanes)
        + plane_buffers(deep, rows, lanes)
        + [pltpu.VMEM((deep, rows, lanes), BF16)],
        compiler_params=params(collective_id=2, has_side_effects=True),
        name="back",
    )(
        pm, gm, lse, seg, wa, xt, gbt, gb,
        accb, part, vg, bg,
        *weights, *means, *squares,
    )


def apply_kernel(*refs):
    grads, updates, sums = refs[0:5], refs[5:10], refs[10]
    weights, means, squares = refs[11:16], refs[16:21], refs[21:26]
    passed, outs, norms = refs[26:28], refs[28:43], refs[43]
    wide, sem = refs[46], refs[47]
    stores = [pltpu.make_async_copy(passed[0], refs[44], sem.at[0])]
    stores[0].start()
    rows = wide.shape[0] // 4
    for k in range(4):
        here = pl.ds(k * rows, rows)
        wide[here] = passed[1][here].astype(F32)
        stores.append(pltpu.make_async_copy(wide.at[here], refs[45].at[here], sem.at[1 + k]))
        stores[-1].start()
    roots = jnp.sqrt(sums[...])
    norms[...] = roots[0:2, 0:15]
    ratio = LEARN_RATE * roots[0:1] / (roots[1:2] + ADAM_EPS)
    for i in range(5):
        grad = grads[i][...]
        outs[3 * i][...] = MOMENT_DECAY * means[i][...] + (1.0 - MOMENT_DECAY) * grad
        outs[3 * i + 1][...] = (
            MOMENT_DECAY * squares[i][...] + (1.0 - MOMENT_DECAY) * grad * grad
        )
        target = outs[3 * i + 2]
        if i == 0:
            for k in range(3):
                target[k] = weights[i][k] - ratio[:, k : k + 1] * updates[i][k]
        elif i < 4:
            target[...] = weights[i][...] - ratio[:, 2 + i : 3 + i] * updates[i][...]
        else:
            for row in range(target.shape[0]):
                here = slice(row, row + 1)
                step = ratio[:, 6 + min(row, 8) : 7 + min(row, 8)]
                target[here] = weights[i][here] - step * updates[i][here]
    for move in stores:
        move.wait()


def apply(grads, updates, sums, weights, means, squares, passed):
    inside = pl.BlockSpec(memory_space=pltpu.VMEM)
    shapes = []
    for weight in weights:
        shapes += [jax.ShapeDtypeStruct(weight.shape, F32)] * 3
    shapes.append(jax.ShapeDtypeStruct((2, 15), F32))
    shapes += [jax.ShapeDtypeStruct(passed[0].shape, BF16)]
    shapes += [jax.ShapeDtypeStruct(passed[1].shape, F32)]
    anywhere = [pl.BlockSpec(memory_space=pl.ANY)] * 2
    return pl.pallas_call(
        apply_kernel,
        in_specs=[inside] * 28,
        out_specs=[inside] * 16 + anywhere,
        out_shape=shapes,
        scratch_shapes=[
            pltpu.VMEM(passed[1].shape, F32),
            pltpu.SemaphoreType.DMA((5,)),
        ],
        compiler_params=params(),
        name="apply",
    )(*grads, *updates, sums, *weights, *means, *squares, *passed)


def make_body(sizes):
    def body(
        tokens, cotangent, segments,
        qkv_weight, out_weight, inner_weight, outer_weight, vectors,
        qkv_mean, out_mean, inner_mean, outer_mean, vector_mean,
        qkv_square, out_square, inner_square, outer_square, vector_square,
    ):
        groups = sizes[1]
        token_count, width = tokens.shape
        length = segments.shape[1]
        seqs = token_count // length
        cols = qkv_weight.shape[2]
        tensor_index = lax.axis_index("tensor")
        weights = (qkv_weight, out_weight, inner_weight, outer_weight, vectors)
        old_means = (qkv_mean, out_mean, inner_mean, outer_mean, vector_mean)
        old_squares = (qkv_square, out_square, inner_square, outer_square, vector_square)
        if sizes[0] % 2 == 0 and groups == 4 and qkv_weight.shape[1] % 96 == 0:
            weights, old_means, old_squares = (
                entry[:3] + (entry[3].T, entry[4]) for entry in (weights, old_means, old_squares)
            )
            wa, wb, wc, full, pm, lse, hid, slope, nlt, xt, n1, inv1 = gather_attend(
                weights, tokens, segments, sizes
            )
            result, gb, gm, gbt, accb, part, vg, bg = layer(
                cotangent, hid, slope, n1, inv1, nlt, wa, wb, wc, full, sizes
            )
            *changes, sums, input_grad = back(
                pm, gm, lse, segments, wa, xt, gbt, gb, accb, part, vg, bg,
                weights, old_means, old_squares, sizes,
            )
            passed = (result, input_grad)
            new = list(
                apply(changes[:5], changes[5:], sums, weights, old_means, old_squares, passed)
            )
            new[9:12] = [entry.T for entry in new[9:12]]
            return tuple(new[16:]) + tuple(new[:16])
        seg = lax.dynamic_slice_in_dim(segments, tensor_index * seqs, seqs, 0)
        seg = jnp.broadcast_to(seg[:, None, :], (seqs, 8, length))
        pack_a = spread(qkv_weight[0], qkv_weight[1], qkv_weight[2], out_weight.T).astype(BF16)
        pack_b = inner_weight.astype(BF16)
        pack_c = outer_weight.T.astype(BF16)
        wa, wb, wc = (gather_blocks(pack, sizes) for pack in (pack_a, pack_b, pack_c))
        full = lax.all_gather(vectors, ("dp", "tensor"), axis=1, tiled=True)
        q_bias = full[6].reshape(groups, cols)
        v_bias = full[7].reshape(groups, cols)
        none = jnp.zeros_like(q_bias)
        proj_bias = spread(q_bias, none, v_bias, none)
        proj_bias = jnp.broadcast_to(proj_bias[:, None, :], (groups, 8, 4 * cols))
        inner_bias = full[8:].reshape(groups, -1)
        pm, lse = attend_fwd(tokens, wa, proj_bias, seg, length)
        result, hid, gi, nl, gsl, gbl, gb, gm, vg, bg = ffn(
            tokens, cotangent, pm, wa, wb, wc, full, inner_bias
        )
        gp, gsum = attend_bwd(pm, gm, lse, seg)

        grad_c = jnp.einsum("td,gtf->gdf", gsl, hid, preferred_element_type=F32).astype(BF16)
        grad_b = jnp.einsum("td,gtf->gdf", nl, gi, preferred_element_type=F32).astype(BF16)
        from_tokens = jnp.einsum("td,gtc->gdc", tokens, gp, preferred_element_type=F32)
        from_branch = jnp.einsum("td,gtc->gdc", gbl, pm, preferred_element_type=F32)
        lane = lax.broadcasted_iota(jnp.int32, (1, 1, LANES), 2)
        is_mixed = (lane >= 512) & ((lane < 640) | (lane >= 704))
        grad_a = jnp.where(is_mixed, from_branch, from_tokens).astype(BF16)
        input_grad = gb + jnp.einsum(
            "gtc,gdc->td",
            jnp.where(is_mixed, jnp.zeros((), BF16), gp),
            wa,
            preferred_element_type=F32,
        )
        head_rows = jnp.stack([collect(gsum[:, 0], at).reshape(-1) for at in (Q_AT, V_AT)])
        vector_grad = jnp.concatenate([vg[:6], head_rows, bg[:groups].reshape(-1, width)], axis=0)
        sum_a, sum_b, sum_c = (
            scatter_blocks(grad, sizes).astype(F32) for grad in (grad_a, grad_b, grad_c)
        )
        vector_sum = lax.psum_scatter(
            vector_grad, ("dp", "tensor"), scatter_dimension=1, tiled=True
        )
        new = lamb_plain(sum_a, sum_b, sum_c, vector_sum, weights, old_means, old_squares)
        return (result, input_grad) + tuple(new)

    return body

def solution(mesh):
    sizes = (mesh.shape["dp"], mesh.shape["tensor"])
    rows = P(("dp", "tensor"), None)
    qkv = P(None, "dp", "tensor")
    out = P("tensor", "dp")
    inner = P("dp", "tensor")
    vec = P(None, ("dp", "tensor"))
    weights = (qkv, out, inner, out, vec)
    return jax.shard_map(
        make_body(sizes),
        mesh=mesh,
        in_specs=(rows, rows, P("dp", None)) + weights * 3,
        out_specs=(rows, rows) + (qkv,) * 3 + (out,) * 3 + (inner,) * 3 + (out,) * 3 + (vec,) * 3 + (P(),),
        check_vma=False,
    )
```

```python
import functools

import jax
import jax.numpy as jnp
from jax import lax
from jax.experimental import pallas as pl
from jax.experimental.pallas import tpu as pltpu
from jax.sharding import PartitionSpec as P

HD = 64
STEP = 5
NORM_EPS = 1e-05
ADAM_EPS = 1e-06
MOMENT_DECAY = 0.5
LEARN_RATE = 0.5
WEIGHT_DECAY = 0.01
MASKED = -1e30
SCALE = HD ** (-0.5)
F32 = jnp.float32
BF16 = jnp.bfloat16
NT = (((1,), (1,)), ((), ()))
NN = (((1,), (0,)), ((), ()))
TN = (((0,), (0,)), ((), ()))
VMEM_LIMIT = 60 * 1024 * 1024


def dot(a, b, dims=NN):
    return lax.dot_general(a, b, dims, preferred_element_type=F32)


def params(**kw):
    return pltpu.CompilerParams(vmem_limit_bytes=VMEM_LIMIT, **kw)


HEADS = 3
DOCS = 4
LANES = 768
Q_AT, K_AT, V_AT, O_AT = (0, 64, 384), (128, 192, 640), (256, 320, 448), (512, 576, 704)
Q_TILE, K_TILE, V_TILE = (0, 0, 3), (1, 1, 5), (2, 2, 3)
UPPER = (False, True, False)
V_UPPER = (False, True, True)


def spread(q, k, v, o):
    parts = {}
    for places, values in ((Q_AT, q), (K_AT, k), (V_AT, v), (O_AT, o)):
        for h, at in enumerate(places):
            parts[at] = values[:, h * HD : (h + 1) * HD]
    return jnp.concatenate([parts[at] for at in sorted(parts)], axis=1)


def collect(values, places):
    return jnp.concatenate([values[:, at : at + HD] for at in places], axis=1)


def tile_of(ref, n, rows=slice(None)):
    return ref[rows, n * 128 : (n + 1) * 128]


def is_low(shape):
    return lax.broadcasted_iota(jnp.int32, shape, 1) < HD


def halves(low, high):
    return jnp.where(is_low(low.shape), low, high)


def document_lanes(row):
    length = row.shape[1]
    number = jnp.broadcast_to(row.astype(F32), (128, length)).T
    lane = lax.broadcasted_iota(jnp.int32, (length, 128), 1) % HD
    same = number == lane.astype(F32)
    for_query = jnp.where(same, 1.0, 0.0).astype(BF16)
    for_key = jnp.where(same, 0.0, jnp.where(lane < DOCS, MASKED, 0.0)).astype(BF16)
    return for_query, for_key


def attend_heads(pm_ref, row, lse_ref, chunk):
    length = pm_ref.shape[0]
    chunks = length // chunk
    doc_q, doc_k = document_lanes(row)
    ones = jnp.ones((16, length), BF16)
    units = [(h, c) for h in range(HEADS) for c in range(chunks)]
    keys, queries, values = {}, {}, {}
    for h in range(HEADS):
        q, k = tile_of(pm_ref, Q_TILE[h]) * SCALE, tile_of(pm_ref, K_TILE[h])
        queries[h] = halves(doc_q, q) if UPPER[h] else halves(q, doc_q)
        keys[h] = halves(doc_k, k) if UPPER[h] else halves(k, doc_k)
        vt = tile_of(pm_ref, V_TILE[h]).T
        vt = vt[HD:] if V_UPPER[h] else vt[:HD]
        values[h] = jnp.concatenate([vt, ones], axis=0)

    def scores(unit):
        h, c = unit
        return dot(keys[h], queries[h][c * chunk : (c + 1) * chunk], NT)

    outs = {h: [] for h in range(HEADS)}
    ahead = scores(units[0])
    for n, (h, c) in enumerate(units):
        s = ahead
        if n + 1 < len(units):
            ahead = scores(units[n + 1])
        m = jnp.max(s, axis=0, keepdims=True)
        p = jnp.exp(s - m).astype(BF16)
        ot = dot(values[h], p)
        total = ot[HD : HD + 1]
        outs[h].append((ot[:HD] * (1.0 / total)).astype(BF16))
        lse_ref[0, 0, h : h + 1, c * chunk : (c + 1) * chunk] = m + jnp.log(total)
    out = [jnp.concatenate(outs[h], axis=1) for h in range(HEADS)]
    pm_ref[:, 512:640] = jnp.concatenate([out[0], out[1]], axis=0).T
    last = jnp.concatenate([jnp.zeros_like(out[2]), out[2]], axis=0).T
    pm_ref[:, 640:768] = halves(tile_of(pm_ref, 5), last)


def attend_fwd_kernel(x_ref, w_ref, bias_ref, seg_ref, pm_ref, lse_ref, *, chunk):
    proj = dot(x_ref[...], w_ref[0]) + bias_ref[0, 0:1, :]
    pm_ref[0] = proj.astype(BF16)
    attend_heads(pm_ref.at[0], seg_ref[0, 0:1], lse_ref, chunk)


def attend_fwd(x, wa, bias, seg, length):
    tokens, width = x.shape
    groups, _, lanes = wa.shape
    seqs = tokens // length
    return pl.pallas_call(
        functools.partial(attend_fwd_kernel, chunk=min(256, length)),
        grid=(groups, seqs),
        in_specs=[
            pl.BlockSpec((length, width), lambda t, s: (s, 0)),
            pl.BlockSpec((1, width, lanes), lambda t, s: (t, 0, 0)),
            pl.BlockSpec((1, 8, lanes), lambda t, s: (t, 0, 0)),
            pl.BlockSpec((1, 8, length), lambda t, s: (s, 0, 0)),
        ],
        out_specs=[
            pl.BlockSpec((1, length, lanes), lambda t, s: (t, s, 0)),
            pl.BlockSpec((1, 1, 8, length), lambda t, s: (t, s, 0, 0)),
        ],
        out_shape=[
            jax.ShapeDtypeStruct((groups, tokens, lanes), BF16),
            jax.ShapeDtypeStruct((groups, seqs, 8, length), F32),
        ],
        compiler_params=params(),
        name="attend_fwd",
    )(x, wa, bias, seg)


def attend_back(pm_ref, gm_ref, lse_ref, row, gp_ref, chunk):
    length = pm_ref.shape[0]
    chunks = length // chunk
    prod = gm_ref[...].astype(F32) * pm_ref[:, 512:768].astype(F32)
    hi = prod.astype(BF16)
    lo = (prod - hi.astype(F32)).astype(BF16)
    lane = lax.broadcasted_iota(jnp.int32, (8, 256), 1)
    line = lax.broadcasted_iota(jnp.int32, (8, 256), 0)
    start = jnp.where(line == 2, O_AT[2] - 512, line * HD)
    pick = jnp.where((lane >= start) & (lane < start + HD) & (line < HEADS), 1.0, 0.0).astype(BF16)
    dsum = dot(pick, hi, NT) + dot(pick, lo, NT)
    doc_q, doc_k = document_lanes(row)
    none = jnp.zeros((length, 128), BF16)
    units = [(h, c) for h in range(HEADS) for c in range(chunks)]
    keys, queries, plain, values, kts, grads = {}, {}, {}, {}, {}, {}
    for h in range(HEADS):
        q, k = tile_of(pm_ref, Q_TILE[h]) * SCALE, tile_of(pm_ref, K_TILE[h])
        plain[h] = q
        queries[h] = halves(doc_q, q) if UPPER[h] else halves(q, doc_q)
        keys[h] = halves(doc_k, k) if UPPER[h] else halves(k, doc_k)
        kt = k.T
        kts[h] = kt[HD:] if UPPER[h] else kt[:HD]
        v = tile_of(pm_ref, V_TILE[h])
        values[h] = halves(none, v) if V_UPPER[h] else halves(v, none)
        grads[h] = tile_of(gm_ref, 0 if h < 2 else 1)

    def rows_of(c):
        return slice(c * chunk, (c + 1) * chunk)

    def products(unit):
        h, c = unit
        return dot(keys[h], queries[h][rows_of(c)], NT), dot(values[h], grads[h][rows_of(c)], NT)

    dqs = {h: [] for h in range(HEADS)}
    dks, dvs = {}, {}
    ahead = products(units[0])
    for n, (h, c) in enumerate(units):
        s, dp = ahead
        if n + 1 < len(units):
            ahead = products(units[n + 1])
        rows = rows_of(c)
        p = jnp.exp(s - lse_ref[0, 0, h : h + 1, rows])
        ds = (p * (dp - dsum[h : h + 1, rows])).astype(BF16)
        dv = dot(p.astype(BF16), grads[h][rows])
        dk = dot(ds, plain[h][rows])
        dvs[h] = dv if c == 0 else dvs[h] + dv
        dks[h] = dk if c == 0 else dks[h] + dk
        dqs[h].append((dot(kts[h], ds) * SCALE).astype(BF16))
    dq = [jnp.concatenate(dqs[h], axis=1) for h in range(HEADS)]
    gp_ref[:, 0:128] = jnp.concatenate([dq[0], dq[1]], axis=0).T
    gp_ref[:, 128:256] = halves(dks[0], dks[1]).astype(BF16)
    gp_ref[:, 256:384] = halves(dvs[0], dvs[1]).astype(BF16)
    last = jnp.concatenate([dq[2], jnp.zeros_like(dq[2])], axis=0).T
    gp_ref[:, 384:512] = halves(last, dvs[2].astype(BF16))
    gp_ref[:, 512:640] = tile_of(pm_ref, 4)
    gp_ref[:, 640:768] = halves(dks[2].astype(BF16), tile_of(pm_ref, 5))


def attend_bwd_kernel(pm_ref, gm_ref, lse_ref, seg_ref, gp_ref, gsum_ref, *, chunk):
    attend_back(pm_ref.at[0], gm_ref.at[0], lse_ref, seg_ref[0, 0:1], gp_ref.at[0], chunk)

    @pl.when(pl.program_id(1) == 0)
    def _():
        gsum_ref[...] = jnp.zeros_like(gsum_ref)

    gsum_ref[0, 0:1, :] += jnp.sum(gp_ref[0].astype(F32), axis=0, keepdims=True)


def attend_bwd(pm, gm, lse, seg):
    groups, tokens, lanes = pm.shape
    seqs, length = lse.shape[1], lse.shape[3]
    return pl.pallas_call(
        functools.partial(attend_bwd_kernel, chunk=min(256, length)),
        grid=(groups, seqs),
        in_specs=[
            pl.BlockSpec((1, length, lanes), lambda t, s: (t, s, 0)),
            pl.BlockSpec((1, length, gm.shape[2]), lambda t, s: (t, s, 0)),
            pl.BlockSpec((1, 1, 8, length), lambda t, s: (t, s, 0, 0)),
            pl.BlockSpec((1, 8, length), lambda t, s: (s, 0, 0)),
        ],
        out_specs=[
            pl.BlockSpec((1, length, lanes), lambda t, s: (t, s, 0)),
            pl.BlockSpec((1, 8, lanes), lambda t, s: (t, 0, 0)),
        ],
        out_shape=[
            jax.ShapeDtypeStruct((groups, tokens, lanes), BF16),
            jax.ShapeDtypeStruct((groups, 8, lanes), F32),
        ],
        compiler_params=params(),
        name="attend_bwd",
    )(pm, gm, lse, seg)


def mixed_only(tail):
    lane = lax.broadcasted_iota(jnp.int32, tail.shape, 1)
    return jnp.where((lane < 128) | (lane >= 192), tail, jnp.zeros((), BF16))


def gelu_parts(pre):
    cdf = 0.5 * (1.0 + lax.erf(pre * (2.0**-0.5)))
    pdf = jnp.exp(-0.5 * pre * pre) * 0.3989422804014327
    return pre * cdf, cdf + pre * pdf


def mean_of(values):
    return jnp.mean(values, axis=-1, keepdims=True)


def norm_parts(values):
    centred = values - mean_of(values)
    inverse = lax.rsqrt(mean_of(centred * centred) + NORM_EPS)
    return centred * inverse, inverse


def norm_back(incoming, normal, inverse, gain):
    scaled = incoming * gain
    return inverse * (scaled - mean_of(scaled) - normal * mean_of(scaled * normal))


def ffn_kernel(
    x_ref, cot_ref, pm_ref, wo_ref, wb_ref, wc_ref, vec_ref, bias_ref,
    out_ref, hid_ref, gi_ref, nl_ref, gsl_ref, gbl_ref, gb_ref, gm_ref, vg_ref, bg_ref,
    slope_ref,
):
    groups = wb_ref.shape[0]

    @pl.when(pl.program_id(0) == 0)
    def _():
        vg_ref[...] = jnp.zeros_like(vg_ref)
        bg_ref[...] = jnp.zeros_like(bg_ref)

    total = x_ref[...].astype(F32) + vec_ref[4:5, :]
    for t in range(groups):
        total = total + dot(mixed_only(pm_ref[t]), wo_ref[t], NT)
    normal_one, inverse_one = norm_parts(total)
    normed = normal_one * vec_ref[0:1, :] + vec_ref[1:2, :]
    low = normed.astype(BF16)
    nl_ref[...] = low
    second = normed + vec_ref[5:6, :]
    for t in range(groups):
        pre = dot(low, wb_ref[t]) + bias_ref[t : t + 1, :]
        act, slope = gelu_parts(pre)
        act = act.astype(BF16)
        hid_ref[t] = act
        slope_ref[t] = slope
        second = second + dot(act, wc_ref[t], NT)
    normal_two, inverse_two = norm_parts(second)
    out_ref[...] = (normal_two * vec_ref[2:3, :] + vec_ref[3:4, :]).astype(BF16)
    cot = cot_ref[...].astype(F32)
    grad_second = norm_back(cot, normal_two, inverse_two, vec_ref[2:3, :])
    vg_ref[2:3, :] += jnp.sum(cot * normal_two, axis=0, keepdims=True)
    vg_ref[3:4, :] += jnp.sum(cot, axis=0, keepdims=True)
    vg_ref[5:6, :] += jnp.sum(grad_second, axis=0, keepdims=True)
    gs_low = grad_second.astype(BF16)
    gsl_ref[...] = gs_low
    grad_normed = grad_second
    for t in range(groups):
        grad_inner = (dot(gs_low, wc_ref[t]) * slope_ref[t]).astype(BF16)
        gi_ref[t] = grad_inner
        bg_ref[t : t + 1, :] += jnp.sum(grad_inner.astype(F32), axis=0, keepdims=True)
        grad_normed = grad_normed + dot(grad_inner, wb_ref[t], NT)
    grad_branch = norm_back(grad_normed, normal_one, inverse_one, vec_ref[0:1, :])
    vg_ref[0:1, :] += jnp.sum(grad_normed * normal_one, axis=0, keepdims=True)
    vg_ref[1:2, :] += jnp.sum(grad_normed, axis=0, keepdims=True)
    vg_ref[4:5, :] += jnp.sum(grad_branch, axis=0, keepdims=True)
    gb_ref[...] = grad_branch
    gb_low = grad_branch.astype(BF16)
    gbl_ref[...] = gb_low
    for t in range(groups):
        gm_ref[t] = dot(gb_low, wo_ref[t]).astype(BF16)


def ffn(x, cot, pm, wa, wb, wc, vec, bias):
    tokens, width = x.shape
    groups, _, lanes = wa.shape
    hidden = wb.shape[2]
    tail = 256
    tile = 256
    last = lanes // tail - 1
    once = pl.Buffered(1)
    row = pl.BlockSpec((tile, width), lambda i: (i, 0))
    wide = pl.BlockSpec((groups, tile, hidden), lambda i: (0, i, 0))
    return pl.pallas_call(
        ffn_kernel,
        grid=(tokens // tile,),
        in_specs=[
            row,
            row,
            pl.BlockSpec((groups, tile, tail), lambda i: (0, i, last)),
            pl.BlockSpec((groups, width, tail), lambda i: (0, 0, last), pipeline_mode=once),
            pl.BlockSpec((groups, width, hidden), lambda i: (0, 0, 0), pipeline_mode=once),
            pl.BlockSpec((groups, width, hidden), lambda i: (0, 0, 0), pipeline_mode=once),
            pl.BlockSpec(vec.shape, lambda i: (0, 0)),
            pl.BlockSpec(bias.shape, lambda i: (0, 0)),
        ],
        out_specs=[
            row,
            wide,
            wide,
            row,
            row,
            row,
            row,
            pl.BlockSpec((groups, tile, tail), lambda i: (0, i, 0)),
            pl.BlockSpec((8, width), lambda i: (0, 0)),
            pl.BlockSpec((8, hidden), lambda i: (0, 0)),
        ],
        out_shape=[
            jax.ShapeDtypeStruct((tokens, width), BF16),
            jax.ShapeDtypeStruct((groups, tokens, hidden), BF16),
            jax.ShapeDtypeStruct((groups, tokens, hidden), BF16),
            jax.ShapeDtypeStruct((tokens, width), BF16),
            jax.ShapeDtypeStruct((tokens, width), BF16),
            jax.ShapeDtypeStruct((tokens, width), BF16),
            jax.ShapeDtypeStruct((tokens, width), F32),
            jax.ShapeDtypeStruct((groups, tokens, tail), BF16),
            jax.ShapeDtypeStruct((8, width), F32),
            jax.ShapeDtypeStruct((8, hidden), F32),
        ],
        scratch_shapes=[pltpu.VMEM((groups, tile, hidden), F32)],
        compiler_params=params(),
        name="ffn",
    )(x, cot, pm, wa, wb, wc, vec, bias)


MESH = pl.DeviceIdType.MESH


class Place:
    def __init__(self, sizes):
        dp, tensor = lax.axis_index("dp"), lax.axis_index("tensor")
        self.deep = sizes[0] // 2
        self.z, self.y = dp // 2, dp % 2
        self.x, self.c = tensor // 2, tensor % 2

    def to_z(self, step):
        return {"dp": lax.rem(self.z + step, self.deep) * 2 + self.y}

    def to_y(self):
        return {"dp": self.z * 2 + 1 - self.y}

    def to_x(self):
        return {"tensor": (1 - self.x) * 2 + self.c}

    def to_c(self):
        return {"tensor": self.x * 2 + 1 - self.c}

    def from_z(self, step):
        return lax.rem(self.z + self.deep - step, self.deep)

    def partners(self):
        return [self.to_z(j) for j in range(1, self.deep)] + [self.to_y(), self.to_x(), self.to_c()]

    def peers(self):
        found = []
        for r in range(1, 8):
            x = 1 - self.x if r & 4 else self.x
            y = 1 - self.y if r & 2 else self.y
            c = 1 - self.c if r & 1 else self.c
            found.append((x * 4 + y * 2 + c, {"dp": self.z * 2 + y, "tensor": x * 2 + c}))
        return found

    def greet(self, everyone=False):
        barrier = pltpu.get_barrier_semaphore()
        partners = self.partners()
        if everyone:
            partners = partners[: self.deep - 1] + [device for _, device in self.peers()]
        for partner in partners:
            pl.semaphore_signal(barrier, inc=1, device_id=partner, device_id_type=MESH)
        pl.semaphore_wait(barrier, len(partners))


class Links:
    def __init__(self, send, recv):
        self.send, self.recv = send, recv

    def copy(self, k, ref, to, dst=None):
        return pltpu.make_async_remote_copy(
            src_ref=ref,
            dst_ref=ref if dst is None else dst,
            send_sem=self.send.at[k],
            recv_sem=self.recv.at[k],
            device_id=to,
            device_id_type=MESH,
        )

    def landed(self, k, ref, to):
        self.copy(k, ref, to).wait_recv()


def add_everywhere(place, links, base, own, slots):
    deep = place.deep
    hops = [place.to_c(), place.to_y(), place.to_x()]

    def start(i):
        def run():
            if i:
                links.copy(base + i - 1, own, hops[i - 1], slots.at[i - 1]).wait_send()
                links.landed(base + i - 1, slots.at[i - 1], hops[i - 1])
                own[...] = own[...] + slots[i - 1]
            if i < 3:
                links.copy(base + i, own, hops[i], slots.at[i]).start()
            else:
                for j in range(1, deep):
                    links.copy(base + 2 + j, own, place.to_z(j), slots.at[2 + j]).start()

        return run

    def last():
        for j in range(1, deep):
            links.copy(base + 2 + j, own, place.to_z(j), slots.at[2 + j]).wait_send()
            links.landed(base + 2 + j, slots.at[2 + j], place.to_z(j))
        slots[2] = own[...]
        total = slots[2 + lax.rem(place.z + deep, deep)]
        for z in range(1, deep):
            total = total + slots[2 + lax.rem(place.z + deep - z, deep)]
        own[...] = total

    return [start(0), start(1), start(2), start(3), last]


def add_in_two(place, links, base, own, slots):
    p, deep = place, place.deep
    me = p.x * 4 + p.y * 2 + p.c
    peers = p.peers()

    def near(r):
        return links.copy(base + r, own, peers[r - 1][1], slots.at[me])

    def far(j):
        return links.copy(base + 7 + j, own, p.to_z(j), slots.at[8 + p.z])

    def start():
        for r in range(1, 8):
            near(r).start()
        slots[me] = own[...]

    def middle():
        for r in range(1, 8):
            near(r).wait_send()
            links.landed(base + r, slots.at[peers[r - 1][0]], peers[r - 1][1])
        total = slots[0]
        for k in range(1, 8):
            total = total + slots[k]
        own[...] = total
        for j in range(1, deep):
            far(j).start()
        slots[8 + p.z] = total

    def last():
        for j in range(1, deep):
            far(j).wait_send()
            links.landed(base + 7 + j, slots.at[8 + p.from_z(j)], p.to_z(j))
        total = slots[8]
        for k in range(1, deep):
            total = total + slots[8 + k]
        own[...] = total

    return [start, middle, last]


def gather_stages(place, links, base, own, whole, start=0, count=None):
    p, deep = place, place.deep
    count = own.shape[0] if count is None else count
    half = count // 2
    rows, first, later = pl.ds(start, count), pl.ds(start, half), pl.ds(start + half, half)
    own = own.at[rows]
    mine = whole.at[p.x, p.c, p.z, p.y, rows]
    line = whole.at[p.x, p.c, :, p.y, rows]
    ax = whole.at[p.x, p.c, :, p.y, first]
    ax_in = whole.at[1 - p.x, p.c, :, p.y, first]
    by = whole.at[p.x, p.c, :, p.y, later]
    by_in = whole.at[p.x, p.c, :, 1 - p.y, later]
    ay = whole.at[:, p.c, :, p.y, first]
    ay_in = whole.at[:, p.c, :, 1 - p.y, first]
    bx = whole.at[p.x, p.c, :, :, later]
    bx_in = whole.at[1 - p.x, p.c, :, :, later]
    kz, ka, kb, ks = base, base + deep, base + deep + 2, base + deep + 4

    def keep():
        return pltpu.make_async_copy(own, mine, links.send.at[kz])

    def stage0():
        keep().start()
        for j in range(1, deep):
            links.copy(kz + j, own, p.to_z(j), mine).start()

    def stage1():
        keep().wait()
        for j in range(1, deep):
            links.landed(kz + j, whole.at[p.x, p.c, p.from_z(j), p.y, rows], p.to_z(j))
        links.copy(ka, ax, p.to_x()).start()
        links.copy(kb, by, p.to_y()).start()
        links.copy(ks, line, p.to_c()).start()

    def stage2():
        links.landed(ka, ax_in, p.to_x())
        links.copy(ka + 1, ay, p.to_y()).start()
        links.copy(ks + 1, ax_in, p.to_c()).start()
        links.landed(kb, by_in, p.to_y())
        links.copy(kb + 1, bx, p.to_x()).start()
        links.copy(ks + 2, by_in, p.to_c()).start()

    def stage3():
        links.landed(ka + 1, ay_in, p.to_y())
        links.copy(ks + 3, ay_in, p.to_c()).start()
        links.landed(kb + 1, bx_in, p.to_x())
        links.copy(ks + 4, bx_in, p.to_c()).start()

    def stage4():
        o = 1 - p.c
        links.landed(ks, whole.at[p.x, o, :, p.y, rows], p.to_c())
        links.landed(ks + 1, whole.at[1 - p.x, o, :, p.y, first], p.to_c())
        links.landed(ks + 2, whole.at[p.x, o, :, 1 - p.y, later], p.to_c())
        links.landed(ks + 3, whole.at[:, o, :, 1 - p.y, first], p.to_c())
        links.landed(ks + 4, whole.at[1 - p.x, o, :, :, later], p.to_c())
        for j in range(1, deep):
            links.copy(kz + j, own, p.to_z(j), mine).wait_send()
        links.copy(ka, ax, p.to_x()).wait_send()
        links.copy(kb, by, p.to_y()).wait_send()
        links.copy(ka + 1, ay, p.to_y()).wait_send()
        links.copy(kb + 1, bx, p.to_x()).wait_send()
        links.copy(ks, line, p.to_c()).wait_send()
        links.copy(ks + 1, ax_in, p.to_c()).wait_send()
        links.copy(ks + 2, by_in, p.to_c()).wait_send()
        links.copy(ks + 3, ay_in, p.to_c()).wait_send()
        links.copy(ks + 4, bx_in, p.to_c()).wait_send()

    return [stage0, stage1, stage2, stage3, stage4]


def gather_stages_late(place, links, base, own, whole, start=0, count=None):
    p, deep = place, place.deep
    count = own.shape[0] if count is None else count
    half = count // 2
    rows, first, later = pl.ds(start, count), pl.ds(start, half), pl.ds(start + half, half)
    mine = whole.at[p.x, p.c, p.z, p.y]
    pair_f, pair_l = whole.at[:, p.c, p.z, p.y, first], whole.at[p.x, p.c, p.z, :, later]
    line_f, line_l = whole.at[:, p.c, :, p.y, first], whole.at[p.x, p.c, :, :, later]
    line_f_in = whole.at[:, p.c, :, 1 - p.y, first]
    line_l_in = whole.at[1 - p.x, p.c, :, :, later]
    kf, kl = base + 8, base + 8 + deep

    def keep():
        return pltpu.make_async_copy(own.at[rows], mine.at[rows], links.send.at[base])

    def to_x():
        return links.copy(base + 1, own.at[first], p.to_x(), mine.at[first])

    def to_y():
        return links.copy(base + 2, own.at[later], p.to_y(), mine.at[later])

    def stage0():
        keep().start()
        to_x().start()
        to_y().start()

    def stage1():
        keep().wait()
        links.landed(base + 1, whole.at[1 - p.x, p.c, p.z, p.y, first], p.to_x())
        links.landed(base + 2, whole.at[p.x, p.c, p.z, 1 - p.y, later], p.to_y())
        for j in range(1, deep):
            links.copy(kf + j, pair_f, p.to_z(j)).start()
            links.copy(kl + j, pair_l, p.to_z(j)).start()

    def stage2():
        for j in range(1, deep):
            z = p.from_z(j)
            links.landed(kf + j, whole.at[:, p.c, z, p.y, first], p.to_z(j))
            links.landed(kl + j, whole.at[p.x, p.c, z, :, later], p.to_z(j))
        links.copy(base + 3, line_f, p.to_y()).start()
        links.copy(base + 4, line_l, p.to_x()).start()
        links.copy(base + 5, line_f, p.to_c()).start()
        links.copy(base + 6, line_l, p.to_c()).start()

    def stage3():
        links.landed(base + 3, line_f_in, p.to_y())
        links.copy(base + 7, line_f_in, p.to_c()).start()
        links.landed(base + 4, line_l_in, p.to_x())
        links.copy(base + 8, line_l_in, p.to_c()).start()

    def stage4():
        o = 1 - p.c
        links.landed(base + 5, whole.at[:, o, :, p.y, first], p.to_c())
        links.landed(base + 6, whole.at[p.x, o, :, :, later], p.to_c())
        links.landed(base + 7, whole.at[:, o, :, 1 - p.y, first], p.to_c())
        links.landed(base + 8, whole.at[1 - p.x, o, :, :, later], p.to_c())
        to_x().wait_send()
        to_y().wait_send()
        for j in range(1, deep):
            links.copy(kf + j, pair_f, p.to_z(j)).wait_send()
            links.copy(kl + j, pair_l, p.to_z(j)).wait_send()
        links.copy(base + 3, line_f, p.to_y()).wait_send()
        links.copy(base + 4, line_l, p.to_x()).wait_send()
        links.copy(base + 5, line_f, p.to_c()).wait_send()
        links.copy(base + 6, line_l, p.to_c()).wait_send()
        links.copy(base + 7, line_f_in, p.to_c()).wait_send()
        links.copy(base + 8, line_l_in, p.to_c()).wait_send()

    return [stage0, stage1, stage2, stage3, stage4]


GATHER_COPIES = 9


def add_into(out, one, two):
    out[...] = one[...] + two[...]


def scatter_core(place, links, base, acc, in_c):
    def move(part):
        return links.copy(base + part, acc.at[2 + part], place.to_c(), in_c.at[part])

    def send(part):
        return lambda: move(part).start()

    def add(part, x):
        def run():
            move(part).wait_send()
            links.landed(base + part, in_c.at[part], place.to_c())

            def one(z, _):
                for y in range(2):
                    there = acc.at[x, z, y]
                    add_into(there, there, in_c.at[part, z, y])
                return 0

            lax.fori_loop(0, place.deep, one, 0)

        return run

    return send, add


def add_line(place, acc, x, y, rows, arrived):
    def add(z, _):
        there = acc.at[x, z, y, rows]
        add_into(there, there, arrived.at[z])
        return 0

    lax.fori_loop(0, place.deep, add, 0)


def scatter_plane(place, links, base, acc, ay_in, ax_in, bx_in, by_in):
    p = place
    half = acc.shape[3] // 2
    first, later, both = pl.ds(0, half), pl.ds(half, half), pl.ds(0, 2)

    def ay():
        return links.copy(base, acc.at[both, :, 1 - p.y, first], p.to_y(), ay_in)

    def bx():
        return links.copy(base + 1, acc.at[1 - p.x, :, :, later], p.to_x(), bx_in)

    def ax():
        return links.copy(base + 2, acc.at[1 - p.x, :, p.y, first], p.to_x(), ax_in)

    def by():
        return links.copy(base + 3, acc.at[p.x, :, 1 - p.y, later], p.to_y(), by_in)

    def start():
        ay().start()
        bx().start()

    def middle():
        links.landed(base, ay_in, p.to_y())
        for x in range(2):
            add_line(p, acc, x, p.y, first, ay_in.at[x])
        ax().start()
        links.landed(base + 1, bx_in, p.to_x())
        for y in range(2):
            add_line(p, acc, p.x, y, later, bx_in.at[:, y])
        by().start()

    def finish():
        links.landed(base + 2, ax_in, p.to_x())
        add_line(p, acc, p.x, p.y, first, ax_in)
        links.landed(base + 3, by_in, p.to_y())
        add_line(p, acc, p.x, p.y, later, by_in)

    def settle():
        for move in (ay, bx, ax, by):
            move().wait_send()

    return start, middle, finish, settle


def scatter_in_pairs(place, links, base, acc, in_c, ay_in, ax_in, bx_in, by_in, in_z, out):
    p, deep = place, place.deep
    half = acc.shape[3] // 2
    first, later = pl.ds(0, half), pl.ds(half, half)
    far, near = 1 - p.x, p.x
    kf, kl = base + 6, base + 6 + deep
    send, add = scatter_core(place, links, base, acc, in_c)

    def over_y(part, x):
        return links.copy(base + 2 + part, acc.at[x, :, 1 - p.y, first], p.to_y(), ay_in.at[part])

    def far_later():
        return links.copy(base + 4, acc.at[far, :, :, later], p.to_x(), bx_in)

    def far_first():
        return links.copy(base + 5, acc.at[far, :, p.y, first], p.to_x(), ax_in)

    def near_later():
        return links.copy(base + 6, acc.at[near, :, 1 - p.y, later], p.to_y(), by_in)

    def over_z(k, j, rows):
        to = lax.rem(p.z + j, deep)
        return links.copy(k + j, acc.at[near, to, p.y, rows], p.to_z(j), in_z.at[j, rows])

    def far1():
        add(0, far)()
        over_y(0, far).start()
        far_later().start()

    def far2():
        links.landed(base + 2, ay_in.at[0], p.to_y())
        add_line(p, acc, far, p.y, first, ay_in.at[0])
        far_first().start()

    def near1():
        over_y(1, near).start()

    def near_x():
        links.landed(base + 4, bx_in, p.to_x())
        for y in range(2):
            add_line(p, acc, near, y, later, bx_in.at[:, y])
        near_later().start()

    def near2():
        links.landed(base + 3, ay_in.at[1], p.to_y())
        add_line(p, acc, near, p.y, first, ay_in.at[1])
        links.landed(base + 5, ax_in, p.to_x())
        add_line(p, acc, near, p.y, first, ax_in)
        for j in range(1, deep):
            over_z(kf, j, first).start()

    def near3():
        links.landed(base + 6, by_in, p.to_y())
        add_line(p, acc, near, p.y, later, by_in)
        for j in range(1, deep):
            over_z(kl, j, later).start()

    def near4():
        for k, rows in ((kf, first), (kl, later)):
            total = acc[near, p.z, p.y, rows].astype(F32)
            for j in range(1, deep):
                links.landed(k + j, in_z.at[j, rows], p.to_z(j))
                total = total + in_z[j, rows].astype(F32)
            out[rows] = total
            for j in range(1, deep):
                over_z(k, j, rows).wait_send()
        over_y(0, far).wait_send()
        over_y(1, near).wait_send()
        far_later().wait_send()
        far_first().wait_send()
        near_later().wait_send()

    return [send(0), far1, far2, send(1), add(1, near), near1, near_x, near2, near3, near4]


def scatter_tail(place, links, base, part, in_z, out):
    deep = place.deep

    def send(j):
        return links.copy(
            base + j, part.at[lax.rem(place.z + j, deep)], place.to_z(j), in_z.at[j]
        )

    def stage0():
        for j in range(1, deep):
            send(j).start()

    def stage1():
        for j in range(1, deep):
            links.landed(base + j, in_z.at[j], place.to_z(j))
        total = part[place.z].astype(F32)
        for j in range(1, deep):
            total = total + in_z[j].astype(F32)
        out[...] = total
        for j in range(1, deep):
            send(j).wait_send()

    return [stage0, stage1]


def core_buffers(deep, rows, lanes):
    return [
        pltpu.VMEM((4, deep, 2, rows, lanes), BF16),
        pltpu.VMEM((2, deep, 2, rows, lanes), BF16),
    ]


def plane_buffers(deep, rows, lanes):
    half = rows // 2
    return [
        pltpu.VMEM((2, deep, half, lanes), BF16),
        pltpu.VMEM((deep, half, lanes), BF16),
        pltpu.VMEM((deep, 2, half, lanes), BF16),
        pltpu.VMEM((deep, half, lanes), BF16),
    ]


def gather_blocks(block, sizes):
    whole = lax.all_gather(block, ("dp", "tensor"), axis=0, tiled=False)
    whole = whole.reshape(sizes + block.shape)
    return jnp.swapaxes(whole, 0, 1).reshape((sizes[1], -1) + block.shape[1:])


def scatter_blocks(grads, sizes):
    parts = grads.reshape((sizes[1], sizes[0], -1) + grads.shape[2:])
    parts = jnp.swapaxes(parts, 0, 1).reshape((sizes[0] * sizes[1],) + parts.shape[2:])
    return lax.psum_scatter(parts, ("dp", "tensor"), scatter_dimension=0, tiled=False)


def adam_parts(grad, mean, square):
    new_mean = MOMENT_DECAY * mean + (1.0 - MOMENT_DECAY) * grad
    new_square = MOMENT_DECAY * square + (1.0 - MOMENT_DECAY) * grad * grad
    correction = 1.0 - MOMENT_DECAY**STEP
    direction = new_mean / correction / (jnp.sqrt(new_square / correction) + ADAM_EPS)
    return new_mean, new_square, direction


def sum_all(values):
    return jnp.sum(jnp.sum(values, axis=1, keepdims=True), axis=0, keepdims=True)


def group_squares(qkv_part, out_part, inner_part, outer_part, vector_part):
    return jnp.concatenate(
        [
            jnp.sum(qkv_part * qkv_part, axis=(1, 2)),
            jnp.sum(out_part * out_part)[None],
            jnp.sum(inner_part * inner_part)[None],
            jnp.sum(outer_part * outer_part)[None],
            jnp.sum(vector_part[:8] * vector_part[:8], axis=1),
            jnp.sum(vector_part[8:] * vector_part[8:])[None],
        ]
    )


def lamb_apply(weight_list, update_list, trust_ratio, row_number):
    qkv_new = weight_list[0] - LEARN_RATE * trust_ratio[0:3, None, None] * update_list[0]
    out_new = weight_list[1] - LEARN_RATE * trust_ratio[3] * update_list[1]
    inner_new = weight_list[2] - LEARN_RATE * trust_ratio[4] * update_list[2]
    outer_new = weight_list[3] - LEARN_RATE * trust_ratio[5] * update_list[3]
    row_ratio = jnp.concatenate(
        [trust_ratio[6:14], jnp.broadcast_to(trust_ratio[14], (row_number - 8,))]
    )
    vector_new = weight_list[4] - LEARN_RATE * row_ratio[:, None] * update_list[4]
    return (qkv_new, out_new, inner_new, outer_new, vector_new)


def lamb_plain(sum_a, sum_b, sum_c, vector_sum, weights, old_means, old_squares):
    qkv_sum = jnp.stack([collect(sum_a, at) for at in (Q_AT, K_AT, V_AT)])
    grad_sums = (qkv_sum, collect(sum_a, O_AT).T, sum_b, sum_c.T, vector_sum)
    decays = (WEIGHT_DECAY, WEIGHT_DECAY, WEIGHT_DECAY, WEIGHT_DECAY, 0.0)
    stats = [adam_parts(*entry) for entry in zip(grad_sums, old_means, old_squares)]
    updates = [stats[i][2] + decays[i] * weights[i] for i in range(5)]
    weight_squares, update_squares = lax.psum(
        (group_squares(*weights), group_squares(*updates)), ("dp", "tensor")
    )
    weight_norms = jnp.sqrt(weight_squares)
    update_norms = jnp.sqrt(update_squares)
    trust_ratio = weight_norms / (update_norms + ADAM_EPS)
    new = lamb_apply(weights, updates, trust_ratio, weights[4].shape[0])
    outs = []
    for i in range(5):
        outs += [stats[i][0], stats[i][1], new[i]]
    return outs + [jnp.stack([weight_norms, update_norms])]


A_PIECES = 3
C_ROWS = ((0, 64), (64, 32))


def own_first(order):
    tensor = lax.axis_index("tensor")
    x, c = tensor // 2, tensor % 2
    return jnp.where(order % 2 == 0, x, 1 - x) * 2 + jnp.where(order < 2, c, 1 - c)


def gather_attend_kernel(
    qkv_ref, out_ref, inner_ref, outer_ref, vec_ref, x_ref, seg_ref,
    wa_hbm, wb_hbm, wc_hbm, hid_hbm, nlt_hbm, xt_hbm, n1_hbm,
    full, pm_ref, lse_ref, slope_ref, acc, inv_ref,
    send, recv, slots, pack_a, pack_b, pack_c, wa, wb, wc, hid, nlt_ref, xt_ref, n1_ref,
    bias, low, out_sem, xp, proj_acc,
    *, sizes, chunk,
):
    step = pl.program_id(0)
    groups, deep = sizes[1], sizes[0] // 2
    place = Place(sizes)
    links = Links(send, recv)
    each = GATHER_COPIES + deep
    cols = qkv_ref.shape[2]
    tokens, width = x_ref.shape
    lanes = pack_a.shape[1]
    length = tokens // 2
    tail = 256
    count = pack_a.shape[0] // A_PIECES
    ga = [
        gather_stages(place, links, k * each, pack_a, wa, k * count, count) for k in range(A_PIECES)
    ]
    gb = gather_stages(place, links, A_PIECES * each, pack_b, wb)
    more = (A_PIECES + 1) * each
    small = add_everywhere(place, links, more, full, slots)
    more += deep + 2
    gc = [
        gather_stages_late(place, links, more + k * (each + deep), pack_c, wc, *rows)
        for k, rows in enumerate(C_ROWS)
    ]
    t, s = own_first(jnp.minimum(step // 2, groups - 1)), step % 2
    last = 4 * groups - 1

    def keep(k):
        pairs = (
            (wa, wa_hbm), (wb, wb_hbm), (wc, wc_hbm), (hid, hid_hbm),
            (nlt_ref, nlt_hbm), (xt_ref, xt_hbm), (n1_ref, n1_hbm),
        )
        return pltpu.make_async_copy(*pairs[k], out_sem.at[k])

    def project(piece):
        here = pl.ds(piece * count, count)
        for x in range(2):
            part = dot(xp[piece], wa[x, place.c, :, :, here].reshape(sizes[0] * count, lanes))
            proj_acc[x] = part if piece == 0 else proj_acc[x] + part

    @pl.when(step == 0)
    def _():
        out_rows = out_ref[...].T
        pack_a[...] = spread(qkv_ref[0], qkv_ref[1], qkv_ref[2], out_rows).astype(BF16)
        place.greet()
        for k in range(A_PIECES):
            ga[k][0]()
        pack_c[...] = outer_ref[...].astype(BF16)
        gc[0][0]()
        gc[1][0]()
        pack_b[...] = inner_ref[...].astype(BF16)
        xt_ref[...] = x_ref[...].T
        each_dp = pack_a.shape[0]
        for k in range(A_PIECES):
            picked = [
                xt_ref[dp * each_dp + k * count : dp * each_dp + (k + 1) * count]
                for dp in range(sizes[0])
            ]
            xp[k] = jnp.concatenate(picked, axis=0).T
        full[...] = jnp.zeros_like(full)
        mine = vec_ref.shape[1]
        full[0 : vec_ref.shape[0], 0:mine] = vec_ref[...]
        index = lax.axis_index("dp") * groups + lax.axis_index("tensor")
        full[...] = pltpu.roll(full[...], index * mine, 1)
        small[0]()
        small[1]()
        ga[0][1]()
        small[2]()
        ga[0][2]()
        ga[1][1]()
        small[3]()
        gb[0]()
        ga[2][1]()
        ga[1][2]()
        ga[2][2]()
        ga[0][3]()
        project(0)
        small[4]()
        for g in range(groups):
            bias[g] = jnp.zeros(bias.shape[1:], F32)
            for h in range(HEADS):
                mine = slice(g * cols + h * HD, g * cols + (h + 1) * HD)
                bias[g, 0:1, Q_AT[h] : Q_AT[h] + HD] = full[6:7, mine]
                bias[g, 0:1, V_AT[h] : V_AT[h] + HD] = full[7:8, mine]
        n1_ref[...] = x_ref[...].astype(F32) + full[4:5, :]
        ga[1][3]()
        project(1)
        ga[2][3]()
        project(2)

    @pl.when(step == groups)
    def _():
        gb[2]()
        for k in range(A_PIECES):
            ga[k][4]()
        keep(0).start()

    @pl.when(step == 1)
    def _():
        gb[1]()
        gc[0][1]()

    @pl.when(step == 5)
    def _():
        gc[1][1]()

    @pl.when(step == 2 * groups + 2)
    def _():
        gb[4]()
        keep(1).start()
        gc[1][2]()

    @pl.when(step == 3 * groups)
    def _():
        gc[0][3]()
        gc[1][3]()
        keep(3).start()

    @pl.when(step == 3 * groups + 2)
    def _():
        gc[0][4]()
        gc[1][4]()
        keep(2).start()

    @pl.when((step < groups) & (s == 0))
    def _():
        pm_ref[0] = (proj_acc[t // 2] + bias[t, 0:1]).astype(BF16)

    @pl.when((step >= groups) & (step < 2 * groups) & (s == 0))
    def _():
        weight = wa[t // 2, t % 2].reshape(width, lanes)
        for n in range(lanes // 256):
            here = slice(n * 256, (n + 1) * 256)
            proj = dot(x_ref[...], weight[:, here]) + bias[t, 0:1, here]
            pm_ref[0, :, here] = proj.astype(BF16)

    @pl.when(step < 2 * groups)
    def _():
        rows = pl.ds(pl.multiple_of(s * length, length), length)
        row = seg_ref[pl.ds(lax.axis_index("tensor") * 2 + s, 1)]
        attend_heads(pm_ref.at[0, rows], row, lse_ref, chunk)

    @pl.when((step < 2 * groups) & (s == 1))
    def _():
        mixed = mixed_only(pm_ref[0, :, lanes - tail :])
        weight = wa[t // 2, t % 2, :, :, :, lanes - tail :].reshape(width, tail)
        n1_ref[...] += dot(mixed, weight, NT)

    @pl.when(step == 2 * groups)
    def _():
        for r in range(tokens // 256):
            rows = slice(r * 256, (r + 1) * 256)
            normal_one, inverse_one = norm_parts(n1_ref[rows])
            n1_ref[rows] = normal_one
            inv_ref[rows] = inverse_one
            normed = normal_one * full[0:1, :] + full[1:2, :]
            acc[rows] = normed + full[5:6, :]
            part = normed.astype(BF16)
            low[rows] = part
            nlt_ref[:, rows] = part.T
        for k in range(4, 7):
            keep(k).start()
        gc[0][2]()
        gb[3]()

    @pl.when((step >= 2 * groups) & (step < 3 * groups))
    def _():
        g = own_first(step - 2 * groups)
        weight = wb[g // 2, g % 2].reshape(width, lanes)
        for n in range(lanes // 256):
            here = slice(n * 256, (n + 1) * 256)
            pre = dot(low[...], weight[:, here]) + full[pl.ds(8 + g, 1), here]
            act, turn = gelu_parts(pre)
            hid[g, :, here] = act.astype(BF16)
            slope_ref[0, :, here] = turn.astype(BF16)

    @pl.when(step >= 3 * groups)
    def _():
        g = own_first(step - 3 * groups)
        weight = wc[g // 2, g % 2].reshape(width, lanes)
        acc[...] += dot(hid[g], weight, NT)

    @pl.when(step == last)
    def _():
        for k in range(7):
            keep(k).wait()


def once(shape):
    return pl.BlockSpec(shape, lambda *_: (0,) * len(shape), pipeline_mode=pl.Buffered(1))


def gather_attend(weights, x, seg, sizes):
    qkv, out, inner, outer, vec = weights
    deep, groups = sizes[0] // 2, sizes[1]
    copies = (A_PIECES + 1) * (GATHER_COPIES + deep) + deep + 2
    copies += len(C_ROWS) * (GATHER_COPIES + 2 * deep)
    tokens, width = x.shape
    length = seg.shape[1]
    seqs = tokens // length
    rows, lanes = inner.shape
    steps = groups * seqs
    anywhere = pl.BlockSpec(memory_space=pl.ANY)
    parts = (2, 2, deep, 2, rows, lanes)
    whole = jax.ShapeDtypeStruct(parts, BF16)

    def now(i):
        i = jnp.minimum(i, steps - 1)
        return own_first(i // 2), i % 2

    def part(i):
        return own_first(jnp.clip(i - steps, 0, groups - 1))

    wa, wb, wc, hid, nlt, xt, n1, *rest = pl.pallas_call(
        functools.partial(gather_attend_kernel, sizes=sizes, chunk=min(256, length)),
        grid=(steps + 2 * groups,),
        in_specs=[once(w.shape) for w in weights]
        + [
            once(x.shape),
            once(seg.shape),
        ],
        out_specs=[anywhere] * 7
        + [
            once((16, width)),
            pl.BlockSpec((1, tokens, lanes), lambda i: (now(i)[0], 0, 0)),
            pl.BlockSpec((1, 1, 8, length), lambda i: (*now(i), 0, 0)),
            pl.BlockSpec((1, tokens, lanes), lambda i: (part(i), 0, 0)),
            once((tokens, width)),
            once((tokens, 1)),
        ],
        out_shape=[whole] * 3
        + [
            jax.ShapeDtypeStruct((groups, tokens, lanes), BF16),
            jax.ShapeDtypeStruct((width, tokens), BF16),
            jax.ShapeDtypeStruct((width, tokens), BF16),
            jax.ShapeDtypeStruct((tokens, width), F32),
            jax.ShapeDtypeStruct((16, width), F32),
            jax.ShapeDtypeStruct((groups, tokens, lanes), BF16),
            jax.ShapeDtypeStruct((groups, seqs, 8, length), F32),
            jax.ShapeDtypeStruct((groups, tokens, lanes), BF16),
            jax.ShapeDtypeStruct((tokens, width), F32),
            jax.ShapeDtypeStruct((tokens, 1), F32),
        ],
        scratch_shapes=[
            pltpu.SemaphoreType.DMA((copies,)),
            pltpu.SemaphoreType.DMA((copies,)),
            pltpu.VMEM((deep + 2, 16, width), F32),
            pltpu.VMEM((rows, lanes), BF16),
            pltpu.VMEM((rows, lanes), BF16),
            pltpu.VMEM((rows, lanes), BF16),
            pltpu.VMEM(parts, BF16),
            pltpu.VMEM(parts, BF16),
            pltpu.VMEM(parts, BF16),
            pltpu.VMEM((groups, tokens, lanes), BF16),
            pltpu.VMEM((width, tokens), BF16),
            pltpu.VMEM((width, tokens), BF16),
            pltpu.VMEM((tokens, width), F32),
            pltpu.VMEM((groups, 8, lanes), F32),
            pltpu.VMEM((tokens, width), BF16),
            pltpu.SemaphoreType.DMA((7,)),
            pltpu.VMEM((A_PIECES, tokens, width // A_PIECES), BF16),
            pltpu.VMEM((2, tokens, lanes), F32),
        ],
        compiler_params=params(collective_id=0, has_side_effects=True),
        name="gather_attend",
    )(*weights, x, seg)
    shape = (groups, sizes[0] * rows, lanes)
    return [wa.reshape(shape), wb.reshape(shape), wc.reshape(shape), hid, nlt, xt, n1] + rest


def other_first(order):
    c = lax.axis_index("tensor") % 2
    return order % 2 * 2 + jnp.where(order < 2, 1 - c, c)


def layer_kernel(
    cot_ref, hid_ref, slope_ref, inv_ref, vec_ref, second_hbm, n1_hbm, nlt_hbm, wa_hbm, wb_hbm,
    wc_hbm,
    out_hbm, gb_hbm, gm_hbm, gbt_hbm, accb_hbm, part_ref, vg_ref, bg_ref,
    n1_ref, nlt_ref, wo_ref, wb_ref, wc_ref, acc, low, gst, gi, out_ref, gm_ref, gbt_ref,
    in_sem, out_sem, send, recv, accc, in_cc, accb, in_cb, ay_in, ax_in, bx_in, by_in, *, sizes,
):
    step = pl.program_id(0)
    tokens, width = acc.shape
    groups, deep = sizes[1], sizes[0] // 2
    lanes = wa_hbm.shape[2]
    tail = wo_ref.shape[2]
    last = 2 * groups - 1
    place = Place(sizes)
    links = Links(send, recv)
    send_c, add_c = scatter_core(place, links, 0, accc, in_cc)
    send_b, add_b = scatter_core(place, links, 2, accb, in_cb)
    start, middle, finish, settle = scatter_plane(
        place, links, 4, accc, ay_in, ax_in, bx_in, by_in
    )
    blocks = [slice(r * 256, (r + 1) * 256) for r in range(tokens // 256)]
    columns = [slice(n * 256, (n + 1) * 256) for n in range(width // 256)]

    def outer(t):
        return pltpu.make_async_copy(wc_hbm.at[t], wc_ref.at[t], in_sem.at[t])

    def inner(t):
        return pltpu.make_async_copy(wb_hbm.at[t], wb_ref.at[t], in_sem.at[groups + t])

    def load(k):
        pairs = (
            (second_hbm, acc), (n1_hbm, n1_ref), (nlt_hbm, nlt_ref),
            (wa_hbm.at[:, :, pl.ds(lanes - tail, tail)], wo_ref),
        )
        return pltpu.make_async_copy(*pairs[k], in_sem.at[2 * groups + k])

    def store(k):
        pairs = (
            (out_ref, out_hbm), (gbt_ref, gbt_hbm), (accb.at[pl.ds(0, 2)], accb_hbm), (acc, gb_hbm)
        )
        return pltpu.make_async_copy(*pairs[k], out_sem.at[k])

    def store_mixed(t):
        return pltpu.make_async_copy(gm_ref.at[t], gm_hbm.at[t], out_sem.at[4 + t])

    @pl.when(step == 0)
    def _():
        load(0).start()
        for t in range(groups):
            outer(t).start()
            inner(t).start()
        for k in range(1, 4):
            load(k).start()
        place.greet()
        vg_ref[...] = jnp.zeros_like(vg_ref)
        bg_ref[...] = jnp.zeros_like(bg_ref)
        load(0).wait()
        for rows in blocks:
            normal_two, inverse_two = norm_parts(acc[rows])
            out_ref[rows] = (normal_two * vec_ref[2:3, :] + vec_ref[3:4, :]).astype(BF16)
            cot = cot_ref[rows].astype(F32)
            grad_second = norm_back(cot, normal_two, inverse_two, vec_ref[2:3, :])
            vg_ref[2:3, :] += jnp.sum(cot * normal_two, axis=0, keepdims=True)
            vg_ref[3:4, :] += jnp.sum(cot, axis=0, keepdims=True)
            vg_ref[5:6, :] += jnp.sum(grad_second, axis=0, keepdims=True)
            acc[rows] = grad_second
            part = grad_second.astype(BF16)
            low[rows] = part
            gst[:, rows] = part.T
        store(0).start()

    @pl.when(step < groups)
    def _():
        slot = lax.rem(step + 2, 4)
        for here in columns:
            part = dot(gst[...], hid_ref[0, :, here]).astype(BF16)
            accc[slot, :, :, :, here] = part.reshape(deep, 2, -1, 256)

    @pl.when(step == 1)
    def _():
        send_c(0)()

    @pl.when(step == 2)
    def _():
        send_c(1)()

    @pl.when(step == groups)
    def _():
        add_c(0, 0)()
        add_c(1, 1)()
        start()
        for t in range(groups):
            outer(t).wait()
            inner(t).wait()
        for k in range(1, 4):
            load(k).wait()

    @pl.when(step == last)
    def _():
        middle()

    @pl.when(step >= groups)
    def _():
        order = step - groups
        slot = lax.rem(order + 2, 4)
        t = other_first(order)
        for here in columns:
            grad_hidden = dot(low[...], wc_ref[t, :, here])
            part = (grad_hidden * slope_ref[0, :, here].astype(F32)).astype(BF16)
            gi[:, here] = part
            bg_ref[pl.ds(t, 1), here] = jnp.sum(part.astype(F32), axis=0, keepdims=True)
        acc[...] += dot(gi[...], wb_ref[t], NT)
        for here in columns:
            part = dot(nlt_ref[...], gi[:, here]).astype(BF16)
            accb[slot, :, :, :, here] = part.reshape(deep, 2, -1, 256)

    @pl.when(step == groups + 1)
    def _():
        send_b(0)()

    @pl.when(step == groups + 2)
    def _():
        send_b(1)()

    @pl.when(step == last)
    def _():
        for rows in blocks:
            grad_normed = acc[rows]
            normal_one = n1_ref[rows]
            grad_branch = norm_back(grad_normed, normal_one, inv_ref[rows], vec_ref[0:1, :])
            vg_ref[0:1, :] += jnp.sum(grad_normed * normal_one, axis=0, keepdims=True)
            vg_ref[1:2, :] += jnp.sum(grad_normed, axis=0, keepdims=True)
            vg_ref[4:5, :] += jnp.sum(grad_branch, axis=0, keepdims=True)
            acc[rows] = grad_branch
            part = grad_branch.astype(BF16)
            low[rows] = part
            gbt_ref[:, rows] = part.T
        store(3).start()
        store(1).start()
        for t in range(groups):
            gm_ref[t] = dot(low[...], wo_ref[t]).astype(BF16)
            store_mixed(t).start()
        add_b(0, 0)()
        add_b(1, 1)()
        store(2).start()
        finish()
        part_ref[...] = accc[place.x, :, place.y]
        settle()
        for k in range(4):
            store(k).wait()
        for t in range(groups):
            store_mixed(t).wait()


def layer(cot, hid, slope, second, n1, inv1, nlt, wa, wb, wc, vec, sizes):
    tokens, width = cot.shape
    groups, _, lanes = wa.shape
    hidden = wb.shape[2]
    deep = sizes[0] // 2
    rows = width // sizes[0]
    tail = 256
    anywhere = pl.BlockSpec(memory_space=pl.ANY)

    def used(i):
        return other_first(jnp.minimum(i, groups - 1))

    def back_group(i):
        return other_first(jnp.clip(i - groups, 0, groups - 1))

    copies = 8
    parts = (2, deep, 2, rows, hidden)
    matrix = pltpu.VMEM((groups, width, hidden), BF16)
    return pl.pallas_call(
        functools.partial(layer_kernel, sizes=sizes),
        grid=(2 * groups,),
        in_specs=[
            once(cot.shape),
            pl.BlockSpec((1, tokens, hidden), lambda i: (used(i), 0, 0)),
            pl.BlockSpec((1, tokens, hidden), lambda i: (back_group(i), 0, 0)),
            once(inv1.shape),
            once(vec.shape),
        ]
        + [anywhere] * 6,
        out_specs=[anywhere] * 5
        + [once((deep, rows, hidden)), once((8, width)), once((8, hidden))],
        out_shape=[
            jax.ShapeDtypeStruct((tokens, width), BF16),
            jax.ShapeDtypeStruct((tokens, width), F32),
            jax.ShapeDtypeStruct((groups, tokens, tail), BF16),
            jax.ShapeDtypeStruct((width, tokens), BF16),
            jax.ShapeDtypeStruct(parts, BF16),
            jax.ShapeDtypeStruct((deep, rows, hidden), BF16),
            jax.ShapeDtypeStruct((8, width), F32),
            jax.ShapeDtypeStruct((8, hidden), F32),
        ],
        scratch_shapes=[
            pltpu.VMEM(n1.shape, F32),
            pltpu.VMEM((width, tokens), BF16),
            pltpu.VMEM((groups, width, tail), BF16),
            matrix,
            matrix,
            pltpu.VMEM((tokens, width), F32),
            pltpu.VMEM((tokens, width), BF16),
            pltpu.VMEM((width, tokens), BF16),
            pltpu.VMEM((tokens, hidden), BF16),
            pltpu.VMEM((tokens, width), BF16),
            pltpu.VMEM((groups, tokens, tail), BF16),
            pltpu.VMEM((width, tokens), BF16),
            pltpu.SemaphoreType.DMA((2 * groups + 4,)),
            pltpu.SemaphoreType.DMA((4 + groups,)),
            pltpu.SemaphoreType.DMA((copies,)),
            pltpu.SemaphoreType.DMA((copies,)),
        ]
        + core_buffers(deep, rows, hidden) * 2
        + plane_buffers(deep, rows, hidden),
        compiler_params=params(collective_id=1, has_side_effects=True),
        name="layer",
    )(cot, hid, slope, inv1, vec, second, n1, nlt, wa, wb, wc)


def far_first(step, groups):
    tensor = lax.axis_index("tensor")
    x, c = tensor // 2, tensor % 2
    return jnp.where(step < groups, 1 - x, x) * 2 + jnp.where(step % groups < 2, 1 - c, c)


def back_kernel(
    pm_ref, gm_ref, lse_ref, seg_ref, wa_hbm, xt_hbm, gbt_hbm, gb_hbm,
    accb_hbm, part_ref, vg_ref, bg_ref, *refs, sizes, chunk,
):
    weights, means, squares = refs[0:5], refs[5:10], refs[10:15]
    grads, updates, norms, ig_ref = refs[15:20], refs[20:25], refs[25], refs[26]
    gp, gsum, send, recv, slots, hslots, nslots, vec, hvec, load_sem, sa = refs[27:38]
    wa_ref, xt_ref, gbt_ref, gb_ref, accb, inz_b, inz_c = refs[38:45]
    bufs_b, bufs_a, acc = refs[45:49], refs[49:56], refs[49]
    sb, sc = grads[2], grads[3]
    step = pl.program_id(0)
    groups, deep = sizes[1], sizes[0] // 2
    cols = HEADS * HD
    tokens, width = gb_ref.shape
    lanes = pm_ref.shape[2]
    last = 2 * groups - 1
    length = pm_ref.shape[1]
    place = Place(sizes)
    links = Links(send, recv)
    a = scatter_in_pairs(place, links, 0, *bufs_a, sa)
    more = 7 + 2 * deep
    start, middle, finish, settle = scatter_plane(place, links, more, accb, *bufs_b)
    b = scatter_tail(place, links, more + 4, accb.at[place.x, :, place.y], inz_b, sb)
    c = scatter_tail(place, links, more + 4 + deep, part_ref, inz_c, sc)
    early = add_everywhere(place, links, more + 4 + 2 * deep, vec, slots)
    small = add_everywhere(place, links, more + 6 + 3 * deep, hvec, hslots)
    final = add_in_two(place, links, more + 8 + 4 * deep, norms, nslots)
    t, s = far_first(step, groups), step % 2

    def load(k):
        pairs = ((accb_hbm, accb), (xt_hbm, xt_ref), (gbt_hbm, gbt_ref), (wa_hbm, wa_ref), (gb_hbm, gb_ref))
        return pltpu.make_async_copy(*pairs[k], load_sem.at[k])

    @pl.when(step == 0)
    def _():
        load(0).start()
        place.greet(everyone=True)
        c[0]()
        load(0).wait()
        start()
        for k in range(1, 5):
            load(k).start()
        gsum[...] = jnp.zeros_like(gsum)
        vec[...] = jnp.zeros_like(vec)
        hvec[...] = jnp.zeros_like(hvec)
        vec[0:6] = vg_ref[0:6]
        vec[8 : 8 + groups] = bg_ref[0:groups]
        early[0]()

    @pl.when(step == 1)
    def _():
        load(1).wait()
        load(2).wait()

    @pl.when(step == 2)
    def _():
        a[0]()
        early[1]()

    @pl.when(step == 4)
    def _():
        early[2]()
        middle()
        a[1]()

    @pl.when(step == 5)
    def _():
        c[1]()

    @pl.when(step == 6)
    def _():
        a[3]()
        early[3]()

    @pl.when(step == 7)
    def _():
        finish()
        b[0]()

    rows = pl.ds(pl.multiple_of(s * length, length), length)
    row = seg_ref[pl.ds(lax.axis_index("tensor") * 2 + s, 1)]
    attend_back(pm_ref.at[0], gm_ref.at[0], lse_ref, row, gp.at[t, rows], chunk)

    for n in (0, 2, 3):
        here = slice(n * 128, (n + 1) * 128)
        gsum[t, 0:1, here] += jnp.sum(gp[t, rows, here].astype(F32), axis=0, keepdims=True)

    @pl.when(s == 1)
    def _():
        order = step // 2
        slot = jnp.where(order % 2 == 0, 2 + order // 2, t // 2)
        for n in range(2):
            here = slice(n * 256, (n + 1) * 256)
            part = dot(xt_ref[...], gp[t, :, here]).astype(BF16)
            acc[slot, :, :, :, here] = part.reshape(deep, 2, -1, 256)
        from_x = dot(xt_ref[...], gp[t, :, 512:768])
        part = dot(gbt_ref[...], gp[t, :, 512:768])
        lane = lax.broadcasted_iota(jnp.int32, part.shape, 1)
        part = jnp.where((lane >= 128) & (lane < 192), from_x, part).astype(BF16)
        acc[slot, :, :, :, 512:768] = part.reshape(deep, 2, -1, 256)

    def input_columns(n):
        here = slice(n * 256, (n + 1) * 256)
        total = gb_ref[:, here]
        for g in range(groups):
            part = gp[g, :, 640:768]
            part = halves(part, jnp.zeros_like(part))
            total = total + dot(gp[g, :, 0:512], wa_ref[g, here, 0:512], NT)
            total = total + dot(part, wa_ref[g, here, 640:768], NT)
        ig_ref[:, here] = total.astype(BF16)

    @pl.when(step == last)
    def _():
        for g in range(groups):
            for h in range(HEADS):
                at = g * cols + h * HD
                line, lane = at // 256, slice(at % 256, at % 256 + HD)
                hvec[line : line + 1, lane] = gsum[g, 0:1, Q_AT[h] : Q_AT[h] + HD]
                hvec[3 + line : 4 + line, lane] = gsum[g, 0:1, V_AT[h] : V_AT[h] + HD]
        small[0]()
        a[4]()
        a[5]()
        a[2]()
        load(3).wait()
        load(4).wait()
        input_columns(0)
        small[1]()
        a[6]()
        early[4]()
        input_columns(1)
        small[2]()
        a[7]()
        input_columns(2)
        a[8]()
        small[3]()
        b[1]()
        settle()
        found = group_sums([None] * 4 + [sb[...], sc[...], None], weights, means, squares, updates)
        small[4]()
        for k in range(3):
            lanes_of = slice(k * 256, (k + 1) * 256)
            vec[6:7, lanes_of] = hvec[k : k + 1]
            vec[7:8, lanes_of] = hvec[3 + k : 4 + k]
        count, mine = weights[4].shape
        index = lax.axis_index("dp") * groups + lax.axis_index("tensor")
        turned = pltpu.roll(vec[...], width - index * mine, 1)
        grads[4][...] = turned[0:count, 0:mine]
        found = found + group_sums(
            [None] * 6 + [grads[4][...]], weights, means, squares, updates
        )
        a[9]()
        total = sa[...]
        for k, at in enumerate((Q_AT, K_AT, V_AT)):
            grads[0][k] = collect(total, at)
        grads[1][...] = collect(total, O_AT).T
        parts = [grads[0][k] for k in range(3)] + [grads[1][...]]
        norms[...] = found + group_sums(parts + [None] * 3, weights, means, squares, updates)
        for run in final:
            run()


def group_sums(grads, weights, means, squares, updates):
    lane = lax.broadcasted_iota(jnp.int32, (8, 128), 1)
    line = lax.broadcasted_iota(jnp.int32, (8, 128), 0)
    found = jnp.zeros((8, 128), F32)
    for group, grad in enumerate(grads):
        if grad is None:
            continue
        i, k = (0, group) if group < 3 else (group - 2, ...)
        weight, mean, square = (ref[i][k] for ref in (weights, means, squares))
        update = adam_parts(grad, mean, square)[2]
        if i < 4:
            update = update + WEIGHT_DECAY * weight
        updates[i][k] = update
        if i < 4:
            pair = (sum_all(weight * weight), sum_all(update * update))
            for which in range(2):
                hit = (lane == group) & (line == which)
                found = found + jnp.where(hit, pair[which], 0.0)
            continue
        for which, values in enumerate((weight, update)):
            per_row = jnp.sum(values * values, axis=1, keepdims=True)
            for row in range(weight.shape[0]):
                hit = (lane == 6 + min(row, 8)) & (line == which)
                found = found + jnp.where(hit, per_row[row : row + 1], 0.0)
    return found


def back(pm, gm, lse, seg, wa, xt, gbt, gb, accb, part, vg, bg,
         weights, means, squares, sizes):
    deep, groups = sizes[0] // 2, sizes[1]
    tokens, width = gb.shape
    lanes = pm.shape[2]
    length = seg.shape[1]
    seqs = tokens // length
    rows = width // sizes[0]
    copies = 7 + 2 * deep + 4 + 2 * deep + 2 * (deep + 2) + 7 + deep
    small = [weights, means, squares]
    anywhere = pl.BlockSpec(memory_space=pl.ANY)
    outs = [jax.ShapeDtypeStruct(weight.shape, F32) for weight in weights] * 2 + [
        jax.ShapeDtypeStruct((8, 128), F32),
        jax.ShapeDtypeStruct((tokens, width), BF16),
    ]
    return pl.pallas_call(
        functools.partial(back_kernel, sizes=sizes, chunk=min(256, length)),
        grid=(groups * seqs,),
        in_specs=[
            pl.BlockSpec((1, length, lanes), lambda i: (far_first(i, groups), i % 2, 0)),
            pl.BlockSpec((1, length, gm.shape[2]), lambda i: (far_first(i, groups), i % 2, 0)),
            pl.BlockSpec((1, 1, 8, length), lambda i: (far_first(i, groups), i % 2, 0, 0)),
            once(seg.shape),
            anywhere,
            anywhere,
            anywhere,
            anywhere,
            anywhere,
            once(part.shape),
            once(vg.shape),
            once(bg.shape),
        ]
        + [once(ref.shape) for group in small for ref in group],
        out_specs=[once(ref.shape) for ref in outs],
        out_shape=outs,
        scratch_shapes=[
            pltpu.VMEM((groups, tokens, lanes), BF16),
            pltpu.VMEM((groups, 8, lanes), F32),
            pltpu.SemaphoreType.DMA((copies,)),
            pltpu.SemaphoreType.DMA((copies,)),
            pltpu.VMEM((deep + 2, 16, width), F32),
            pltpu.VMEM((deep + 2, 8, 256), F32),
            pltpu.VMEM((8 + deep, 8, 128), F32),
            pltpu.VMEM((16, width), F32),
            pltpu.VMEM((8, 256), F32),
            pltpu.SemaphoreType.DMA((5,)),
            pltpu.VMEM((rows, lanes), F32),
            pltpu.VMEM(wa.shape, BF16),
            pltpu.VMEM(xt.shape, BF16),
            pltpu.VMEM(gbt.shape, BF16),
            pltpu.VMEM(gb.shape, F32),
            pltpu.VMEM(accb.shape, BF16),
            pltpu.VMEM((deep, rows, lanes), BF16),
            pltpu.VMEM((deep, rows, lanes), BF16),
        ]
        + plane_buffers(deep, rows, lanes)
        + core_buffers(deep, rows, lanes)
        + plane_buffers(deep, rows, lanes)
        + [pltpu.VMEM((deep, rows, lanes), BF16)],
        compiler_params=params(collective_id=2, has_side_effects=True),
        name="back",
    )(
        pm, gm, lse, seg, wa, xt, gbt, gb,
        accb, part, vg, bg,
        *weights, *means, *squares,
    )


def apply_kernel(*refs):
    sums, ins, passed = refs[0], refs[1:26], refs[26:28]
    norms, outs, finals = refs[28], refs[29:44], refs[44:46]
    held, kept, narrow, wide = refs[46:71], refs[71], refs[72], refs[73]
    in_sem, out_sem = refs[74], refs[75]
    loads = [pltpu.make_async_copy(ins[k], held[k], in_sem.at[k]) for k in range(25)]
    result = pltpu.make_async_copy(passed[0], kept, in_sem.at[25])
    gradient = pltpu.make_async_copy(passed[1], narrow, in_sem.at[26])
    gradient.start()
    order = [(i, k) for i in range(5) for k in (0, 3, 4, 1, 2)]
    for i, k in order:
        loads[5 * k + i].start()
    result.start()
    stores = []

    def store(src, dst):
        stores.append(pltpu.make_async_copy(src, dst, out_sem.at[len(stores)]))
        stores[-1].start()

    roots = jnp.sqrt(sums[...])
    norms[...] = roots[0:2, 0:15]
    ratio = LEARN_RATE * roots[0:1] / (roots[1:2] + ADAM_EPS)
    rows = wide.shape[0] // 4
    gradient.wait()
    for k in range(4):
        here = pl.ds(k * rows, rows)
        wide[here] = narrow[here].astype(F32)
        store(wide.at[here], finals[1].at[here])
    for i in range(5):
        for k in (0, 3, 4, 1, 2):
            loads[5 * k + i].wait()
        grad, update, weight, mean, square = (held[5 * k + i] for k in range(5))
        value = grad[...]
        mean[...] = MOMENT_DECAY * mean[...] + (1.0 - MOMENT_DECAY) * value
        square[...] = MOMENT_DECAY * square[...] + (1.0 - MOMENT_DECAY) * value * value
        if i == 0:
            for k in range(3):
                weight[k] = weight[k] - ratio[:, k : k + 1] * update[k]
        elif i < 4:
            weight[...] = weight[...] - ratio[:, 2 + i : 3 + i] * update[...]
        else:
            for row in range(weight.shape[0]):
                here = slice(row, row + 1)
                step = ratio[:, 6 + min(row, 8) : 7 + min(row, 8)]
                weight[here] = weight[here] - step * update[here]
        store(mean, outs[3 * i])
        store(square, outs[3 * i + 1])
        store(weight, outs[3 * i + 2])
    result.wait()
    store(kept, finals[0])
    for move in stores:
        move.wait()


def apply(grads, updates, sums, weights, means, squares, passed):
    inside, anywhere = pl.BlockSpec(memory_space=pltpu.VMEM), pl.BlockSpec(memory_space=pl.ANY)
    shapes = [jax.ShapeDtypeStruct((2, 15), F32)]
    for weight in weights:
        shapes += [jax.ShapeDtypeStruct(weight.shape, F32)] * 3
    shapes += [jax.ShapeDtypeStruct(passed[0].shape, BF16)]
    shapes += [jax.ShapeDtypeStruct(passed[1].shape, F32)]
    norms, *rest = pl.pallas_call(
        apply_kernel,
        in_specs=[inside] + [anywhere] * 27,
        out_specs=[inside] + [anywhere] * 17,
        out_shape=shapes,
        scratch_shapes=[pltpu.VMEM(weight.shape, F32) for _ in range(5) for weight in weights]
        + [
            pltpu.VMEM(passed[0].shape, BF16),
            pltpu.VMEM(passed[1].shape, BF16),
            pltpu.VMEM(passed[1].shape, F32),
            pltpu.SemaphoreType.DMA((27,)),
            pltpu.SemaphoreType.DMA((20,)),
        ],
        compiler_params=params(),
        name="apply",
    )(sums, *grads, *updates, *weights, *means, *squares, *passed)
    return rest[:15] + [norms] + rest[15:]


def make_body(sizes):
    def body(
        tokens, cotangent, segments,
        qkv_weight, out_weight, inner_weight, outer_weight, vectors,
        qkv_mean, out_mean, inner_mean, outer_mean, vector_mean,
        qkv_square, out_square, inner_square, outer_square, vector_square,
    ):
        groups = sizes[1]
        token_count, width = tokens.shape
        length = segments.shape[1]
        seqs = token_count // length
        cols = qkv_weight.shape[2]
        tensor_index = lax.axis_index("tensor")
        weights = (qkv_weight, out_weight, inner_weight, outer_weight, vectors)
        old_means = (qkv_mean, out_mean, inner_mean, outer_mean, vector_mean)
        old_squares = (qkv_square, out_square, inner_square, outer_square, vector_square)
        if sizes[0] % 2 == 0 and groups == 4 and qkv_weight.shape[1] % 96 == 0:
            weights, old_means, old_squares = (
                entry[:3] + (entry[3].T, entry[4]) for entry in (weights, old_means, old_squares)
            )
            wa, wb, wc, hid, nlt, xt, n1, full, pm, lse, slope, second, inv1 = gather_attend(
                weights, tokens, segments, sizes
            )
            result, gb, gm, gbt, accb, part, vg, bg = layer(
                cotangent, hid, slope, second, n1, inv1, nlt, wa, wb, wc, full, sizes
            )
            *changes, sums, input_grad = back(
                pm, gm, lse, segments, wa, xt, gbt, gb, accb, part, vg, bg,
                weights, old_means, old_squares, sizes,
            )
            passed = (result, input_grad)
            new = list(
                apply(changes[:5], changes[5:], sums, weights, old_means, old_squares, passed)
            )
            new[9:12] = [entry.T for entry in new[9:12]]
            return tuple(new[16:]) + tuple(new[:16])
        seg = lax.dynamic_slice_in_dim(segments, tensor_index * seqs, seqs, 0)
        seg = jnp.broadcast_to(seg[:, None, :], (seqs, 8, length))
        pack_a = spread(qkv_weight[0], qkv_weight[1], qkv_weight[2], out_weight.T).astype(BF16)
        pack_b = inner_weight.astype(BF16)
        pack_c = outer_weight.T.astype(BF16)
        wa, wb, wc = (gather_blocks(pack, sizes) for pack in (pack_a, pack_b, pack_c))
        full = lax.all_gather(vectors, ("dp", "tensor"), axis=1, tiled=True)
        q_bias = full[6].reshape(groups, cols)
        v_bias = full[7].reshape(groups, cols)
        none = jnp.zeros_like(q_bias)
        proj_bias = spread(q_bias, none, v_bias, none)
        proj_bias = jnp.broadcast_to(proj_bias[:, None, :], (groups, 8, 4 * cols))
        inner_bias = full[8:].reshape(groups, -1)
        pm, lse = attend_fwd(tokens, wa, proj_bias, seg, length)
        result, hid, gi, nl, gsl, gbl, gb, gm, vg, bg = ffn(
            tokens, cotangent, pm, wa, wb, wc, full, inner_bias
        )
        gp, gsum = attend_bwd(pm, gm, lse, seg)

        grad_c = jnp.einsum("td,gtf->gdf", gsl, hid, preferred_element_type=F32).astype(BF16)
        grad_b = jnp.einsum("td,gtf->gdf", nl, gi, preferred_element_type=F32).astype(BF16)
        from_tokens = jnp.einsum("td,gtc->gdc", tokens, gp, preferred_element_type=F32)
        from_branch = jnp.einsum("td,gtc->gdc", gbl, pm, preferred_element_type=F32)
        lane = lax.broadcasted_iota(jnp.int32, (1, 1, LANES), 2)
        is_mixed = (lane >= 512) & ((lane < 640) | (lane >= 704))
        grad_a = jnp.where(is_mixed, from_branch, from_tokens).astype(BF16)
        input_grad = gb + jnp.einsum(
            "gtc,gdc->td",
            jnp.where(is_mixed, jnp.zeros((), BF16), gp),
            wa,
            preferred_element_type=F32,
        )
        head_rows = jnp.stack([collect(gsum[:, 0], at).reshape(-1) for at in (Q_AT, V_AT)])
        vector_grad = jnp.concatenate([vg[:6], head_rows, bg[:groups].reshape(-1, width)], axis=0)
        sum_a, sum_b, sum_c = (
            scatter_blocks(grad, sizes).astype(F32) for grad in (grad_a, grad_b, grad_c)
        )
        vector_sum = lax.psum_scatter(
            vector_grad, ("dp", "tensor"), scatter_dimension=1, tiled=True
        )
        new = lamb_plain(sum_a, sum_b, sum_c, vector_sum, weights, old_means, old_squares)
        return (result, input_grad) + tuple(new)

    return body

def solution(mesh):
    sizes = (mesh.shape["dp"], mesh.shape["tensor"])
    rows = P(("dp", "tensor"), None)
    qkv = P(None, "dp", "tensor")
    out = P("tensor", "dp")
    inner = P("dp", "tensor")
    vec = P(None, ("dp", "tensor"))
    weights = (qkv, out, inner, out, vec)
    return jax.shard_map(
        make_body(sizes),
        mesh=mesh,
        in_specs=(rows, rows, P("dp", None)) + weights * 3,
        out_specs=(rows, rows) + (qkv,) * 3 + (out,) * 3 + (inner,) * 3 + (out,) * 3 + (vec,) * 3 + (P(),),
        check_vma=False,
    )
```

```python
import functools

import jax
import jax.numpy as jnp
from jax import lax
from jax.experimental import pallas as pl
from jax.experimental.pallas import tpu as pltpu
from jax.sharding import PartitionSpec as P

HD = 64
STEP = 5
NORM_EPS = 1e-05
ADAM_EPS = 1e-06
MOMENT_DECAY = 0.5
LEARN_RATE = 0.5
WEIGHT_DECAY = 0.01
MASKED = -1e30
SCALE = HD ** (-0.5)
F32 = jnp.float32
BF16 = jnp.bfloat16
NT = (((1,), (1,)), ((), ()))
NN = (((1,), (0,)), ((), ()))
TN = (((0,), (0,)), ((), ()))
VMEM_LIMIT = 60 * 1024 * 1024


def dot(a, b, dims=NN):
    return lax.dot_general(a, b, dims, preferred_element_type=F32)


def params(**kw):
    return pltpu.CompilerParams(vmem_limit_bytes=VMEM_LIMIT, **kw)


HEADS = 3
DOCS = 4
LANES = 768
Q_AT, K_AT, V_AT, O_AT = (0, 64, 384), (128, 192, 640), (256, 320, 448), (512, 576, 704)
Q_TILE, K_TILE, V_TILE = (0, 0, 3), (1, 1, 5), (2, 2, 3)
UPPER = (False, True, False)
V_UPPER = (False, True, True)


def spread(q, k, v, o):
    parts = {}
    for places, values in ((Q_AT, q), (K_AT, k), (V_AT, v), (O_AT, o)):
        for h, at in enumerate(places):
            parts[at] = values[:, h * HD : (h + 1) * HD]
    return jnp.concatenate([parts[at] for at in sorted(parts)], axis=1)


def collect(values, places):
    return jnp.concatenate([values[:, at : at + HD] for at in places], axis=1)


def tile_of(ref, n, rows=slice(None)):
    return ref[rows, n * 128 : (n + 1) * 128]


def is_low(shape):
    return lax.broadcasted_iota(jnp.int32, shape, 1) < HD


def halves(low, high):
    return jnp.where(is_low(low.shape), low, high)


def document_lanes(row):
    length = row.shape[1]
    number = jnp.broadcast_to(row.astype(F32), (128, length)).T
    lane = lax.broadcasted_iota(jnp.int32, (length, 128), 1) % HD
    same = number == lane.astype(F32)
    for_query = jnp.where(same, 1.0, 0.0).astype(BF16)
    for_key = jnp.where(same, 0.0, jnp.where(lane < DOCS, MASKED, 0.0)).astype(BF16)
    return for_query, for_key


def attend_heads(pm_ref, row, lse_ref, chunk):
    length = pm_ref.shape[0]
    chunks = length // chunk
    doc_q, doc_k = document_lanes(row)
    ones = jnp.ones((16, length), BF16)
    units = [(h, c) for h in range(HEADS) for c in range(chunks)]
    keys, queries, values = {}, {}, {}
    for h in range(HEADS):
        q, k = tile_of(pm_ref, Q_TILE[h]) * SCALE, tile_of(pm_ref, K_TILE[h])
        queries[h] = halves(doc_q, q) if UPPER[h] else halves(q, doc_q)
        keys[h] = halves(doc_k, k) if UPPER[h] else halves(k, doc_k)
        vt = tile_of(pm_ref, V_TILE[h]).T
        vt = vt[HD:] if V_UPPER[h] else vt[:HD]
        values[h] = jnp.concatenate([vt, ones], axis=0)

    def scores(unit):
        h, c = unit
        return dot(keys[h], queries[h][c * chunk : (c + 1) * chunk], NT)

    outs = {h: [] for h in range(HEADS)}
    ahead = scores(units[0])
    for n, (h, c) in enumerate(units):
        s = ahead
        if n + 1 < len(units):
            ahead = scores(units[n + 1])
        m = jnp.max(s, axis=0, keepdims=True)
        p = jnp.exp(s - m).astype(BF16)
        ot = dot(values[h], p)
        total = ot[HD : HD + 1]
        outs[h].append((ot[:HD] * (1.0 / total)).astype(BF16))
        lse_ref[0, 0, h : h + 1, c * chunk : (c + 1) * chunk] = m + jnp.log(total)
    out = [jnp.concatenate(outs[h], axis=1) for h in range(HEADS)]
    pm_ref[:, 512:640] = jnp.concatenate([out[0], out[1]], axis=0).T
    last = jnp.concatenate([jnp.zeros_like(out[2]), out[2]], axis=0).T
    pm_ref[:, 640:768] = halves(tile_of(pm_ref, 5), last)


def attend_fwd_kernel(x_ref, w_ref, bias_ref, seg_ref, pm_ref, lse_ref, *, chunk):
    proj = dot(x_ref[...], w_ref[0]) + bias_ref[0, 0:1, :]
    pm_ref[0] = proj.astype(BF16)
    attend_heads(pm_ref.at[0], seg_ref[0, 0:1], lse_ref, chunk)


def attend_fwd(x, wa, bias, seg, length):
    tokens, width = x.shape
    groups, _, lanes = wa.shape
    seqs = tokens // length
    return pl.pallas_call(
        functools.partial(attend_fwd_kernel, chunk=min(256, length)),
        grid=(groups, seqs),
        in_specs=[
            pl.BlockSpec((length, width), lambda t, s: (s, 0)),
            pl.BlockSpec((1, width, lanes), lambda t, s: (t, 0, 0)),
            pl.BlockSpec((1, 8, lanes), lambda t, s: (t, 0, 0)),
            pl.BlockSpec((1, 8, length), lambda t, s: (s, 0, 0)),
        ],
        out_specs=[
            pl.BlockSpec((1, length, lanes), lambda t, s: (t, s, 0)),
            pl.BlockSpec((1, 1, 8, length), lambda t, s: (t, s, 0, 0)),
        ],
        out_shape=[
            jax.ShapeDtypeStruct((groups, tokens, lanes), BF16),
            jax.ShapeDtypeStruct((groups, seqs, 8, length), F32),
        ],
        compiler_params=params(),
        name="attend_fwd",
    )(x, wa, bias, seg)


def attend_back(pm_ref, gm_ref, lse_ref, row, gp_ref, chunk):
    length = pm_ref.shape[0]
    chunks = length // chunk
    prod = gm_ref[...].astype(F32) * pm_ref[:, 512:768].astype(F32)
    hi = prod.astype(BF16)
    lo = (prod - hi.astype(F32)).astype(BF16)
    lane = lax.broadcasted_iota(jnp.int32, (8, 256), 1)
    line = lax.broadcasted_iota(jnp.int32, (8, 256), 0)
    start = jnp.where(line == 2, O_AT[2] - 512, line * HD)
    pick = jnp.where((lane >= start) & (lane < start + HD) & (line < HEADS), 1.0, 0.0).astype(BF16)
    dsum = dot(pick, hi, NT) + dot(pick, lo, NT)
    doc_q, doc_k = document_lanes(row)
    none = jnp.zeros((length, 128), BF16)
    units = [(h, c) for h in range(HEADS) for c in range(chunks)]
    keys, queries, plain, values, kts, grads = {}, {}, {}, {}, {}, {}
    for h in range(HEADS):
        q, k = tile_of(pm_ref, Q_TILE[h]) * SCALE, tile_of(pm_ref, K_TILE[h])
        plain[h] = q
        queries[h] = halves(doc_q, q) if UPPER[h] else halves(q, doc_q)
        keys[h] = halves(doc_k, k) if UPPER[h] else halves(k, doc_k)
        kt = k.T
        kts[h] = kt[HD:] if UPPER[h] else kt[:HD]
        v = tile_of(pm_ref, V_TILE[h])
        values[h] = halves(none, v) if V_UPPER[h] else halves(v, none)
        grads[h] = tile_of(gm_ref, 0 if h < 2 else 1)

    def rows_of(c):
        return slice(c * chunk, (c + 1) * chunk)

    def products(unit):
        h, c = unit
        return dot(keys[h], queries[h][rows_of(c)], NT), dot(values[h], grads[h][rows_of(c)], NT)

    dqs = {h: [] for h in range(HEADS)}
    dks, dvs = {}, {}
    ahead = products(units[0])
    for n, (h, c) in enumerate(units):
        s, dp = ahead
        if n + 1 < len(units):
            ahead = products(units[n + 1])
        rows = rows_of(c)
        p = jnp.exp(s - lse_ref[0, 0, h : h + 1, rows])
        ds = (p * (dp - dsum[h : h + 1, rows])).astype(BF16)
        dv = dot(p.astype(BF16), grads[h][rows])
        dk = dot(ds, plain[h][rows])
        dvs[h] = dv if c == 0 else dvs[h] + dv
        dks[h] = dk if c == 0 else dks[h] + dk
        dqs[h].append((dot(kts[h], ds) * SCALE).astype(BF16))
    dq = [jnp.concatenate(dqs[h], axis=1) for h in range(HEADS)]
    gp_ref[:, 0:128] = jnp.concatenate([dq[0], dq[1]], axis=0).T
    gp_ref[:, 128:256] = halves(dks[0], dks[1]).astype(BF16)
    gp_ref[:, 256:384] = halves(dvs[0], dvs[1]).astype(BF16)
    last = jnp.concatenate([dq[2], jnp.zeros_like(dq[2])], axis=0).T
    gp_ref[:, 384:512] = halves(last, dvs[2].astype(BF16))
    gp_ref[:, 512:640] = tile_of(pm_ref, 4)
    gp_ref[:, 640:768] = halves(dks[2].astype(BF16), tile_of(pm_ref, 5))


def attend_bwd_kernel(pm_ref, gm_ref, lse_ref, seg_ref, gp_ref, gsum_ref, *, chunk):
    attend_back(pm_ref.at[0], gm_ref.at[0], lse_ref, seg_ref[0, 0:1], gp_ref.at[0], chunk)

    @pl.when(pl.program_id(1) == 0)
    def _():
        gsum_ref[...] = jnp.zeros_like(gsum_ref)

    gsum_ref[0, 0:1, :] += jnp.sum(gp_ref[0].astype(F32), axis=0, keepdims=True)


def attend_bwd(pm, gm, lse, seg):
    groups, tokens, lanes = pm.shape
    seqs, length = lse.shape[1], lse.shape[3]
    return pl.pallas_call(
        functools.partial(attend_bwd_kernel, chunk=min(256, length)),
        grid=(groups, seqs),
        in_specs=[
            pl.BlockSpec((1, length, lanes), lambda t, s: (t, s, 0)),
            pl.BlockSpec((1, length, gm.shape[2]), lambda t, s: (t, s, 0)),
            pl.BlockSpec((1, 1, 8, length), lambda t, s: (t, s, 0, 0)),
            pl.BlockSpec((1, 8, length), lambda t, s: (s, 0, 0)),
        ],
        out_specs=[
            pl.BlockSpec((1, length, lanes), lambda t, s: (t, s, 0)),
            pl.BlockSpec((1, 8, lanes), lambda t, s: (t, 0, 0)),
        ],
        out_shape=[
            jax.ShapeDtypeStruct((groups, tokens, lanes), BF16),
            jax.ShapeDtypeStruct((groups, 8, lanes), F32),
        ],
        compiler_params=params(),
        name="attend_bwd",
    )(pm, gm, lse, seg)


def mixed_only(tail):
    lane = lax.broadcasted_iota(jnp.int32, tail.shape, 1)
    return jnp.where((lane < 128) | (lane >= 192), tail, jnp.zeros((), BF16))


def gelu_parts(pre):
    cdf = 0.5 * (1.0 + lax.erf(pre * (2.0**-0.5)))
    pdf = jnp.exp(-0.5 * pre * pre) * 0.3989422804014327
    return pre * cdf, cdf + pre * pdf


def mean_of(values):
    return jnp.mean(values, axis=-1, keepdims=True)


def norm_parts(values):
    centred = values - mean_of(values)
    inverse = lax.rsqrt(mean_of(centred * centred) + NORM_EPS)
    return centred * inverse, inverse


def norm_back(incoming, normal, inverse, gain):
    scaled = incoming * gain
    return inverse * (scaled - mean_of(scaled) - normal * mean_of(scaled * normal))


def ffn_kernel(
    x_ref, cot_ref, pm_ref, wo_ref, wb_ref, wc_ref, vec_ref, bias_ref,
    out_ref, hid_ref, gi_ref, nl_ref, gsl_ref, gbl_ref, gb_ref, gm_ref, vg_ref, bg_ref,
    slope_ref,
):
    groups = wb_ref.shape[0]

    @pl.when(pl.program_id(0) == 0)
    def _():
        vg_ref[...] = jnp.zeros_like(vg_ref)
        bg_ref[...] = jnp.zeros_like(bg_ref)

    total = x_ref[...].astype(F32) + vec_ref[4:5, :]
    for t in range(groups):
        total = total + dot(mixed_only(pm_ref[t]), wo_ref[t], NT)
    normal_one, inverse_one = norm_parts(total)
    normed = normal_one * vec_ref[0:1, :] + vec_ref[1:2, :]
    low = normed.astype(BF16)
    nl_ref[...] = low
    second = normed + vec_ref[5:6, :]
    for t in range(groups):
        pre = dot(low, wb_ref[t]) + bias_ref[t : t + 1, :]
        act, slope = gelu_parts(pre)
        act = act.astype(BF16)
        hid_ref[t] = act
        slope_ref[t] = slope
        second = second + dot(act, wc_ref[t], NT)
    normal_two, inverse_two = norm_parts(second)
    out_ref[...] = (normal_two * vec_ref[2:3, :] + vec_ref[3:4, :]).astype(BF16)
    cot = cot_ref[...].astype(F32)
    grad_second = norm_back(cot, normal_two, inverse_two, vec_ref[2:3, :])
    vg_ref[2:3, :] += jnp.sum(cot * normal_two, axis=0, keepdims=True)
    vg_ref[3:4, :] += jnp.sum(cot, axis=0, keepdims=True)
    vg_ref[5:6, :] += jnp.sum(grad_second, axis=0, keepdims=True)
    gs_low = grad_second.astype(BF16)
    gsl_ref[...] = gs_low
    grad_normed = grad_second
    for t in range(groups):
        grad_inner = (dot(gs_low, wc_ref[t]) * slope_ref[t]).astype(BF16)
        gi_ref[t] = grad_inner
        bg_ref[t : t + 1, :] += jnp.sum(grad_inner.astype(F32), axis=0, keepdims=True)
        grad_normed = grad_normed + dot(grad_inner, wb_ref[t], NT)
    grad_branch = norm_back(grad_normed, normal_one, inverse_one, vec_ref[0:1, :])
    vg_ref[0:1, :] += jnp.sum(grad_normed * normal_one, axis=0, keepdims=True)
    vg_ref[1:2, :] += jnp.sum(grad_normed, axis=0, keepdims=True)
    vg_ref[4:5, :] += jnp.sum(grad_branch, axis=0, keepdims=True)
    gb_ref[...] = grad_branch
    gb_low = grad_branch.astype(BF16)
    gbl_ref[...] = gb_low
    for t in range(groups):
        gm_ref[t] = dot(gb_low, wo_ref[t]).astype(BF16)


def ffn(x, cot, pm, wa, wb, wc, vec, bias):
    tokens, width = x.shape
    groups, _, lanes = wa.shape
    hidden = wb.shape[2]
    tail = 256
    tile = 256
    last = lanes // tail - 1
    once = pl.Buffered(1)
    row = pl.BlockSpec((tile, width), lambda i: (i, 0))
    wide = pl.BlockSpec((groups, tile, hidden), lambda i: (0, i, 0))
    return pl.pallas_call(
        ffn_kernel,
        grid=(tokens // tile,),
        in_specs=[
            row,
            row,
            pl.BlockSpec((groups, tile, tail), lambda i: (0, i, last)),
            pl.BlockSpec((groups, width, tail), lambda i: (0, 0, last), pipeline_mode=once),
            pl.BlockSpec((groups, width, hidden), lambda i: (0, 0, 0), pipeline_mode=once),
            pl.BlockSpec((groups, width, hidden), lambda i: (0, 0, 0), pipeline_mode=once),
            pl.BlockSpec(vec.shape, lambda i: (0, 0)),
            pl.BlockSpec(bias.shape, lambda i: (0, 0)),
        ],
        out_specs=[
            row,
            wide,
            wide,
            row,
            row,
            row,
            row,
            pl.BlockSpec((groups, tile, tail), lambda i: (0, i, 0)),
            pl.BlockSpec((8, width), lambda i: (0, 0)),
            pl.BlockSpec((8, hidden), lambda i: (0, 0)),
        ],
        out_shape=[
            jax.ShapeDtypeStruct((tokens, width), BF16),
            jax.ShapeDtypeStruct((groups, tokens, hidden), BF16),
            jax.ShapeDtypeStruct((groups, tokens, hidden), BF16),
            jax.ShapeDtypeStruct((tokens, width), BF16),
            jax.ShapeDtypeStruct((tokens, width), BF16),
            jax.ShapeDtypeStruct((tokens, width), BF16),
            jax.ShapeDtypeStruct((tokens, width), F32),
            jax.ShapeDtypeStruct((groups, tokens, tail), BF16),
            jax.ShapeDtypeStruct((8, width), F32),
            jax.ShapeDtypeStruct((8, hidden), F32),
        ],
        scratch_shapes=[pltpu.VMEM((groups, tile, hidden), F32)],
        compiler_params=params(),
        name="ffn",
    )(x, cot, pm, wa, wb, wc, vec, bias)


MESH = pl.DeviceIdType.MESH


class Place:
    def __init__(self, sizes):
        dp, tensor = lax.axis_index("dp"), lax.axis_index("tensor")
        self.deep = sizes[0] // 2
        self.z, self.y = dp // 2, dp % 2
        self.x, self.c = tensor // 2, tensor % 2

    def to_z(self, step):
        return {"dp": lax.rem(self.z + step, self.deep) * 2 + self.y}

    def to_y(self):
        return {"dp": self.z * 2 + 1 - self.y}

    def to_x(self):
        return {"tensor": (1 - self.x) * 2 + self.c}

    def to_c(self):
        return {"tensor": self.x * 2 + 1 - self.c}

    def from_z(self, step):
        return lax.rem(self.z + self.deep - step, self.deep)

    def partners(self):
        return [self.to_z(j) for j in range(1, self.deep)] + [self.to_y(), self.to_x(), self.to_c()]

    def peers(self):
        found = []
        for r in range(1, 8):
            x = 1 - self.x if r & 4 else self.x
            y = 1 - self.y if r & 2 else self.y
            c = 1 - self.c if r & 1 else self.c
            found.append((x * 4 + y * 2 + c, {"dp": self.z * 2 + y, "tensor": x * 2 + c}))
        return found

    def greet(self, everyone=False):
        barrier = pltpu.get_barrier_semaphore()
        partners = self.partners()
        if everyone:
            partners = partners[: self.deep - 1] + [device for _, device in self.peers()]
        for partner in partners:
            pl.semaphore_signal(barrier, inc=1, device_id=partner, device_id_type=MESH)
        pl.semaphore_wait(barrier, len(partners))


class Links:
    def __init__(self, send, recv):
        self.send, self.recv = send, recv

    def copy(self, k, ref, to, dst=None):
        return pltpu.make_async_remote_copy(
            src_ref=ref,
            dst_ref=ref if dst is None else dst,
            send_sem=self.send.at[k],
            recv_sem=self.recv.at[k],
            device_id=to,
            device_id_type=MESH,
        )

    def landed(self, k, ref, to):
        self.copy(k, ref, to).wait_recv()


def add_everywhere(place, links, base, own, slots):
    deep = place.deep
    hops = [place.to_c(), place.to_y(), place.to_x()]

    def start(i):
        def run():
            if i:
                links.copy(base + i - 1, own, hops[i - 1], slots.at[i - 1]).wait_send()
                links.landed(base + i - 1, slots.at[i - 1], hops[i - 1])
                own[...] = own[...] + slots[i - 1]
            if i < 3:
                links.copy(base + i, own, hops[i], slots.at[i]).start()
            else:
                for j in range(1, deep):
                    links.copy(base + 2 + j, own, place.to_z(j), slots.at[2 + j]).start()

        return run

    def last():
        for j in range(1, deep):
            links.copy(base + 2 + j, own, place.to_z(j), slots.at[2 + j]).wait_send()
            links.landed(base + 2 + j, slots.at[2 + j], place.to_z(j))
        slots[2] = own[...]
        total = slots[2 + lax.rem(place.z + deep, deep)]
        for z in range(1, deep):
            total = total + slots[2 + lax.rem(place.z + deep - z, deep)]
        own[...] = total

    return [start(0), start(1), start(2), start(3), last]


def add_in_two(place, links, base, own, slots):
    p, deep = place, place.deep
    me = p.x * 4 + p.y * 2 + p.c
    peers = p.peers()

    def near(r):
        return links.copy(base + r, own, peers[r - 1][1], slots.at[me])

    def far(j):
        return links.copy(base + 7 + j, own, p.to_z(j), slots.at[8 + p.z])

    def start():
        for r in range(1, 8):
            near(r).start()
        slots[me] = own[...]

    def middle():
        for r in range(1, 8):
            near(r).wait_send()
            links.landed(base + r, slots.at[peers[r - 1][0]], peers[r - 1][1])
        total = slots[0]
        for k in range(1, 8):
            total = total + slots[k]
        own[...] = total
        for j in range(1, deep):
            far(j).start()
        slots[8 + p.z] = total

    def last():
        for j in range(1, deep):
            far(j).wait_send()
            links.landed(base + 7 + j, slots.at[8 + p.from_z(j)], p.to_z(j))
        total = slots[8]
        for k in range(1, deep):
            total = total + slots[8 + k]
        own[...] = total

    return [start, middle, last]


def gather_stages(place, links, base, own, whole, start=0, count=None):
    p, deep = place, place.deep
    count = own.shape[0] if count is None else count
    half = count // 2
    rows, first, later = pl.ds(start, count), pl.ds(start, half), pl.ds(start + half, half)
    own = own.at[rows]
    mine = whole.at[p.x, p.c, p.z, p.y, rows]
    half_in = whole.at[:, p.c, :, :, rows]
    ax = whole.at[p.x, p.c, :, p.y, first]
    ax_in = whole.at[1 - p.x, p.c, :, p.y, first]
    by = whole.at[p.x, p.c, :, p.y, later]
    by_in = whole.at[p.x, p.c, :, 1 - p.y, later]
    ay = whole.at[:, p.c, :, p.y, first]
    ay_in = whole.at[:, p.c, :, 1 - p.y, first]
    bx = whole.at[p.x, p.c, :, :, later]
    bx_in = whole.at[1 - p.x, p.c, :, :, later]
    kz, ka, kb, ks = base, base + deep, base + deep + 2, base + deep + 4

    def keep():
        return pltpu.make_async_copy(own, mine, links.send.at[kz])

    def stage0():
        keep().start()
        for j in range(1, deep):
            links.copy(kz + j, own, p.to_z(j), mine).start()

    def stage1():
        keep().wait()
        for j in range(1, deep):
            links.landed(kz + j, whole.at[p.x, p.c, p.from_z(j), p.y, rows], p.to_z(j))
        links.copy(ka, ax, p.to_x()).start()
        links.copy(kb, by, p.to_y()).start()

    def stage2():
        links.landed(ka, ax_in, p.to_x())
        links.copy(ka + 1, ay, p.to_y()).start()
        links.landed(kb, by_in, p.to_y())
        links.copy(kb + 1, bx, p.to_x()).start()

    def stage3():
        links.landed(ka + 1, ay_in, p.to_y())
        links.landed(kb + 1, bx_in, p.to_x())
        links.copy(ks, half_in, p.to_c()).start()

    def stage4():
        links.landed(ks, whole.at[:, 1 - p.c, :, :, rows], p.to_c())
        for j in range(1, deep):
            links.copy(kz + j, own, p.to_z(j), mine).wait_send()
        links.copy(ka, ax, p.to_x()).wait_send()
        links.copy(kb, by, p.to_y()).wait_send()
        links.copy(ka + 1, ay, p.to_y()).wait_send()
        links.copy(kb + 1, bx, p.to_x()).wait_send()
        links.copy(ks, half_in, p.to_c()).wait_send()

    return [stage0, stage1, stage2, stage3, stage4]


def gather_stages_late(place, links, base, own, whole, start=0, count=None):
    p, deep = place, place.deep
    count = own.shape[0] if count is None else count
    half = count // 2
    rows, first, later = pl.ds(start, count), pl.ds(start, half), pl.ds(start + half, half)
    mine = whole.at[p.x, p.c, p.z, p.y]
    pair_f, pair_l = whole.at[:, p.c, p.z, p.y, first], whole.at[p.x, p.c, p.z, :, later]
    line_f, line_l = whole.at[:, p.c, :, p.y, first], whole.at[p.x, p.c, :, :, later]
    line_f_in = whole.at[:, p.c, :, 1 - p.y, first]
    line_l_in = whole.at[1 - p.x, p.c, :, :, later]
    kf, kl = base + 8, base + 8 + deep

    def keep():
        return pltpu.make_async_copy(own.at[rows], mine.at[rows], links.send.at[base])

    def to_x():
        return links.copy(base + 1, own.at[first], p.to_x(), mine.at[first])

    def to_y():
        return links.copy(base + 2, own.at[later], p.to_y(), mine.at[later])

    def stage0():
        keep().start()
        to_x().start()
        to_y().start()

    def stage1():
        keep().wait()
        links.landed(base + 1, whole.at[1 - p.x, p.c, p.z, p.y, first], p.to_x())
        links.landed(base + 2, whole.at[p.x, p.c, p.z, 1 - p.y, later], p.to_y())
        for j in range(1, deep):
            links.copy(kf + j, pair_f, p.to_z(j)).start()
            links.copy(kl + j, pair_l, p.to_z(j)).start()

    def stage2():
        for j in range(1, deep):
            z = p.from_z(j)
            links.landed(kf + j, whole.at[:, p.c, z, p.y, first], p.to_z(j))
            links.landed(kl + j, whole.at[p.x, p.c, z, :, later], p.to_z(j))
        links.copy(base + 3, line_f, p.to_y()).start()
        links.copy(base + 4, line_l, p.to_x()).start()
        links.copy(base + 5, line_f, p.to_c()).start()
        links.copy(base + 6, line_l, p.to_c()).start()

    def stage3():
        links.landed(base + 3, line_f_in, p.to_y())
        links.copy(base + 7, line_f_in, p.to_c()).start()
        links.landed(base + 4, line_l_in, p.to_x())
        links.copy(base + 8, line_l_in, p.to_c()).start()

    def stage4():
        o = 1 - p.c
        links.landed(base + 5, whole.at[:, o, :, p.y, first], p.to_c())
        links.landed(base + 6, whole.at[p.x, o, :, :, later], p.to_c())
        links.landed(base + 7, whole.at[:, o, :, 1 - p.y, first], p.to_c())
        links.landed(base + 8, whole.at[1 - p.x, o, :, :, later], p.to_c())
        to_x().wait_send()
        to_y().wait_send()
        for j in range(1, deep):
            links.copy(kf + j, pair_f, p.to_z(j)).wait_send()
            links.copy(kl + j, pair_l, p.to_z(j)).wait_send()
        links.copy(base + 3, line_f, p.to_y()).wait_send()
        links.copy(base + 4, line_l, p.to_x()).wait_send()
        links.copy(base + 5, line_f, p.to_c()).wait_send()
        links.copy(base + 6, line_l, p.to_c()).wait_send()
        links.copy(base + 7, line_f_in, p.to_c()).wait_send()
        links.copy(base + 8, line_l_in, p.to_c()).wait_send()

    return [stage0, stage1, stage2, stage3, stage4]


GATHER_COPIES = 9


def add_into(out, one, two):
    out[...] = one[...] + two[...]


def scatter_core(place, links, base, acc, in_c):
    def move(part):
        return links.copy(base + part, acc.at[2 + part], place.to_c(), in_c.at[part])

    def send(part):
        return lambda: move(part).start()

    def add(part, x):
        def run():
            move(part).wait_send()
            links.landed(base + part, in_c.at[part], place.to_c())

            def one(z, _):
                for y in range(2):
                    there = acc.at[x, z, y]
                    add_into(there, there, in_c.at[part, z, y])
                return 0

            lax.fori_loop(0, place.deep, one, 0)

        return run

    return send, add


def add_line(place, acc, x, y, rows, arrived):
    def add(z, _):
        there = acc.at[x, z, y, rows]
        add_into(there, there, arrived.at[z])
        return 0

    lax.fori_loop(0, place.deep, add, 0)


def scatter_plane(place, links, base, acc, ay_in, ax_in, bx_in, by_in):
    p = place
    half = acc.shape[3] // 2
    first, later, both = pl.ds(0, half), pl.ds(half, half), pl.ds(0, 2)

    def ay():
        return links.copy(base, acc.at[both, :, 1 - p.y, first], p.to_y(), ay_in)

    def bx():
        return links.copy(base + 1, acc.at[1 - p.x, :, :, later], p.to_x(), bx_in)

    def ax():
        return links.copy(base + 2, acc.at[1 - p.x, :, p.y, first], p.to_x(), ax_in)

    def by():
        return links.copy(base + 3, acc.at[p.x, :, 1 - p.y, later], p.to_y(), by_in)

    def start():
        ay().start()
        bx().start()

    def middle():
        links.landed(base, ay_in, p.to_y())
        for x in range(2):
            add_line(p, acc, x, p.y, first, ay_in.at[x])
        ax().start()
        links.landed(base + 1, bx_in, p.to_x())
        for y in range(2):
            add_line(p, acc, p.x, y, later, bx_in.at[:, y])
        by().start()

    def finish():
        links.landed(base + 2, ax_in, p.to_x())
        add_line(p, acc, p.x, p.y, first, ax_in)
        links.landed(base + 3, by_in, p.to_y())
        add_line(p, acc, p.x, p.y, later, by_in)

    def settle():
        for move in (ay, bx, ax, by):
            move().wait_send()

    return start, middle, finish, settle


def scatter_in_pairs(place, links, base, acc, in_c, ay_in, ax_in, bx_in, by_in, in_z, out):
    p, deep = place, place.deep
    half = acc.shape[3] // 2
    first, later = pl.ds(0, half), pl.ds(half, half)
    far, near = 1 - p.x, p.x
    kf, kl = base + 6, base + 6 + deep
    send, add = scatter_core(place, links, base, acc, in_c)

    def over_y(part, x):
        return links.copy(base + 2 + part, acc.at[x, :, 1 - p.y, first], p.to_y(), ay_in.at[part])

    def far_later():
        return links.copy(base + 4, acc.at[far, :, :, later], p.to_x(), bx_in)

    def far_first():
        return links.copy(base + 5, acc.at[far, :, p.y, first], p.to_x(), ax_in)

    def near_later():
        return links.copy(base + 6, acc.at[near, :, 1 - p.y, later], p.to_y(), by_in)

    def over_z(k, j, rows):
        to = lax.rem(p.z + j, deep)
        return links.copy(k + j, acc.at[near, to, p.y, rows], p.to_z(j), in_z.at[j, rows])

    def far1():
        add(0, far)()
        over_y(0, far).start()
        far_later().start()

    def far2():
        links.landed(base + 2, ay_in.at[0], p.to_y())
        add_line(p, acc, far, p.y, first, ay_in.at[0])
        far_first().start()

    def near1():
        over_y(1, near).start()

    def near_x():
        links.landed(base + 4, bx_in, p.to_x())
        for y in range(2):
            add_line(p, acc, near, y, later, bx_in.at[:, y])
        near_later().start()

    def near2():
        links.landed(base + 3, ay_in.at[1], p.to_y())
        add_line(p, acc, near, p.y, first, ay_in.at[1])
        links.landed(base + 5, ax_in, p.to_x())
        add_line(p, acc, near, p.y, first, ax_in)
        for j in range(1, deep):
            over_z(kf, j, first).start()

    def near3():
        links.landed(base + 6, by_in, p.to_y())
        add_line(p, acc, near, p.y, later, by_in)
        for j in range(1, deep):
            over_z(kl, j, later).start()

    def near4():
        for k, rows in ((kf, first), (kl, later)):
            total = acc[near, p.z, p.y, rows].astype(F32)
            for j in range(1, deep):
                links.landed(k + j, in_z.at[j, rows], p.to_z(j))
                total = total + in_z[j, rows].astype(F32)
            out[rows] = total
            for j in range(1, deep):
                over_z(k, j, rows).wait_send()
        over_y(0, far).wait_send()
        over_y(1, near).wait_send()
        far_later().wait_send()
        far_first().wait_send()
        near_later().wait_send()

    return [send(0), far1, far2, send(1), add(1, near), near1, near_x, near2, near3, near4]


def scatter_tail(place, links, base, part, in_z, out):
    deep = place.deep

    def send(j):
        return links.copy(
            base + j, part.at[lax.rem(place.z + j, deep)], place.to_z(j), in_z.at[j]
        )

    def stage0():
        for j in range(1, deep):
            send(j).start()

    def stage1():
        for j in range(1, deep):
            links.landed(base + j, in_z.at[j], place.to_z(j))
        total = part[place.z].astype(F32)
        for j in range(1, deep):
            total = total + in_z[j].astype(F32)
        out[...] = total
        for j in range(1, deep):
            send(j).wait_send()

    return [stage0, stage1]


def core_buffers(deep, rows, lanes):
    return [
        pltpu.VMEM((4, deep, 2, rows, lanes), BF16),
        pltpu.VMEM((2, deep, 2, rows, lanes), BF16),
    ]


def plane_buffers(deep, rows, lanes):
    half = rows // 2
    return [
        pltpu.VMEM((2, deep, half, lanes), BF16),
        pltpu.VMEM((deep, half, lanes), BF16),
        pltpu.VMEM((deep, 2, half, lanes), BF16),
        pltpu.VMEM((deep, half, lanes), BF16),
    ]


def gather_blocks(block, sizes):
    whole = lax.all_gather(block, ("dp", "tensor"), axis=0, tiled=False)
    whole = whole.reshape(sizes + block.shape)
    return jnp.swapaxes(whole, 0, 1).reshape((sizes[1], -1) + block.shape[1:])


def scatter_blocks(grads, sizes):
    parts = grads.reshape((sizes[1], sizes[0], -1) + grads.shape[2:])
    parts = jnp.swapaxes(parts, 0, 1).reshape((sizes[0] * sizes[1],) + parts.shape[2:])
    return lax.psum_scatter(parts, ("dp", "tensor"), scatter_dimension=0, tiled=False)


def adam_parts(grad, mean, square):
    new_mean = MOMENT_DECAY * mean + (1.0 - MOMENT_DECAY) * grad
    new_square = MOMENT_DECAY * square + (1.0 - MOMENT_DECAY) * grad * grad
    correction = 1.0 - MOMENT_DECAY**STEP
    direction = new_mean / correction / (jnp.sqrt(new_square / correction) + ADAM_EPS)
    return new_mean, new_square, direction


def sum_all(values):
    return jnp.sum(jnp.sum(values, axis=1, keepdims=True), axis=0, keepdims=True)


def group_squares(qkv_part, out_part, inner_part, outer_part, vector_part):
    return jnp.concatenate(
        [
            jnp.sum(qkv_part * qkv_part, axis=(1, 2)),
            jnp.sum(out_part * out_part)[None],
            jnp.sum(inner_part * inner_part)[None],
            jnp.sum(outer_part * outer_part)[None],
            jnp.sum(vector_part[:8] * vector_part[:8], axis=1),
            jnp.sum(vector_part[8:] * vector_part[8:])[None],
        ]
    )


def lamb_apply(weight_list, update_list, trust_ratio, row_number):
    qkv_new = weight_list[0] - LEARN_RATE * trust_ratio[0:3, None, None] * update_list[0]
    out_new = weight_list[1] - LEARN_RATE * trust_ratio[3] * update_list[1]
    inner_new = weight_list[2] - LEARN_RATE * trust_ratio[4] * update_list[2]
    outer_new = weight_list[3] - LEARN_RATE * trust_ratio[5] * update_list[3]
    row_ratio = jnp.concatenate(
        [trust_ratio[6:14], jnp.broadcast_to(trust_ratio[14], (row_number - 8,))]
    )
    vector_new = weight_list[4] - LEARN_RATE * row_ratio[:, None] * update_list[4]
    return (qkv_new, out_new, inner_new, outer_new, vector_new)


def lamb_plain(sum_a, sum_b, sum_c, vector_sum, weights, old_means, old_squares):
    qkv_sum = jnp.stack([collect(sum_a, at) for at in (Q_AT, K_AT, V_AT)])
    grad_sums = (qkv_sum, collect(sum_a, O_AT).T, sum_b, sum_c.T, vector_sum)
    decays = (WEIGHT_DECAY, WEIGHT_DECAY, WEIGHT_DECAY, WEIGHT_DECAY, 0.0)
    stats = [adam_parts(*entry) for entry in zip(grad_sums, old_means, old_squares)]
    updates = [stats[i][2] + decays[i] * weights[i] for i in range(5)]
    weight_squares, update_squares = lax.psum(
        (group_squares(*weights), group_squares(*updates)), ("dp", "tensor")
    )
    weight_norms = jnp.sqrt(weight_squares)
    update_norms = jnp.sqrt(update_squares)
    trust_ratio = weight_norms / (update_norms + ADAM_EPS)
    new = lamb_apply(weights, updates, trust_ratio, weights[4].shape[0])
    outs = []
    for i in range(5):
        outs += [stats[i][0], stats[i][1], new[i]]
    return outs + [jnp.stack([weight_norms, update_norms])]


A_ROWS = ((0, 64), (64, 32))
C_ROWS = ((0, 96),)


def own_first(order):
    tensor = lax.axis_index("tensor")
    x, c = tensor // 2, tensor % 2
    return jnp.where(order % 2 == 0, x, 1 - x) * 2 + jnp.where(order < 2, c, 1 - c)


def gather_attend_kernel(
    qkv_ref, out_ref, inner_ref, outer_ref, vec_ref, x_ref, seg_ref,
    wa_hbm, wb_hbm, wc_hbm, hid_hbm, nlt_hbm, xt_hbm, n1_hbm,
    full, pm_ref, lse_ref, slope_ref, acc, inv_ref,
    send, recv, slots, pack_a, pack_b, pack_c, wa, wb, wc, hid, nlt_ref, xt_ref, n1_ref,
    bias, low, out_sem, xp, proj_acc,
    *, sizes, chunk,
):
    step = pl.program_id(0)
    groups, deep = sizes[1], sizes[0] // 2
    place = Place(sizes)
    links = Links(send, recv)
    each = GATHER_COPIES + deep
    cols = qkv_ref.shape[2]
    tokens, width = x_ref.shape
    lanes = pack_a.shape[1]
    length = tokens // 2
    tail = 256
    ga = [
        gather_stages(place, links, n * each, pack_a, wa, *rows) for n, rows in enumerate(A_ROWS)
    ]
    gb = gather_stages(place, links, len(A_ROWS) * each, pack_b, wb)
    more = (len(A_ROWS) + 1) * each
    small = add_everywhere(place, links, more, full, slots)
    more += deep + 2
    gc = [
        gather_stages_late(place, links, more + k * (each + deep), pack_c, wc, *rows)
        for k, rows in enumerate(C_ROWS)
    ]
    t, s = own_first(jnp.minimum(step // 2, groups - 1)), step % 2
    last = 4 * groups - 1

    def keep(k):
        pairs = (
            (wa, wa_hbm), (wb, wb_hbm), (wc, wc_hbm), (hid, hid_hbm),
            (nlt_ref, nlt_hbm), (xt_ref, xt_hbm), (n1_ref, n1_hbm),
        )
        return pltpu.make_async_copy(*pairs[k], out_sem.at[k])

    def project(piece):
        start, count = A_ROWS[piece]
        here, columns = pl.ds(start, count), pl.ds(start * sizes[0], count * sizes[0])
        for x in range(2):
            weight = wa[x, place.c, :, :, here].reshape(sizes[0] * count, lanes)
            part = dot(xp[:, columns], weight)
            proj_acc[x] = part if piece == 0 else proj_acc[x] + part

    @pl.when(step == 0)
    def _():
        out_rows = out_ref[...].T
        pack_a[...] = spread(qkv_ref[0], qkv_ref[1], qkv_ref[2], out_rows).astype(BF16)
        place.greet()
        for piece in ga:
            piece[0]()
        pack_c[...] = outer_ref[...].astype(BF16)
        gc[0][0]()
        pack_b[...] = inner_ref[...].astype(BF16)
        xt_ref[...] = x_ref[...].T
        block = pack_a.shape[0]
        for start, count in A_ROWS:
            picked = [xt_ref[dp * block + start : dp * block + start + count] for dp in range(sizes[0])]
            xp[:, start * sizes[0] : (start + count) * sizes[0]] = jnp.concatenate(picked, axis=0).T
        full[...] = jnp.zeros_like(full)
        mine = vec_ref.shape[1]
        full[0 : vec_ref.shape[0], 0:mine] = vec_ref[...]
        index = lax.axis_index("dp") * groups + lax.axis_index("tensor")
        full[...] = pltpu.roll(full[...], index * mine, 1)
        small[0]()
        small[1]()
        ga[0][1]()
        small[2]()
        ga[1][1]()
        ga[0][2]()
        small[3]()
        gb[0]()
        ga[1][2]()
        ga[0][3]()
        project(0)
        small[4]()
        for g in range(groups):
            bias[g] = jnp.zeros(bias.shape[1:], F32)
            for h in range(HEADS):
                mine = slice(g * cols + h * HD, g * cols + (h + 1) * HD)
                bias[g, 0:1, Q_AT[h] : Q_AT[h] + HD] = full[6:7, mine]
                bias[g, 0:1, V_AT[h] : V_AT[h] + HD] = full[7:8, mine]
        n1_ref[...] = x_ref[...].astype(F32) + full[4:5, :]
        ga[1][3]()
        project(1)

    @pl.when(step == groups)
    def _():
        gb[2]()
        for piece in ga:
            piece[4]()
        keep(0).start()

    @pl.when(step == 1)
    def _():
        gb[1]()
        gc[0][1]()

    @pl.when(step == 2 * groups + 2)
    def _():
        gb[4]()
        keep(1).start()

    @pl.when(step == 3 * groups)
    def _():
        gc[0][3]()
        keep(3).start()

    @pl.when(step == 3 * groups + 2)
    def _():
        gc[0][4]()
        keep(2).start()

    @pl.when((step < groups) & (s == 0))
    def _():
        pm_ref[0] = (proj_acc[t // 2] + bias[t, 0:1]).astype(BF16)

    @pl.when((step >= groups) & (step < 2 * groups) & (s == 0))
    def _():
        weight = wa[t // 2, t % 2].reshape(width, lanes)
        for n in range(lanes // 256):
            here = slice(n * 256, (n + 1) * 256)
            proj = dot(x_ref[...], weight[:, here]) + bias[t, 0:1, here]
            pm_ref[0, :, here] = proj.astype(BF16)

    @pl.when(step < 2 * groups)
    def _():
        rows = pl.ds(pl.multiple_of(s * length, length), length)
        row = seg_ref[pl.ds(lax.axis_index("tensor") * 2 + s, 1)]
        attend_heads(pm_ref.at[0, rows], row, lse_ref, chunk)

    @pl.when((step < 2 * groups) & (s == 1))
    def _():
        mixed = mixed_only(pm_ref[0, :, lanes - tail :])
        weight = wa[t // 2, t % 2, :, :, :, lanes - tail :].reshape(width, tail)
        n1_ref[...] += dot(mixed, weight, NT)

    @pl.when(step == 2 * groups)
    def _():
        for r in range(tokens // 256):
            rows = slice(r * 256, (r + 1) * 256)
            normal_one, inverse_one = norm_parts(n1_ref[rows])
            n1_ref[rows] = normal_one
            inv_ref[rows] = inverse_one
            normed = normal_one * full[0:1, :] + full[1:2, :]
            acc[rows] = normed + full[5:6, :]
            part = normed.astype(BF16)
            low[rows] = part
            nlt_ref[:, rows] = part.T
        for k in range(4, 7):
            keep(k).start()
        gc[0][2]()
        gb[3]()

    @pl.when((step >= 2 * groups) & (step < 3 * groups))
    def _():
        g = own_first(step - 2 * groups)
        weight = wb[g // 2, g % 2].reshape(width, lanes)
        for n in range(lanes // 256):
            here = slice(n * 256, (n + 1) * 256)
            pre = dot(low[...], weight[:, here]) + full[pl.ds(8 + g, 1), here]
            act, turn = gelu_parts(pre)
            hid[g, :, here] = act.astype(BF16)
            slope_ref[0, :, here] = turn.astype(BF16)

    @pl.when(step >= 3 * groups)
    def _():
        g = own_first(step - 3 * groups)
        weight = wc[g // 2, g % 2].reshape(width, lanes)
        acc[...] += dot(hid[g], weight, NT)

    @pl.when(step == last)
    def _():
        for k in range(7):
            keep(k).wait()


def once(shape):
    return pl.BlockSpec(shape, lambda *_: (0,) * len(shape), pipeline_mode=pl.Buffered(1))


def gather_attend(weights, x, seg, sizes):
    qkv, out, inner, outer, vec = weights
    deep, groups = sizes[0] // 2, sizes[1]
    copies = (len(A_ROWS) + 1) * (GATHER_COPIES + deep) + deep + 2
    copies += len(C_ROWS) * (GATHER_COPIES + 2 * deep)
    tokens, width = x.shape
    length = seg.shape[1]
    seqs = tokens // length
    rows, lanes = inner.shape
    steps = groups * seqs
    anywhere = pl.BlockSpec(memory_space=pl.ANY)
    parts = (2, 2, deep, 2, rows, lanes)
    whole = jax.ShapeDtypeStruct(parts, BF16)

    def now(i):
        i = jnp.minimum(i, steps - 1)
        return own_first(i // 2), i % 2

    def part(i):
        return own_first(jnp.clip(i - steps, 0, groups - 1))

    wa, wb, wc, hid, nlt, xt, n1, *rest = pl.pallas_call(
        functools.partial(gather_attend_kernel, sizes=sizes, chunk=min(256, length)),
        grid=(steps + 2 * groups,),
        in_specs=[once(w.shape) for w in weights]
        + [
            once(x.shape),
            once(seg.shape),
        ],
        out_specs=[anywhere] * 7
        + [
            once((16, width)),
            pl.BlockSpec((1, tokens, lanes), lambda i: (now(i)[0], 0, 0)),
            pl.BlockSpec((1, 1, 8, length), lambda i: (*now(i), 0, 0)),
            pl.BlockSpec((1, tokens, lanes), lambda i: (part(i), 0, 0)),
            once((tokens, width)),
            once((tokens, 1)),
        ],
        out_shape=[whole] * 3
        + [
            jax.ShapeDtypeStruct((groups, tokens, lanes), BF16),
            jax.ShapeDtypeStruct((width, tokens), BF16),
            jax.ShapeDtypeStruct((width, tokens), BF16),
            jax.ShapeDtypeStruct((tokens, width), F32),
            jax.ShapeDtypeStruct((16, width), F32),
            jax.ShapeDtypeStruct((groups, tokens, lanes), BF16),
            jax.ShapeDtypeStruct((groups, seqs, 8, length), F32),
            jax.ShapeDtypeStruct((groups, tokens, lanes), BF16),
            jax.ShapeDtypeStruct((tokens, width), F32),
            jax.ShapeDtypeStruct((tokens, 1), F32),
        ],
        scratch_shapes=[
            pltpu.SemaphoreType.DMA((copies,)),
            pltpu.SemaphoreType.DMA((copies,)),
            pltpu.VMEM((deep + 2, 16, width), F32),
            pltpu.VMEM((rows, lanes), BF16),
            pltpu.VMEM((rows, lanes), BF16),
            pltpu.VMEM((rows, lanes), BF16),
            pltpu.VMEM(parts, BF16),
            pltpu.VMEM(parts, BF16),
            pltpu.VMEM(parts, BF16),
            pltpu.VMEM((groups, tokens, lanes), BF16),
            pltpu.VMEM((width, tokens), BF16),
            pltpu.VMEM((width, tokens), BF16),
            pltpu.VMEM((tokens, width), F32),
            pltpu.VMEM((groups, 8, lanes), F32),
            pltpu.VMEM((tokens, width), BF16),
            pltpu.SemaphoreType.DMA((7,)),
            pltpu.VMEM((tokens, width), BF16),
            pltpu.VMEM((2, tokens, lanes), F32),
        ],
        compiler_params=params(collective_id=0, has_side_effects=True),
        name="gather_attend",
    )(*weights, x, seg)
    shape = (groups, sizes[0] * rows, lanes)
    return [wa.reshape(shape), wb.reshape(shape), wc.reshape(shape), hid, nlt, xt, n1] + rest


def other_first(order):
    c = lax.axis_index("tensor") % 2
    return order % 2 * 2 + jnp.where(order < 2, 1 - c, c)


def layer_kernel(
    cot_ref, hid_ref, slope_ref, inv_ref, vec_ref, second_hbm, n1_hbm, nlt_hbm, wa_hbm, wb_hbm,
    wc_hbm,
    out_hbm, gb_hbm, gm_hbm, gbt_hbm, accb_hbm, part_ref, vg_ref, bg_ref,
    n1_ref, nlt_ref, wo_ref, wb_ref, wc_ref, acc, low, gst, gi, out_ref, gm_ref, gbt_ref,
    in_sem, out_sem, send, recv, accc, in_cc, accb, in_cb, ay_in, ax_in, bx_in, by_in, *, sizes,
):
    step = pl.program_id(0)
    tokens, width = acc.shape
    groups, deep = sizes[1], sizes[0] // 2
    lanes = wa_hbm.shape[2]
    tail = wo_ref.shape[2]
    last = 2 * groups - 1
    place = Place(sizes)
    links = Links(send, recv)
    send_c, add_c = scatter_core(place, links, 0, accc, in_cc)
    send_b, add_b = scatter_core(place, links, 2, accb, in_cb)
    start, middle, finish, settle = scatter_plane(
        place, links, 4, accc, ay_in, ax_in, bx_in, by_in
    )
    blocks = [slice(r * 256, (r + 1) * 256) for r in range(tokens // 256)]
    columns = [slice(n * 256, (n + 1) * 256) for n in range(width // 256)]

    def outer(t):
        return pltpu.make_async_copy(wc_hbm.at[t], wc_ref.at[t], in_sem.at[t])

    def inner(t):
        return pltpu.make_async_copy(wb_hbm.at[t], wb_ref.at[t], in_sem.at[groups + t])

    def load(k):
        pairs = (
            (second_hbm, acc), (n1_hbm, n1_ref), (nlt_hbm, nlt_ref),
            (wa_hbm.at[:, :, pl.ds(lanes - tail, tail)], wo_ref),
        )
        return pltpu.make_async_copy(*pairs[k], in_sem.at[2 * groups + k])

    def store(k):
        pairs = (
            (out_ref, out_hbm), (gbt_ref, gbt_hbm), (accb.at[pl.ds(0, 2)], accb_hbm), (acc, gb_hbm)
        )
        return pltpu.make_async_copy(*pairs[k], out_sem.at[k])

    def store_mixed(t):
        return pltpu.make_async_copy(gm_ref.at[t], gm_hbm.at[t], out_sem.at[4 + t])

    @pl.when(step == 0)
    def _():
        load(0).start()
        for t in range(groups):
            outer(t).start()
            inner(t).start()
        for k in range(1, 4):
            load(k).start()
        place.greet()
        vg_ref[...] = jnp.zeros_like(vg_ref)
        bg_ref[...] = jnp.zeros_like(bg_ref)
        load(0).wait()
        for rows in blocks:
            normal_two, inverse_two = norm_parts(acc[rows])
            out_ref[rows] = (normal_two * vec_ref[2:3, :] + vec_ref[3:4, :]).astype(BF16)
            cot = cot_ref[rows].astype(F32)
            grad_second = norm_back(cot, normal_two, inverse_two, vec_ref[2:3, :])
            vg_ref[2:3, :] += jnp.sum(cot * normal_two, axis=0, keepdims=True)
            vg_ref[3:4, :] += jnp.sum(cot, axis=0, keepdims=True)
            vg_ref[5:6, :] += jnp.sum(grad_second, axis=0, keepdims=True)
            acc[rows] = grad_second
            part = grad_second.astype(BF16)
            low[rows] = part
            gst[:, rows] = part.T
        store(0).start()

    @pl.when(step < groups)
    def _():
        slot = lax.rem(step + 2, 4)
        for here in columns:
            part = dot(gst[...], hid_ref[0, :, here]).astype(BF16)
            accc[slot, :, :, :, here] = part.reshape(deep, 2, -1, 256)

    @pl.when(step == 1)
    def _():
        send_c(0)()

    @pl.when(step == 2)
    def _():
        send_c(1)()

    @pl.when(step == groups)
    def _():
        add_c(0, 0)()
        add_c(1, 1)()
        start()
        for t in range(groups):
            outer(t).wait()
            inner(t).wait()
        for k in range(1, 4):
            load(k).wait()

    @pl.when(step == last)
    def _():
        middle()

    @pl.when(step >= groups)
    def _():
        order = step - groups
        slot = lax.rem(order + 2, 4)
        t = other_first(order)
        for here in columns:
            grad_hidden = dot(low[...], wc_ref[t, :, here])
            part = (grad_hidden * slope_ref[0, :, here].astype(F32)).astype(BF16)
            gi[:, here] = part
            bg_ref[pl.ds(t, 1), here] = jnp.sum(part.astype(F32), axis=0, keepdims=True)
        acc[...] += dot(gi[...], wb_ref[t], NT)
        for here in columns:
            part = dot(nlt_ref[...], gi[:, here]).astype(BF16)
            accb[slot, :, :, :, here] = part.reshape(deep, 2, -1, 256)

    @pl.when(step == groups + 1)
    def _():
        send_b(0)()

    @pl.when(step == groups + 2)
    def _():
        send_b(1)()

    @pl.when(step == last)
    def _():
        for rows in blocks:
            grad_normed = acc[rows]
            normal_one = n1_ref[rows]
            grad_branch = norm_back(grad_normed, normal_one, inv_ref[rows], vec_ref[0:1, :])
            vg_ref[0:1, :] += jnp.sum(grad_normed * normal_one, axis=0, keepdims=True)
            vg_ref[1:2, :] += jnp.sum(grad_normed, axis=0, keepdims=True)
            vg_ref[4:5, :] += jnp.sum(grad_branch, axis=0, keepdims=True)
            acc[rows] = grad_branch
            part = grad_branch.astype(BF16)
            low[rows] = part
            gbt_ref[:, rows] = part.T
        store(3).start()
        store(1).start()
        for t in range(groups):
            gm_ref[t] = dot(low[...], wo_ref[t]).astype(BF16)
            store_mixed(t).start()
        add_b(0, 0)()
        add_b(1, 1)()
        store(2).start()
        finish()
        part_ref[...] = accc[place.x, :, place.y]
        settle()
        for k in range(4):
            store(k).wait()
        for t in range(groups):
            store_mixed(t).wait()


def layer(cot, hid, slope, second, n1, inv1, nlt, wa, wb, wc, vec, sizes):
    tokens, width = cot.shape
    groups, _, lanes = wa.shape
    hidden = wb.shape[2]
    deep = sizes[0] // 2
    rows = width // sizes[0]
    tail = 256
    anywhere = pl.BlockSpec(memory_space=pl.ANY)

    def used(i):
        return other_first(jnp.minimum(i, groups - 1))

    def back_group(i):
        return other_first(jnp.clip(i - groups, 0, groups - 1))

    copies = 8
    parts = (2, deep, 2, rows, hidden)
    matrix = pltpu.VMEM((groups, width, hidden), BF16)
    return pl.pallas_call(
        functools.partial(layer_kernel, sizes=sizes),
        grid=(2 * groups,),
        in_specs=[
            once(cot.shape),
            pl.BlockSpec((1, tokens, hidden), lambda i: (used(i), 0, 0)),
            pl.BlockSpec((1, tokens, hidden), lambda i: (back_group(i), 0, 0)),
            once(inv1.shape),
            once(vec.shape),
        ]
        + [anywhere] * 6,
        out_specs=[anywhere] * 5
        + [once((deep, rows, hidden)), once((8, width)), once((8, hidden))],
        out_shape=[
            jax.ShapeDtypeStruct((tokens, width), BF16),
            jax.ShapeDtypeStruct((tokens, width), F32),
            jax.ShapeDtypeStruct((groups, tokens, tail), BF16),
            jax.ShapeDtypeStruct((width, tokens), BF16),
            jax.ShapeDtypeStruct(parts, BF16),
            jax.ShapeDtypeStruct((deep, rows, hidden), BF16),
            jax.ShapeDtypeStruct((8, width), F32),
            jax.ShapeDtypeStruct((8, hidden), F32),
        ],
        scratch_shapes=[
            pltpu.VMEM(n1.shape, F32),
            pltpu.VMEM((width, tokens), BF16),
            pltpu.VMEM((groups, width, tail), BF16),
            matrix,
            matrix,
            pltpu.VMEM((tokens, width), F32),
            pltpu.VMEM((tokens, width), BF16),
            pltpu.VMEM((width, tokens), BF16),
            pltpu.VMEM((tokens, hidden), BF16),
            pltpu.VMEM((tokens, width), BF16),
            pltpu.VMEM((groups, tokens, tail), BF16),
            pltpu.VMEM((width, tokens), BF16),
            pltpu.SemaphoreType.DMA((2 * groups + 4,)),
            pltpu.SemaphoreType.DMA((4 + groups,)),
            pltpu.SemaphoreType.DMA((copies,)),
            pltpu.SemaphoreType.DMA((copies,)),
        ]
        + core_buffers(deep, rows, hidden) * 2
        + plane_buffers(deep, rows, hidden),
        compiler_params=params(collective_id=1, has_side_effects=True),
        name="layer",
    )(cot, hid, slope, inv1, vec, second, n1, nlt, wa, wb, wc)


def far_first(step, groups):
    tensor = lax.axis_index("tensor")
    x, c = tensor // 2, tensor % 2
    return jnp.where(step < groups, 1 - x, x) * 2 + jnp.where(step % groups < 2, 1 - c, c)


def changes_of(refs):
    qkv, out, hidden, vec = refs
    return [
        [qkv.at[k], out.at[k], hidden.at[k, 0], hidden.at[k, 1], vec.at[k]] for k in range(2)
    ]


def back_kernel(
    pm_ref, gm_ref, lse_ref, seg_ref, wa_hbm, xt_hbm, gbt_hbm, gb_hbm,
    accb_hbm, part_ref, vg_ref, bg_ref, *refs, sizes, chunk,
):
    weights, means, squares = refs[0:5], refs[5:10], refs[10:15]
    (grads, updates), norms, ig_ref = changes_of(refs[15:19]), refs[19], refs[20]
    gp, gsum, send, recv, slots, hslots, nslots, vec, hvec, load_sem, sa = refs[21:32]
    wa_ref, xt_ref, gbt_ref, gb_ref, accb, inz_b, inz_c = refs[32:39]
    bufs_b, bufs_a, acc = refs[39:43], refs[43:50], refs[43]
    sb, sc = grads[2], grads[3]
    step = pl.program_id(0)
    groups, deep = sizes[1], sizes[0] // 2
    cols = HEADS * HD
    tokens, width = gb_ref.shape
    lanes = pm_ref.shape[2]
    last = 2 * groups - 1
    length = pm_ref.shape[1]
    place = Place(sizes)
    links = Links(send, recv)
    a = scatter_in_pairs(place, links, 0, *bufs_a, sa)
    more = 7 + 2 * deep
    start, middle, finish, settle = scatter_plane(place, links, more, accb, *bufs_b)
    b = scatter_tail(place, links, more + 4, accb.at[place.x, :, place.y], inz_b, sb)
    c = scatter_tail(place, links, more + 4 + deep, part_ref, inz_c, sc)
    early = add_everywhere(place, links, more + 4 + 2 * deep, vec, slots)
    small = add_everywhere(place, links, more + 6 + 3 * deep, hvec, hslots)
    final = add_in_two(place, links, more + 8 + 4 * deep, norms, nslots)
    t, s = far_first(step, groups), step % 2

    def load(k):
        pairs = ((accb_hbm, accb), (xt_hbm, xt_ref), (gbt_hbm, gbt_ref), (wa_hbm, wa_ref), (gb_hbm, gb_ref))
        return pltpu.make_async_copy(*pairs[k], load_sem.at[k])

    @pl.when(step == 0)
    def _():
        load(0).start()
        place.greet(everyone=True)
        c[0]()
        load(0).wait()
        start()
        for k in range(1, 5):
            load(k).start()
        gsum[...] = jnp.zeros_like(gsum)
        vec[...] = jnp.zeros_like(vec)
        hvec[...] = jnp.zeros_like(hvec)
        vec[0:6] = vg_ref[0:6]
        vec[8 : 8 + groups] = bg_ref[0:groups]
        early[0]()

    @pl.when(step == 1)
    def _():
        load(1).wait()
        load(2).wait()

    @pl.when(step == 2)
    def _():
        a[0]()
        early[1]()

    @pl.when(step == 4)
    def _():
        early[2]()
        middle()
        a[1]()

    @pl.when(step == 5)
    def _():
        c[1]()

    @pl.when(step == 6)
    def _():
        a[3]()
        early[3]()

    @pl.when(step == 7)
    def _():
        finish()
        b[0]()

    rows = pl.ds(pl.multiple_of(s * length, length), length)
    row = seg_ref[pl.ds(lax.axis_index("tensor") * 2 + s, 1)]
    attend_back(pm_ref.at[0], gm_ref.at[0], lse_ref, row, gp.at[t, rows], chunk)

    for n in (0, 2, 3):
        here = slice(n * 128, (n + 1) * 128)
        gsum[t, 0:1, here] += jnp.sum(gp[t, rows, here].astype(F32), axis=0, keepdims=True)

    @pl.when(s == 1)
    def _():
        order = step // 2
        slot = jnp.where(order % 2 == 0, 2 + order // 2, t // 2)
        for n in range(2):
            here = slice(n * 256, (n + 1) * 256)
            part = dot(xt_ref[...], gp[t, :, here]).astype(BF16)
            acc[slot, :, :, :, here] = part.reshape(deep, 2, -1, 256)
        from_x = dot(xt_ref[...], gp[t, :, 512:768])
        part = dot(gbt_ref[...], gp[t, :, 512:768])
        lane = lax.broadcasted_iota(jnp.int32, part.shape, 1)
        part = jnp.where((lane >= 128) & (lane < 192), from_x, part).astype(BF16)
        acc[slot, :, :, :, 512:768] = part.reshape(deep, 2, -1, 256)

    def input_columns(n):
        here = slice(n * 256, (n + 1) * 256)
        total = gb_ref[:, here]
        for g in range(groups):
            part = gp[g, :, 640:768]
            part = halves(part, jnp.zeros_like(part))
            total = total + dot(gp[g, :, 0:512], wa_ref[g, here, 0:512], NT)
            total = total + dot(part, wa_ref[g, here, 640:768], NT)
        ig_ref[:, here] = total.astype(BF16)

    @pl.when(step == last)
    def _():
        for g in range(groups):
            for h in range(HEADS):
                at = g * cols + h * HD
                line, lane = at // 256, slice(at % 256, at % 256 + HD)
                hvec[line : line + 1, lane] = gsum[g, 0:1, Q_AT[h] : Q_AT[h] + HD]
                hvec[3 + line : 4 + line, lane] = gsum[g, 0:1, V_AT[h] : V_AT[h] + HD]
        small[0]()
        a[4]()
        a[5]()
        a[2]()
        load(3).wait()
        load(4).wait()
        input_columns(0)
        small[1]()
        a[6]()
        early[4]()
        input_columns(1)
        small[2]()
        a[7]()
        input_columns(2)
        a[8]()
        small[3]()
        b[1]()
        settle()
        found = group_sums([None] * 4 + [sb[...], sc[...], None], weights, means, squares, updates)
        small[4]()
        for k in range(3):
            lanes_of = slice(k * 256, (k + 1) * 256)
            vec[6:7, lanes_of] = hvec[k : k + 1]
            vec[7:8, lanes_of] = hvec[3 + k : 4 + k]
        count, mine = weights[4].shape
        index = lax.axis_index("dp") * groups + lax.axis_index("tensor")
        turned = pltpu.roll(vec[...], width - index * mine, 1)
        grads[4][...] = turned[0:count, 0:mine]
        found = found + group_sums(
            [None] * 6 + [grads[4][...]], weights, means, squares, updates
        )
        a[9]()
        total = sa[...]
        for k, at in enumerate((Q_AT, K_AT, V_AT)):
            grads[0][k] = collect(total, at)
        grads[1][...] = collect(total, O_AT).T
        parts = [grads[0][k] for k in range(3)] + [grads[1][...]]
        norms[...] = found + group_sums(parts + [None] * 3, weights, means, squares, updates)
        for run in final:
            run()


def group_sums(grads, weights, means, squares, updates):
    lane = lax.broadcasted_iota(jnp.int32, (8, 128), 1)
    line = lax.broadcasted_iota(jnp.int32, (8, 128), 0)
    found = jnp.zeros((8, 128), F32)
    for group, grad in enumerate(grads):
        if grad is None:
            continue
        i, k = (0, group) if group < 3 else (group - 2, ...)
        weight, mean, square = (ref[i][k] for ref in (weights, means, squares))
        update = adam_parts(grad, mean, square)[2]
        if i < 4:
            update = update + WEIGHT_DECAY * weight
        updates[i][k] = update
        if i < 4:
            pair = (sum_all(weight * weight), sum_all(update * update))
            for which in range(2):
                hit = (lane == group) & (line == which)
                found = found + jnp.where(hit, pair[which], 0.0)
            continue
        for which, values in enumerate((weight, update)):
            per_row = jnp.sum(values * values, axis=1, keepdims=True)
            for row in range(weight.shape[0]):
                hit = (lane == 6 + min(row, 8)) & (line == which)
                found = found + jnp.where(hit, per_row[row : row + 1], 0.0)
    return found


def back(pm, gm, lse, seg, wa, xt, gbt, gb, accb, part, vg, bg,
         weights, means, squares, sizes):
    deep, groups = sizes[0] // 2, sizes[1]
    tokens, width = gb.shape
    lanes = pm.shape[2]
    length = seg.shape[1]
    seqs = tokens // length
    rows = width // sizes[0]
    copies = 7 + 2 * deep + 4 + 2 * deep + 2 * (deep + 2) + 7 + deep
    small = [weights, means, squares]
    anywhere = pl.BlockSpec(memory_space=pl.ANY)
    outs = [
        jax.ShapeDtypeStruct((2,) + weights[0].shape, F32),
        jax.ShapeDtypeStruct((2,) + weights[1].shape, F32),
        jax.ShapeDtypeStruct((2, 2) + weights[2].shape, F32),
        jax.ShapeDtypeStruct((2,) + weights[4].shape, F32),
        jax.ShapeDtypeStruct((8, 128), F32),
        jax.ShapeDtypeStruct((tokens, width), BF16),
    ]
    return pl.pallas_call(
        functools.partial(back_kernel, sizes=sizes, chunk=min(256, length)),
        grid=(groups * seqs,),
        in_specs=[
            pl.BlockSpec((1, length, lanes), lambda i: (far_first(i, groups), i % 2, 0)),
            pl.BlockSpec((1, length, gm.shape[2]), lambda i: (far_first(i, groups), i % 2, 0)),
            pl.BlockSpec((1, 1, 8, length), lambda i: (far_first(i, groups), i % 2, 0, 0)),
            once(seg.shape),
            anywhere,
            anywhere,
            anywhere,
            anywhere,
            anywhere,
            once(part.shape),
            once(vg.shape),
            once(bg.shape),
        ]
        + [once(ref.shape) for group in small for ref in group],
        out_specs=[once(ref.shape) for ref in outs],
        out_shape=outs,
        scratch_shapes=[
            pltpu.VMEM((groups, tokens, lanes), BF16),
            pltpu.VMEM((groups, 8, lanes), F32),
            pltpu.SemaphoreType.DMA((copies,)),
            pltpu.SemaphoreType.DMA((copies,)),
            pltpu.VMEM((deep + 2, 16, width), F32),
            pltpu.VMEM((deep + 2, 8, 256), F32),
            pltpu.VMEM((8 + deep, 8, 128), F32),
            pltpu.VMEM((16, width), F32),
            pltpu.VMEM((8, 256), F32),
            pltpu.SemaphoreType.DMA((5,)),
            pltpu.VMEM((rows, lanes), F32),
            pltpu.VMEM(wa.shape, BF16),
            pltpu.VMEM(xt.shape, BF16),
            pltpu.VMEM(gbt.shape, BF16),
            pltpu.VMEM(gb.shape, F32),
            pltpu.VMEM(accb.shape, BF16),
            pltpu.VMEM((deep, rows, lanes), BF16),
            pltpu.VMEM((deep, rows, lanes), BF16),
        ]
        + plane_buffers(deep, rows, lanes)
        + core_buffers(deep, rows, lanes)
        + plane_buffers(deep, rows, lanes)
        + [pltpu.VMEM((deep, rows, lanes), BF16)],
        compiler_params=params(collective_id=2, has_side_effects=True),
        name="back",
    )(
        pm, gm, lse, seg, wa, xt, gbt, gb,
        accb, part, vg, bg,
        *weights, *means, *squares,
    )


def apply_kernel(*refs):
    (grads, updates), sums = changes_of(refs[0:4]), refs[4]
    weights, means, squares = refs[5:10], refs[10:15], refs[15:20]
    passed, outs, norms = refs[20:22], refs[22:37], refs[37]
    wide, sem = refs[40], refs[41]
    stores = [pltpu.make_async_copy(passed[0], refs[38], sem.at[0])]
    stores[0].start()
    rows = wide.shape[0] // 4
    for k in range(4):
        here = pl.ds(k * rows, rows)
        wide[here] = passed[1][here].astype(F32)
        stores.append(pltpu.make_async_copy(wide.at[here], refs[39].at[here], sem.at[1 + k]))
        stores[-1].start()
    roots = jnp.sqrt(sums[...])
    norms[...] = roots[0:2, 0:15]
    ratio = LEARN_RATE * roots[0:1] / (roots[1:2] + ADAM_EPS)
    for i in range(5):
        grad = grads[i][...]
        outs[3 * i][...] = MOMENT_DECAY * means[i][...] + (1.0 - MOMENT_DECAY) * grad
        outs[3 * i + 1][...] = (
            MOMENT_DECAY * squares[i][...] + (1.0 - MOMENT_DECAY) * grad * grad
        )
        target = outs[3 * i + 2]
        if i == 0:
            for k in range(3):
                target[k] = weights[i][k] - ratio[:, k : k + 1] * updates[i][k]
        elif i < 4:
            target[...] = weights[i][...] - ratio[:, 2 + i : 3 + i] * updates[i][...]
        else:
            for row in range(target.shape[0]):
                here = slice(row, row + 1)
                step = ratio[:, 6 + min(row, 8) : 7 + min(row, 8)]
                target[here] = weights[i][here] - step * updates[i][here]
    for move in stores:
        move.wait()


def apply(changes, sums, weights, means, squares, passed):
    inside = pl.BlockSpec(memory_space=pltpu.VMEM)
    shapes = []
    for weight in weights:
        shapes += [jax.ShapeDtypeStruct(weight.shape, F32)] * 3
    shapes.append(jax.ShapeDtypeStruct((2, 15), F32))
    shapes += [jax.ShapeDtypeStruct(passed[0].shape, BF16)]
    shapes += [jax.ShapeDtypeStruct(passed[1].shape, F32)]
    anywhere = [pl.BlockSpec(memory_space=pl.ANY)] * 2
    return pl.pallas_call(
        apply_kernel,
        in_specs=[inside] * 22,
        out_specs=[inside] * 16 + anywhere,
        out_shape=shapes,
        scratch_shapes=[
            pltpu.VMEM(passed[1].shape, F32),
            pltpu.SemaphoreType.DMA((5,)),
        ],
        compiler_params=params(),
        name="apply",
    )(*changes, sums, *weights, *means, *squares, *passed)


def make_body(sizes):
    def body(
        tokens, cotangent, segments,
        qkv_weight, out_weight, inner_weight, outer_weight, vectors,
        qkv_mean, out_mean, inner_mean, outer_mean, vector_mean,
        qkv_square, out_square, inner_square, outer_square, vector_square,
    ):
        groups = sizes[1]
        token_count, width = tokens.shape
        length = segments.shape[1]
        seqs = token_count // length
        cols = qkv_weight.shape[2]
        tensor_index = lax.axis_index("tensor")
        weights = (qkv_weight, out_weight, inner_weight, outer_weight, vectors)
        old_means = (qkv_mean, out_mean, inner_mean, outer_mean, vector_mean)
        old_squares = (qkv_square, out_square, inner_square, outer_square, vector_square)
        if sizes[0] % 2 == 0 and groups == 4 and qkv_weight.shape[1] == sum(A_ROWS[-1]):
            weights, old_means, old_squares = (
                entry[:3] + (entry[3].T, entry[4]) for entry in (weights, old_means, old_squares)
            )
            wa, wb, wc, hid, nlt, xt, n1, full, pm, lse, slope, second, inv1 = gather_attend(
                weights, tokens, segments, sizes
            )
            result, gb, gm, gbt, accb, part, vg, bg = layer(
                cotangent, hid, slope, second, n1, inv1, nlt, wa, wb, wc, full, sizes
            )
            *changes, sums, input_grad = back(
                pm, gm, lse, segments, wa, xt, gbt, gb, accb, part, vg, bg,
                weights, old_means, old_squares, sizes,
            )
            passed = (result, input_grad)
            new = list(
                apply(changes, sums, weights, old_means, old_squares, passed)
            )
            new[9:12] = [entry.T for entry in new[9:12]]
            return tuple(new[16:]) + tuple(new[:16])
        seg = lax.dynamic_slice_in_dim(segments, tensor_index * seqs, seqs, 0)
        seg = jnp.broadcast_to(seg[:, None, :], (seqs, 8, length))
        pack_a = spread(qkv_weight[0], qkv_weight[1], qkv_weight[2], out_weight.T).astype(BF16)
        pack_b = inner_weight.astype(BF16)
        pack_c = outer_weight.T.astype(BF16)
        wa, wb, wc = (gather_blocks(pack, sizes) for pack in (pack_a, pack_b, pack_c))
        full = lax.all_gather(vectors, ("dp", "tensor"), axis=1, tiled=True)
        q_bias = full[6].reshape(groups, cols)
        v_bias = full[7].reshape(groups, cols)
        none = jnp.zeros_like(q_bias)
        proj_bias = spread(q_bias, none, v_bias, none)
        proj_bias = jnp.broadcast_to(proj_bias[:, None, :], (groups, 8, 4 * cols))
        inner_bias = full[8:].reshape(groups, -1)
        pm, lse = attend_fwd(tokens, wa, proj_bias, seg, length)
        result, hid, gi, nl, gsl, gbl, gb, gm, vg, bg = ffn(
            tokens, cotangent, pm, wa, wb, wc, full, inner_bias
        )
        gp, gsum = attend_bwd(pm, gm, lse, seg)

        grad_c = jnp.einsum("td,gtf->gdf", gsl, hid, preferred_element_type=F32).astype(BF16)
        grad_b = jnp.einsum("td,gtf->gdf", nl, gi, preferred_element_type=F32).astype(BF16)
        from_tokens = jnp.einsum("td,gtc->gdc", tokens, gp, preferred_element_type=F32)
        from_branch = jnp.einsum("td,gtc->gdc", gbl, pm, preferred_element_type=F32)
        lane = lax.broadcasted_iota(jnp.int32, (1, 1, LANES), 2)
        is_mixed = (lane >= 512) & ((lane < 640) | (lane >= 704))
        grad_a = jnp.where(is_mixed, from_branch, from_tokens).astype(BF16)
        input_grad = gb + jnp.einsum(
            "gtc,gdc->td",
            jnp.where(is_mixed, jnp.zeros((), BF16), gp),
            wa,
            preferred_element_type=F32,
        )
        head_rows = jnp.stack([collect(gsum[:, 0], at).reshape(-1) for at in (Q_AT, V_AT)])
        vector_grad = jnp.concatenate([vg[:6], head_rows, bg[:groups].reshape(-1, width)], axis=0)
        sum_a, sum_b, sum_c = (
            scatter_blocks(grad, sizes).astype(F32) for grad in (grad_a, grad_b, grad_c)
        )
        vector_sum = lax.psum_scatter(
            vector_grad, ("dp", "tensor"), scatter_dimension=1, tiled=True
        )
        new = lamb_plain(sum_a, sum_b, sum_c, vector_sum, weights, old_means, old_squares)
        return (result, input_grad) + tuple(new)

    return body

def solution(mesh):
    sizes = (mesh.shape["dp"], mesh.shape["tensor"])
    rows = P(("dp", "tensor"), None)
    qkv = P(None, "dp", "tensor")
    out = P("tensor", "dp")
    inner = P("dp", "tensor")
    vec = P(None, ("dp", "tensor"))
    weights = (qkv, out, inner, out, vec)
    return jax.shard_map(
        make_body(sizes),
        mesh=mesh,
        in_specs=(rows, rows, P("dp", None)) + weights * 3,
        out_specs=(rows, rows) + (qkv,) * 3 + (out,) * 3 + (inner,) * 3 + (out,) * 3 + (vec,) * 3 + (P(),),
        check_vma=False,
    )
```

```python
import functools

import jax
import jax.numpy as jnp
from jax import lax
from jax.experimental import pallas as pl
from jax.experimental.pallas import tpu as pltpu
from jax.sharding import PartitionSpec as P

HD = 64
STEP = 5
NORM_EPS = 1e-05
ADAM_EPS = 1e-06
MOMENT_DECAY = 0.5
LEARN_RATE = 0.5
WEIGHT_DECAY = 0.01
MASKED = -1e30
SCALE = HD ** (-0.5)
F32 = jnp.float32
BF16 = jnp.bfloat16
NT = (((1,), (1,)), ((), ()))
NN = (((1,), (0,)), ((), ()))
TN = (((0,), (0,)), ((), ()))
VMEM_LIMIT = 60 * 1024 * 1024


def dot(a, b, dims=NN):
    return lax.dot_general(a, b, dims, preferred_element_type=F32)


def params(**kw):
    return pltpu.CompilerParams(vmem_limit_bytes=VMEM_LIMIT, **kw)


HEADS = 3
DOCS = 4
LANES = 768
Q_AT, K_AT, V_AT, O_AT = (0, 64, 384), (128, 192, 640), (256, 320, 448), (512, 576, 704)
Q_TILE, K_TILE, V_TILE = (0, 0, 3), (1, 1, 5), (2, 2, 3)
UPPER = (False, True, False)
V_UPPER = (False, True, True)


def spread(q, k, v, o):
    parts = {}
    for places, values in ((Q_AT, q), (K_AT, k), (V_AT, v), (O_AT, o)):
        for h, at in enumerate(places):
            parts[at] = values[:, h * HD : (h + 1) * HD]
    return jnp.concatenate([parts[at] for at in sorted(parts)], axis=1)


def collect(values, places):
    return jnp.concatenate([values[:, at : at + HD] for at in places], axis=1)


def tile_of(ref, n, rows=slice(None)):
    return ref[rows, n * 128 : (n + 1) * 128]


def is_low(shape):
    return lax.broadcasted_iota(jnp.int32, shape, 1) < HD


def halves(low, high):
    return jnp.where(is_low(low.shape), low, high)


def document_lanes(row):
    length = row.shape[1]
    number = jnp.broadcast_to(row.astype(F32), (128, length)).T
    lane = lax.broadcasted_iota(jnp.int32, (length, 128), 1) % HD
    same = number == lane.astype(F32)
    for_query = jnp.where(same, 1.0, 0.0).astype(BF16)
    for_key = jnp.where(same, 0.0, jnp.where(lane < DOCS, MASKED, 0.0)).astype(BF16)
    return for_query, for_key


def attend_heads(pm_ref, row, lse_ref, chunk):
    length = pm_ref.shape[0]
    chunks = length // chunk
    doc_q, doc_k = document_lanes(row)
    ones = jnp.ones((16, length), BF16)
    units = [(h, c) for h in range(HEADS) for c in range(chunks)]
    keys, queries, values = {}, {}, {}
    for h in range(HEADS):
        q, k = tile_of(pm_ref, Q_TILE[h]) * SCALE, tile_of(pm_ref, K_TILE[h])
        queries[h] = halves(doc_q, q) if UPPER[h] else halves(q, doc_q)
        keys[h] = halves(doc_k, k) if UPPER[h] else halves(k, doc_k)
        vt = tile_of(pm_ref, V_TILE[h]).T
        vt = vt[HD:] if V_UPPER[h] else vt[:HD]
        values[h] = jnp.concatenate([vt, ones], axis=0)

    def scores(unit):
        h, c = unit
        return dot(keys[h], queries[h][c * chunk : (c + 1) * chunk], NT)

    outs = {h: [] for h in range(HEADS)}
    ahead = scores(units[0])
    for n, (h, c) in enumerate(units):
        s = ahead
        if n + 1 < len(units):
            ahead = scores(units[n + 1])
        m = jnp.max(s, axis=0, keepdims=True)
        p = jnp.exp(s - m).astype(BF16)
        ot = dot(values[h], p)
        total = ot[HD : HD + 1]
        outs[h].append((ot[:HD] * (1.0 / total)).astype(BF16))
        lse_ref[0, 0, h : h + 1, c * chunk : (c + 1) * chunk] = m + jnp.log(total)
    out = [jnp.concatenate(outs[h], axis=1) for h in range(HEADS)]
    pm_ref[:, 512:640] = jnp.concatenate([out[0], out[1]], axis=0).T
    last = jnp.concatenate([jnp.zeros_like(out[2]), out[2]], axis=0).T
    pm_ref[:, 640:768] = halves(tile_of(pm_ref, 5), last)


def attend_fwd_kernel(x_ref, w_ref, bias_ref, seg_ref, pm_ref, lse_ref, *, chunk):
    proj = dot(x_ref[...], w_ref[0]) + bias_ref[0, 0:1, :]
    pm_ref[0] = proj.astype(BF16)
    attend_heads(pm_ref.at[0], seg_ref[0, 0:1], lse_ref, chunk)


def attend_fwd(x, wa, bias, seg, length):
    tokens, width = x.shape
    groups, _, lanes = wa.shape
    seqs = tokens // length
    return pl.pallas_call(
        functools.partial(attend_fwd_kernel, chunk=min(256, length)),
        grid=(groups, seqs),
        in_specs=[
            pl.BlockSpec((length, width), lambda t, s: (s, 0)),
            pl.BlockSpec((1, width, lanes), lambda t, s: (t, 0, 0)),
            pl.BlockSpec((1, 8, lanes), lambda t, s: (t, 0, 0)),
            pl.BlockSpec((1, 8, length), lambda t, s: (s, 0, 0)),
        ],
        out_specs=[
            pl.BlockSpec((1, length, lanes), lambda t, s: (t, s, 0)),
            pl.BlockSpec((1, 1, 8, length), lambda t, s: (t, s, 0, 0)),
        ],
        out_shape=[
            jax.ShapeDtypeStruct((groups, tokens, lanes), BF16),
            jax.ShapeDtypeStruct((groups, seqs, 8, length), F32),
        ],
        compiler_params=params(),
        name="attend_fwd",
    )(x, wa, bias, seg)


def attend_back(pm_ref, gm_ref, lse_ref, row, gp_ref, chunk):
    length = pm_ref.shape[0]
    chunks = length // chunk
    prod = gm_ref[...].astype(F32) * pm_ref[:, 512:768].astype(F32)
    hi = prod.astype(BF16)
    lo = (prod - hi.astype(F32)).astype(BF16)
    lane = lax.broadcasted_iota(jnp.int32, (8, 256), 1)
    line = lax.broadcasted_iota(jnp.int32, (8, 256), 0)
    start = jnp.where(line == 2, O_AT[2] - 512, line * HD)
    pick = jnp.where((lane >= start) & (lane < start + HD) & (line < HEADS), 1.0, 0.0).astype(BF16)
    dsum = dot(pick, hi, NT) + dot(pick, lo, NT)
    doc_q, doc_k = document_lanes(row)
    none = jnp.zeros((length, 128), BF16)
    units = [(h, c) for h in range(HEADS) for c in range(chunks)]
    keys, queries, plain, values, kts, grads = {}, {}, {}, {}, {}, {}
    for h in range(HEADS):
        q, k = tile_of(pm_ref, Q_TILE[h]) * SCALE, tile_of(pm_ref, K_TILE[h])
        plain[h] = q
        queries[h] = halves(doc_q, q) if UPPER[h] else halves(q, doc_q)
        keys[h] = halves(doc_k, k) if UPPER[h] else halves(k, doc_k)
        kt = k.T
        kts[h] = kt[HD:] if UPPER[h] else kt[:HD]
        v = tile_of(pm_ref, V_TILE[h])
        values[h] = halves(none, v) if V_UPPER[h] else halves(v, none)
        grads[h] = tile_of(gm_ref, 0 if h < 2 else 1)

    def rows_of(c):
        return slice(c * chunk, (c + 1) * chunk)

    def products(unit):
        h, c = unit
        return dot(keys[h], queries[h][rows_of(c)], NT), dot(values[h], grads[h][rows_of(c)], NT)

    dqs = {h: [] for h in range(HEADS)}
    dks, dvs = {}, {}
    ahead = products(units[0])
    for n, (h, c) in enumerate(units):
        s, dp = ahead
        if n + 1 < len(units):
            ahead = products(units[n + 1])
        rows = rows_of(c)
        p = jnp.exp(s - lse_ref[0, 0, h : h + 1, rows])
        ds = (p * (dp - dsum[h : h + 1, rows])).astype(BF16)
        dv = dot(p.astype(BF16), grads[h][rows])
        dk = dot(ds, plain[h][rows])
        dvs[h] = dv if c == 0 else dvs[h] + dv
        dks[h] = dk if c == 0 else dks[h] + dk
        dqs[h].append((dot(kts[h], ds) * SCALE).astype(BF16))
    dq = [jnp.concatenate(dqs[h], axis=1) for h in range(HEADS)]
    gp_ref[:, 0:128] = jnp.concatenate([dq[0], dq[1]], axis=0).T
    gp_ref[:, 128:256] = halves(dks[0], dks[1]).astype(BF16)
    gp_ref[:, 256:384] = halves(dvs[0], dvs[1]).astype(BF16)
    last = jnp.concatenate([dq[2], jnp.zeros_like(dq[2])], axis=0).T
    gp_ref[:, 384:512] = halves(last, dvs[2].astype(BF16))
    gp_ref[:, 512:640] = tile_of(pm_ref, 4)
    gp_ref[:, 640:768] = halves(dks[2].astype(BF16), tile_of(pm_ref, 5))


def attend_bwd_kernel(pm_ref, gm_ref, lse_ref, seg_ref, gp_ref, gsum_ref, *, chunk):
    attend_back(pm_ref.at[0], gm_ref.at[0], lse_ref, seg_ref[0, 0:1], gp_ref.at[0], chunk)

    @pl.when(pl.program_id(1) == 0)
    def _():
        gsum_ref[...] = jnp.zeros_like(gsum_ref)

    gsum_ref[0, 0:1, :] += jnp.sum(gp_ref[0].astype(F32), axis=0, keepdims=True)


def attend_bwd(pm, gm, lse, seg):
    groups, tokens, lanes = pm.shape
    seqs, length = lse.shape[1], lse.shape[3]
    return pl.pallas_call(
        functools.partial(attend_bwd_kernel, chunk=min(256, length)),
        grid=(groups, seqs),
        in_specs=[
            pl.BlockSpec((1, length, lanes), lambda t, s: (t, s, 0)),
            pl.BlockSpec((1, length, gm.shape[2]), lambda t, s: (t, s, 0)),
            pl.BlockSpec((1, 1, 8, length), lambda t, s: (t, s, 0, 0)),
            pl.BlockSpec((1, 8, length), lambda t, s: (s, 0, 0)),
        ],
        out_specs=[
            pl.BlockSpec((1, length, lanes), lambda t, s: (t, s, 0)),
            pl.BlockSpec((1, 8, lanes), lambda t, s: (t, 0, 0)),
        ],
        out_shape=[
            jax.ShapeDtypeStruct((groups, tokens, lanes), BF16),
            jax.ShapeDtypeStruct((groups, 8, lanes), F32),
        ],
        compiler_params=params(),
        name="attend_bwd",
    )(pm, gm, lse, seg)


def mixed_only(tail):
    lane = lax.broadcasted_iota(jnp.int32, tail.shape, 1)
    return jnp.where((lane < 128) | (lane >= 192), tail, jnp.zeros((), BF16))


def gelu_parts(pre):
    cdf = 0.5 * (1.0 + lax.erf(pre * (2.0**-0.5)))
    pdf = jnp.exp(-0.5 * pre * pre) * 0.3989422804014327
    return pre * cdf, cdf + pre * pdf


def mean_of(values):
    return jnp.mean(values, axis=-1, keepdims=True)


def norm_parts(values):
    centred = values - mean_of(values)
    inverse = lax.rsqrt(mean_of(centred * centred) + NORM_EPS)
    return centred * inverse, inverse


def norm_back(incoming, normal, inverse, gain):
    scaled = incoming * gain
    return inverse * (scaled - mean_of(scaled) - normal * mean_of(scaled * normal))


def ffn_kernel(
    x_ref, cot_ref, pm_ref, wo_ref, wb_ref, wc_ref, vec_ref, bias_ref,
    out_ref, hid_ref, gi_ref, nl_ref, gsl_ref, gbl_ref, gb_ref, gm_ref, vg_ref, bg_ref,
    slope_ref,
):
    groups = wb_ref.shape[0]

    @pl.when(pl.program_id(0) == 0)
    def _():
        vg_ref[...] = jnp.zeros_like(vg_ref)
        bg_ref[...] = jnp.zeros_like(bg_ref)

    total = x_ref[...].astype(F32) + vec_ref[4:5, :]
    for t in range(groups):
        total = total + dot(mixed_only(pm_ref[t]), wo_ref[t], NT)
    normal_one, inverse_one = norm_parts(total)
    normed = normal_one * vec_ref[0:1, :] + vec_ref[1:2, :]
    low = normed.astype(BF16)
    nl_ref[...] = low
    second = normed + vec_ref[5:6, :]
    for t in range(groups):
        pre = dot(low, wb_ref[t]) + bias_ref[t : t + 1, :]
        act, slope = gelu_parts(pre)
        act = act.astype(BF16)
        hid_ref[t] = act
        slope_ref[t] = slope
        second = second + dot(act, wc_ref[t], NT)
    normal_two, inverse_two = norm_parts(second)
    out_ref[...] = (normal_two * vec_ref[2:3, :] + vec_ref[3:4, :]).astype(BF16)
    cot = cot_ref[...].astype(F32)
    grad_second = norm_back(cot, normal_two, inverse_two, vec_ref[2:3, :])
    vg_ref[2:3, :] += jnp.sum(cot * normal_two, axis=0, keepdims=True)
    vg_ref[3:4, :] += jnp.sum(cot, axis=0, keepdims=True)
    vg_ref[5:6, :] += jnp.sum(grad_second, axis=0, keepdims=True)
    gs_low = grad_second.astype(BF16)
    gsl_ref[...] = gs_low
    grad_normed = grad_second
    for t in range(groups):
        grad_inner = (dot(gs_low, wc_ref[t]) * slope_ref[t]).astype(BF16)
        gi_ref[t] = grad_inner
        bg_ref[t : t + 1, :] += jnp.sum(grad_inner.astype(F32), axis=0, keepdims=True)
        grad_normed = grad_normed + dot(grad_inner, wb_ref[t], NT)
    grad_branch = norm_back(grad_normed, normal_one, inverse_one, vec_ref[0:1, :])
    vg_ref[0:1, :] += jnp.sum(grad_normed * normal_one, axis=0, keepdims=True)
    vg_ref[1:2, :] += jnp.sum(grad_normed, axis=0, keepdims=True)
    vg_ref[4:5, :] += jnp.sum(grad_branch, axis=0, keepdims=True)
    gb_ref[...] = grad_branch
    gb_low = grad_branch.astype(BF16)
    gbl_ref[...] = gb_low
    for t in range(groups):
        gm_ref[t] = dot(gb_low, wo_ref[t]).astype(BF16)


def ffn(x, cot, pm, wa, wb, wc, vec, bias):
    tokens, width = x.shape
    groups, _, lanes = wa.shape
    hidden = wb.shape[2]
    tail = 256
    tile = 256
    last = lanes // tail - 1
    once = pl.Buffered(1)
    row = pl.BlockSpec((tile, width), lambda i: (i, 0))
    wide = pl.BlockSpec((groups, tile, hidden), lambda i: (0, i, 0))
    return pl.pallas_call(
        ffn_kernel,
        grid=(tokens // tile,),
        in_specs=[
            row,
            row,
            pl.BlockSpec((groups, tile, tail), lambda i: (0, i, last)),
            pl.BlockSpec((groups, width, tail), lambda i: (0, 0, last), pipeline_mode=once),
            pl.BlockSpec((groups, width, hidden), lambda i: (0, 0, 0), pipeline_mode=once),
            pl.BlockSpec((groups, width, hidden), lambda i: (0, 0, 0), pipeline_mode=once),
            pl.BlockSpec(vec.shape, lambda i: (0, 0)),
            pl.BlockSpec(bias.shape, lambda i: (0, 0)),
        ],
        out_specs=[
            row,
            wide,
            wide,
            row,
            row,
            row,
            row,
            pl.BlockSpec((groups, tile, tail), lambda i: (0, i, 0)),
            pl.BlockSpec((8, width), lambda i: (0, 0)),
            pl.BlockSpec((8, hidden), lambda i: (0, 0)),
        ],
        out_shape=[
            jax.ShapeDtypeStruct((tokens, width), BF16),
            jax.ShapeDtypeStruct((groups, tokens, hidden), BF16),
            jax.ShapeDtypeStruct((groups, tokens, hidden), BF16),
            jax.ShapeDtypeStruct((tokens, width), BF16),
            jax.ShapeDtypeStruct((tokens, width), BF16),
            jax.ShapeDtypeStruct((tokens, width), BF16),
            jax.ShapeDtypeStruct((tokens, width), F32),
            jax.ShapeDtypeStruct((groups, tokens, tail), BF16),
            jax.ShapeDtypeStruct((8, width), F32),
            jax.ShapeDtypeStruct((8, hidden), F32),
        ],
        scratch_shapes=[pltpu.VMEM((groups, tile, hidden), F32)],
        compiler_params=params(),
        name="ffn",
    )(x, cot, pm, wa, wb, wc, vec, bias)


MESH = pl.DeviceIdType.MESH


class Place:
    def __init__(self, sizes):
        dp, tensor = lax.axis_index("dp"), lax.axis_index("tensor")
        self.deep = sizes[0] // 2
        self.z, self.y = dp // 2, dp % 2
        self.x, self.c = tensor // 2, tensor % 2

    def to_z(self, step):
        return {"dp": lax.rem(self.z + step, self.deep) * 2 + self.y}

    def to_y(self):
        return {"dp": self.z * 2 + 1 - self.y}

    def to_x(self):
        return {"tensor": (1 - self.x) * 2 + self.c}

    def to_c(self):
        return {"tensor": self.x * 2 + 1 - self.c}

    def far_z(self):
        if self.deep != 4:
            return list(range(1, self.deep))
        z = self.z
        return [
            jnp.where(z == 0, 3, jnp.where(z == 3, 1, 2)),
            jnp.where(z == 1, 3, jnp.where(z == 2, 1, 2)),
            jnp.where(z < 2, 1, 3),
        ]

    def from_z(self, step):
        return lax.rem(self.z + self.deep - step, self.deep)

    def partners(self):
        return [self.to_z(j) for j in range(1, self.deep)] + [self.to_y(), self.to_x(), self.to_c()]

    def peers(self):
        found = []
        for r in range(1, 8):
            x = 1 - self.x if r & 4 else self.x
            y = 1 - self.y if r & 2 else self.y
            c = 1 - self.c if r & 1 else self.c
            found.append((x * 4 + y * 2 + c, {"dp": self.z * 2 + y, "tensor": x * 2 + c}))
        return found

    def greet(self, everyone=False):
        barrier = pltpu.get_barrier_semaphore()
        partners = self.partners()
        if everyone:
            partners = partners[: self.deep - 1] + [device for _, device in self.peers()]
        for partner in partners:
            pl.semaphore_signal(barrier, inc=1, device_id=partner, device_id_type=MESH)
        pl.semaphore_wait(barrier, len(partners))


class Links:
    def __init__(self, send, recv):
        self.send, self.recv = send, recv

    def copy(self, k, ref, to, dst=None):
        return pltpu.make_async_remote_copy(
            src_ref=ref,
            dst_ref=ref if dst is None else dst,
            send_sem=self.send.at[k],
            recv_sem=self.recv.at[k],
            device_id=to,
            device_id_type=MESH,
        )

    def landed(self, k, ref, to):
        self.copy(k, ref, to).wait_recv()


def add_everywhere(place, links, base, own, slots):
    deep = place.deep
    hops = [place.to_c(), place.to_y(), place.to_x()]

    def start(i):
        def run():
            if i:
                links.copy(base + i - 1, own, hops[i - 1], slots.at[i - 1]).wait_send()
                links.landed(base + i - 1, slots.at[i - 1], hops[i - 1])
                own[...] = own[...] + slots[i - 1]
            if i < 3:
                links.copy(base + i, own, hops[i], slots.at[i]).start()
            else:
                for j in range(1, deep):
                    links.copy(base + 2 + j, own, place.to_z(j), slots.at[2 + j]).start()

        return run

    def last():
        for j in range(1, deep):
            links.copy(base + 2 + j, own, place.to_z(j), slots.at[2 + j]).wait_send()
            links.landed(base + 2 + j, slots.at[2 + j], place.to_z(j))
        slots[2] = own[...]
        total = slots[2 + lax.rem(place.z + deep, deep)]
        for z in range(1, deep):
            total = total + slots[2 + lax.rem(place.z + deep - z, deep)]
        own[...] = total

    return [start(0), start(1), start(2), start(3), last]


def add_in_two(place, links, base, own, slots):
    p, deep = place, place.deep
    me = p.x * 4 + p.y * 2 + p.c
    peers = p.peers()

    def near(r):
        return links.copy(base + r, own, peers[r - 1][1], slots.at[me])

    def far(j):
        return links.copy(base + 7 + j, own, p.to_z(j), slots.at[8 + p.z])

    def start():
        for r in range(1, 8):
            near(r).start()
        slots[me] = own[...]

    def middle():
        for r in range(1, 8):
            near(r).wait_send()
            links.landed(base + r, slots.at[peers[r - 1][0]], peers[r - 1][1])
        total = slots[0]
        for k in range(1, 8):
            total = total + slots[k]
        own[...] = total
        for j in range(1, deep):
            far(j).start()
        slots[8 + p.z] = total

    def last():
        for j in range(1, deep):
            far(j).wait_send()
            links.landed(base + 7 + j, slots.at[8 + p.from_z(j)], p.to_z(j))
        total = slots[8]
        for k in range(1, deep):
            total = total + slots[8 + k]
        own[...] = total

    return [start, middle, last]


def gather_stages(place, links, base, own, whole, start=0, count=None):
    p, deep = place, place.deep
    count = own.shape[0] if count is None else count
    half = count // 2
    rows, first, later = pl.ds(start, count), pl.ds(start, half), pl.ds(start + half, half)
    own = own.at[rows]
    mine = whole.at[p.x, p.c, p.z, p.y, rows]
    line = whole.at[p.x, p.c, :, p.y, rows]
    ax = whole.at[p.x, p.c, :, p.y, first]
    ax_in = whole.at[1 - p.x, p.c, :, p.y, first]
    by = whole.at[p.x, p.c, :, p.y, later]
    by_in = whole.at[p.x, p.c, :, 1 - p.y, later]
    ay = whole.at[:, p.c, :, p.y, first]
    ay_in = whole.at[:, p.c, :, 1 - p.y, first]
    bx = whole.at[p.x, p.c, :, :, later]
    bx_in = whole.at[1 - p.x, p.c, :, :, later]
    kz, ka, kb, ks = base, base + deep, base + deep + 2, base + deep + 4

    def keep():
        return pltpu.make_async_copy(own, mine, links.send.at[kz])

    def stage0():
        keep().start()
        for j in p.far_z():
            links.copy(kz + j, own, p.to_z(j), mine).start()

    def stage1():
        keep().wait()
        for j in range(1, deep):
            links.landed(kz + j, whole.at[p.x, p.c, p.from_z(j), p.y, rows], p.to_z(j))
        links.copy(ka, ax, p.to_x()).start()
        links.copy(kb, by, p.to_y()).start()
        links.copy(ks, line, p.to_c()).start()

    def stage2():
        links.landed(ka, ax_in, p.to_x())
        links.copy(ka + 1, ay, p.to_y()).start()
        links.copy(ks + 1, ax_in, p.to_c()).start()
        links.landed(kb, by_in, p.to_y())
        links.copy(kb + 1, bx, p.to_x()).start()
        links.copy(ks + 2, by_in, p.to_c()).start()

    def stage3():
        links.landed(ka + 1, ay_in, p.to_y())
        links.copy(ks + 3, ay_in, p.to_c()).start()
        links.landed(kb + 1, bx_in, p.to_x())
        links.copy(ks + 4, bx_in, p.to_c()).start()

    def stage4():
        o = 1 - p.c
        links.landed(ks, whole.at[p.x, o, :, p.y, rows], p.to_c())
        links.landed(ks + 1, whole.at[1 - p.x, o, :, p.y, first], p.to_c())
        links.landed(ks + 2, whole.at[p.x, o, :, 1 - p.y, later], p.to_c())
        links.landed(ks + 3, whole.at[:, o, :, 1 - p.y, first], p.to_c())
        links.landed(ks + 4, whole.at[1 - p.x, o, :, :, later], p.to_c())
        for j in range(1, deep):
            links.copy(kz + j, own, p.to_z(j), mine).wait_send()
        links.copy(ka, ax, p.to_x()).wait_send()
        links.copy(kb, by, p.to_y()).wait_send()
        links.copy(ka + 1, ay, p.to_y()).wait_send()
        links.copy(kb + 1, bx, p.to_x()).wait_send()
        links.copy(ks, line, p.to_c()).wait_send()
        links.copy(ks + 1, ax_in, p.to_c()).wait_send()
        links.copy(ks + 2, by_in, p.to_c()).wait_send()
        links.copy(ks + 3, ay_in, p.to_c()).wait_send()
        links.copy(ks + 4, bx_in, p.to_c()).wait_send()

    return [stage0, stage1, stage2, stage3, stage4]


def gather_stages_late(place, links, base, own, whole, start=0, count=None):
    p, deep = place, place.deep
    count = own.shape[0] if count is None else count
    half = count // 2
    rows, first, later = pl.ds(start, count), pl.ds(start, half), pl.ds(start + half, half)
    mine = whole.at[p.x, p.c, p.z, p.y]
    pair_f, pair_l = whole.at[:, p.c, p.z, p.y, first], whole.at[p.x, p.c, p.z, :, later]
    line_f, line_l = whole.at[:, p.c, :, p.y, first], whole.at[p.x, p.c, :, :, later]
    line_f_in = whole.at[:, p.c, :, 1 - p.y, first]
    line_l_in = whole.at[1 - p.x, p.c, :, :, later]
    kf, kl = base + 8, base + 8 + deep

    def keep():
        return pltpu.make_async_copy(own.at[rows], mine.at[rows], links.send.at[base])

    def to_x():
        return links.copy(base + 1, own.at[first], p.to_x(), mine.at[first])

    def to_y():
        return links.copy(base + 2, own.at[later], p.to_y(), mine.at[later])

    def stage0():
        keep().start()
        to_x().start()
        to_y().start()

    def stage1():
        keep().wait()
        links.landed(base + 1, whole.at[1 - p.x, p.c, p.z, p.y, first], p.to_x())
        links.landed(base + 2, whole.at[p.x, p.c, p.z, 1 - p.y, later], p.to_y())
        for j in p.far_z():
            links.copy(kf + j, pair_f, p.to_z(j)).start()
            links.copy(kl + j, pair_l, p.to_z(j)).start()

    def stage2():
        for j in range(1, deep):
            z = p.from_z(j)
            links.landed(kf + j, whole.at[:, p.c, z, p.y, first], p.to_z(j))
            links.landed(kl + j, whole.at[p.x, p.c, z, :, later], p.to_z(j))
        links.copy(base + 3, line_f, p.to_y()).start()
        links.copy(base + 4, line_l, p.to_x()).start()
        links.copy(base + 5, line_f, p.to_c()).start()
        links.copy(base + 6, line_l, p.to_c()).start()

    def stage3():
        links.landed(base + 3, line_f_in, p.to_y())
        links.copy(base + 7, line_f_in, p.to_c()).start()
        links.landed(base + 4, line_l_in, p.to_x())
        links.copy(base + 8, line_l_in, p.to_c()).start()

    def stage4():
        o = 1 - p.c
        links.landed(base + 5, whole.at[:, o, :, p.y, first], p.to_c())
        links.landed(base + 6, whole.at[p.x, o, :, :, later], p.to_c())
        links.landed(base + 7, whole.at[:, o, :, 1 - p.y, first], p.to_c())
        links.landed(base + 8, whole.at[1 - p.x, o, :, :, later], p.to_c())
        to_x().wait_send()
        to_y().wait_send()
        for j in range(1, deep):
            links.copy(kf + j, pair_f, p.to_z(j)).wait_send()
            links.copy(kl + j, pair_l, p.to_z(j)).wait_send()
        links.copy(base + 3, line_f, p.to_y()).wait_send()
        links.copy(base + 4, line_l, p.to_x()).wait_send()
        links.copy(base + 5, line_f, p.to_c()).wait_send()
        links.copy(base + 6, line_l, p.to_c()).wait_send()
        links.copy(base + 7, line_f_in, p.to_c()).wait_send()
        links.copy(base + 8, line_l_in, p.to_c()).wait_send()

    return [stage0, stage1, stage2, stage3, stage4]


GATHER_COPIES = 9


def add_into(out, one, two):
    out[...] = one[...] + two[...]


def scatter_core(place, links, base, acc, in_c):
    def move(part):
        return links.copy(base + part, acc.at[2 + part], place.to_c(), in_c.at[part])

    def send(part):
        return lambda: move(part).start()

    def add(part, x):
        def run():
            move(part).wait_send()
            links.landed(base + part, in_c.at[part], place.to_c())

            def one(z, _):
                for y in range(2):
                    there = acc.at[x, z, y]
                    add_into(there, there, in_c.at[part, z, y])
                return 0

            lax.fori_loop(0, place.deep, one, 0)

        return run

    return send, add


def add_line(place, acc, x, y, rows, arrived):
    def add(z, _):
        there = acc.at[x, z, y, rows]
        add_into(there, there, arrived.at[z])
        return 0

    lax.fori_loop(0, place.deep, add, 0)


def scatter_plane(place, links, base, acc, ay_in, ax_in, bx_in, by_in):
    p = place
    half = acc.shape[3] // 2
    first, later, both = pl.ds(0, half), pl.ds(half, half), pl.ds(0, 2)

    def ay():
        return links.copy(base, acc.at[both, :, 1 - p.y, first], p.to_y(), ay_in)

    def bx():
        return links.copy(base + 1, acc.at[1 - p.x, :, :, later], p.to_x(), bx_in)

    def ax():
        return links.copy(base + 2, acc.at[1 - p.x, :, p.y, first], p.to_x(), ax_in)

    def by():
        return links.copy(base + 3, acc.at[p.x, :, 1 - p.y, later], p.to_y(), by_in)

    def start():
        ay().start()
        bx().start()

    def middle():
        links.landed(base, ay_in, p.to_y())
        for x in range(2):
            add_line(p, acc, x, p.y, first, ay_in.at[x])
        ax().start()
        links.landed(base + 1, bx_in, p.to_x())
        for y in range(2):
            add_line(p, acc, p.x, y, later, bx_in.at[:, y])
        by().start()

    def finish():
        links.landed(base + 2, ax_in, p.to_x())
        add_line(p, acc, p.x, p.y, first, ax_in)
        links.landed(base + 3, by_in, p.to_y())
        add_line(p, acc, p.x, p.y, later, by_in)

    def settle():
        for move in (ay, bx, ax, by):
            move().wait_send()

    return start, middle, finish, settle


def scatter_in_pairs(place, links, base, acc, in_c, ay_in, ax_in, bx_in, by_in, in_z, out):
    p, deep = place, place.deep
    half = acc.shape[3] // 2
    first, later = pl.ds(0, half), pl.ds(half, half)
    far, near = 1 - p.x, p.x
    kf, kl = base + 6, base + 6 + deep
    send, add = scatter_core(place, links, base, acc, in_c)

    def over_y(part, x):
        return links.copy(base + 2 + part, acc.at[x, :, 1 - p.y, first], p.to_y(), ay_in.at[part])

    def far_later():
        return links.copy(base + 4, acc.at[far, :, :, later], p.to_x(), bx_in)

    def far_first():
        return links.copy(base + 5, acc.at[far, :, p.y, first], p.to_x(), ax_in)

    def near_later():
        return links.copy(base + 6, acc.at[near, :, 1 - p.y, later], p.to_y(), by_in)

    def over_z(k, j, rows):
        to = lax.rem(p.z + j, deep)
        return links.copy(k + j, acc.at[near, to, p.y, rows], p.to_z(j), in_z.at[j, rows])

    def far1():
        add(0, far)()
        over_y(0, far).start()
        far_later().start()

    def far2():
        links.landed(base + 2, ay_in.at[0], p.to_y())
        add_line(p, acc, far, p.y, first, ay_in.at[0])
        far_first().start()

    def near1():
        over_y(1, near).start()

    def near_x():
        links.landed(base + 4, bx_in, p.to_x())
        for y in range(2):
            add_line(p, acc, near, y, later, bx_in.at[:, y])
        near_later().start()

    def near2():
        links.landed(base + 3, ay_in.at[1], p.to_y())
        add_line(p, acc, near, p.y, first, ay_in.at[1])
        links.landed(base + 5, ax_in, p.to_x())
        add_line(p, acc, near, p.y, first, ax_in)
        for j in range(1, deep):
            over_z(kf, j, first).start()

    def near3():
        links.landed(base + 6, by_in, p.to_y())
        add_line(p, acc, near, p.y, later, by_in)
        for j in range(1, deep):
            over_z(kl, j, later).start()

    def near4():
        for k, rows in ((kf, first), (kl, later)):
            total = acc[near, p.z, p.y, rows].astype(F32)
            for j in range(1, deep):
                links.landed(k + j, in_z.at[j, rows], p.to_z(j))
                total = total + in_z[j, rows].astype(F32)
            out[rows] = total
            for j in range(1, deep):
                over_z(k, j, rows).wait_send()
        over_y(0, far).wait_send()
        over_y(1, near).wait_send()
        far_later().wait_send()
        far_first().wait_send()
        near_later().wait_send()

    return [send(0), far1, far2, send(1), add(1, near), near1, near_x, near2, near3, near4]


def scatter_tail(place, links, base, part, in_z, out):
    deep = place.deep

    def send(j):
        return links.copy(
            base + j, part.at[lax.rem(place.z + j, deep)], place.to_z(j), in_z.at[j]
        )

    def stage0():
        for j in range(1, deep):
            send(j).start()

    def stage1():
        for j in range(1, deep):
            links.landed(base + j, in_z.at[j], place.to_z(j))
        total = part[place.z].astype(F32)
        for j in range(1, deep):
            total = total + in_z[j].astype(F32)
        out[...] = total
        for j in range(1, deep):
            send(j).wait_send()

    return [stage0, stage1]


def core_buffers(deep, rows, lanes):
    return [
        pltpu.VMEM((4, deep, 2, rows, lanes), BF16),
        pltpu.VMEM((2, deep, 2, rows, lanes), BF16),
    ]


def plane_buffers(deep, rows, lanes):
    half = rows // 2
    return [
        pltpu.VMEM((2, deep, half, lanes), BF16),
        pltpu.VMEM((deep, half, lanes), BF16),
        pltpu.VMEM((deep, 2, half, lanes), BF16),
        pltpu.VMEM((deep, half, lanes), BF16),
    ]


def gather_blocks(block, sizes):
    whole = lax.all_gather(block, ("dp", "tensor"), axis=0, tiled=False)
    whole = whole.reshape(sizes + block.shape)
    return jnp.swapaxes(whole, 0, 1).reshape((sizes[1], -1) + block.shape[1:])


def scatter_blocks(grads, sizes):
    parts = grads.reshape((sizes[1], sizes[0], -1) + grads.shape[2:])
    parts = jnp.swapaxes(parts, 0, 1).reshape((sizes[0] * sizes[1],) + parts.shape[2:])
    return lax.psum_scatter(parts, ("dp", "tensor"), scatter_dimension=0, tiled=False)


def adam_parts(grad, mean, square):
    new_mean = MOMENT_DECAY * mean + (1.0 - MOMENT_DECAY) * grad
    new_square = MOMENT_DECAY * square + (1.0 - MOMENT_DECAY) * grad * grad
    correction = 1.0 - MOMENT_DECAY**STEP
    direction = new_mean / correction / (jnp.sqrt(new_square / correction) + ADAM_EPS)
    return new_mean, new_square, direction


def sum_all(values):
    return jnp.sum(jnp.sum(values, axis=1, keepdims=True), axis=0, keepdims=True)


def group_squares(qkv_part, out_part, inner_part, outer_part, vector_part):
    return jnp.concatenate(
        [
            jnp.sum(qkv_part * qkv_part, axis=(1, 2)),
            jnp.sum(out_part * out_part)[None],
            jnp.sum(inner_part * inner_part)[None],
            jnp.sum(outer_part * outer_part)[None],
            jnp.sum(vector_part[:8] * vector_part[:8], axis=1),
            jnp.sum(vector_part[8:] * vector_part[8:])[None],
        ]
    )


def lamb_apply(weight_list, update_list, trust_ratio, row_number):
    qkv_new = weight_list[0] - LEARN_RATE * trust_ratio[0:3, None, None] * update_list[0]
    out_new = weight_list[1] - LEARN_RATE * trust_ratio[3] * update_list[1]
    inner_new = weight_list[2] - LEARN_RATE * trust_ratio[4] * update_list[2]
    outer_new = weight_list[3] - LEARN_RATE * trust_ratio[5] * update_list[3]
    row_ratio = jnp.concatenate(
        [trust_ratio[6:14], jnp.broadcast_to(trust_ratio[14], (row_number - 8,))]
    )
    vector_new = weight_list[4] - LEARN_RATE * row_ratio[:, None] * update_list[4]
    return (qkv_new, out_new, inner_new, outer_new, vector_new)


def lamb_plain(sum_a, sum_b, sum_c, vector_sum, weights, old_means, old_squares):
    qkv_sum = jnp.stack([collect(sum_a, at) for at in (Q_AT, K_AT, V_AT)])
    grad_sums = (qkv_sum, collect(sum_a, O_AT).T, sum_b, sum_c.T, vector_sum)
    decays = (WEIGHT_DECAY, WEIGHT_DECAY, WEIGHT_DECAY, WEIGHT_DECAY, 0.0)
    stats = [adam_parts(*entry) for entry in zip(grad_sums, old_means, old_squares)]
    updates = [stats[i][2] + decays[i] * weights[i] for i in range(5)]
    weight_squares, update_squares = lax.psum(
        (group_squares(*weights), group_squares(*updates)), ("dp", "tensor")
    )
    weight_norms = jnp.sqrt(weight_squares)
    update_norms = jnp.sqrt(update_squares)
    trust_ratio = weight_norms / (update_norms + ADAM_EPS)
    new = lamb_apply(weights, updates, trust_ratio, weights[4].shape[0])
    outs = []
    for i in range(5):
        outs += [stats[i][0], stats[i][1], new[i]]
    return outs + [jnp.stack([weight_norms, update_norms])]


A_PIECES = 3
C_ROWS = ((0, 64), (64, 32))


def own_first(order):
    tensor = lax.axis_index("tensor")
    x, c = tensor // 2, tensor % 2
    return jnp.where(order % 2 == 0, x, 1 - x) * 2 + jnp.where(order < 2, c, 1 - c)


def gather_attend_kernel(
    qkv_ref, out_ref, inner_ref, outer_ref, vec_ref, x_ref, seg_ref,
    wa_hbm, wb_hbm, wc_hbm, hid_hbm, nlt_hbm, xt_hbm, n1_hbm,
    full, pm_ref, lse_ref, slope_ref, acc, inv_ref,
    send, recv, slots, pack_a, pack_b, pack_c, wa, wb, wc, hid, nlt_ref, xt_ref, n1_ref,
    bias, low, out_sem, xp, proj_acc,
    *, sizes, chunk,
):
    step = pl.program_id(0)
    groups, deep = sizes[1], sizes[0] // 2
    place = Place(sizes)
    links = Links(send, recv)
    each = GATHER_COPIES + deep
    cols = qkv_ref.shape[2]
    tokens, width = x_ref.shape
    lanes = pack_a.shape[1]
    length = tokens // 2
    tail = 256
    count = pack_a.shape[0] // A_PIECES
    ga = [
        gather_stages(place, links, k * each, pack_a, wa, k * count, count) for k in range(A_PIECES)
    ]
    gb = gather_stages(place, links, A_PIECES * each, pack_b, wb)
    more = (A_PIECES + 1) * each
    small = add_everywhere(place, links, more, full, slots)
    more += deep + 2
    gc = [
        gather_stages_late(place, links, more + k * (each + deep), pack_c, wc, *rows)
        for k, rows in enumerate(C_ROWS)
    ]
    t, s = own_first(jnp.minimum(step // 2, groups - 1)), step % 2
    last = 4 * groups - 1

    def keep(k):
        pairs = (
            (wa, wa_hbm), (wb, wb_hbm), (wc, wc_hbm), (hid, hid_hbm),
            (nlt_ref, nlt_hbm), (xt_ref, xt_hbm), (n1_ref, n1_hbm),
        )
        return pltpu.make_async_copy(*pairs[k], out_sem.at[k])

    def project(piece):
        here = pl.ds(piece * count, count)
        for x in range(2):
            part = dot(xp[piece], wa[x, place.c, :, :, here].reshape(sizes[0] * count, lanes))
            proj_acc[x] = part if piece == 0 else proj_acc[x] + part

    @pl.when(step == 0)
    def _():
        out_rows = out_ref[...].T
        pack_a[...] = spread(qkv_ref[0], qkv_ref[1], qkv_ref[2], out_rows).astype(BF16)
        place.greet()
        for k in range(A_PIECES):
            ga[k][0]()
        pack_c[...] = outer_ref[...].astype(BF16)
        gc[0][0]()
        gc[1][0]()
        pack_b[...] = inner_ref[...].astype(BF16)
        xt_ref[...] = x_ref[...].T
        each_dp = pack_a.shape[0]
        for k in range(A_PIECES):
            picked = [
                xt_ref[dp * each_dp + k * count : dp * each_dp + (k + 1) * count]
                for dp in range(sizes[0])
            ]
            xp[k] = jnp.concatenate(picked, axis=0).T
        full[...] = jnp.zeros_like(full)
        mine = vec_ref.shape[1]
        full[0 : vec_ref.shape[0], 0:mine] = vec_ref[...]
        index = lax.axis_index("dp") * groups + lax.axis_index("tensor")
        full[...] = pltpu.roll(full[...], index * mine, 1)
        small[0]()
        small[1]()
        ga[0][1]()
        small[2]()
        ga[0][2]()
        ga[1][1]()
        small[3]()
        gb[0]()
        ga[2][1]()
        ga[1][2]()
        ga[2][2]()
        ga[0][3]()
        project(0)
        small[4]()
        for g in range(groups):
            bias[g] = jnp.zeros(bias.shape[1:], F32)
            for h in range(HEADS):
                mine = slice(g * cols + h * HD, g * cols + (h + 1) * HD)
                bias[g, 0:1, Q_AT[h] : Q_AT[h] + HD] = full[6:7, mine]
                bias[g, 0:1, V_AT[h] : V_AT[h] + HD] = full[7:8, mine]
        n1_ref[...] = x_ref[...].astype(F32) + full[4:5, :]
        ga[1][3]()
        project(1)
        ga[2][3]()
        project(2)

    @pl.when(step == groups)
    def _():
        gb[2]()
        gc[1][1]()
        for k in range(A_PIECES):
            ga[k][4]()
        keep(0).start()

    @pl.when(step == 1)
    def _():
        gb[1]()
        gc[0][1]()

    @pl.when(step == 2 * groups + 2)
    def _():
        gb[4]()
        keep(1).start()
        gc[1][2]()

    @pl.when(step == 3 * groups)
    def _():
        gc[0][3]()
        gc[1][3]()
        keep(3).start()

    @pl.when(step == 3 * groups + 2)
    def _():
        gc[0][4]()
        gc[1][4]()
        keep(2).start()

    @pl.when((step < groups) & (s == 0))
    def _():
        pm_ref[0] = (proj_acc[t // 2] + bias[t, 0:1]).astype(BF16)

    @pl.when((step >= groups) & (step < 2 * groups) & (s == 0))
    def _():
        weight = wa[t // 2, t % 2].reshape(width, lanes)
        for n in range(lanes // 256):
            here = slice(n * 256, (n + 1) * 256)
            proj = dot(x_ref[...], weight[:, here]) + bias[t, 0:1, here]
            pm_ref[0, :, here] = proj.astype(BF16)

    @pl.when(step < 2 * groups)
    def _():
        rows = pl.ds(pl.multiple_of(s * length, length), length)
        row = seg_ref[pl.ds(lax.axis_index("tensor") * 2 + s, 1)]
        attend_heads(pm_ref.at[0, rows], row, lse_ref, chunk)

    @pl.when((step < 2 * groups) & (s == 1))
    def _():
        mixed = mixed_only(pm_ref[0, :, lanes - tail :])
        weight = wa[t // 2, t % 2, :, :, :, lanes - tail :].reshape(width, tail)
        n1_ref[...] += dot(mixed, weight, NT)

    @pl.when(step == 2 * groups)
    def _():
        gc[0][2]()
        for r in range(tokens // 256):
            rows = slice(r * 256, (r + 1) * 256)
            normal_one, inverse_one = norm_parts(n1_ref[rows])
            n1_ref[rows] = normal_one
            inv_ref[rows] = inverse_one
            normed = normal_one * full[0:1, :] + full[1:2, :]
            acc[rows] = normed + full[5:6, :]
            part = normed.astype(BF16)
            low[rows] = part
            nlt_ref[:, rows] = part.T
        for k in range(4, 7):
            keep(k).start()
        gb[3]()

    @pl.when((step >= 2 * groups) & (step < 3 * groups))
    def _():
        g = own_first(step - 2 * groups)
        weight = wb[g // 2, g % 2].reshape(width, lanes)
        for n in range(lanes // 256):
            here = slice(n * 256, (n + 1) * 256)
            pre = dot(low[...], weight[:, here]) + full[pl.ds(8 + g, 1), here]
            act, turn = gelu_parts(pre)
            hid[g, :, here] = act.astype(BF16)
            slope_ref[0, :, here] = turn.astype(BF16)

    @pl.when(step >= 3 * groups)
    def _():
        g = own_first(step - 3 * groups)
        weight = wc[g // 2, g % 2].reshape(width, lanes)
        acc[...] += dot(hid[g], weight, NT)

    @pl.when(step == last)
    def _():
        for k in range(7):
            keep(k).wait()


def once(shape):
    return pl.BlockSpec(shape, lambda *_: (0,) * len(shape), pipeline_mode=pl.Buffered(1))


def gather_attend(weights, x, seg, sizes):
    qkv, out, inner, outer, vec = weights
    deep, groups = sizes[0] // 2, sizes[1]
    copies = (A_PIECES + 1) * (GATHER_COPIES + deep) + deep + 2
    copies += len(C_ROWS) * (GATHER_COPIES + 2 * deep)
    tokens, width = x.shape
    length = seg.shape[1]
    seqs = tokens // length
    rows, lanes = inner.shape
    steps = groups * seqs
    anywhere = pl.BlockSpec(memory_space=pl.ANY)
    parts = (2, 2, deep, 2, rows, lanes)
    whole = jax.ShapeDtypeStruct(parts, BF16)

    def now(i):
        i = jnp.minimum(i, steps - 1)
        return own_first(i // 2), i % 2

    def part(i):
        return own_first(jnp.clip(i - steps, 0, groups - 1))

    wa, wb, wc, hid, nlt, xt, n1, *rest = pl.pallas_call(
        functools.partial(gather_attend_kernel, sizes=sizes, chunk=min(256, length)),
        grid=(steps + 2 * groups,),
        in_specs=[once(w.shape) for w in weights]
        + [
            once(x.shape),
            once(seg.shape),
        ],
        out_specs=[anywhere] * 7
        + [
            once((16, width)),
            pl.BlockSpec((1, tokens, lanes), lambda i: (now(i)[0], 0, 0)),
            pl.BlockSpec((1, 1, 8, length), lambda i: (*now(i), 0, 0)),
            pl.BlockSpec((1, tokens, lanes), lambda i: (part(i), 0, 0)),
            once((tokens, width)),
            once((tokens, 1)),
        ],
        out_shape=[whole] * 3
        + [
            jax.ShapeDtypeStruct((groups, tokens, lanes), BF16),
            jax.ShapeDtypeStruct((width, tokens), BF16),
            jax.ShapeDtypeStruct((width, tokens), BF16),
            jax.ShapeDtypeStruct((tokens, width), F32),
            jax.ShapeDtypeStruct((16, width), F32),
            jax.ShapeDtypeStruct((groups, tokens, lanes), BF16),
            jax.ShapeDtypeStruct((groups, seqs, 8, length), F32),
            jax.ShapeDtypeStruct((groups, tokens, lanes), BF16),
            jax.ShapeDtypeStruct((tokens, width), F32),
            jax.ShapeDtypeStruct((tokens, 1), F32),
        ],
        scratch_shapes=[
            pltpu.SemaphoreType.DMA((copies,)),
            pltpu.SemaphoreType.DMA((copies,)),
            pltpu.VMEM((deep + 2, 16, width), F32),
            pltpu.VMEM((rows, lanes), BF16),
            pltpu.VMEM((rows, lanes), BF16),
            pltpu.VMEM((rows, lanes), BF16),
            pltpu.VMEM(parts, BF16),
            pltpu.VMEM(parts, BF16),
            pltpu.VMEM(parts, BF16),
            pltpu.VMEM((groups, tokens, lanes), BF16),
            pltpu.VMEM((width, tokens), BF16),
            pltpu.VMEM((width, tokens), BF16),
            pltpu.VMEM((tokens, width), F32),
            pltpu.VMEM((groups, 8, lanes), F32),
            pltpu.VMEM((tokens, width), BF16),
            pltpu.SemaphoreType.DMA((7,)),
            pltpu.VMEM((A_PIECES, tokens, width // A_PIECES), BF16),
            pltpu.VMEM((2, tokens, lanes), F32),
        ],
        compiler_params=params(collective_id=0, has_side_effects=True),
        name="gather_attend",
    )(*weights, x, seg)
    shape = (groups, sizes[0] * rows, lanes)
    return [wa.reshape(shape), wb.reshape(shape), wc.reshape(shape), hid, nlt, xt, n1] + rest


def other_first(order):
    c = lax.axis_index("tensor") % 2
    return order % 2 * 2 + jnp.where(order < 2, 1 - c, c)


def layer_kernel(
    cot_ref, hid_ref, slope_ref, inv_ref, vec_ref, second_hbm, n1_hbm, nlt_hbm, wa_hbm, wb_hbm,
    wc_hbm,
    out_hbm, gb_hbm, gm_hbm, gbt_hbm, accb_hbm, part_ref, vg_ref, bg_ref,
    n1_ref, nlt_ref, wo_ref, wb_ref, wc_ref, acc, low, gst, gi, out_ref, gm_ref, gbt_ref,
    in_sem, out_sem, send, recv, accc, in_cc, accb, in_cb, ay_in, ax_in, bx_in, by_in, *, sizes,
):
    step = pl.program_id(0)
    tokens, width = acc.shape
    groups, deep = sizes[1], sizes[0] // 2
    lanes = wa_hbm.shape[2]
    tail = wo_ref.shape[2]
    last = 2 * groups - 1
    place = Place(sizes)
    links = Links(send, recv)
    send_c, add_c = scatter_core(place, links, 0, accc, in_cc)
    send_b, add_b = scatter_core(place, links, 2, accb, in_cb)
    start, middle, finish, settle = scatter_plane(
        place, links, 4, accc, ay_in, ax_in, bx_in, by_in
    )
    blocks = [slice(r * 256, (r + 1) * 256) for r in range(tokens // 256)]
    columns = [slice(n * 256, (n + 1) * 256) for n in range(width // 256)]

    def outer(t):
        return pltpu.make_async_copy(wc_hbm.at[t], wc_ref.at[t], in_sem.at[t])

    def inner(t):
        return pltpu.make_async_copy(wb_hbm.at[t], wb_ref.at[t], in_sem.at[groups + t])

    def load(k):
        pairs = (
            (second_hbm, acc), (n1_hbm, n1_ref), (nlt_hbm, nlt_ref),
            (wa_hbm.at[:, :, pl.ds(lanes - tail, tail)], wo_ref),
        )
        return pltpu.make_async_copy(*pairs[k], in_sem.at[2 * groups + k])

    def store(k):
        pairs = (
            (out_ref, out_hbm), (gbt_ref, gbt_hbm), (accb.at[pl.ds(0, 2)], accb_hbm), (acc, gb_hbm)
        )
        return pltpu.make_async_copy(*pairs[k], out_sem.at[k])

    def store_mixed(t):
        return pltpu.make_async_copy(gm_ref.at[t], gm_hbm.at[t], out_sem.at[4 + t])

    @pl.when(step == 0)
    def _():
        load(0).start()
        for t in range(groups):
            outer(t).start()
            inner(t).start()
        for k in range(1, 4):
            load(k).start()
        place.greet()
        vg_ref[...] = jnp.zeros_like(vg_ref)
        bg_ref[...] = jnp.zeros_like(bg_ref)
        load(0).wait()
        for rows in blocks:
            normal_two, inverse_two = norm_parts(acc[rows])
            out_ref[rows] = (normal_two * vec_ref[2:3, :] + vec_ref[3:4, :]).astype(BF16)
            cot = cot_ref[rows].astype(F32)
            grad_second = norm_back(cot, normal_two, inverse_two, vec_ref[2:3, :])
            vg_ref[2:3, :] += jnp.sum(cot * normal_two, axis=0, keepdims=True)
            vg_ref[3:4, :] += jnp.sum(cot, axis=0, keepdims=True)
            vg_ref[5:6, :] += jnp.sum(grad_second, axis=0, keepdims=True)
            acc[rows] = grad_second
            part = grad_second.astype(BF16)
            low[rows] = part
            gst[:, rows] = part.T
        store(0).start()

    @pl.when(step < groups)
    def _():
        slot = lax.rem(step + 2, 4)
        for here in columns:
            part = dot(gst[...], hid_ref[0, :, here]).astype(BF16)
            accc[slot, :, :, :, here] = part.reshape(deep, 2, -1, 256)

    @pl.when(step == 1)
    def _():
        send_c(0)()

    @pl.when(step == 2)
    def _():
        send_c(1)()

    @pl.when(step == groups)
    def _():
        add_c(0, 0)()
        add_c(1, 1)()
        start()
        for t in range(groups):
            outer(t).wait()
            inner(t).wait()
        for k in range(1, 4):
            load(k).wait()

    @pl.when(step == last)
    def _():
        middle()

    @pl.when(step >= groups)
    def _():
        order = step - groups
        slot = lax.rem(order + 2, 4)
        t = other_first(order)
        for here in columns:
            grad_hidden = dot(low[...], wc_ref[t, :, here])
            part = (grad_hidden * slope_ref[0, :, here].astype(F32)).astype(BF16)
            gi[:, here] = part
            bg_ref[pl.ds(t, 1), here] = jnp.sum(part.astype(F32), axis=0, keepdims=True)
        acc[...] += dot(gi[...], wb_ref[t], NT)
        for here in columns:
            part = dot(nlt_ref[...], gi[:, here]).astype(BF16)
            accb[slot, :, :, :, here] = part.reshape(deep, 2, -1, 256)

    @pl.when(step == groups + 1)
    def _():
        send_b(0)()

    @pl.when(step == groups + 2)
    def _():
        send_b(1)()

    @pl.when(step == last)
    def _():
        for rows in blocks:
            grad_normed = acc[rows]
            normal_one = n1_ref[rows]
            grad_branch = norm_back(grad_normed, normal_one, inv_ref[rows], vec_ref[0:1, :])
            vg_ref[0:1, :] += jnp.sum(grad_normed * normal_one, axis=0, keepdims=True)
            vg_ref[1:2, :] += jnp.sum(grad_normed, axis=0, keepdims=True)
            vg_ref[4:5, :] += jnp.sum(grad_branch, axis=0, keepdims=True)
            acc[rows] = grad_branch
            part = grad_branch.astype(BF16)
            low[rows] = part
            gbt_ref[:, rows] = part.T
        store(3).start()
        store(1).start()
        for t in range(groups):
            gm_ref[t] = dot(low[...], wo_ref[t]).astype(BF16)
            store_mixed(t).start()
        add_b(0, 0)()
        add_b(1, 1)()
        store(2).start()
        finish()
        part_ref[...] = accc[place.x, :, place.y]
        settle()
        for k in range(4):
            store(k).wait()
        for t in range(groups):
            store_mixed(t).wait()


def layer(cot, hid, slope, second, n1, inv1, nlt, wa, wb, wc, vec, sizes):
    tokens, width = cot.shape
    groups, _, lanes = wa.shape
    hidden = wb.shape[2]
    deep = sizes[0] // 2
    rows = width // sizes[0]
    tail = 256
    anywhere = pl.BlockSpec(memory_space=pl.ANY)

    def used(i):
        return other_first(jnp.minimum(i, groups - 1))

    def back_group(i):
        return other_first(jnp.clip(i - groups, 0, groups - 1))

    copies = 8
    parts = (2, deep, 2, rows, hidden)
    matrix = pltpu.VMEM((groups, width, hidden), BF16)
    return pl.pallas_call(
        functools.partial(layer_kernel, sizes=sizes),
        grid=(2 * groups,),
        in_specs=[
            once(cot.shape),
            pl.BlockSpec((1, tokens, hidden), lambda i: (used(i), 0, 0)),
            pl.BlockSpec((1, tokens, hidden), lambda i: (back_group(i), 0, 0)),
            once(inv1.shape),
            once(vec.shape),
        ]
        + [anywhere] * 6,
        out_specs=[anywhere] * 5
        + [once((deep, rows, hidden)), once((8, width)), once((8, hidden))],
        out_shape=[
            jax.ShapeDtypeStruct((tokens, width), BF16),
            jax.ShapeDtypeStruct((tokens, width), F32),
            jax.ShapeDtypeStruct((groups, tokens, tail), BF16),
            jax.ShapeDtypeStruct((width, tokens), BF16),
            jax.ShapeDtypeStruct(parts, BF16),
            jax.ShapeDtypeStruct((deep, rows, hidden), BF16),
            jax.ShapeDtypeStruct((8, width), F32),
            jax.ShapeDtypeStruct((8, hidden), F32),
        ],
        scratch_shapes=[
            pltpu.VMEM(n1.shape, F32),
            pltpu.VMEM((width, tokens), BF16),
            pltpu.VMEM((groups, width, tail), BF16),
            matrix,
            matrix,
            pltpu.VMEM((tokens, width), F32),
            pltpu.VMEM((tokens, width), BF16),
            pltpu.VMEM((width, tokens), BF16),
            pltpu.VMEM((tokens, hidden), BF16),
            pltpu.VMEM((tokens, width), BF16),
            pltpu.VMEM((groups, tokens, tail), BF16),
            pltpu.VMEM((width, tokens), BF16),
            pltpu.SemaphoreType.DMA((2 * groups + 4,)),
            pltpu.SemaphoreType.DMA((4 + groups,)),
            pltpu.SemaphoreType.DMA((copies,)),
            pltpu.SemaphoreType.DMA((copies,)),
        ]
        + core_buffers(deep, rows, hidden) * 2
        + plane_buffers(deep, rows, hidden),
        compiler_params=params(collective_id=1, has_side_effects=True),
        name="layer",
    )(cot, hid, slope, inv1, vec, second, n1, nlt, wa, wb, wc)


def far_first(step, groups):
    tensor = lax.axis_index("tensor")
    x, c = tensor // 2, tensor % 2
    return jnp.where(step < groups, 1 - x, x) * 2 + jnp.where(step % groups < 2, 1 - c, c)


def changes_of(refs):
    qkv, out, hidden, vec = refs
    return [
        [qkv.at[k], out.at[k], hidden.at[k, 0], hidden.at[k, 1], vec.at[k]] for k in range(2)
    ]


def back_kernel(
    pm_ref, gm_ref, lse_ref, seg_ref, wa_hbm, xt_hbm, gbt_hbm, gb_hbm,
    accb_hbm, part_ref, vg_ref, bg_ref, *refs, sizes, chunk,
):
    weights, means, squares = refs[0:5], refs[5:10], refs[10:15]
    (grads, updates), norms, ig_ref = changes_of(refs[15:19]), refs[19], refs[20]
    gp, gsum, send, recv, slots, hslots, nslots, vec, hvec, load_sem, sa = refs[21:32]
    wa_ref, xt_ref, gbt_ref, gb_ref, accb, inz_b, inz_c = refs[32:39]
    bufs_b, bufs_a, acc = refs[39:43], refs[43:50], refs[43]
    sb, sc = grads[2], grads[3]
    step = pl.program_id(0)
    groups, deep = sizes[1], sizes[0] // 2
    cols = HEADS * HD
    tokens, width = gb_ref.shape
    lanes = pm_ref.shape[2]
    last = 2 * groups - 1
    length = pm_ref.shape[1]
    place = Place(sizes)
    links = Links(send, recv)
    a = scatter_in_pairs(place, links, 0, *bufs_a, sa)
    more = 7 + 2 * deep
    start, middle, finish, settle = scatter_plane(place, links, more, accb, *bufs_b)
    b = scatter_tail(place, links, more + 4, accb.at[place.x, :, place.y], inz_b, sb)
    c = scatter_tail(place, links, more + 4 + deep, part_ref, inz_c, sc)
    early = add_everywhere(place, links, more + 4 + 2 * deep, vec, slots)
    small = add_everywhere(place, links, more + 6 + 3 * deep, hvec, hslots)
    final = add_in_two(place, links, more + 8 + 4 * deep, norms, nslots)
    t, s = far_first(step, groups), step % 2

    def load(k):
        pairs = ((accb_hbm, accb), (xt_hbm, xt_ref), (gbt_hbm, gbt_ref), (wa_hbm, wa_ref), (gb_hbm, gb_ref))
        return pltpu.make_async_copy(*pairs[k], load_sem.at[k])

    @pl.when(step == 0)
    def _():
        load(0).start()
        place.greet(everyone=True)
        c[0]()
        load(0).wait()
        start()
        for k in range(1, 5):
            load(k).start()
        gsum[...] = jnp.zeros_like(gsum)
        vec[...] = jnp.zeros_like(vec)
        hvec[...] = jnp.zeros_like(hvec)
        vec[0:6] = vg_ref[0:6]
        vec[8 : 8 + groups] = bg_ref[0:groups]
        early[0]()

    @pl.when(step == 1)
    def _():
        load(1).wait()
        load(2).wait()

    @pl.when(step == 2)
    def _():
        a[0]()
        early[1]()

    @pl.when(step == 4)
    def _():
        early[2]()
        middle()
        a[1]()

    @pl.when(step == 5)
    def _():
        c[1]()

    @pl.when(step == 6)
    def _():
        a[3]()
        early[3]()

    @pl.when(step == 7)
    def _():
        finish()
        b[0]()

    rows = pl.ds(pl.multiple_of(s * length, length), length)
    row = seg_ref[pl.ds(lax.axis_index("tensor") * 2 + s, 1)]
    attend_back(pm_ref.at[0], gm_ref.at[0], lse_ref, row, gp.at[t, rows], chunk)

    for n in (0, 2, 3):
        here = slice(n * 128, (n + 1) * 128)
        gsum[t, 0:1, here] += jnp.sum(gp[t, rows, here].astype(F32), axis=0, keepdims=True)

    @pl.when(s == 1)
    def _():
        order = step // 2
        slot = jnp.where(order % 2 == 0, 2 + order // 2, t // 2)
        for n in range(2):
            here = slice(n * 256, (n + 1) * 256)
            part = dot(xt_ref[...], gp[t, :, here]).astype(BF16)
            acc[slot, :, :, :, here] = part.reshape(deep, 2, -1, 256)
        from_x = dot(xt_ref[...], gp[t, :, 512:768])
        part = dot(gbt_ref[...], gp[t, :, 512:768])
        lane = lax.broadcasted_iota(jnp.int32, part.shape, 1)
        part = jnp.where((lane >= 128) & (lane < 192), from_x, part).astype(BF16)
        acc[slot, :, :, :, 512:768] = part.reshape(deep, 2, -1, 256)

    def input_columns(n):
        here = slice(n * 256, (n + 1) * 256)
        total = gb_ref[:, here]
        for g in range(groups):
            part = gp[g, :, 640:768]
            part = halves(part, jnp.zeros_like(part))
            total = total + dot(gp[g, :, 0:512], wa_ref[g, here, 0:512], NT)
            total = total + dot(part, wa_ref[g, here, 640:768], NT)
        ig_ref[:, here] = total.astype(BF16)

    @pl.when(step == last)
    def _():
        for g in range(groups):
            for h in range(HEADS):
                at = g * cols + h * HD
                line, lane = at // 256, slice(at % 256, at % 256 + HD)
                hvec[line : line + 1, lane] = gsum[g, 0:1, Q_AT[h] : Q_AT[h] + HD]
                hvec[3 + line : 4 + line, lane] = gsum[g, 0:1, V_AT[h] : V_AT[h] + HD]
        small[0]()
        a[4]()
        a[5]()
        a[2]()
        load(3).wait()
        load(4).wait()
        input_columns(0)
        small[1]()
        a[6]()
        early[4]()
        input_columns(1)
        small[2]()
        a[7]()
        input_columns(2)
        a[8]()
        small[3]()
        b[1]()
        settle()
        found = group_sums([None] * 4 + [sb[...], sc[...], None], weights, means, squares, updates)
        small[4]()
        for k in range(3):
            lanes_of = slice(k * 256, (k + 1) * 256)
            vec[6:7, lanes_of] = hvec[k : k + 1]
            vec[7:8, lanes_of] = hvec[3 + k : 4 + k]
        count, mine = weights[4].shape
        index = lax.axis_index("dp") * groups + lax.axis_index("tensor")
        turned = pltpu.roll(vec[...], width - index * mine, 1)
        grads[4][...] = turned[0:count, 0:mine]
        found = found + group_sums(
            [None] * 6 + [grads[4][...]], weights, means, squares, updates
        )
        a[9]()
        total = sa[...]
        for k, at in enumerate((Q_AT, K_AT, V_AT)):
            grads[0][k] = collect(total, at)
        grads[1][...] = collect(total, O_AT).T
        parts = [grads[0][k] for k in range(3)] + [grads[1][...]]
        norms[...] = found + group_sums(parts + [None] * 3, weights, means, squares, updates)
        for run in final:
            run()


def group_sums(grads, weights, means, squares, updates):
    lane = lax.broadcasted_iota(jnp.int32, (8, 128), 1)
    line = lax.broadcasted_iota(jnp.int32, (8, 128), 0)
    found = jnp.zeros((8, 128), F32)
    for group, grad in enumerate(grads):
        if grad is None:
            continue
        i, k = (0, group) if group < 3 else (group - 2, ...)
        weight, mean, square = (ref[i][k] for ref in (weights, means, squares))
        update = adam_parts(grad, mean, square)[2]
        if i < 4:
            update = update + WEIGHT_DECAY * weight
        updates[i][k] = update
        if i < 4:
            pair = (sum_all(weight * weight), sum_all(update * update))
            for which in range(2):
                hit = (lane == group) & (line == which)
                found = found + jnp.where(hit, pair[which], 0.0)
            continue
        for which, values in enumerate((weight, update)):
            per_row = jnp.sum(values * values, axis=1, keepdims=True)
            for row in range(weight.shape[0]):
                hit = (lane == 6 + min(row, 8)) & (line == which)
                found = found + jnp.where(hit, per_row[row : row + 1], 0.0)
    return found


def back(pm, gm, lse, seg, wa, xt, gbt, gb, accb, part, vg, bg,
         weights, means, squares, sizes):
    deep, groups = sizes[0] // 2, sizes[1]
    tokens, width = gb.shape
    lanes = pm.shape[2]
    length = seg.shape[1]
    seqs = tokens // length
    rows = width // sizes[0]
    copies = 7 + 2 * deep + 4 + 2 * deep + 2 * (deep + 2) + 7 + deep
    small = [weights, means, squares]
    anywhere = pl.BlockSpec(memory_space=pl.ANY)
    outs = [
        jax.ShapeDtypeStruct((2,) + weights[0].shape, F32),
        jax.ShapeDtypeStruct((2,) + weights[1].shape, F32),
        jax.ShapeDtypeStruct((2, 2) + weights[2].shape, F32),
        jax.ShapeDtypeStruct((2,) + weights[4].shape, F32),
        jax.ShapeDtypeStruct((8, 128), F32),
        jax.ShapeDtypeStruct((tokens, width), BF16),
    ]
    return pl.pallas_call(
        functools.partial(back_kernel, sizes=sizes, chunk=min(256, length)),
        grid=(groups * seqs,),
        in_specs=[
            pl.BlockSpec((1, length, lanes), lambda i: (far_first(i, groups), i % 2, 0)),
            pl.BlockSpec((1, length, gm.shape[2]), lambda i: (far_first(i, groups), i % 2, 0)),
            pl.BlockSpec((1, 1, 8, length), lambda i: (far_first(i, groups), i % 2, 0, 0)),
            once(seg.shape),
            anywhere,
            anywhere,
            anywhere,
            anywhere,
            anywhere,
            once(part.shape),
            once(vg.shape),
            once(bg.shape),
        ]
        + [once(ref.shape) for group in small for ref in group],
        out_specs=[once(ref.shape) for ref in outs],
        out_shape=outs,
        scratch_shapes=[
            pltpu.VMEM((groups, tokens, lanes), BF16),
            pltpu.VMEM((groups, 8, lanes), F32),
            pltpu.SemaphoreType.DMA((copies,)),
            pltpu.SemaphoreType.DMA((copies,)),
            pltpu.VMEM((deep + 2, 16, width), F32),
            pltpu.VMEM((deep + 2, 8, 256), F32),
            pltpu.VMEM((8 + deep, 8, 128), F32),
            pltpu.VMEM((16, width), F32),
            pltpu.VMEM((8, 256), F32),
            pltpu.SemaphoreType.DMA((5,)),
            pltpu.VMEM((rows, lanes), F32),
            pltpu.VMEM(wa.shape, BF16),
            pltpu.VMEM(xt.shape, BF16),
            pltpu.VMEM(gbt.shape, BF16),
            pltpu.VMEM(gb.shape, F32),
            pltpu.VMEM(accb.shape, BF16),
            pltpu.VMEM((deep, rows, lanes), BF16),
            pltpu.VMEM((deep, rows, lanes), BF16),
        ]
        + plane_buffers(deep, rows, lanes)
        + core_buffers(deep, rows, lanes)
        + plane_buffers(deep, rows, lanes)
        + [pltpu.VMEM((deep, rows, lanes), BF16)],
        compiler_params=params(collective_id=2, has_side_effects=True),
        name="back",
    )(
        pm, gm, lse, seg, wa, xt, gbt, gb,
        accb, part, vg, bg,
        *weights, *means, *squares,
    )


def apply_kernel(*refs):
    (grads, updates), sums = changes_of(refs[0:4]), refs[4]
    weights, means, squares = refs[5:10], refs[10:15], refs[15:20]
    passed, outs, norms = refs[20:22], refs[22:37], refs[37]
    wide, sem = refs[40], refs[41]
    stores = [pltpu.make_async_copy(passed[0], refs[38], sem.at[0])]
    stores[0].start()
    rows = wide.shape[0] // 4
    for k in range(4):
        here = pl.ds(k * rows, rows)
        wide[here] = passed[1][here].astype(F32)
        stores.append(pltpu.make_async_copy(wide.at[here], refs[39].at[here], sem.at[1 + k]))
        stores[-1].start()
    roots = jnp.sqrt(sums[...])
    norms[...] = roots[0:2, 0:15]
    ratio = LEARN_RATE * roots[0:1] / (roots[1:2] + ADAM_EPS)
    for i in range(5):
        grad = grads[i][...]
        outs[3 * i][...] = MOMENT_DECAY * means[i][...] + (1.0 - MOMENT_DECAY) * grad
        outs[3 * i + 1][...] = (
            MOMENT_DECAY * squares[i][...] + (1.0 - MOMENT_DECAY) * grad * grad
        )
        target = outs[3 * i + 2]
        if i == 0:
            for k in range(3):
                target[k] = weights[i][k] - ratio[:, k : k + 1] * updates[i][k]
        elif i < 4:
            target[...] = weights[i][...] - ratio[:, 2 + i : 3 + i] * updates[i][...]
        else:
            for row in range(target.shape[0]):
                here = slice(row, row + 1)
                step = ratio[:, 6 + min(row, 8) : 7 + min(row, 8)]
                target[here] = weights[i][here] - step * updates[i][here]
    for move in stores:
        move.wait()


def apply(changes, sums, weights, means, squares, passed):
    inside = pl.BlockSpec(memory_space=pltpu.VMEM)
    shapes = []
    for weight in weights:
        shapes += [jax.ShapeDtypeStruct(weight.shape, F32)] * 3
    shapes.append(jax.ShapeDtypeStruct((2, 15), F32))
    shapes += [jax.ShapeDtypeStruct(passed[0].shape, BF16)]
    shapes += [jax.ShapeDtypeStruct(passed[1].shape, F32)]
    anywhere = [pl.BlockSpec(memory_space=pl.ANY)] * 2
    return pl.pallas_call(
        apply_kernel,
        in_specs=[inside] * 22,
        out_specs=[inside] * 16 + anywhere,
        out_shape=shapes,
        scratch_shapes=[
            pltpu.VMEM(passed[1].shape, F32),
            pltpu.SemaphoreType.DMA((5,)),
        ],
        compiler_params=params(),
        name="apply",
    )(*changes, sums, *weights, *means, *squares, *passed)


def make_body(sizes):
    def body(
        tokens, cotangent, segments,
        qkv_weight, out_weight, inner_weight, outer_weight, vectors,
        qkv_mean, out_mean, inner_mean, outer_mean, vector_mean,
        qkv_square, out_square, inner_square, outer_square, vector_square,
    ):
        groups = sizes[1]
        token_count, width = tokens.shape
        length = segments.shape[1]
        seqs = token_count // length
        cols = qkv_weight.shape[2]
        tensor_index = lax.axis_index("tensor")
        weights = (qkv_weight, out_weight, inner_weight, outer_weight, vectors)
        old_means = (qkv_mean, out_mean, inner_mean, outer_mean, vector_mean)
        old_squares = (qkv_square, out_square, inner_square, outer_square, vector_square)
        if sizes[0] % 2 == 0 and groups == 4 and qkv_weight.shape[1] == sum(C_ROWS[-1]):
            weights, old_means, old_squares = (
                entry[:3] + (entry[3].T, entry[4]) for entry in (weights, old_means, old_squares)
            )
            wa, wb, wc, hid, nlt, xt, n1, full, pm, lse, slope, second, inv1 = gather_attend(
                weights, tokens, segments, sizes
            )
            result, gb, gm, gbt, accb, part, vg, bg = layer(
                cotangent, hid, slope, second, n1, inv1, nlt, wa, wb, wc, full, sizes
            )
            *changes, sums, input_grad = back(
                pm, gm, lse, segments, wa, xt, gbt, gb, accb, part, vg, bg,
                weights, old_means, old_squares, sizes,
            )
            passed = (result, input_grad)
            new = list(
                apply(changes, sums, weights, old_means, old_squares, passed)
            )
            new[9:12] = [entry.T for entry in new[9:12]]
            return tuple(new[16:]) + tuple(new[:16])
        seg = lax.dynamic_slice_in_dim(segments, tensor_index * seqs, seqs, 0)
        seg = jnp.broadcast_to(seg[:, None, :], (seqs, 8, length))
        pack_a = spread(qkv_weight[0], qkv_weight[1], qkv_weight[2], out_weight.T).astype(BF16)
        pack_b = inner_weight.astype(BF16)
        pack_c = outer_weight.T.astype(BF16)
        wa, wb, wc = (gather_blocks(pack, sizes) for pack in (pack_a, pack_b, pack_c))
        full = lax.all_gather(vectors, ("dp", "tensor"), axis=1, tiled=True)
        q_bias = full[6].reshape(groups, cols)
        v_bias = full[7].reshape(groups, cols)
        none = jnp.zeros_like(q_bias)
        proj_bias = spread(q_bias, none, v_bias, none)
        proj_bias = jnp.broadcast_to(proj_bias[:, None, :], (groups, 8, 4 * cols))
        inner_bias = full[8:].reshape(groups, -1)
        pm, lse = attend_fwd(tokens, wa, proj_bias, seg, length)
        result, hid, gi, nl, gsl, gbl, gb, gm, vg, bg = ffn(
            tokens, cotangent, pm, wa, wb, wc, full, inner_bias
        )
        gp, gsum = attend_bwd(pm, gm, lse, seg)

        grad_c = jnp.einsum("td,gtf->gdf", gsl, hid, preferred_element_type=F32).astype(BF16)
        grad_b = jnp.einsum("td,gtf->gdf", nl, gi, preferred_element_type=F32).astype(BF16)
        from_tokens = jnp.einsum("td,gtc->gdc", tokens, gp, preferred_element_type=F32)
        from_branch = jnp.einsum("td,gtc->gdc", gbl, pm, preferred_element_type=F32)
        lane = lax.broadcasted_iota(jnp.int32, (1, 1, LANES), 2)
        is_mixed = (lane >= 512) & ((lane < 640) | (lane >= 704))
        grad_a = jnp.where(is_mixed, from_branch, from_tokens).astype(BF16)
        input_grad = gb + jnp.einsum(
            "gtc,gdc->td",
            jnp.where(is_mixed, jnp.zeros((), BF16), gp),
            wa,
            preferred_element_type=F32,
        )
        head_rows = jnp.stack([collect(gsum[:, 0], at).reshape(-1) for at in (Q_AT, V_AT)])
        vector_grad = jnp.concatenate([vg[:6], head_rows, bg[:groups].reshape(-1, width)], axis=0)
        sum_a, sum_b, sum_c = (
            scatter_blocks(grad, sizes).astype(F32) for grad in (grad_a, grad_b, grad_c)
        )
        vector_sum = lax.psum_scatter(
            vector_grad, ("dp", "tensor"), scatter_dimension=1, tiled=True
        )
        new = lamb_plain(sum_a, sum_b, sum_c, vector_sum, weights, old_means, old_squares)
        return (result, input_grad) + tuple(new)

    return body

def solution(mesh):
    sizes = (mesh.shape["dp"], mesh.shape["tensor"])
    rows = P(("dp", "tensor"), None)
    qkv = P(None, "dp", "tensor")
    out = P("tensor", "dp")
    inner = P("dp", "tensor")
    vec = P(None, ("dp", "tensor"))
    weights = (qkv, out, inner, out, vec)
    return jax.shard_map(
        make_body(sizes),
        mesh=mesh,
        in_specs=(rows, rows, P("dp", None)) + weights * 3,
        out_specs=(rows, rows) + (qkv,) * 3 + (out,) * 3 + (inner,) * 3 + (out,) * 3 + (vec,) * 3 + (P(),),
        check_vma=False,
    )
```

```python
import functools

import jax
import jax.numpy as jnp
from jax import lax
from jax.experimental import pallas as pl
from jax.experimental.pallas import tpu as pltpu
from jax.sharding import PartitionSpec as P

HD = 64
STEP = 5
NORM_EPS = 1e-05
ADAM_EPS = 1e-06
MOMENT_DECAY = 0.5
LEARN_RATE = 0.5
WEIGHT_DECAY = 0.01
MASKED = -1e30
SCALE = HD ** (-0.5)
F32 = jnp.float32
BF16 = jnp.bfloat16
NT = (((1,), (1,)), ((), ()))
NN = (((1,), (0,)), ((), ()))
TN = (((0,), (0,)), ((), ()))
VMEM_LIMIT = 60 * 1024 * 1024


def dot(a, b, dims=NN):
    return lax.dot_general(a, b, dims, preferred_element_type=F32)


def params(**kw):
    return pltpu.CompilerParams(vmem_limit_bytes=VMEM_LIMIT, **kw)


HEADS = 3
DOCS = 4
LANES = 768
Q_AT, K_AT, V_AT, O_AT = (0, 64, 384), (128, 192, 640), (256, 320, 448), (512, 576, 704)
Q_TILE, K_TILE, V_TILE = (0, 0, 3), (1, 1, 5), (2, 2, 3)
UPPER = (False, True, False)
V_UPPER = (False, True, True)


def spread(q, k, v, o):
    parts = {}
    for places, values in ((Q_AT, q), (K_AT, k), (V_AT, v), (O_AT, o)):
        for h, at in enumerate(places):
            parts[at] = values[:, h * HD : (h + 1) * HD]
    return jnp.concatenate([parts[at] for at in sorted(parts)], axis=1)


def collect(values, places):
    return jnp.concatenate([values[:, at : at + HD] for at in places], axis=1)


def tile_of(ref, n, rows=slice(None)):
    return ref[rows, n * 128 : (n + 1) * 128]


def is_low(shape):
    return lax.broadcasted_iota(jnp.int32, shape, 1) < HD


def halves(low, high):
    return jnp.where(is_low(low.shape), low, high)


def document_lanes(row):
    length = row.shape[1]
    number = jnp.broadcast_to(row.astype(F32), (128, length)).T
    lane = lax.broadcasted_iota(jnp.int32, (length, 128), 1) % HD
    same = number == lane.astype(F32)
    for_query = jnp.where(same, 1.0, 0.0).astype(BF16)
    for_key = jnp.where(same, 0.0, jnp.where(lane < DOCS, MASKED, 0.0)).astype(BF16)
    return for_query, for_key


def attend_heads(pm_ref, row, lse_ref, chunk):
    length = pm_ref.shape[0]
    chunks = length // chunk
    doc_q, doc_k = document_lanes(row)
    ones = jnp.ones((16, length), BF16)
    units = [(h, c) for h in range(HEADS) for c in range(chunks)]
    keys, queries, values = {}, {}, {}
    for h in range(HEADS):
        q, k = tile_of(pm_ref, Q_TILE[h]) * SCALE, tile_of(pm_ref, K_TILE[h])
        queries[h] = halves(doc_q, q) if UPPER[h] else halves(q, doc_q)
        keys[h] = halves(doc_k, k) if UPPER[h] else halves(k, doc_k)
        vt = tile_of(pm_ref, V_TILE[h]).T
        vt = vt[HD:] if V_UPPER[h] else vt[:HD]
        values[h] = jnp.concatenate([vt, ones], axis=0)

    def scores(unit):
        h, c = unit
        return dot(keys[h], queries[h][c * chunk : (c + 1) * chunk], NT)

    outs = {h: [] for h in range(HEADS)}
    ahead = scores(units[0])
    for n, (h, c) in enumerate(units):
        s = ahead
        if n + 1 < len(units):
            ahead = scores(units[n + 1])
        m = jnp.max(s, axis=0, keepdims=True)
        p = jnp.exp(s - m).astype(BF16)
        ot = dot(values[h], p)
        total = ot[HD : HD + 1]
        outs[h].append((ot[:HD] * (1.0 / total)).astype(BF16))
        lse_ref[0, 0, h : h + 1, c * chunk : (c + 1) * chunk] = m + jnp.log(total)
    out = [jnp.concatenate(outs[h], axis=1) for h in range(HEADS)]
    pm_ref[:, 512:640] = jnp.concatenate([out[0], out[1]], axis=0).T
    last = jnp.concatenate([jnp.zeros_like(out[2]), out[2]], axis=0).T
    pm_ref[:, 640:768] = halves(tile_of(pm_ref, 5), last)


def attend_fwd_kernel(x_ref, w_ref, bias_ref, seg_ref, pm_ref, lse_ref, *, chunk):
    proj = dot(x_ref[...], w_ref[0]) + bias_ref[0, 0:1, :]
    pm_ref[0] = proj.astype(BF16)
    attend_heads(pm_ref.at[0], seg_ref[0, 0:1], lse_ref, chunk)


def attend_fwd(x, wa, bias, seg, length):
    tokens, width = x.shape
    groups, _, lanes = wa.shape
    seqs = tokens // length
    return pl.pallas_call(
        functools.partial(attend_fwd_kernel, chunk=min(256, length)),
        grid=(groups, seqs),
        in_specs=[
            pl.BlockSpec((length, width), lambda t, s: (s, 0)),
            pl.BlockSpec((1, width, lanes), lambda t, s: (t, 0, 0)),
            pl.BlockSpec((1, 8, lanes), lambda t, s: (t, 0, 0)),
            pl.BlockSpec((1, 8, length), lambda t, s: (s, 0, 0)),
        ],
        out_specs=[
            pl.BlockSpec((1, length, lanes), lambda t, s: (t, s, 0)),
            pl.BlockSpec((1, 1, 8, length), lambda t, s: (t, s, 0, 0)),
        ],
        out_shape=[
            jax.ShapeDtypeStruct((groups, tokens, lanes), BF16),
            jax.ShapeDtypeStruct((groups, seqs, 8, length), F32),
        ],
        compiler_params=params(),
        name="attend_fwd",
    )(x, wa, bias, seg)


def attend_back(pm_ref, gm_ref, lse_ref, row, gp_ref, chunk):
    length = pm_ref.shape[0]
    chunks = length // chunk
    prod = gm_ref[...].astype(F32) * pm_ref[:, 512:768].astype(F32)
    hi = prod.astype(BF16)
    lo = (prod - hi.astype(F32)).astype(BF16)
    lane = lax.broadcasted_iota(jnp.int32, (8, 256), 1)
    line = lax.broadcasted_iota(jnp.int32, (8, 256), 0)
    start = jnp.where(line == 2, O_AT[2] - 512, line * HD)
    pick = jnp.where((lane >= start) & (lane < start + HD) & (line < HEADS), 1.0, 0.0).astype(BF16)
    dsum = dot(pick, hi, NT) + dot(pick, lo, NT)
    doc_q, doc_k = document_lanes(row)
    none = jnp.zeros((length, 128), BF16)
    units = [(h, c) for h in range(HEADS) for c in range(chunks)]
    keys, queries, plain, values, kts, grads = {}, {}, {}, {}, {}, {}
    for h in range(HEADS):
        q, k = tile_of(pm_ref, Q_TILE[h]) * SCALE, tile_of(pm_ref, K_TILE[h])
        plain[h] = q
        queries[h] = halves(doc_q, q) if UPPER[h] else halves(q, doc_q)
        keys[h] = halves(doc_k, k) if UPPER[h] else halves(k, doc_k)
        kt = k.T
        kts[h] = kt[HD:] if UPPER[h] else kt[:HD]
        v = tile_of(pm_ref, V_TILE[h])
        values[h] = halves(none, v) if V_UPPER[h] else halves(v, none)
        grads[h] = tile_of(gm_ref, 0 if h < 2 else 1)

    def rows_of(c):
        return slice(c * chunk, (c + 1) * chunk)

    def products(unit):
        h, c = unit
        return dot(keys[h], queries[h][rows_of(c)], NT), dot(values[h], grads[h][rows_of(c)], NT)

    dqs = {h: [] for h in range(HEADS)}
    dks, dvs = {}, {}
    ahead = products(units[0])
    for n, (h, c) in enumerate(units):
        s, dp = ahead
        if n + 1 < len(units):
            ahead = products(units[n + 1])
        rows = rows_of(c)
        p = jnp.exp(s - lse_ref[0, 0, h : h + 1, rows])
        ds = (p * (dp - dsum[h : h + 1, rows])).astype(BF16)
        dv = dot(p.astype(BF16), grads[h][rows])
        dk = dot(ds, plain[h][rows])
        dvs[h] = dv if c == 0 else dvs[h] + dv
        dks[h] = dk if c == 0 else dks[h] + dk
        dqs[h].append((dot(kts[h], ds) * SCALE).astype(BF16))
    dq = [jnp.concatenate(dqs[h], axis=1) for h in range(HEADS)]
    gp_ref[:, 0:128] = jnp.concatenate([dq[0], dq[1]], axis=0).T
    gp_ref[:, 128:256] = halves(dks[0], dks[1]).astype(BF16)
    gp_ref[:, 256:384] = halves(dvs[0], dvs[1]).astype(BF16)
    last = jnp.concatenate([dq[2], jnp.zeros_like(dq[2])], axis=0).T
    gp_ref[:, 384:512] = halves(last, dvs[2].astype(BF16))
    gp_ref[:, 512:640] = tile_of(pm_ref, 4)
    gp_ref[:, 640:768] = halves(dks[2].astype(BF16), tile_of(pm_ref, 5))


def attend_bwd_kernel(pm_ref, gm_ref, lse_ref, seg_ref, gp_ref, gsum_ref, *, chunk):
    attend_back(pm_ref.at[0], gm_ref.at[0], lse_ref, seg_ref[0, 0:1], gp_ref.at[0], chunk)

    @pl.when(pl.program_id(1) == 0)
    def _():
        gsum_ref[...] = jnp.zeros_like(gsum_ref)

    gsum_ref[0, 0:1, :] += jnp.sum(gp_ref[0].astype(F32), axis=0, keepdims=True)


def attend_bwd(pm, gm, lse, seg):
    groups, tokens, lanes = pm.shape
    seqs, length = lse.shape[1], lse.shape[3]
    return pl.pallas_call(
        functools.partial(attend_bwd_kernel, chunk=min(256, length)),
        grid=(groups, seqs),
        in_specs=[
            pl.BlockSpec((1, length, lanes), lambda t, s: (t, s, 0)),
            pl.BlockSpec((1, length, gm.shape[2]), lambda t, s: (t, s, 0)),
            pl.BlockSpec((1, 1, 8, length), lambda t, s: (t, s, 0, 0)),
            pl.BlockSpec((1, 8, length), lambda t, s: (s, 0, 0)),
        ],
        out_specs=[
            pl.BlockSpec((1, length, lanes), lambda t, s: (t, s, 0)),
            pl.BlockSpec((1, 8, lanes), lambda t, s: (t, 0, 0)),
        ],
        out_shape=[
            jax.ShapeDtypeStruct((groups, tokens, lanes), BF16),
            jax.ShapeDtypeStruct((groups, 8, lanes), F32),
        ],
        compiler_params=params(),
        name="attend_bwd",
    )(pm, gm, lse, seg)


def mixed_only(tail):
    lane = lax.broadcasted_iota(jnp.int32, tail.shape, 1)
    return jnp.where((lane < 128) | (lane >= 192), tail, jnp.zeros((), BF16))


def gelu_parts(pre):
    cdf = 0.5 * (1.0 + lax.erf(pre * (2.0**-0.5)))
    pdf = jnp.exp(-0.5 * pre * pre) * 0.3989422804014327
    return pre * cdf, cdf + pre * pdf


def mean_of(values):
    return jnp.mean(values, axis=-1, keepdims=True)


def norm_parts(values):
    centred = values - mean_of(values)
    inverse = lax.rsqrt(mean_of(centred * centred) + NORM_EPS)
    return centred * inverse, inverse


def norm_back(incoming, normal, inverse, gain):
    scaled = incoming * gain
    return inverse * (scaled - mean_of(scaled) - normal * mean_of(scaled * normal))


def ffn_kernel(
    x_ref, cot_ref, pm_ref, wo_ref, wb_ref, wc_ref, vec_ref, bias_ref,
    out_ref, hid_ref, gi_ref, nl_ref, gsl_ref, gbl_ref, gb_ref, gm_ref, vg_ref, bg_ref,
    slope_ref,
):
    groups = wb_ref.shape[0]

    @pl.when(pl.program_id(0) == 0)
    def _():
        vg_ref[...] = jnp.zeros_like(vg_ref)
        bg_ref[...] = jnp.zeros_like(bg_ref)

    total = x_ref[...].astype(F32) + vec_ref[4:5, :]
    for t in range(groups):
        total = total + dot(mixed_only(pm_ref[t]), wo_ref[t], NT)
    normal_one, inverse_one = norm_parts(total)
    normed = normal_one * vec_ref[0:1, :] + vec_ref[1:2, :]
    low = normed.astype(BF16)
    nl_ref[...] = low
    second = normed + vec_ref[5:6, :]
    for t in range(groups):
        pre = dot(low, wb_ref[t]) + bias_ref[t : t + 1, :]
        act, slope = gelu_parts(pre)
        act = act.astype(BF16)
        hid_ref[t] = act
        slope_ref[t] = slope
        second = second + dot(act, wc_ref[t], NT)
    normal_two, inverse_two = norm_parts(second)
    out_ref[...] = (normal_two * vec_ref[2:3, :] + vec_ref[3:4, :]).astype(BF16)
    cot = cot_ref[...].astype(F32)
    grad_second = norm_back(cot, normal_two, inverse_two, vec_ref[2:3, :])
    vg_ref[2:3, :] += jnp.sum(cot * normal_two, axis=0, keepdims=True)
    vg_ref[3:4, :] += jnp.sum(cot, axis=0, keepdims=True)
    vg_ref[5:6, :] += jnp.sum(grad_second, axis=0, keepdims=True)
    gs_low = grad_second.astype(BF16)
    gsl_ref[...] = gs_low
    grad_normed = grad_second
    for t in range(groups):
        grad_inner = (dot(gs_low, wc_ref[t]) * slope_ref[t]).astype(BF16)
        gi_ref[t] = grad_inner
        bg_ref[t : t + 1, :] += jnp.sum(grad_inner.astype(F32), axis=0, keepdims=True)
        grad_normed = grad_normed + dot(grad_inner, wb_ref[t], NT)
    grad_branch = norm_back(grad_normed, normal_one, inverse_one, vec_ref[0:1, :])
    vg_ref[0:1, :] += jnp.sum(grad_normed * normal_one, axis=0, keepdims=True)
    vg_ref[1:2, :] += jnp.sum(grad_normed, axis=0, keepdims=True)
    vg_ref[4:5, :] += jnp.sum(grad_branch, axis=0, keepdims=True)
    gb_ref[...] = grad_branch
    gb_low = grad_branch.astype(BF16)
    gbl_ref[...] = gb_low
    for t in range(groups):
        gm_ref[t] = dot(gb_low, wo_ref[t]).astype(BF16)


def ffn(x, cot, pm, wa, wb, wc, vec, bias):
    tokens, width = x.shape
    groups, _, lanes = wa.shape
    hidden = wb.shape[2]
    tail = 256
    tile = 256
    last = lanes // tail - 1
    once = pl.Buffered(1)
    row = pl.BlockSpec((tile, width), lambda i: (i, 0))
    wide = pl.BlockSpec((groups, tile, hidden), lambda i: (0, i, 0))
    return pl.pallas_call(
        ffn_kernel,
        grid=(tokens // tile,),
        in_specs=[
            row,
            row,
            pl.BlockSpec((groups, tile, tail), lambda i: (0, i, last)),
            pl.BlockSpec((groups, width, tail), lambda i: (0, 0, last), pipeline_mode=once),
            pl.BlockSpec((groups, width, hidden), lambda i: (0, 0, 0), pipeline_mode=once),
            pl.BlockSpec((groups, width, hidden), lambda i: (0, 0, 0), pipeline_mode=once),
            pl.BlockSpec(vec.shape, lambda i: (0, 0)),
            pl.BlockSpec(bias.shape, lambda i: (0, 0)),
        ],
        out_specs=[
            row,
            wide,
            wide,
            row,
            row,
            row,
            row,
            pl.BlockSpec((groups, tile, tail), lambda i: (0, i, 0)),
            pl.BlockSpec((8, width), lambda i: (0, 0)),
            pl.BlockSpec((8, hidden), lambda i: (0, 0)),
        ],
        out_shape=[
            jax.ShapeDtypeStruct((tokens, width), BF16),
            jax.ShapeDtypeStruct((groups, tokens, hidden), BF16),
            jax.ShapeDtypeStruct((groups, tokens, hidden), BF16),
            jax.ShapeDtypeStruct((tokens, width), BF16),
            jax.ShapeDtypeStruct((tokens, width), BF16),
            jax.ShapeDtypeStruct((tokens, width), BF16),
            jax.ShapeDtypeStruct((tokens, width), F32),
            jax.ShapeDtypeStruct((groups, tokens, tail), BF16),
            jax.ShapeDtypeStruct((8, width), F32),
            jax.ShapeDtypeStruct((8, hidden), F32),
        ],
        scratch_shapes=[pltpu.VMEM((groups, tile, hidden), F32)],
        compiler_params=params(),
        name="ffn",
    )(x, cot, pm, wa, wb, wc, vec, bias)


MESH = pl.DeviceIdType.MESH


class Place:
    def __init__(self, sizes):
        dp, tensor = lax.axis_index("dp"), lax.axis_index("tensor")
        self.deep = sizes[0] // 2
        self.z, self.y = dp // 2, dp % 2
        self.x, self.c = tensor // 2, tensor % 2

    def to_z(self, step):
        return {"dp": lax.rem(self.z + step, self.deep) * 2 + self.y}

    def to_y(self):
        return {"dp": self.z * 2 + 1 - self.y}

    def to_x(self):
        return {"tensor": (1 - self.x) * 2 + self.c}

    def to_c(self):
        return {"tensor": self.x * 2 + 1 - self.c}

    def far_z(self):
        if self.deep != 4:
            return list(range(1, self.deep))
        z = self.z
        return [
            jnp.where(z == 0, 3, jnp.where(z == 3, 1, 2)),
            jnp.where(z == 1, 3, jnp.where(z == 2, 1, 2)),
            jnp.where(z < 2, 1, 3),
        ]

    def from_z(self, step):
        return lax.rem(self.z + self.deep - step, self.deep)

    def partners(self):
        return [self.to_z(j) for j in range(1, self.deep)] + [self.to_y(), self.to_x(), self.to_c()]

    def peers(self):
        found = []
        for r in range(1, 8):
            x = 1 - self.x if r & 4 else self.x
            y = 1 - self.y if r & 2 else self.y
            c = 1 - self.c if r & 1 else self.c
            found.append((x * 4 + y * 2 + c, {"dp": self.z * 2 + y, "tensor": x * 2 + c}))
        return found

    def greet(self, everyone=False):
        barrier = pltpu.get_barrier_semaphore()
        partners = self.partners()
        if everyone:
            partners = partners[: self.deep - 1] + [device for _, device in self.peers()]
        for partner in partners:
            pl.semaphore_signal(barrier, inc=1, device_id=partner, device_id_type=MESH)
        pl.semaphore_wait(barrier, len(partners))


class Links:
    def __init__(self, send, recv):
        self.send, self.recv = send, recv

    def copy(self, k, ref, to, dst=None):
        return pltpu.make_async_remote_copy(
            src_ref=ref,
            dst_ref=ref if dst is None else dst,
            send_sem=self.send.at[k],
            recv_sem=self.recv.at[k],
            device_id=to,
            device_id_type=MESH,
        )

    def landed(self, k, ref, to):
        self.copy(k, ref, to).wait_recv()


def add_everywhere(place, links, base, own, slots):
    deep = place.deep
    hops = [place.to_c(), place.to_y(), place.to_x()]

    def start(i):
        def run():
            if i:
                links.copy(base + i - 1, own, hops[i - 1], slots.at[i - 1]).wait_send()
                links.landed(base + i - 1, slots.at[i - 1], hops[i - 1])
                own[...] = own[...] + slots[i - 1]
            if i < 3:
                links.copy(base + i, own, hops[i], slots.at[i]).start()
            else:
                for j in range(1, deep):
                    links.copy(base + 2 + j, own, place.to_z(j), slots.at[2 + j]).start()

        return run

    def last():
        for j in range(1, deep):
            links.copy(base + 2 + j, own, place.to_z(j), slots.at[2 + j]).wait_send()
            links.landed(base + 2 + j, slots.at[2 + j], place.to_z(j))
        slots[2] = own[...]
        total = slots[2 + lax.rem(place.z + deep, deep)]
        for z in range(1, deep):
            total = total + slots[2 + lax.rem(place.z + deep - z, deep)]
        own[...] = total

    return [start(0), start(1), start(2), start(3), last]


def add_in_two(place, links, base, own, slots):
    p, deep = place, place.deep
    me = p.x * 4 + p.y * 2 + p.c
    peers = p.peers()

    def near(r):
        return links.copy(base + r, own, peers[r - 1][1], slots.at[me])

    def far(j):
        return links.copy(base + 7 + j, own, p.to_z(j), slots.at[8 + p.z])

    def start():
        for r in range(1, 8):
            near(r).start()
        slots[me] = own[...]

    def middle():
        for r in range(1, 8):
            near(r).wait_send()
            links.landed(base + r, slots.at[peers[r - 1][0]], peers[r - 1][1])
        total = slots[0]
        for k in range(1, 8):
            total = total + slots[k]
        own[...] = total
        for j in p.far_z():
            far(j).start()
        slots[8 + p.z] = total

    def last():
        for j in range(1, deep):
            far(j).wait_send()
            links.landed(base + 7 + j, slots.at[8 + p.from_z(j)], p.to_z(j))
        total = slots[8]
        for k in range(1, deep):
            total = total + slots[8 + k]
        own[...] = total

    return [start, middle, last]


def gather_stages(place, links, base, own, whole, start=0, count=None):
    p, deep = place, place.deep
    count = own.shape[0] if count is None else count
    half = count // 2
    rows, first, later = pl.ds(start, count), pl.ds(start, half), pl.ds(start + half, half)
    own = own.at[rows]
    mine = whole.at[p.x, p.c, p.z, p.y, rows]
    line = whole.at[p.x, p.c, :, p.y, rows]
    ax = whole.at[p.x, p.c, :, p.y, first]
    ax_in = whole.at[1 - p.x, p.c, :, p.y, first]
    by = whole.at[p.x, p.c, :, p.y, later]
    by_in = whole.at[p.x, p.c, :, 1 - p.y, later]
    ay = whole.at[:, p.c, :, p.y, first]
    ay_in = whole.at[:, p.c, :, 1 - p.y, first]
    bx = whole.at[p.x, p.c, :, :, later]
    bx_in = whole.at[1 - p.x, p.c, :, :, later]
    kz, ka, kb, ks = base, base + deep, base + deep + 2, base + deep + 4

    def keep():
        return pltpu.make_async_copy(own, mine, links.send.at[kz])

    def stage0():
        keep().start()
        for j in p.far_z():
            links.copy(kz + j, own, p.to_z(j), mine).start()

    def stage1():
        keep().wait()
        for j in range(1, deep):
            links.landed(kz + j, whole.at[p.x, p.c, p.from_z(j), p.y, rows], p.to_z(j))
        links.copy(ka, ax, p.to_x()).start()
        links.copy(kb, by, p.to_y()).start()
        links.copy(ks, line, p.to_c()).start()

    def stage2():
        links.landed(ka, ax_in, p.to_x())
        links.copy(ka + 1, ay, p.to_y()).start()
        links.copy(ks + 1, ax_in, p.to_c()).start()
        links.landed(kb, by_in, p.to_y())
        links.copy(kb + 1, bx, p.to_x()).start()
        links.copy(ks + 2, by_in, p.to_c()).start()

    def stage3():
        links.landed(ka + 1, ay_in, p.to_y())
        links.copy(ks + 3, ay_in, p.to_c()).start()
        links.landed(kb + 1, bx_in, p.to_x())
        links.copy(ks + 4, bx_in, p.to_c()).start()

    def stage4():
        o = 1 - p.c
        links.landed(ks, whole.at[p.x, o, :, p.y, rows], p.to_c())
        links.landed(ks + 1, whole.at[1 - p.x, o, :, p.y, first], p.to_c())
        links.landed(ks + 2, whole.at[p.x, o, :, 1 - p.y, later], p.to_c())
        links.landed(ks + 3, whole.at[:, o, :, 1 - p.y, first], p.to_c())
        links.landed(ks + 4, whole.at[1 - p.x, o, :, :, later], p.to_c())
        for j in range(1, deep):
            links.copy(kz + j, own, p.to_z(j), mine).wait_send()
        links.copy(ka, ax, p.to_x()).wait_send()
        links.copy(kb, by, p.to_y()).wait_send()
        links.copy(ka + 1, ay, p.to_y()).wait_send()
        links.copy(kb + 1, bx, p.to_x()).wait_send()
        links.copy(ks, line, p.to_c()).wait_send()
        links.copy(ks + 1, ax_in, p.to_c()).wait_send()
        links.copy(ks + 2, by_in, p.to_c()).wait_send()
        links.copy(ks + 3, ay_in, p.to_c()).wait_send()
        links.copy(ks + 4, bx_in, p.to_c()).wait_send()

    return [stage0, stage1, stage2, stage3, stage4]


def gather_stages_late(place, links, base, own, whole, start=0, count=None):
    p, deep = place, place.deep
    count = own.shape[0] if count is None else count
    half = count // 2
    rows, first, later = pl.ds(start, count), pl.ds(start, half), pl.ds(start + half, half)
    mine = whole.at[p.x, p.c, p.z, p.y]
    pair_f, pair_l = whole.at[:, p.c, p.z, p.y, first], whole.at[p.x, p.c, p.z, :, later]
    line_f, line_l = whole.at[:, p.c, :, p.y, first], whole.at[p.x, p.c, :, :, later]
    line_f_in = whole.at[:, p.c, :, 1 - p.y, first]
    line_l_in = whole.at[1 - p.x, p.c, :, :, later]
    kf, kl = base + 8, base + 8 + deep

    def keep():
        return pltpu.make_async_copy(own.at[rows], mine.at[rows], links.send.at[base])

    def to_x():
        return links.copy(base + 1, own.at[first], p.to_x(), mine.at[first])

    def to_y():
        return links.copy(base + 2, own.at[later], p.to_y(), mine.at[later])

    def stage0():
        keep().start()
        to_x().start()
        to_y().start()

    def stage1():
        keep().wait()
        links.landed(base + 1, whole.at[1 - p.x, p.c, p.z, p.y, first], p.to_x())
        links.landed(base + 2, whole.at[p.x, p.c, p.z, 1 - p.y, later], p.to_y())
        for j in p.far_z():
            links.copy(kf + j, pair_f, p.to_z(j)).start()
            links.copy(kl + j, pair_l, p.to_z(j)).start()

    def stage2():
        for j in range(1, deep):
            z = p.from_z(j)
            links.landed(kf + j, whole.at[:, p.c, z, p.y, first], p.to_z(j))
            links.landed(kl + j, whole.at[p.x, p.c, z, :, later], p.to_z(j))
        links.copy(base + 3, line_f, p.to_y()).start()
        links.copy(base + 4, line_l, p.to_x()).start()
        links.copy(base + 5, line_f, p.to_c()).start()
        links.copy(base + 6, line_l, p.to_c()).start()

    def stage3():
        links.landed(base + 3, line_f_in, p.to_y())
        links.copy(base + 7, line_f_in, p.to_c()).start()
        links.landed(base + 4, line_l_in, p.to_x())
        links.copy(base + 8, line_l_in, p.to_c()).start()

    def stage4():
        o = 1 - p.c
        links.landed(base + 5, whole.at[:, o, :, p.y, first], p.to_c())
        links.landed(base + 6, whole.at[p.x, o, :, :, later], p.to_c())
        links.landed(base + 7, whole.at[:, o, :, 1 - p.y, first], p.to_c())
        links.landed(base + 8, whole.at[1 - p.x, o, :, :, later], p.to_c())
        to_x().wait_send()
        to_y().wait_send()
        for j in range(1, deep):
            links.copy(kf + j, pair_f, p.to_z(j)).wait_send()
            links.copy(kl + j, pair_l, p.to_z(j)).wait_send()
        links.copy(base + 3, line_f, p.to_y()).wait_send()
        links.copy(base + 4, line_l, p.to_x()).wait_send()
        links.copy(base + 5, line_f, p.to_c()).wait_send()
        links.copy(base + 6, line_l, p.to_c()).wait_send()
        links.copy(base + 7, line_f_in, p.to_c()).wait_send()
        links.copy(base + 8, line_l_in, p.to_c()).wait_send()

    return [stage0, stage1, stage2, stage3, stage4]


GATHER_COPIES = 9


def add_into(out, one, two):
    out[...] = one[...] + two[...]


def scatter_core(place, links, base, acc, in_c):
    def move(part):
        return links.copy(base + part, acc.at[2 + part], place.to_c(), in_c.at[part])

    def send(part):
        return lambda: move(part).start()

    def add(part, x):
        def run():
            move(part).wait_send()
            links.landed(base + part, in_c.at[part], place.to_c())

            def one(z, _):
                for y in range(2):
                    there = acc.at[x, z, y]
                    add_into(there, there, in_c.at[part, z, y])
                return 0

            lax.fori_loop(0, place.deep, one, 0)

        return run

    return send, add


def add_line(place, acc, x, y, rows, arrived):
    def add(z, _):
        there = acc.at[x, z, y, rows]
        add_into(there, there, arrived.at[z])
        return 0

    lax.fori_loop(0, place.deep, add, 0)


def scatter_plane(place, links, base, acc, ay_in, ax_in, bx_in, by_in):
    p = place
    half = acc.shape[3] // 2
    first, later, both = pl.ds(0, half), pl.ds(half, half), pl.ds(0, 2)

    def ay():
        return links.copy(base, acc.at[both, :, 1 - p.y, first], p.to_y(), ay_in)

    def bx():
        return links.copy(base + 1, acc.at[1 - p.x, :, :, later], p.to_x(), bx_in)

    def ax():
        return links.copy(base + 2, acc.at[1 - p.x, :, p.y, first], p.to_x(), ax_in)

    def by():
        return links.copy(base + 3, acc.at[p.x, :, 1 - p.y, later], p.to_y(), by_in)

    def start():
        ay().start()
        bx().start()

    def middle():
        links.landed(base, ay_in, p.to_y())
        for x in range(2):
            add_line(p, acc, x, p.y, first, ay_in.at[x])
        ax().start()
        links.landed(base + 1, bx_in, p.to_x())
        for y in range(2):
            add_line(p, acc, p.x, y, later, bx_in.at[:, y])
        by().start()

    def finish():
        links.landed(base + 2, ax_in, p.to_x())
        add_line(p, acc, p.x, p.y, first, ax_in)
        links.landed(base + 3, by_in, p.to_y())
        add_line(p, acc, p.x, p.y, later, by_in)

    def settle():
        for move in (ay, bx, ax, by):
            move().wait_send()

    return start, middle, finish, settle


def scatter_in_pairs(place, links, base, acc, in_c, ay_in, ax_in, bx_in, by_in, in_z, out):
    p, deep = place, place.deep
    half = acc.shape[3] // 2
    first, later = pl.ds(0, half), pl.ds(half, half)
    far, near = 1 - p.x, p.x
    kf, kl = base + 6, base + 6 + deep
    send, add = scatter_core(place, links, base, acc, in_c)

    def over_y(part, x):
        return links.copy(base + 2 + part, acc.at[x, :, 1 - p.y, first], p.to_y(), ay_in.at[part])

    def far_later():
        return links.copy(base + 4, acc.at[far, :, :, later], p.to_x(), bx_in)

    def far_first():
        return links.copy(base + 5, acc.at[far, :, p.y, first], p.to_x(), ax_in)

    def near_later():
        return links.copy(base + 6, acc.at[near, :, 1 - p.y, later], p.to_y(), by_in)

    def over_z(k, j, rows):
        to = lax.rem(p.z + j, deep)
        return links.copy(k + j, acc.at[near, to, p.y, rows], p.to_z(j), in_z.at[j, rows])

    def far1():
        add(0, far)()
        over_y(0, far).start()
        far_later().start()

    def far2():
        links.landed(base + 2, ay_in.at[0], p.to_y())
        add_line(p, acc, far, p.y, first, ay_in.at[0])
        far_first().start()

    def near1():
        over_y(1, near).start()

    def near_x():
        links.landed(base + 4, bx_in, p.to_x())
        for y in range(2):
            add_line(p, acc, near, y, later, bx_in.at[:, y])
        near_later().start()

    def near2():
        links.landed(base + 3, ay_in.at[1], p.to_y())
        add_line(p, acc, near, p.y, first, ay_in.at[1])
        links.landed(base + 5, ax_in, p.to_x())
        add_line(p, acc, near, p.y, first, ax_in)
        for j in p.far_z():
            over_z(kf, j, first).start()

    def near3():
        links.landed(base + 6, by_in, p.to_y())
        add_line(p, acc, near, p.y, later, by_in)
        for j in p.far_z():
            over_z(kl, j, later).start()

    def near4():
        for k, rows in ((kf, first), (kl, later)):
            total = acc[near, p.z, p.y, rows].astype(F32)
            for j in range(1, deep):
                links.landed(k + j, in_z.at[j, rows], p.to_z(j))
                total = total + in_z[j, rows].astype(F32)
            out[rows] = total
            for j in range(1, deep):
                over_z(k, j, rows).wait_send()
        over_y(0, far).wait_send()
        over_y(1, near).wait_send()
        far_later().wait_send()
        far_first().wait_send()
        near_later().wait_send()

    return [send(0), far1, far2, send(1), add(1, near), near1, near_x, near2, near3, near4]


def scatter_tail(place, links, base, part, in_z, out):
    deep = place.deep

    def send(j):
        return links.copy(
            base + j, part.at[lax.rem(place.z + j, deep)], place.to_z(j), in_z.at[j]
        )

    def stage0():
        for j in place.far_z():
            send(j).start()

    def stage1():
        for j in range(1, deep):
            links.landed(base + j, in_z.at[j], place.to_z(j))
        total = part[place.z].astype(F32)
        for j in range(1, deep):
            total = total + in_z[j].astype(F32)
        out[...] = total
        for j in range(1, deep):
            send(j).wait_send()

    return [stage0, stage1]


def core_buffers(deep, rows, lanes):
    return [
        pltpu.VMEM((4, deep, 2, rows, lanes), BF16),
        pltpu.VMEM((2, deep, 2, rows, lanes), BF16),
    ]


def plane_buffers(deep, rows, lanes):
    half = rows // 2
    return [
        pltpu.VMEM((2, deep, half, lanes), BF16),
        pltpu.VMEM((deep, half, lanes), BF16),
        pltpu.VMEM((deep, 2, half, lanes), BF16),
        pltpu.VMEM((deep, half, lanes), BF16),
    ]


def gather_blocks(block, sizes):
    whole = lax.all_gather(block, ("dp", "tensor"), axis=0, tiled=False)
    whole = whole.reshape(sizes + block.shape)
    return jnp.swapaxes(whole, 0, 1).reshape((sizes[1], -1) + block.shape[1:])


def scatter_blocks(grads, sizes):
    parts = grads.reshape((sizes[1], sizes[0], -1) + grads.shape[2:])
    parts = jnp.swapaxes(parts, 0, 1).reshape((sizes[0] * sizes[1],) + parts.shape[2:])
    return lax.psum_scatter(parts, ("dp", "tensor"), scatter_dimension=0, tiled=False)


def adam_parts(grad, mean, square):
    new_mean = MOMENT_DECAY * mean + (1.0 - MOMENT_DECAY) * grad
    new_square = MOMENT_DECAY * square + (1.0 - MOMENT_DECAY) * grad * grad
    correction = 1.0 - MOMENT_DECAY**STEP
    direction = new_mean / correction / (jnp.sqrt(new_square / correction) + ADAM_EPS)
    return new_mean, new_square, direction


def sum_all(values):
    return jnp.sum(jnp.sum(values, axis=1, keepdims=True), axis=0, keepdims=True)


def group_squares(qkv_part, out_part, inner_part, outer_part, vector_part):
    return jnp.concatenate(
        [
            jnp.sum(qkv_part * qkv_part, axis=(1, 2)),
            jnp.sum(out_part * out_part)[None],
            jnp.sum(inner_part * inner_part)[None],
            jnp.sum(outer_part * outer_part)[None],
            jnp.sum(vector_part[:8] * vector_part[:8], axis=1),
            jnp.sum(vector_part[8:] * vector_part[8:])[None],
        ]
    )


def lamb_apply(weight_list, update_list, trust_ratio, row_number):
    qkv_new = weight_list[0] - LEARN_RATE * trust_ratio[0:3, None, None] * update_list[0]
    out_new = weight_list[1] - LEARN_RATE * trust_ratio[3] * update_list[1]
    inner_new = weight_list[2] - LEARN_RATE * trust_ratio[4] * update_list[2]
    outer_new = weight_list[3] - LEARN_RATE * trust_ratio[5] * update_list[3]
    row_ratio = jnp.concatenate(
        [trust_ratio[6:14], jnp.broadcast_to(trust_ratio[14], (row_number - 8,))]
    )
    vector_new = weight_list[4] - LEARN_RATE * row_ratio[:, None] * update_list[4]
    return (qkv_new, out_new, inner_new, outer_new, vector_new)


def lamb_plain(sum_a, sum_b, sum_c, vector_sum, weights, old_means, old_squares):
    qkv_sum = jnp.stack([collect(sum_a, at) for at in (Q_AT, K_AT, V_AT)])
    grad_sums = (qkv_sum, collect(sum_a, O_AT).T, sum_b, sum_c.T, vector_sum)
    decays = (WEIGHT_DECAY, WEIGHT_DECAY, WEIGHT_DECAY, WEIGHT_DECAY, 0.0)
    stats = [adam_parts(*entry) for entry in zip(grad_sums, old_means, old_squares)]
    updates = [stats[i][2] + decays[i] * weights[i] for i in range(5)]
    weight_squares, update_squares = lax.psum(
        (group_squares(*weights), group_squares(*updates)), ("dp", "tensor")
    )
    weight_norms = jnp.sqrt(weight_squares)
    update_norms = jnp.sqrt(update_squares)
    trust_ratio = weight_norms / (update_norms + ADAM_EPS)
    new = lamb_apply(weights, updates, trust_ratio, weights[4].shape[0])
    outs = []
    for i in range(5):
        outs += [stats[i][0], stats[i][1], new[i]]
    return outs + [jnp.stack([weight_norms, update_norms])]


A_PIECES = 3
C_ROWS = ((0, 64), (64, 32))


def own_first(order):
    tensor = lax.axis_index("tensor")
    x, c = tensor // 2, tensor % 2
    return jnp.where(order % 2 == 0, x, 1 - x) * 2 + jnp.where(order < 2, c, 1 - c)


def gather_attend_kernel(
    qkv_ref, out_ref, inner_ref, outer_ref, vec_ref, x_ref, seg_ref,
    wa_hbm, wb_hbm, wc_hbm, hid_hbm, nlt_hbm, xt_hbm, n1_hbm,
    full, pm_ref, lse_ref, slope_ref, acc, inv_ref,
    send, recv, slots, pack_a, pack_b, pack_c, wa, wb, wc, hid, nlt_ref, xt_ref, n1_ref,
    bias, low, out_sem, xp, proj_acc,
    *, sizes, chunk,
):
    step = pl.program_id(0)
    groups, deep = sizes[1], sizes[0] // 2
    place = Place(sizes)
    links = Links(send, recv)
    each = GATHER_COPIES + deep
    cols = qkv_ref.shape[2]
    tokens, width = x_ref.shape
    lanes = pack_a.shape[1]
    length = tokens // 2
    tail = 256
    count = pack_a.shape[0] // A_PIECES
    ga = [
        gather_stages(place, links, k * each, pack_a, wa, k * count, count) for k in range(A_PIECES)
    ]
    gb = gather_stages(place, links, A_PIECES * each, pack_b, wb)
    more = (A_PIECES + 1) * each
    small = add_everywhere(place, links, more, full, slots)
    more += deep + 2
    gc = [
        gather_stages_late(place, links, more + k * (each + deep), pack_c, wc, *rows)
        for k, rows in enumerate(C_ROWS)
    ]
    t, s = own_first(jnp.minimum(step // 2, groups - 1)), step % 2
    last = 4 * groups - 1

    def keep(k):
        pairs = (
            (wa, wa_hbm), (wb, wb_hbm), (wc, wc_hbm), (hid, hid_hbm),
            (nlt_ref, nlt_hbm), (xt_ref, xt_hbm), (n1_ref, n1_hbm),
        )
        return pltpu.make_async_copy(*pairs[k], out_sem.at[k])

    def project(piece):
        here = pl.ds(piece * count, count)
        for x in range(2):
            part = dot(xp[piece], wa[x, place.c, :, :, here].reshape(sizes[0] * count, lanes))
            proj_acc[x] = part if piece == 0 else proj_acc[x] + part

    @pl.when(step == 0)
    def _():
        out_rows = out_ref[...].T
        pack_a[...] = spread(qkv_ref[0], qkv_ref[1], qkv_ref[2], out_rows).astype(BF16)
        place.greet()
        for k in range(A_PIECES):
            ga[k][0]()
        pack_c[...] = outer_ref[...].astype(BF16)
        gc[0][0]()
        gc[1][0]()
        pack_b[...] = inner_ref[...].astype(BF16)
        xt_ref[...] = x_ref[...].T
        each_dp = pack_a.shape[0]
        for k in range(A_PIECES):
            picked = [
                xt_ref[dp * each_dp + k * count : dp * each_dp + (k + 1) * count]
                for dp in range(sizes[0])
            ]
            xp[k] = jnp.concatenate(picked, axis=0).T
        full[...] = jnp.zeros_like(full)
        mine = vec_ref.shape[1]
        full[0 : vec_ref.shape[0], 0:mine] = vec_ref[...]
        index = lax.axis_index("dp") * groups + lax.axis_index("tensor")
        full[...] = pltpu.roll(full[...], index * mine, 1)
        small[0]()
        small[1]()
        ga[0][1]()
        small[2]()
        ga[0][2]()
        ga[1][1]()
        small[3]()
        gb[0]()
        ga[2][1]()
        ga[1][2]()
        ga[2][2]()
        ga[0][3]()
        project(0)
        small[4]()
        for g in range(groups):
            bias[g] = jnp.zeros(bias.shape[1:], F32)
            for h in range(HEADS):
                mine = slice(g * cols + h * HD, g * cols + (h + 1) * HD)
                bias[g, 0:1, Q_AT[h] : Q_AT[h] + HD] = full[6:7, mine]
                bias[g, 0:1, V_AT[h] : V_AT[h] + HD] = full[7:8, mine]
        n1_ref[...] = x_ref[...].astype(F32) + full[4:5, :]
        ga[1][3]()
        project(1)
        ga[2][3]()
        project(2)

    @pl.when(step == groups)
    def _():
        gb[2]()
        gc[1][1]()
        for k in range(A_PIECES):
            ga[k][4]()
        keep(0).start()

    @pl.when(step == 1)
    def _():
        gb[1]()
        gc[0][1]()

    @pl.when(step == 2 * groups + 2)
    def _():
        gb[4]()
        keep(1).start()
        gc[1][2]()

    @pl.when(step == 3 * groups)
    def _():
        gc[0][3]()
        gc[1][3]()
        keep(3).start()

    @pl.when(step == 3 * groups + 2)
    def _():
        gc[0][4]()
        gc[1][4]()
        keep(2).start()

    @pl.when((step < groups) & (s == 0))
    def _():
        pm_ref[0] = (proj_acc[t // 2] + bias[t, 0:1]).astype(BF16)

    @pl.when((step >= groups) & (step < 2 * groups) & (s == 0))
    def _():
        weight = wa[t // 2, t % 2].reshape(width, lanes)
        for n in range(lanes // 256):
            here = slice(n * 256, (n + 1) * 256)
            proj = dot(x_ref[...], weight[:, here]) + bias[t, 0:1, here]
            pm_ref[0, :, here] = proj.astype(BF16)

    @pl.when(step < 2 * groups)
    def _():
        rows = pl.ds(pl.multiple_of(s * length, length), length)
        row = seg_ref[pl.ds(lax.axis_index("tensor") * 2 + s, 1)]
        attend_heads(pm_ref.at[0, rows], row, lse_ref, chunk)

    @pl.when((step < 2 * groups) & (s == 1))
    def _():
        mixed = mixed_only(pm_ref[0, :, lanes - tail :])
        weight = wa[t // 2, t % 2, :, :, :, lanes - tail :].reshape(width, tail)
        n1_ref[...] += dot(mixed, weight, NT)

    @pl.when(step == 2 * groups)
    def _():
        gc[0][2]()
        for r in range(tokens // 256):
            rows = slice(r * 256, (r + 1) * 256)
            normal_one, inverse_one = norm_parts(n1_ref[rows])
            n1_ref[rows] = normal_one
            inv_ref[rows] = inverse_one
            normed = normal_one * full[0:1, :] + full[1:2, :]
            acc[rows] = normed + full[5:6, :]
            part = normed.astype(BF16)
            low[rows] = part
            nlt_ref[:, rows] = part.T
        for k in range(4, 7):
            keep(k).start()
        gb[3]()

    @pl.when((step >= 2 * groups) & (step < 3 * groups))
    def _():
        g = own_first(step - 2 * groups)
        weight = wb[g // 2, g % 2].reshape(width, lanes)
        for n in range(lanes // 256):
            here = slice(n * 256, (n + 1) * 256)
            pre = dot(low[...], weight[:, here]) + full[pl.ds(8 + g, 1), here]
            act, turn = gelu_parts(pre)
            hid[g, :, here] = act.astype(BF16)
            slope_ref[0, :, here] = turn.astype(BF16)

    @pl.when(step >= 3 * groups)
    def _():
        g = own_first(step - 3 * groups)
        weight = wc[g // 2, g % 2].reshape(width, lanes)
        acc[...] += dot(hid[g], weight, NT)

    @pl.when(step == last)
    def _():
        for k in range(7):
            keep(k).wait()


def once(shape):
    return pl.BlockSpec(shape, lambda *_: (0,) * len(shape), pipeline_mode=pl.Buffered(1))


def gather_attend(weights, x, seg, sizes):
    qkv, out, inner, outer, vec = weights
    deep, groups = sizes[0] // 2, sizes[1]
    copies = (A_PIECES + 1) * (GATHER_COPIES + deep) + deep + 2
    copies += len(C_ROWS) * (GATHER_COPIES + 2 * deep)
    tokens, width = x.shape
    length = seg.shape[1]
    seqs = tokens // length
    rows, lanes = inner.shape
    steps = groups * seqs
    anywhere = pl.BlockSpec(memory_space=pl.ANY)
    parts = (2, 2, deep, 2, rows, lanes)
    whole = jax.ShapeDtypeStruct(parts, BF16)

    def now(i):
        i = jnp.minimum(i, steps - 1)
        return own_first(i // 2), i % 2

    def part(i):
        return own_first(jnp.clip(i - steps, 0, groups - 1))

    wa, wb, wc, hid, nlt, xt, n1, *rest = pl.pallas_call(
        functools.partial(gather_attend_kernel, sizes=sizes, chunk=min(256, length)),
        grid=(steps + 2 * groups,),
        in_specs=[once(w.shape) for w in weights]
        + [
            once(x.shape),
            once(seg.shape),
        ],
        out_specs=[anywhere] * 7
        + [
            once((16, width)),
            pl.BlockSpec((1, tokens, lanes), lambda i: (now(i)[0], 0, 0)),
            pl.BlockSpec((1, 1, 8, length), lambda i: (*now(i), 0, 0)),
            pl.BlockSpec((1, tokens, lanes), lambda i: (part(i), 0, 0)),
            once((tokens, width)),
            once((tokens, 1)),
        ],
        out_shape=[whole] * 3
        + [
            jax.ShapeDtypeStruct((groups, tokens, lanes), BF16),
            jax.ShapeDtypeStruct((width, tokens), BF16),
            jax.ShapeDtypeStruct((width, tokens), BF16),
            jax.ShapeDtypeStruct((tokens, width), F32),
            jax.ShapeDtypeStruct((16, width), F32),
            jax.ShapeDtypeStruct((groups, tokens, lanes), BF16),
            jax.ShapeDtypeStruct((groups, seqs, 8, length), F32),
            jax.ShapeDtypeStruct((groups, tokens, lanes), BF16),
            jax.ShapeDtypeStruct((tokens, width), F32),
            jax.ShapeDtypeStruct((tokens, 1), F32),
        ],
        scratch_shapes=[
            pltpu.SemaphoreType.DMA((copies,)),
            pltpu.SemaphoreType.DMA((copies,)),
            pltpu.VMEM((deep + 2, 16, width), F32),
            pltpu.VMEM((rows, lanes), BF16),
            pltpu.VMEM((rows, lanes), BF16),
            pltpu.VMEM((rows, lanes), BF16),
            pltpu.VMEM(parts, BF16),
            pltpu.VMEM(parts, BF16),
            pltpu.VMEM(parts, BF16),
            pltpu.VMEM((groups, tokens, lanes), BF16),
            pltpu.VMEM((width, tokens), BF16),
            pltpu.VMEM((width, tokens), BF16),
            pltpu.VMEM((tokens, width), F32),
            pltpu.VMEM((groups, 8, lanes), F32),
            pltpu.VMEM((tokens, width), BF16),
            pltpu.SemaphoreType.DMA((7,)),
            pltpu.VMEM((A_PIECES, tokens, width // A_PIECES), BF16),
            pltpu.VMEM((2, tokens, lanes), F32),
        ],
        compiler_params=params(collective_id=0, has_side_effects=True),
        name="gather_attend",
    )(*weights, x, seg)
    shape = (groups, sizes[0] * rows, lanes)
    return [wa.reshape(shape), wb.reshape(shape), wc.reshape(shape), hid, nlt, xt, n1] + rest


def other_first(order):
    c = lax.axis_index("tensor") % 2
    return order % 2 * 2 + jnp.where(order < 2, 1 - c, c)


def layer_kernel(
    cot_ref, hid_ref, slope_ref, inv_ref, vec_ref, second_hbm, n1_hbm, nlt_hbm, wa_hbm, wb_hbm,
    wc_hbm,
    out_hbm, gb_hbm, gm_hbm, gbt_hbm, accb_hbm, part_ref, vg_ref, bg_ref,
    n1_ref, nlt_ref, wo_ref, wb_ref, wc_ref, acc, low, gst, gi, out_ref, gm_ref, gbt_ref,
    in_sem, out_sem, send, recv, accc, in_cc, accb, in_cb, ay_in, ax_in, bx_in, by_in, *, sizes,
):
    step = pl.program_id(0)
    tokens, width = acc.shape
    groups, deep = sizes[1], sizes[0] // 2
    lanes = wa_hbm.shape[2]
    tail = wo_ref.shape[2]
    last = 2 * groups - 1
    place = Place(sizes)
    links = Links(send, recv)
    send_c, add_c = scatter_core(place, links, 0, accc, in_cc)
    send_b, add_b = scatter_core(place, links, 2, accb, in_cb)
    start, middle, finish, settle = scatter_plane(
        place, links, 4, accc, ay_in, ax_in, bx_in, by_in
    )
    blocks = [slice(r * 256, (r + 1) * 256) for r in range(tokens // 256)]
    columns = [slice(n * 256, (n + 1) * 256) for n in range(width // 256)]

    def outer(t):
        return pltpu.make_async_copy(wc_hbm.at[t], wc_ref.at[t], in_sem.at[t])

    def inner(t):
        return pltpu.make_async_copy(wb_hbm.at[t], wb_ref.at[t], in_sem.at[groups + t])

    def load(k):
        pairs = (
            (second_hbm, acc), (n1_hbm, n1_ref), (nlt_hbm, nlt_ref),
            (wa_hbm.at[:, :, pl.ds(lanes - tail, tail)], wo_ref),
        )
        return pltpu.make_async_copy(*pairs[k], in_sem.at[2 * groups + k])

    def store(k):
        pairs = (
            (out_ref, out_hbm), (gbt_ref, gbt_hbm), (accb.at[pl.ds(0, 2)], accb_hbm), (acc, gb_hbm)
        )
        return pltpu.make_async_copy(*pairs[k], out_sem.at[k])

    def store_mixed(t):
        return pltpu.make_async_copy(gm_ref.at[t], gm_hbm.at[t], out_sem.at[4 + t])

    @pl.when(step == 0)
    def _():
        load(0).start()
        for t in range(groups):
            outer(t).start()
            inner(t).start()
        for k in range(1, 4):
            load(k).start()
        place.greet()
        vg_ref[...] = jnp.zeros_like(vg_ref)
        bg_ref[...] = jnp.zeros_like(bg_ref)
        load(0).wait()
        for rows in blocks:
            normal_two, inverse_two = norm_parts(acc[rows])
            out_ref[rows] = (normal_two * vec_ref[2:3, :] + vec_ref[3:4, :]).astype(BF16)
            cot = cot_ref[rows].astype(F32)
            grad_second = norm_back(cot, normal_two, inverse_two, vec_ref[2:3, :])
            vg_ref[2:3, :] += jnp.sum(cot * normal_two, axis=0, keepdims=True)
            vg_ref[3:4, :] += jnp.sum(cot, axis=0, keepdims=True)
            vg_ref[5:6, :] += jnp.sum(grad_second, axis=0, keepdims=True)
            acc[rows] = grad_second
            part = grad_second.astype(BF16)
            low[rows] = part
            gst[:, rows] = part.T
        store(0).start()

    @pl.when(step < groups)
    def _():
        slot = lax.rem(step + 2, 4)
        for here in columns:
            part = dot(gst[...], hid_ref[0, :, here]).astype(BF16)
            accc[slot, :, :, :, here] = part.reshape(deep, 2, -1, 256)

    @pl.when(step == 1)
    def _():
        send_c(0)()

    @pl.when(step == 2)
    def _():
        send_c(1)()

    @pl.when(step == groups)
    def _():
        add_c(0, 0)()
        add_c(1, 1)()
        start()
        for t in range(groups):
            outer(t).wait()
            inner(t).wait()
        for k in range(1, 4):
            load(k).wait()

    @pl.when(step == last)
    def _():
        middle()

    @pl.when(step >= groups)
    def _():
        order = step - groups
        slot = lax.rem(order + 2, 4)
        t = other_first(order)
        for here in columns:
            grad_hidden = dot(low[...], wc_ref[t, :, here])
            part = (grad_hidden * slope_ref[0, :, here].astype(F32)).astype(BF16)
            gi[:, here] = part
            bg_ref[pl.ds(t, 1), here] = jnp.sum(part.astype(F32), axis=0, keepdims=True)
        acc[...] += dot(gi[...], wb_ref[t], NT)
        for here in columns:
            part = dot(nlt_ref[...], gi[:, here]).astype(BF16)
            accb[slot, :, :, :, here] = part.reshape(deep, 2, -1, 256)

    @pl.when(step == groups + 1)
    def _():
        send_b(0)()

    @pl.when(step == groups + 2)
    def _():
        send_b(1)()

    @pl.when(step == last)
    def _():
        for rows in blocks:
            grad_normed = acc[rows]
            normal_one = n1_ref[rows]
            grad_branch = norm_back(grad_normed, normal_one, inv_ref[rows], vec_ref[0:1, :])
            vg_ref[0:1, :] += jnp.sum(grad_normed * normal_one, axis=0, keepdims=True)
            vg_ref[1:2, :] += jnp.sum(grad_normed, axis=0, keepdims=True)
            vg_ref[4:5, :] += jnp.sum(grad_branch, axis=0, keepdims=True)
            acc[rows] = grad_branch
            part = grad_branch.astype(BF16)
            low[rows] = part
            gbt_ref[:, rows] = part.T
        store(3).start()
        store(1).start()
        for t in range(groups):
            gm_ref[t] = dot(low[...], wo_ref[t]).astype(BF16)
            store_mixed(t).start()
        add_b(0, 0)()
        add_b(1, 1)()
        store(2).start()
        finish()
        part_ref[...] = accc[place.x, :, place.y]
        settle()
        for k in range(4):
            store(k).wait()
        for t in range(groups):
            store_mixed(t).wait()


def layer(cot, hid, slope, second, n1, inv1, nlt, wa, wb, wc, vec, sizes):
    tokens, width = cot.shape
    groups, _, lanes = wa.shape
    hidden = wb.shape[2]
    deep = sizes[0] // 2
    rows = width // sizes[0]
    tail = 256
    anywhere = pl.BlockSpec(memory_space=pl.ANY)

    def used(i):
        return other_first(jnp.minimum(i, groups - 1))

    def back_group(i):
        return other_first(jnp.clip(i - groups, 0, groups - 1))

    copies = 8
    parts = (2, deep, 2, rows, hidden)
    matrix = pltpu.VMEM((groups, width, hidden), BF16)
    return pl.pallas_call(
        functools.partial(layer_kernel, sizes=sizes),
        grid=(2 * groups,),
        in_specs=[
            once(cot.shape),
            pl.BlockSpec((1, tokens, hidden), lambda i: (used(i), 0, 0)),
            pl.BlockSpec((1, tokens, hidden), lambda i: (back_group(i), 0, 0)),
            once(inv1.shape),
            once(vec.shape),
        ]
        + [anywhere] * 6,
        out_specs=[anywhere] * 5
        + [once((deep, rows, hidden)), once((8, width)), once((8, hidden))],
        out_shape=[
            jax.ShapeDtypeStruct((tokens, width), BF16),
            jax.ShapeDtypeStruct((tokens, width), F32),
            jax.ShapeDtypeStruct((groups, tokens, tail), BF16),
            jax.ShapeDtypeStruct((width, tokens), BF16),
            jax.ShapeDtypeStruct(parts, BF16),
            jax.ShapeDtypeStruct((deep, rows, hidden), BF16),
            jax.ShapeDtypeStruct((8, width), F32),
            jax.ShapeDtypeStruct((8, hidden), F32),
        ],
        scratch_shapes=[
            pltpu.VMEM(n1.shape, F32),
            pltpu.VMEM((width, tokens), BF16),
            pltpu.VMEM((groups, width, tail), BF16),
            matrix,
            matrix,
            pltpu.VMEM((tokens, width), F32),
            pltpu.VMEM((tokens, width), BF16),
            pltpu.VMEM((width, tokens), BF16),
            pltpu.VMEM((tokens, hidden), BF16),
            pltpu.VMEM((tokens, width), BF16),
            pltpu.VMEM((groups, tokens, tail), BF16),
            pltpu.VMEM((width, tokens), BF16),
            pltpu.SemaphoreType.DMA((2 * groups + 4,)),
            pltpu.SemaphoreType.DMA((4 + groups,)),
            pltpu.SemaphoreType.DMA((copies,)),
            pltpu.SemaphoreType.DMA((copies,)),
        ]
        + core_buffers(deep, rows, hidden) * 2
        + plane_buffers(deep, rows, hidden),
        compiler_params=params(collective_id=1, has_side_effects=True),
        name="layer",
    )(cot, hid, slope, inv1, vec, second, n1, nlt, wa, wb, wc)


def far_first(step, groups):
    tensor = lax.axis_index("tensor")
    x, c = tensor // 2, tensor % 2
    return jnp.where(step < groups, 1 - x, x) * 2 + jnp.where(step % groups < 2, 1 - c, c)


def changes_of(refs):
    qkv, out, hidden, vec = refs
    return [
        [qkv.at[k], out.at[k], hidden.at[k, 0], hidden.at[k, 1], vec.at[k]] for k in range(2)
    ]


def back_kernel(
    pm_ref, gm_ref, lse_ref, seg_ref, wa_hbm, xt_hbm, gbt_hbm, gb_hbm,
    accb_hbm, part_ref, vg_ref, bg_ref, *refs, sizes, chunk,
):
    weights, means, squares = refs[0:5], refs[5:10], refs[10:15]
    (grads, updates), norms, ig_ref = changes_of(refs[15:19]), refs[19], refs[20]
    gp, gsum, send, recv, slots, hslots, nslots, vec, hvec, load_sem, sa = refs[21:32]
    wa_ref, xt_ref, gbt_ref, gb_ref, accb, inz_b, inz_c = refs[32:39]
    bufs_b, bufs_a, acc = refs[39:43], refs[43:50], refs[43]
    sb, sc = grads[2], grads[3]
    step = pl.program_id(0)
    groups, deep = sizes[1], sizes[0] // 2
    cols = HEADS * HD
    tokens, width = gb_ref.shape
    lanes = pm_ref.shape[2]
    last = 2 * groups - 1
    length = pm_ref.shape[1]
    place = Place(sizes)
    links = Links(send, recv)
    a = scatter_in_pairs(place, links, 0, *bufs_a, sa)
    more = 7 + 2 * deep
    start, middle, finish, settle = scatter_plane(place, links, more, accb, *bufs_b)
    b = scatter_tail(place, links, more + 4, accb.at[place.x, :, place.y], inz_b, sb)
    c = scatter_tail(place, links, more + 4 + deep, part_ref, inz_c, sc)
    early = add_everywhere(place, links, more + 4 + 2 * deep, vec, slots)
    small = add_everywhere(place, links, more + 6 + 3 * deep, hvec, hslots)
    final = add_in_two(place, links, more + 8 + 4 * deep, norms, nslots)
    t, s = far_first(step, groups), step % 2

    def load(k):
        pairs = ((accb_hbm, accb), (xt_hbm, xt_ref), (gbt_hbm, gbt_ref), (wa_hbm, wa_ref), (gb_hbm, gb_ref))
        return pltpu.make_async_copy(*pairs[k], load_sem.at[k])

    @pl.when(step == 0)
    def _():
        load(0).start()
        place.greet(everyone=True)
        c[0]()
        load(0).wait()
        start()
        for k in range(1, 5):
            load(k).start()
        gsum[...] = jnp.zeros_like(gsum)
        vec[...] = jnp.zeros_like(vec)
        hvec[...] = jnp.zeros_like(hvec)
        vec[0:6] = vg_ref[0:6]
        vec[8 : 8 + groups] = bg_ref[0:groups]
        early[0]()

    @pl.when(step == 1)
    def _():
        load(1).wait()
        load(2).wait()

    @pl.when(step == 2)
    def _():
        a[0]()
        early[1]()

    @pl.when(step == 4)
    def _():
        early[2]()
        middle()
        a[1]()

    @pl.when(step == 5)
    def _():
        c[1]()

    @pl.when(step == 6)
    def _():
        a[3]()
        early[3]()

    @pl.when(step == 7)
    def _():
        finish()
        b[0]()

    rows = pl.ds(pl.multiple_of(s * length, length), length)
    row = seg_ref[pl.ds(lax.axis_index("tensor") * 2 + s, 1)]
    attend_back(pm_ref.at[0], gm_ref.at[0], lse_ref, row, gp.at[t, rows], chunk)

    for n in (0, 2, 3):
        here = slice(n * 128, (n + 1) * 128)
        gsum[t, 0:1, here] += jnp.sum(gp[t, rows, here].astype(F32), axis=0, keepdims=True)

    @pl.when(s == 1)
    def _():
        order = step // 2
        slot = jnp.where(order % 2 == 0, 2 + order // 2, t // 2)
        for n in range(2):
            here = slice(n * 256, (n + 1) * 256)
            part = dot(xt_ref[...], gp[t, :, here]).astype(BF16)
            acc[slot, :, :, :, here] = part.reshape(deep, 2, -1, 256)
        from_x = dot(xt_ref[...], gp[t, :, 512:768])
        part = dot(gbt_ref[...], gp[t, :, 512:768])
        lane = lax.broadcasted_iota(jnp.int32, part.shape, 1)
        part = jnp.where((lane >= 128) & (lane < 192), from_x, part).astype(BF16)
        acc[slot, :, :, :, 512:768] = part.reshape(deep, 2, -1, 256)

    def input_columns(n):
        here = slice(n * 256, (n + 1) * 256)
        total = gb_ref[:, here]
        for g in range(groups):
            part = gp[g, :, 640:768]
            part = halves(part, jnp.zeros_like(part))
            total = total + dot(gp[g, :, 0:512], wa_ref[g, here, 0:512], NT)
            total = total + dot(part, wa_ref[g, here, 640:768], NT)
        ig_ref[:, here] = total.astype(BF16)

    @pl.when(step == last)
    def _():
        for g in range(groups):
            for h in range(HEADS):
                at = g * cols + h * HD
                line, lane = at // 256, slice(at % 256, at % 256 + HD)
                hvec[line : line + 1, lane] = gsum[g, 0:1, Q_AT[h] : Q_AT[h] + HD]
                hvec[3 + line : 4 + line, lane] = gsum[g, 0:1, V_AT[h] : V_AT[h] + HD]
        a[2]()
        a[4]()
        a[5]()
        small[0]()
        load(3).wait()
        load(4).wait()
        input_columns(0)
        small[1]()
        a[6]()
        early[4]()
        input_columns(1)
        small[2]()
        a[7]()
        input_columns(2)
        a[8]()
        small[3]()
        b[1]()
        settle()
        found = group_sums([None] * 4 + [sb[...], sc[...], None], weights, means, squares, updates)
        small[4]()
        for k in range(3):
            lanes_of = slice(k * 256, (k + 1) * 256)
            vec[6:7, lanes_of] = hvec[k : k + 1]
            vec[7:8, lanes_of] = hvec[3 + k : 4 + k]
        count, mine = weights[4].shape
        index = lax.axis_index("dp") * groups + lax.axis_index("tensor")
        turned = pltpu.roll(vec[...], width - index * mine, 1)
        grads[4][...] = turned[0:count, 0:mine]
        found = found + group_sums(
            [None] * 6 + [grads[4][...]], weights, means, squares, updates
        )
        a[9]()
        total = sa[...]
        for k, at in enumerate((Q_AT, K_AT, V_AT)):
            grads[0][k] = collect(total, at)
        grads[1][...] = collect(total, O_AT).T
        parts = [grads[0][k] for k in range(3)] + [grads[1][...]]
        norms[...] = found + group_sums(parts + [None] * 3, weights, means, squares, updates)
        for run in final:
            run()


def group_sums(grads, weights, means, squares, updates):
    lane = lax.broadcasted_iota(jnp.int32, (8, 128), 1)
    line = lax.broadcasted_iota(jnp.int32, (8, 128), 0)
    found = jnp.zeros((8, 128), F32)
    for group, grad in enumerate(grads):
        if grad is None:
            continue
        i, k = (0, group) if group < 3 else (group - 2, ...)
        weight, mean, square = (ref[i][k] for ref in (weights, means, squares))
        update = adam_parts(grad, mean, square)[2]
        if i < 4:
            update = update + WEIGHT_DECAY * weight
        updates[i][k] = update
        if i < 4:
            pair = (sum_all(weight * weight), sum_all(update * update))
            for which in range(2):
                hit = (lane == group) & (line == which)
                found = found + jnp.where(hit, pair[which], 0.0)
            continue
        for which, values in enumerate((weight, update)):
            per_row = jnp.sum(values * values, axis=1, keepdims=True)
            for row in range(weight.shape[0]):
                hit = (lane == 6 + min(row, 8)) & (line == which)
                found = found + jnp.where(hit, per_row[row : row + 1], 0.0)
    return found


def back(pm, gm, lse, seg, wa, xt, gbt, gb, accb, part, vg, bg,
         weights, means, squares, sizes):
    deep, groups = sizes[0] // 2, sizes[1]
    tokens, width = gb.shape
    lanes = pm.shape[2]
    length = seg.shape[1]
    seqs = tokens // length
    rows = width // sizes[0]
    copies = 7 + 2 * deep + 4 + 2 * deep + 2 * (deep + 2) + 7 + deep
    small = [weights, means, squares]
    anywhere = pl.BlockSpec(memory_space=pl.ANY)
    outs = [
        jax.ShapeDtypeStruct((2,) + weights[0].shape, F32),
        jax.ShapeDtypeStruct((2,) + weights[1].shape, F32),
        jax.ShapeDtypeStruct((2, 2) + weights[2].shape, F32),
        jax.ShapeDtypeStruct((2,) + weights[4].shape, F32),
        jax.ShapeDtypeStruct((8, 128), F32),
        jax.ShapeDtypeStruct((tokens, width), BF16),
    ]
    return pl.pallas_call(
        functools.partial(back_kernel, sizes=sizes, chunk=min(256, length)),
        grid=(groups * seqs,),
        in_specs=[
            pl.BlockSpec((1, length, lanes), lambda i: (far_first(i, groups), i % 2, 0)),
            pl.BlockSpec((1, length, gm.shape[2]), lambda i: (far_first(i, groups), i % 2, 0)),
            pl.BlockSpec((1, 1, 8, length), lambda i: (far_first(i, groups), i % 2, 0, 0)),
            once(seg.shape),
            anywhere,
            anywhere,
            anywhere,
            anywhere,
            anywhere,
            once(part.shape),
            once(vg.shape),
            once(bg.shape),
        ]
        + [once(ref.shape) for group in small for ref in group],
        out_specs=[once(ref.shape) for ref in outs],
        out_shape=outs,
        scratch_shapes=[
            pltpu.VMEM((groups, tokens, lanes), BF16),
            pltpu.VMEM((groups, 8, lanes), F32),
            pltpu.SemaphoreType.DMA((copies,)),
            pltpu.SemaphoreType.DMA((copies,)),
            pltpu.VMEM((deep + 2, 16, width), F32),
            pltpu.VMEM((deep + 2, 8, 256), F32),
            pltpu.VMEM((8 + deep, 8, 128), F32),
            pltpu.VMEM((16, width), F32),
            pltpu.VMEM((8, 256), F32),
            pltpu.SemaphoreType.DMA((5,)),
            pltpu.VMEM((rows, lanes), F32),
            pltpu.VMEM(wa.shape, BF16),
            pltpu.VMEM(xt.shape, BF16),
            pltpu.VMEM(gbt.shape, BF16),
            pltpu.VMEM(gb.shape, F32),
            pltpu.VMEM(accb.shape, BF16),
            pltpu.VMEM((deep, rows, lanes), BF16),
            pltpu.VMEM((deep, rows, lanes), BF16),
        ]
        + plane_buffers(deep, rows, lanes)
        + core_buffers(deep, rows, lanes)
        + plane_buffers(deep, rows, lanes)
        + [pltpu.VMEM((deep, rows, lanes), BF16)],
        compiler_params=params(collective_id=2, has_side_effects=True),
        name="back",
    )(
        pm, gm, lse, seg, wa, xt, gbt, gb,
        accb, part, vg, bg,
        *weights, *means, *squares,
    )


def apply_kernel(*refs):
    (grads, updates), sums = changes_of(refs[0:4]), refs[4]
    weights, means, squares = refs[5:10], refs[10:15], refs[15:20]
    passed, outs, norms = refs[20:22], refs[22:37], refs[37]
    wide, sem = refs[40], refs[41]
    stores = [pltpu.make_async_copy(passed[0], refs[38], sem.at[0])]
    stores[0].start()
    rows = wide.shape[0] // 4
    for k in range(4):
        here = pl.ds(k * rows, rows)
        wide[here] = passed[1][here].astype(F32)
        stores.append(pltpu.make_async_copy(wide.at[here], refs[39].at[here], sem.at[1 + k]))
        stores[-1].start()
    roots = jnp.sqrt(sums[...])
    norms[...] = roots[0:2, 0:15]
    ratio = LEARN_RATE * roots[0:1] / (roots[1:2] + ADAM_EPS)
    for i in range(5):
        grad = grads[i][...]
        outs[3 * i][...] = MOMENT_DECAY * means[i][...] + (1.0 - MOMENT_DECAY) * grad
        outs[3 * i + 1][...] = (
            MOMENT_DECAY * squares[i][...] + (1.0 - MOMENT_DECAY) * grad * grad
        )
        target = outs[3 * i + 2]
        if i == 0:
            for k in range(3):
                target[k] = weights[i][k] - ratio[:, k : k + 1] * updates[i][k]
        elif i < 4:
            target[...] = weights[i][...] - ratio[:, 2 + i : 3 + i] * updates[i][...]
        else:
            for row in range(target.shape[0]):
                here = slice(row, row + 1)
                step = ratio[:, 6 + min(row, 8) : 7 + min(row, 8)]
                target[here] = weights[i][here] - step * updates[i][here]
    for move in stores:
        move.wait()


def apply(changes, sums, weights, means, squares, passed):
    inside = pl.BlockSpec(memory_space=pltpu.VMEM)
    shapes = []
    for weight in weights:
        shapes += [jax.ShapeDtypeStruct(weight.shape, F32)] * 3
    shapes.append(jax.ShapeDtypeStruct((2, 15), F32))
    shapes += [jax.ShapeDtypeStruct(passed[0].shape, BF16)]
    shapes += [jax.ShapeDtypeStruct(passed[1].shape, F32)]
    anywhere = [pl.BlockSpec(memory_space=pl.ANY)] * 2
    return pl.pallas_call(
        apply_kernel,
        in_specs=[inside] * 22,
        out_specs=[inside] * 16 + anywhere,
        out_shape=shapes,
        scratch_shapes=[
            pltpu.VMEM(passed[1].shape, F32),
            pltpu.SemaphoreType.DMA((5,)),
        ],
        compiler_params=params(),
        name="apply",
    )(*changes, sums, *weights, *means, *squares, *passed)


def make_body(sizes):
    def body(
        tokens, cotangent, segments,
        qkv_weight, out_weight, inner_weight, outer_weight, vectors,
        qkv_mean, out_mean, inner_mean, outer_mean, vector_mean,
        qkv_square, out_square, inner_square, outer_square, vector_square,
    ):
        groups = sizes[1]
        token_count, width = tokens.shape
        length = segments.shape[1]
        seqs = token_count // length
        cols = qkv_weight.shape[2]
        tensor_index = lax.axis_index("tensor")
        weights = (qkv_weight, out_weight, inner_weight, outer_weight, vectors)
        old_means = (qkv_mean, out_mean, inner_mean, outer_mean, vector_mean)
        old_squares = (qkv_square, out_square, inner_square, outer_square, vector_square)
        if sizes[0] % 2 == 0 and groups == 4 and qkv_weight.shape[1] == sum(C_ROWS[-1]):
            weights, old_means, old_squares = (
                entry[:3] + (entry[3].T, entry[4]) for entry in (weights, old_means, old_squares)
            )
            wa, wb, wc, hid, nlt, xt, n1, full, pm, lse, slope, second, inv1 = gather_attend(
                weights, tokens, segments, sizes
            )
            result, gb, gm, gbt, accb, part, vg, bg = layer(
                cotangent, hid, slope, second, n1, inv1, nlt, wa, wb, wc, full, sizes
            )
            *changes, sums, input_grad = back(
                pm, gm, lse, segments, wa, xt, gbt, gb, accb, part, vg, bg,
                weights, old_means, old_squares, sizes,
            )
            passed = (result, input_grad)
            new = list(
                apply(changes, sums, weights, old_means, old_squares, passed)
            )
            new[9:12] = [entry.T for entry in new[9:12]]
            return tuple(new[16:]) + tuple(new[:16])
        seg = lax.dynamic_slice_in_dim(segments, tensor_index * seqs, seqs, 0)
        seg = jnp.broadcast_to(seg[:, None, :], (seqs, 8, length))
        pack_a = spread(qkv_weight[0], qkv_weight[1], qkv_weight[2], out_weight.T).astype(BF16)
        pack_b = inner_weight.astype(BF16)
        pack_c = outer_weight.T.astype(BF16)
        wa, wb, wc = (gather_blocks(pack, sizes) for pack in (pack_a, pack_b, pack_c))
        full = lax.all_gather(vectors, ("dp", "tensor"), axis=1, tiled=True)
        q_bias = full[6].reshape(groups, cols)
        v_bias = full[7].reshape(groups, cols)
        none = jnp.zeros_like(q_bias)
        proj_bias = spread(q_bias, none, v_bias, none)
        proj_bias = jnp.broadcast_to(proj_bias[:, None, :], (groups, 8, 4 * cols))
        inner_bias = full[8:].reshape(groups, -1)
        pm, lse = attend_fwd(tokens, wa, proj_bias, seg, length)
        result, hid, gi, nl, gsl, gbl, gb, gm, vg, bg = ffn(
            tokens, cotangent, pm, wa, wb, wc, full, inner_bias
        )
        gp, gsum = attend_bwd(pm, gm, lse, seg)

        grad_c = jnp.einsum("td,gtf->gdf", gsl, hid, preferred_element_type=F32).astype(BF16)
        grad_b = jnp.einsum("td,gtf->gdf", nl, gi, preferred_element_type=F32).astype(BF16)
        from_tokens = jnp.einsum("td,gtc->gdc", tokens, gp, preferred_element_type=F32)
        from_branch = jnp.einsum("td,gtc->gdc", gbl, pm, preferred_element_type=F32)
        lane = lax.broadcasted_iota(jnp.int32, (1, 1, LANES), 2)
        is_mixed = (lane >= 512) & ((lane < 640) | (lane >= 704))
        grad_a = jnp.where(is_mixed, from_branch, from_tokens).astype(BF16)
        input_grad = gb + jnp.einsum(
            "gtc,gdc->td",
            jnp.where(is_mixed, jnp.zeros((), BF16), gp),
            wa,
            preferred_element_type=F32,
        )
        head_rows = jnp.stack([collect(gsum[:, 0], at).reshape(-1) for at in (Q_AT, V_AT)])
        vector_grad = jnp.concatenate([vg[:6], head_rows, bg[:groups].reshape(-1, width)], axis=0)
        sum_a, sum_b, sum_c = (
            scatter_blocks(grad, sizes).astype(F32) for grad in (grad_a, grad_b, grad_c)
        )
        vector_sum = lax.psum_scatter(
            vector_grad, ("dp", "tensor"), scatter_dimension=1, tiled=True
        )
        new = lamb_plain(sum_a, sum_b, sum_c, vector_sum, weights, old_means, old_squares)
        return (result, input_grad) + tuple(new)

    return body

def solution(mesh):
    sizes = (mesh.shape["dp"], mesh.shape["tensor"])
    rows = P(("dp", "tensor"), None)
    qkv = P(None, "dp", "tensor")
    out = P("tensor", "dp")
    inner = P("dp", "tensor")
    vec = P(None, ("dp", "tensor"))
    weights = (qkv, out, inner, out, vec)
    return jax.shard_map(
        make_body(sizes),
        mesh=mesh,
        in_specs=(rows, rows, P("dp", None)) + weights * 3,
        out_specs=(rows, rows) + (qkv,) * 3 + (out,) * 3 + (inner,) * 3 + (out,) * 3 + (vec,) * 3 + (P(),),
        check_vma=False,
    )
```
